32 devices in a mesh: parts: 2 (over y), graph: 4 (over z), feat: 2 (over x), rep: 2 (over core).
Axes of the slice: x: 2, y: 2, z: 4, core: 2. Of those that a mesh axis runs over, the one named last changes fastest.
Arguments:
- features: bfloat16 [64, 256, 128], P(('parts', 'graph'), 'feat'), parts along dimension 0, may hold values from -6 to 6
- weight: bfloat16 [256, 256], replicated, may hold values from -0.375 to 0.375
- cotangent: bfloat16 [64, 256, 128], P(('parts', 'graph'), 'feat'), parts along dimension 0, may hold values from -6 to 6
- tiles: bfloat16 [2048, 128, 128], P(('parts', 'graph', 'rep')), parts along dimension 0
- tile_row: int32 [2048], P(('parts', 'graph', 'rep')), parts along dimension 0, may hold values from 0 to 7, as said below
- tile_col: int32 [2048], P(('parts', 'graph', 'rep')), parts along dimension 0, may hold values from 0 to 31, as said below
- tile_count: int32 [16], P(('parts', 'graph', 'rep')), parts along dimension 0, may hold values from 64 to 128, as said below
Outputs:
- activated: bfloat16 [64, 256, 128], P(('parts', 'graph'), 'feat'), parts along dimension 0
- input_grad: bfloat16 [64, 256, 128], P(('parts', 'graph'), 'feat'), parts along dimension 0
- weight_grad: float32 [512, 256], P('parts', 'feat'), parts along dimension 0
The draws below stay inside these ranges and needn't reach their ends.
There are 2 independent parts, one for each index of `parts`. The reference program is written for one: setup_inputs(seed, part) draws one part's arguments, and reference() takes and returns one part's arrays. A program takes and returns all parts, laid end to end along the dimension named above; an argument that names none is the same for every part. Nothing has to cross between parts.
Inputs may be any that keep to these rules, and one draw needn't show every extreme that they name: `tile_row`: within the blocks of the list's graph index. Within each list tile_col never falls; the entries at and after tile_count repeat the last live column; the live entries of one list name at most 2 distinct blocks of any one graph index's blocks, and exactly 2 from every graph index in at least one list. `tile_count`: one list is full in every draw.
All inputs are finite; a program needn't handle non-finite values.
Results may differ from the reference program's by a relative error of at most 0.0067.
Values may be sent and summed in bfloat16 or wider, within the bound.
No kernel may reach another device: no remote copies, remote signals or barrier semaphores. Data moves between devices by JAX's collectives and lax.ppermute only.
A program may use at most 128 MiB of HBM per device.

```python
import jax
import jax.numpy as jnp
from jax import lax

F = 256
BS = 128
BLK_DEV = 8
TILE_DEV = 128
CAP = 2
BLOCKS = 32
LISTS = 8
TILES = 1024
N_REP = 2


def draw_graph(key):
    first, second, third, fourth = jax.random.split(key, 4)
    peers = BLOCKS // BLK_DEV
    scores = jax.random.randint(first, (LISTS, peers, BLK_DEV), 0, 2 ** 20)
    scores = scores * BLK_DEV + jnp.arange(BLK_DEV, dtype=jnp.int32)[None, None, :]
    scores = scores.at[0, 0, 0].set(-1)
    scores = scores.at[0, peers - 1, BLK_DEV - 1].set(-1)
    ranked = jnp.argsort(scores, axis=-1, stable=True).astype(jnp.int32)
    chosen = jnp.sort(ranked[:, :, :CAP], axis=-1)
    offsets = (jnp.arange(peers, dtype=jnp.int32) * BLK_DEV)[None, :, None]
    candidate = (chosen + offsets).reshape(LISTS, peers * CAP)
    extra = jax.random.randint(second, (LISTS, TILE_DEV - peers * CAP), 0, peers * CAP)
    cover = jnp.broadcast_to(jnp.arange(peers * CAP, dtype=jnp.int32)[None, :], (LISTS, peers * CAP))
    picks = jnp.sort(jnp.concatenate([cover, extra], axis=1), axis=1)
    cols = jnp.take_along_axis(candidate, picks, axis=1)
    count = jax.random.randint(third, (LISTS,), TILE_DEV // 2, TILE_DEV + 1)
    count = count.at[0].set(TILE_DEV)
    count = count.at[LISTS - 1].set(TILE_DEV // 2)
    last = jnp.take_along_axis(cols, (count - 1)[:, None], axis=1)
    order = jnp.arange(TILE_DEV, dtype=jnp.int32)[None, :]
    cols = jnp.where(order < count[:, None], cols, last)
    rows = jax.random.randint(fourth, (LISTS, TILE_DEV), 0, BLK_DEV)
    return (rows.reshape(-1).astype(jnp.int32), cols.reshape(-1).astype(jnp.int32), count.astype(jnp.int32))


def draw_tile_row(key, part):
    rows, cols, count = draw_graph(key)
    return rows


def draw_tile_col(key, part):
    rows, cols, count = draw_graph(key)
    return cols


def draw_tile_count(key, part):
    rows, cols, count = draw_graph(key)
    return count


def draw_tiles(key, part):
    key = jax.random.fold_in(key, 11)
    first, second = jax.random.split(key, 2)
    scale = (BS * TILE_DEV / BLK_DEV) ** (-0.5)
    pattern = jax.random.bernoulli(first, 0.5, (TILES, BS, BS)).astype(jnp.float32)
    values = jax.random.uniform(second, (TILES, BS, BS), jnp.float32, 0.25, 1.75)
    return (pattern * values * scale).astype(jnp.bfloat16)


def block_scale(key, shape, pieces, low, largest):
    loudness = 1.0
    for dim, parts in pieces:
        draws = jax.random.uniform(jax.random.fold_in(jax.random.fold_in(key, 6), dim), (parts,), jnp.float32, low / len(pieces), largest / len(pieces))
        loudness = loudness * jnp.repeat(jnp.exp(draws), shape[dim] // parts).reshape((-1,) + (1,) * (len(shape) - 1 - dim))
    return loudness


def centred(key, dims, width, reach, cuts=(), kind=jnp.bfloat16):
    factor_of = block_scale(key, dims, cuts, -0.22, 0.18) if cuts else 1.0
    drawn = jax.random.normal(key, dims, jnp.float32) * width * factor_of
    return jnp.minimum(jnp.maximum(drawn, -reach), reach).astype(kind)


def setup_inputs(seed: int = 0, part: int = 0) -> dict:
    streams_of = jax.random.split(jax.random.key(seed), 8)
    own_keys = jax.random.split(jax.random.fold_in(streams_of[7], part), 8)
    return {
        "features": centred(own_keys[0], (BLOCKS, F, BS), 1.0, 6.0, ((0, 4), (1, 2))),
        "weight": centred(streams_of[1], (F, F), F ** -0.5, 0.375),
        "cotangent": centred(own_keys[2], (BLOCKS, F, BS), 1.0, 6.0, ((0, 4), (1, 2))),
        "tiles": draw_tiles(jax.random.fold_in(jax.random.fold_in(streams_of[7], part), 71), part),
        "tile_row": draw_tile_row(jax.random.fold_in(jax.random.fold_in(streams_of[7], part), 71), part),
        "tile_col": draw_tile_col(jax.random.fold_in(jax.random.fold_in(streams_of[7], part), 71), part),
        "tile_count": draw_tile_count(jax.random.fold_in(jax.random.fold_in(streams_of[7], part), 71), part),
    }


def aggregate(values, tiles, tile_row, tile_col, tile_count):
    vals32 = values.astype(jnp.float32)
    stacked = tiles.reshape(LISTS, TILE_DEV, BS, BS)
    rows = tile_row.reshape(LISTS, TILE_DEV)
    cols = tile_col.reshape(LISTS, TILE_DEV)
    owners = jnp.arange(LISTS, dtype=jnp.int32)

    def step(total, inputs):
        blocks, row_list, col_list, count, owner = inputs
        live = (jnp.arange(TILE_DEV, dtype=jnp.int32) < count).astype(jnp.float32)
        grow = ((owner // N_REP) * BLK_DEV + row_list).astype(jnp.int32)
        blocks32 = blocks.astype(jnp.float32)
        far = vals32[col_list]
        near = vals32[grow]
        own = jnp.einsum('tnm,tfm->tfn', blocks32, far) * live[:, None, None]
        back = jnp.einsum('tnm,tfn->tfm', blocks32, near) * live[:, None, None]
        total = total.at[grow].add(own)
        total = total.at[col_list].add(back)
        return total, None

    start = jnp.zeros(values.shape, jnp.float32)
    total, _ = lax.scan(step, start, (stacked, rows, cols, tile_count, owners))
    return total


def reference(features, weight, cotangent, tiles, tile_row, tile_col, tile_count):
    aggregated = aggregate(features, tiles, tile_row, tile_col, tile_count)
    smoothed = aggregated.astype(jnp.bfloat16)
    wide32 = smoothed.astype(jnp.float32)
    weight32 = weight.astype(jnp.float32)
    pre = jnp.einsum('bin,ij->bjn', wide32, weight32)
    activated = jax.nn.silu(pre).astype(jnp.bfloat16)
    sig = jax.nn.sigmoid(pre)
    pre_grad = (cotangent.astype(jnp.float32) * sig * (1.0 + pre * (1.0 - sig))).astype(jnp.bfloat16)
    grad32 = pre_grad.astype(jnp.float32)
    weight_grad = jnp.einsum('bin,bjn->ij', wide32, grad32)
    spread = jnp.einsum('bjn,ij->bin', grad32, weight32).astype(jnp.bfloat16)
    back_sum = aggregate(spread, tiles, tile_row, tile_col, tile_count)
    input_grad = back_sum.astype(jnp.bfloat16)
    return (activated, input_grad, weight_grad)
```

```python
import functools

import jax
import jax.numpy as jnp
from jax import lax
from jax.experimental import pallas as pl
from jax.experimental.pallas import tpu as pltpu
from jax.sharding import PartitionSpec as P

CAP = 2
GROUP = 8
CHUNK = 16
VMEM_LIMIT = 40 * 2 ** 20

NT = (((1,), (1,)), ((), ()))
TN = (((0,), (0,)), ((), ()))


def vmem():
    return pl.BlockSpec(memory_space=pltpu.VMEM)


def smem():
    return pl.BlockSpec(memory_space=pltpu.SMEM)


def params():
    return pltpu.CompilerParams(vmem_limit_bytes=VMEM_LIMIT)


def cost(flops, bytes_accessed):
    return pl.CostEstimate(flops=flops, bytes_accessed=bytes_accessed, transcendentals=0)


def dot(a, b, dims=None):
    if dims is None:
        return jnp.dot(a, b, preferred_element_type=jnp.float32)
    return lax.dot_general(a, b, dims, preferred_element_type=jnp.float32)


def request_kernel(peers, blocks_dev, count_ref, col_ref, *out_refs):
    me = lax.axis_index("graph")
    col = col_ref[...]
    lane = lax.broadcasted_iota(jnp.int32, col.shape, 1)
    live = lane < count_ref[0]
    for k in range(peers):
        local = col - lax.rem(me + k, peers) * blocks_dev
        inside = live & (local >= 0) & (local < blocks_dev)
        low = jnp.min(jnp.where(inside, local, blocks_dev - 1), axis=1, keepdims=True)
        high = jnp.max(jnp.where(inside, local, 0), axis=1, keepdims=True)
        out_refs[k][...] = jnp.where(lane == 0, low, high)


def request(tile_col, tile_count, peers, blocks_dev):
    per = tile_col.shape[0]
    return pl.pallas_call(
        functools.partial(request_kernel, peers, blocks_dev),
        out_shape=[jax.ShapeDtypeStruct((1, per), jnp.int32)] * peers,
        in_specs=[smem(), vmem()],
        out_specs=[vmem()] * peers,
        compiler_params=params(),
        cost_estimate=cost(1000, 4096),
        name="request",
    )(tile_count, tile_col.reshape(1, per))


def operator_kernel(
    peers, blocks_dev, slots_here, groups, row_ref, col_ref, count_ref, tiles_ref, out_ref, tiles, acc, sems
):
    step = pl.program_id(0)
    per, width = tiles.shape[0], tiles.shape[1]
    chunks = per // CHUNK
    spare = slots_here * blocks_dev

    def chunk_copy(c):
        part = pl.ds(c * CHUNK, CHUNK)
        return pltpu.make_async_copy(tiles_ref.at[part], tiles.at[part], sems.at[c])

    @pl.when(step == 0)
    def _():
        for c in range(chunks):
            chunk_copy(c).start()

    me = lax.axis_index("graph")
    count = count_ref[0]
    acc[...] = jnp.zeros_like(acc)

    def add_chunk(c, carry):
        last_peer, first_col = carry

        @pl.when(step == 0)
        def _():
            chunk_copy(c).wait()

        for u in range(CHUNK):
            t = c * CHUNK + u
            col = col_ref[t]
            peer = col // blocks_dev
            first_col = jnp.where(peer == last_peer, first_col, col)
            last_peer = peer
            ahead = lax.rem(peer - me + peers, peers)
            slot = ahead * CAP + (col != first_col).astype(jnp.int32) - step * slots_here
            here = t < count
            if groups > 1:
                here = here & (slot >= 0) & (slot < slots_here)
            place = jnp.where(here, slot * blocks_dev + row_ref[t], spare)
            acc[place] = acc[place] + tiles[t].astype(jnp.float32)
        return (last_peer, first_col)

    lax.fori_loop(0, chunks, add_chunk, (jnp.int32(-1), jnp.int32(-1)))
    for s in range(slots_here):
        for r in range(blocks_dev):
            out_ref[r * width : (r + 1) * width, s * width : (s + 1) * width] = acc[
                s * blocks_dev + r
            ].astype(jnp.bfloat16)


def list_operator(tiles, tile_row, tile_col, tile_count, peers, blocks_dev):
    per, width = tiles.shape[0], tiles.shape[1]
    slots = peers * CAP
    slots_here = min(slots, GROUP)
    groups = slots // slots_here
    return pl.pallas_call(
        functools.partial(operator_kernel, peers, blocks_dev, slots_here, groups),
        grid=(groups,),
        out_shape=jax.ShapeDtypeStruct((blocks_dev * width, slots * width), jnp.bfloat16),
        in_specs=[smem(), smem(), smem(), pl.BlockSpec(memory_space=pl.ANY)],
        out_specs=pl.BlockSpec((blocks_dev * width, slots_here * width), lambda i: (0, i)),
        scratch_shapes=[
            pltpu.VMEM((per, width, width), jnp.bfloat16),
            pltpu.VMEM((slots_here * blocks_dev + 1, width, width), jnp.float32),
            pltpu.SemaphoreType.DMA((per // CHUNK,)),
        ],
        compiler_params=params(),
        cost_estimate=cost(0, 16 * 2 ** 20),
        name="operator",
    )(tile_row, tile_col, tile_count, tiles)


def fill_sends(peers, x3, m_ref, asked_refs, mir, send_refs, self_ref, extra):
    blocks_dev, _, width = x3.shape
    slots = peers * CAP
    near = jnp.concatenate([x3[b] for b in range(blocks_dev)], axis=1)
    part = min(slots, GROUP) * width
    if slots <= GROUP:
        mir[...] = dot(near, m_ref[...])
    else:

        @pl.loop(0, slots // GROUP)
        def _(i):
            where = pl.ds(pl.multiple_of(i * part, part), part)
            mir[:, where] = dot(near, m_ref[:, where])

    self_ref[...] = mir[:, : CAP * width]
    for k in range(1, peers):
        out = send_refs[k - 1]
        out[:, : CAP * width] = mir[:, k * CAP * width : (k + 1) * CAP * width].astype(jnp.bfloat16)
        asked = asked_refs[peers - k]
        for s in range(CAP):
            at = (CAP + s) * width
            out[:, at : at + width] = x3[asked[0, s]]
        if extra is not None:
            out[:, 2 * CAP * width :] = extra


def send_kernel(peers, *refs):
    asked_refs, refs = refs[:peers], refs[peers:]
    x3, m_ref = refs[0], refs[1]
    send_refs, self_ref, mir = refs[2 : 1 + peers], refs[1 + peers], refs[2 + peers]
    fill_sends(peers, x3, m_ref, asked_refs, mir, send_refs, self_ref, None)


def sends_of(values, operator, asked, peers):
    _, columns, width = values.shape
    slots = peers * CAP
    outs = pl.pallas_call(
        functools.partial(send_kernel, peers),
        out_shape=[jax.ShapeDtypeStruct((columns, 2 * CAP * width), jnp.bfloat16)] * (peers - 1)
        + [jax.ShapeDtypeStruct((columns, CAP * width), jnp.float32)],
        in_specs=[smem()] * peers + [vmem(), vmem()],
        out_specs=[vmem()] * peers,
        scratch_shapes=[pltpu.VMEM((columns, slots * width), jnp.float32)],
        compiler_params=params(),
        cost_estimate=cost(2 ** 29, 4 * 2 ** 20),
        name="mirrored",
    )(*asked, values, operator)
    return outs[:-1], outs[-1]


def sum_rows(peers, x3, m_ref, asked_refs, recv_refs, self_ref, far, acc, out_ref):
    blocks_dev, columns, width = x3.shape
    slots = peers * CAP
    for s in range(CAP):
        far[:, s * width : (s + 1) * width] = x3[asked_refs[0][0, s]]
    for k in range(1, peers):
        at = (peers - k) * CAP * width
        far[:, at : at + CAP * width] = recv_refs[k - 1][:, CAP * width : 2 * CAP * width]
    part = min(slots, GROUP) * width
    if slots <= GROUP:
        own = dot(far[...], m_ref[...], NT)
    else:

        def add_group(i, total):
            where = pl.ds(pl.multiple_of(i * part, part), part)
            return total + dot(far[:, where], m_ref[:, where], NT)

        start = jnp.zeros((columns, blocks_dev * width), jnp.float32)
        own = lax.fori_loop(0, slots // GROUP, add_group, start)
    for b in range(blocks_dev):
        acc[b] = own[:, b * width : (b + 1) * width]
    for s in range(CAP):
        block = asked_refs[0][0, s]
        acc[block] = acc[block] + self_ref[:, s * width : (s + 1) * width]
    for k in range(1, peers):
        for s in range(CAP):
            block = asked_refs[k][0, s]
            came = recv_refs[k - 1][:, s * width : (s + 1) * width]
            acc[block] = acc[block] + came.astype(jnp.float32)
    out_ref[...] = acc[...].astype(jnp.bfloat16)


def rows_kernel(peers, *refs):
    asked_refs, refs = refs[:peers], refs[peers:]
    recv_refs, refs = refs[: peers - 1], refs[peers - 1 :]
    x3, m_ref, self_ref, out_ref, far, acc = refs
    sum_rows(peers, x3, m_ref, asked_refs, recv_refs, self_ref, far, acc, out_ref)


def rows_of(values, operator, asked, received, own_mirror, peers):
    blocks_dev, columns, width = values.shape
    slots = peers * CAP
    return pl.pallas_call(
        functools.partial(rows_kernel, peers),
        out_shape=jax.ShapeDtypeStruct(values.shape, jnp.bfloat16),
        in_specs=[smem()] * peers + [vmem()] * (peers + 2),
        out_specs=vmem(),
        scratch_shapes=[
            pltpu.VMEM((columns, slots * width), jnp.bfloat16),
            pltpu.VMEM((blocks_dev, columns, width), jnp.float32),
        ],
        compiler_params=params(),
        cost_estimate=cost(2 ** 29, 4 * 2 ** 20),
        name="rows",
    )(*asked, *received, values, operator, own_mirror)


def dense_kernel(peers, feats, reps, *refs):
    asked_refs, refs = refs[:peers], refs[peers:]
    sums, refs = refs[: feats * reps], refs[feats * reps :]
    cots, refs = refs[:feats], refs[feats:]
    w_ref, m_ref, refs = refs[0], refs[1], refs[2:]
    send_refs, refs = refs[: peers - 1], refs[peers - 1 :]
    self_ref, act_ref, spread_ref, term_ref, mir, wide, wide_cot, pre_scr, grad = refs
    blocks_dev, columns, width = act_ref.shape
    me = lax.axis_index("feat")
    half = lax.axis_index("rep")
    rows = [pl.ds(pl.multiple_of(lax.rem(me + q, feats) * columns, columns), columns) for q in range(feats)]
    for q in range(feats):
        for b in range(blocks_dev):
            total = sums[q * reps][b].astype(jnp.float32)
            for e in range(1, reps):
                total = total + sums[q * reps + e][b].astype(jnp.float32)
            wide[rows[q], b * width : (b + 1) * width] = total.astype(jnp.bfloat16)
            wide_cot[rows[q], b * width : (b + 1) * width] = cots[q][b]
    weight = w_ref[...]
    pre = dot(weight, wide[...], TN)
    pre_scr[...] = pre
    sig = jax.nn.sigmoid(pre)
    factor = wide_cot[...].astype(jnp.float32) * sig * (1.0 + pre * (1.0 - sig))
    grad[...] = factor.astype(jnp.bfloat16)
    spread = dot(w_ref[rows[0], :], grad[...]).astype(jnp.bfloat16)
    for b in range(blocks_dev):
        spread_ref[b] = spread[:, b * width : (b + 1) * width]
    own = pre_scr[rows[0], :]
    act = (own * jax.nn.sigmoid(own)).astype(jnp.bfloat16)
    for b in range(blocks_dev):
        act_ref[b] = act[:, b * width : (b + 1) * width]
    share = wide.shape[0] // reps
    part = pl.ds(pl.multiple_of(half * share, share), share)
    term = dot(grad[rows[0], :], wide[part, :], NT).astype(jnp.bfloat16)
    term_ref[...] = term
    fill_sends(peers, spread_ref, m_ref, asked_refs, mir, send_refs, self_ref, term)


def dense(sums, cots, weight, operator, asked, peers, feats, reps):
    blocks_dev, columns, width = sums[0].shape
    slots = peers * CAP
    features = weight.shape[0]
    share = features // reps
    outs = pl.pallas_call(
        functools.partial(dense_kernel, peers, feats, reps),
        out_shape=[jax.ShapeDtypeStruct((columns, 2 * CAP * width + share), jnp.bfloat16)] * (peers - 1)
        + [
            jax.ShapeDtypeStruct((columns, CAP * width), jnp.float32),
            jax.ShapeDtypeStruct((blocks_dev, columns, width), jnp.bfloat16),
            jax.ShapeDtypeStruct((blocks_dev, columns, width), jnp.bfloat16),
            jax.ShapeDtypeStruct((columns, share), jnp.bfloat16),
        ],
        in_specs=[smem()] * peers + [vmem()] * (feats * reps + feats + 2),
        out_specs=[vmem()] * (peers + 3),
        scratch_shapes=[
            pltpu.VMEM((columns, slots * width), jnp.float32),
            pltpu.VMEM((features, blocks_dev * width), jnp.bfloat16),
            pltpu.VMEM((features, blocks_dev * width), jnp.bfloat16),
            pltpu.VMEM((features, blocks_dev * width), jnp.float32),
            pltpu.VMEM((features, blocks_dev * width), jnp.bfloat16),
        ],
        compiler_params=params(),
        cost_estimate=cost(2 ** 30, 8 * 2 ** 20),
        name="dense",
    )(*asked, *sums, *cots, weight, operator)
    return outs[: peers - 1], outs[peers - 1], outs[peers], outs[peers + 1], outs[peers + 2]


def last_rows_kernel(peers, *refs):
    asked_refs, refs = refs[:peers], refs[peers:]
    recv_refs, refs = refs[: peers - 1], refs[peers - 1 :]
    x3, m_ref, self_ref, term_ref, out_ref, share_ref, far, acc, terms = refs
    width = x3.shape[2]
    me = lax.axis_index("graph")
    terms[0] = term_ref[...].astype(jnp.float32)
    for k in range(1, peers):
        terms[k] = recv_refs[k - 1][:, 2 * CAP * width :].astype(jnp.float32)
    total = terms[lax.rem(me, peers)]
    for p in range(1, peers):
        total = total + terms[lax.rem(me - p + peers, peers)]
    share_ref[...] = total
    sum_rows(peers, x3, m_ref, asked_refs, recv_refs, self_ref, far, acc, out_ref)


def last_rows(values, operator, asked, received, own_mirror, term, peers):
    blocks_dev, columns, width = values.shape
    slots = peers * CAP
    return pl.pallas_call(
        functools.partial(last_rows_kernel, peers),
        out_shape=[
            jax.ShapeDtypeStruct(values.shape, jnp.bfloat16),
            jax.ShapeDtypeStruct(term.shape, jnp.float32),
        ],
        in_specs=[smem()] * peers + [vmem()] * (peers + 3),
        out_specs=[vmem()] * 2,
        scratch_shapes=[
            pltpu.VMEM((columns, slots * width), jnp.bfloat16),
            pltpu.VMEM((blocks_dev, columns, width), jnp.float32),
            pltpu.VMEM((peers,) + term.shape, jnp.float32),
        ],
        compiler_params=params(),
        cost_estimate=cost(2 ** 29, 4 * 2 ** 20),
        name="last_rows",
    )(*asked, *received, values, operator, own_mirror, term)


def finish_kernel(mine_ref, other_ref, share_ref, other_share_ref, grad_ref, weight_ref):
    half = lax.axis_index("rep")
    share = share_ref.shape[1]
    grad_ref[...] = (mine_ref[...].astype(jnp.float32) + other_ref[...].astype(jnp.float32)).astype(
        jnp.bfloat16
    )
    weight_ref[pl.ds(pl.multiple_of(half * share, share), share), :] = share_ref[...].T
    weight_ref[pl.ds(pl.multiple_of((1 - half) * share, share), share), :] = other_share_ref[...].T


def finish(mine, other, share, other_share):
    columns, width = share.shape
    return pl.pallas_call(
        finish_kernel,
        out_shape=[
            jax.ShapeDtypeStruct(mine.shape, jnp.bfloat16),
            jax.ShapeDtypeStruct((2 * width, columns), jnp.float32),
        ],
        in_specs=[vmem()] * 4,
        out_specs=[vmem()] * 2,
        compiler_params=params(),
        cost_estimate=cost(0, 2 ** 20),
        name="finish",
    )(mine, other, share, other_share)


def ahead(value, axis, size, k):
    return lax.ppermute(value, axis, [(i, (i + k) % size) for i in range(size)])


def local(features, weight, cotangent, tiles, tile_row, tile_col, tile_count):
    blocks_dev, columns, width = features.shape
    peers = lax.axis_size("graph")
    feats = lax.axis_size("feat")
    reps = lax.axis_size("rep")
    wanted = request(tile_col, tile_count, peers, blocks_dev)
    asked = [wanted[0]] + [ahead(wanted[k], "graph", peers, k) for k in range(1, peers)]
    operator = list_operator(tiles, tile_row, tile_col, tile_count, peers, blocks_dev)
    cots = [cotangent] + [ahead(cotangent, "feat", feats, feats - q) for q in range(1, feats)]
    sends, own_mirror = sends_of(features, operator, asked, peers)
    received = [ahead(sends[k - 1], "graph", peers, k) for k in range(1, peers)]
    part = rows_of(features, operator, asked, received, own_mirror, peers)
    sums = []
    for q in range(feats):
        for e in range(reps):
            perm = [
                (f * reps + r, ((f - q) % feats) * reps + (r + e) % reps)
                for f in range(feats)
                for r in range(reps)
            ]
            sums.append(part if q + e == 0 else lax.ppermute(part, ("feat", "rep"), perm))
    sends, own_mirror, activated, spread, term = dense(
        sums, cots, weight, operator, asked, peers, feats, reps
    )
    received = [ahead(sends[k - 1], "graph", peers, k) for k in range(1, peers)]
    part, share = last_rows(spread, operator, asked, received, own_mirror, term, peers)
    input_grad, weight_grad = finish(
        part, ahead(part, "rep", reps, 1), share, ahead(share, "rep", reps, 1)
    )
    return (activated, input_grad, weight_grad)


def solution(mesh):
    placed = (
        P(("parts", "graph"), "feat", None),
        P(),
        P(("parts", "graph"), "feat", None),
        P(("parts", "graph", "rep"), None, None),
        P(("parts", "graph", "rep")),
        P(("parts", "graph", "rep")),
        P(("parts", "graph", "rep")),
    )
    return jax.shard_map(
        local,
        mesh=mesh,
        in_specs=placed,
        out_specs=(
            P(("parts", "graph"), "feat", None),
            P(("parts", "graph"), "feat", None),
            P("parts", "feat"),
        ),
        check_vma=False,
    )
```

```python
import functools

import jax
import jax.numpy as jnp
from jax import lax
from jax.experimental import pallas as pl
from jax.experimental.pallas import tpu as pltpu
from jax.sharding import PartitionSpec as P

CAP = 2
GROUP = 8
CHUNK = 16
TAIL = 16
VMEM_LIMIT = 40 * 2 ** 20
VMEM_MOST = 50 * 2 ** 20

NT = (((1,), (1,)), ((), ()))
TN = (((0,), (0,)), ((), ()))
F32 = jnp.float32
BF16 = jnp.bfloat16


def vmem():
    return pl.BlockSpec(memory_space=pltpu.VMEM)


def smem():
    return pl.BlockSpec(memory_space=pltpu.SMEM)


def hbm():
    return pl.BlockSpec(memory_space=pltpu.HBM)


def shape(dims, dtype):
    return jax.ShapeDtypeStruct(tuple(dims), dtype)


def dot(a, b, dims=None):
    if dims is None:
        return jnp.dot(a, b, preferred_element_type=F32)
    return lax.dot_general(a, b, dims, preferred_element_type=F32)


def call(kernel, name, outs, in_specs, scratch=(), flops=0, moved=2 ** 18, limit=VMEM_LIMIT, **kwargs):
    return pl.pallas_call(
        kernel,
        out_shape=outs,
        in_specs=in_specs,
        scratch_shapes=list(scratch),
        compiler_params=pltpu.CompilerParams(vmem_limit_bytes=limit),
        cost_estimate=pl.CostEstimate(flops=flops, bytes_accessed=moved, transcendentals=0),
        name=name,
        **kwargs,
    )


def lanes(x3):
    return jnp.concatenate([x3[b] for b in range(x3.shape[0])], axis=1)


def wanted_of(col, count, peer, blocks_dev):
    lane = lax.broadcasted_iota(jnp.int32, col.shape, 1)
    local = col - peer * blocks_dev
    inside = (lane < count) & (local >= 0) & (local < blocks_dev)
    low = jnp.min(jnp.where(inside, local, blocks_dev - 1), axis=1, keepdims=True)
    high = jnp.max(jnp.where(inside, local, 0), axis=1, keepdims=True)
    return low, high


def put_mirror(out_ref, sums, low, high):
    columns, both = sums.shape
    out_ref[:columns, :] = sums.astype(BF16)
    lane = lax.broadcasted_iota(jnp.int32, (TAIL, both), 1)
    out_ref[columns:, :] = jnp.where(lane < both // CAP, low, high).astype(F32).astype(BF16)


def mirror_outs(peers, near, m_ref, col_ref, count_ref, blocks_dev, mir, mirror_refs, self_ref, ids_ref):
    me = lax.axis_index("graph")
    width = near.shape[1] // blocks_dev
    both = CAP * width
    slots = peers * CAP
    if slots <= GROUP:
        mir[...] = dot(near, m_ref[...])
    else:
        part = GROUP * width

        @pl.loop(0, slots // GROUP)
        def _(i):
            where = pl.ds(pl.multiple_of(i * part, part), part)
            mir[:, where] = dot(near, m_ref[:, where])

    count = count_ref[0]
    col = col_ref[...]
    self_ref[...] = mir[:, :both]
    low, high = wanted_of(col, count, me, blocks_dev)
    lane = lax.broadcasted_iota(jnp.int32, col.shape, 1)
    ids_ref[...] = jnp.where(lane == 0, low, high)
    for k in range(1, peers):
        low, high = wanted_of(col, count, lax.rem(me + k, peers), blocks_dev)
        put_mirror(mirror_refs[k - 1], mir[:, k * both : (k + 1) * both], low, high)


def operator_kernel(peers, blocks_dev, slots_here, groups, fused, *refs):
    row_ref, col_ref, count_ref, tiles_ref = refs[:4]
    refs = refs[4:]
    if fused:
        lanes_ref, near_ref = refs[:2]
        m_ref = refs[2]
        mirror_refs, self_ref, ids_ref = refs[3 : 2 + peers], refs[2 + peers], refs[3 + peers]
        tiles, acc, sems, mir = refs[4 + peers :]
    else:
        m_ref, tiles, acc, sems = refs
    step = pl.program_id(0)
    per, width = tiles.shape[0], tiles.shape[1]
    chunks = per // CHUNK
    spare = slots_here * blocks_dev

    def chunk_copy(c):
        part = pl.ds(c * CHUNK, CHUNK)
        return pltpu.make_async_copy(tiles_ref.at[part], tiles.at[part], sems.at[c])

    @pl.when(step == 0)
    def _():
        for c in range(chunks):
            chunk_copy(c).start()

    me = lax.axis_index("graph")
    count = count_ref[0]
    acc[...] = jnp.zeros_like(acc)

    def add_chunk(c, carry):
        last_peer, first_col = carry

        @pl.when(step == 0)
        def _():
            chunk_copy(c).wait()

        for u in range(CHUNK):
            t = c * CHUNK + u
            col = col_ref[t]
            peer = col // blocks_dev
            first_col = jnp.where(peer == last_peer, first_col, col)
            last_peer = peer
            ahead_by = lax.rem(peer - me + peers, peers)
            slot = ahead_by * CAP + (col != first_col).astype(jnp.int32) - step * slots_here
            here = t < count
            if groups > 1:
                here = here & (slot >= 0) & (slot < slots_here)
            place = jnp.where(here, slot * blocks_dev + row_ref[t], spare)
            acc[place] = acc[place] + tiles[t].astype(F32)
        return (last_peer, first_col)

    lax.fori_loop(0, chunks, add_chunk, (jnp.int32(-1), jnp.int32(-1)))
    for s in range(slots_here):
        for r in range(blocks_dev):
            m_ref[r * width : (r + 1) * width, s * width : (s + 1) * width] = acc[
                s * blocks_dev + r
            ].astype(BF16)
    if fused:
        mirror_outs(
            peers, lanes(near_ref), m_ref, lanes_ref, count_ref, blocks_dev, mir, mirror_refs, self_ref, ids_ref
        )


def mirror_kernel(peers, blocks_dev, *refs):
    lanes_ref, count_ref, near_ref, m_ref = refs[:4]
    refs = refs[4:]
    mirror_outs(
        peers,
        lanes(near_ref),
        m_ref,
        lanes_ref,
        count_ref,
        blocks_dev,
        refs[peers + 1],
        refs[: peers - 1],
        refs[peers - 1],
        refs[peers],
    )


def list_operator(features, tiles, tile_row, tile_col, tile_count, peers):
    blocks_dev, columns, width = features.shape
    per = tiles.shape[0]
    slots = peers * CAP
    slots_here = min(slots, GROUP)
    groups = slots // slots_here
    fused = groups == 1
    m_shape = shape((blocks_dev * width, slots * width), BF16)
    m_spec = pl.BlockSpec((blocks_dev * width, slots_here * width), lambda i: (0, i))
    outs = [shape((columns + TAIL, CAP * width), BF16)] * (peers - 1) + [
        shape((columns, CAP * width), F32),
        shape((1, per), jnp.int32),
    ]
    mir = pltpu.VMEM((columns, slots * width), F32)
    scratch = [
        pltpu.VMEM((per, width, width), BF16),
        pltpu.VMEM((slots_here * blocks_dev + 1, width, width), F32),
        pltpu.SemaphoreType.DMA((per // CHUNK,)),
    ]
    col_lanes = tile_col.reshape(1, per)
    kernel = functools.partial(operator_kernel, peers, blocks_dev, slots_here, groups, fused)
    ins = [smem(), smem(), smem(), hbm()]
    if fused:
        made = call(
            kernel,
            "operator",
            [m_shape] + outs,
            ins + [vmem(), vmem()],
            scratch + [mir],
            flops=2 ** 28,
            moved=2 ** 24,
            limit=VMEM_MOST,
            grid=(1,),
            out_specs=[m_spec] + [vmem()] * (peers + 1),
        )(tile_row, tile_col, tile_count, tiles, col_lanes, features)
        operator, made = made[0], made[1:]
    else:
        operator = call(
            kernel, "operator", m_shape, ins, scratch, moved=2 ** 24, grid=(groups,), out_specs=m_spec
        )(tile_row, tile_col, tile_count, tiles)
        made = call(
            functools.partial(mirror_kernel, peers, blocks_dev),
            "mirrored",
            outs,
            [vmem(), smem(), vmem(), vmem()],
            [mir],
            flops=2 ** 28,
        )(col_lanes, tile_count, features, operator)
    return operator, list(made[: peers - 1]), made[peers - 1], made[peers]


def far_kernel(came_ref, x3, out_ref, ids_ref):
    _, columns, width = x3.shape
    lane = lax.broadcasted_iota(jnp.int32, ids_ref.shape, 1)
    ids = jnp.zeros(ids_ref.shape, jnp.int32)
    for s in range(CAP):
        tail = came_ref[columns:, s * width : (s + 1) * width].astype(F32)
        block = jnp.max(tail).astype(jnp.int32)
        ids = jnp.where(lane == s, block, ids)
        out_ref[:, s * width : (s + 1) * width] = x3[block]
    ids_ref[...] = ids


def far_of(came, values):
    _, columns, width = values.shape
    return call(
        far_kernel,
        "far_blocks",
        [shape((columns, CAP * width), BF16), shape((1, width), jnp.int32)],
        [vmem(), vmem()],
    )(came, values)


def own_rows(far, m_ref, firsts, width):
    both = CAP * width
    if len(firsts) <= GROUP:
        total = None
        for i, k in enumerate(firsts):
            add = dot(far[:, i * both : (i + 1) * both], m_ref[:, k * both : (k + 1) * both], NT)
            total = add if total is None else total + add
        return total
    first = firsts[0]

    def add_peer(i, total):
        here = pl.ds(pl.multiple_of(i * both, both), both)
        there = pl.ds(pl.multiple_of((i + first) * both, both), both)
        return total + dot(far[:, here], m_ref[:, there], NT)

    return lax.fori_loop(0, len(firsts), add_peer, jnp.zeros((far.shape[0], m_ref.shape[0]), F32))


def rows_kernel(peers, firsts, at, split, *refs):
    ids_refs, refs = refs[:peers], refs[peers:]
    came_refs, refs = refs[: peers - 1], refs[peers - 1 :]
    far_refs, refs = refs[: len(firsts)], refs[len(firsts) :]
    x3, m_ref, self_ref, refs = refs[0], refs[1], refs[2], refs[3:]
    outs, far, acc = refs[:-2], refs[-2], refs[-1]
    blocks_dev, columns, width = x3.shape
    both = CAP * width
    for s in range(CAP):
        far[:, s * width : (s + 1) * width] = x3[ids_refs[0][0, s]]
    for i in range(len(firsts)):
        far[:, (i + 1) * both : (i + 2) * both] = far_refs[i][:, at : at + both]
    own = own_rows(far, m_ref, [0] + firsts, width)
    for b in range(blocks_dev):
        acc[b] = own[:, b * width : (b + 1) * width]
    for s in range(CAP):
        block = ids_refs[0][0, s]
        acc[block] = acc[block] + self_ref[:, s * width : (s + 1) * width]
    for k in range(1, peers):
        for s in range(CAP):
            block = ids_refs[k][0, s]
            acc[block] = acc[block] + came_refs[k - 1][:columns, s * width : (s + 1) * width].astype(F32)
    if split:
        give_ref, keep_ref = outs
        half = lax.axis_index("rep")
        share = give_ref.shape[0]
        give_ref[...] = acc[pl.ds((1 - half) * share, share)].astype(BF16)
        keep_ref[...] = acc[pl.ds(half * share, share)]
    else:
        outs[0][...] = acc[...].astype(BF16)


def rows_of(values, operator, ids, came, fars, at, own_mirror, peers, reps, split):
    blocks_dev, columns, width = values.shape
    firsts = list(range(1, peers))
    share = (blocks_dev // reps, columns, width)
    if split:
        outs = [shape(share, BF16), shape(share, F32)]
    else:
        outs = [shape(values.shape, BF16)]
    return call(
        functools.partial(rows_kernel, peers, firsts, at, split),
        "rows",
        outs,
        [smem()] * peers + [vmem()] * (2 * (peers - 1) + 3),
        [
            pltpu.VMEM((columns, peers * CAP * width), BF16),
            pltpu.VMEM((blocks_dev, columns, width), F32),
        ],
        flops=2 ** 28,
        moved=2 ** 21,
    )(*ids, *came, *fars, values, operator, own_mirror)


def add_kernel(keep_ref, came_ref, out_ref):
    out_ref[...] = (keep_ref[...] + came_ref[...].astype(F32)).astype(BF16)


def add_up(keep, came):
    return call(add_kernel, "add_up", shape(came.shape, BF16), [vmem(), vmem()])(keep, came)


def dense_kernel(feats, *refs):
    sums, cots, refs = refs[:feats], refs[feats : 2 * feats], refs[2 * feats :]
    w_ref, act_ref, give_ref, spread_ref, keep_ref, wide, wide_cot, pre_scr, grad, term = refs
    share, columns, width = act_ref.shape
    me = lax.axis_index("feat")
    half = lax.axis_index("rep")
    rows = [pl.ds(pl.multiple_of(lax.rem(me + q, feats) * columns, columns), columns) for q in range(feats)]
    for q in range(feats):
        for b in range(share):
            wide[rows[q], b * width : (b + 1) * width] = sums[q][b]
            wide_cot[rows[q], b * width : (b + 1) * width] = cots[q][half * share + b]
    pre = dot(w_ref[...], wide[...], TN)
    pre_scr[...] = pre
    sig = jax.nn.sigmoid(pre)
    factor = wide_cot[...].astype(F32) * sig * (1.0 + pre * (1.0 - sig))
    grad[...] = factor.astype(BF16)
    spread = dot(w_ref[rows[0], :], grad[...]).astype(BF16)
    term[...] = dot(grad[rows[0], :], wide[...], NT)
    part = keep_ref.shape[1]
    give_ref[:, : share * width] = spread
    give_ref[:, share * width :] = term[:, pl.ds(pl.multiple_of((1 - half) * part, part), part)].astype(BF16)
    keep_ref[...] = term[:, pl.ds(pl.multiple_of(half * part, part), part)]
    for b in range(share):
        spread_ref[b] = spread[:, b * width : (b + 1) * width]
    own = pre_scr[rows[0], :]
    act = (own * jax.nn.sigmoid(own)).astype(BF16)
    for b in range(share):
        act_ref[b] = act[:, b * width : (b + 1) * width]


def dense(sums, cots, weight, feats, reps):
    share, columns, width = sums[0].shape
    features = weight.shape[0]
    part = features // reps
    return call(
        functools.partial(dense_kernel, feats),
        "dense",
        [
            shape((share, columns, width), BF16),
            shape((columns, share * width + part), BF16),
            shape((share, columns, width), BF16),
            shape((columns, part), F32),
        ],
        [vmem()] * (2 * feats + 1),
        [
            pltpu.VMEM((features, share * width), BF16),
            pltpu.VMEM((features, share * width), BF16),
            pltpu.VMEM((features, share * width), F32),
            pltpu.VMEM((features, share * width), BF16),
            pltpu.VMEM((columns, features), F32),
        ],
        flops=2 ** 28,
        moved=2 ** 20,
    )(*sums, *cots, weight)


def send_kernel(peers, *refs):
    ids_refs, refs = refs[:peers], refs[peers:]
    mine_ref, came_ref, keep_ref, m_ref, refs = refs[0], refs[1], refs[2], refs[3], refs[4:]
    x3, refs = refs[0], refs[1:]
    send_refs, refs = refs[: peers - 1], refs[peers - 1 :]
    self_ref, term_ref, mir = refs
    blocks_dev, columns, width = x3.shape
    share = mine_ref.shape[0]
    both = CAP * width
    half = lax.axis_index("rep")
    x3[pl.ds(half * share, share)] = mine_ref[...]
    for b in range(share):
        x3[(1 - half) * share + b] = came_ref[:, b * width : (b + 1) * width]
    term = (keep_ref[...] + came_ref[:, share * width :].astype(F32)).astype(BF16)
    term_ref[...] = term
    near = lanes(x3)
    slots = peers * CAP
    if slots <= GROUP:
        mir[...] = dot(near, m_ref[...])
    else:
        part = GROUP * width

        @pl.loop(0, slots // GROUP)
        def _(i):
            where = pl.ds(pl.multiple_of(i * part, part), part)
            mir[:, where] = dot(near, m_ref[:, where])

    self_ref[...] = mir[:, :both]
    for k in range(1, peers):
        out = send_refs[k - 1]
        out[:, :both] = mir[:, k * both : (k + 1) * both].astype(BF16)
        for s in range(CAP):
            at = (CAP + s) * width
            out[:, at : at + width] = x3[ids_refs[peers - k][0, s]]
        out[:, 2 * both :] = term


def sends_of(mine, came, keep, operator, ids, peers, reps):
    share, columns, width = mine.shape
    slots = peers * CAP
    return call(
        functools.partial(send_kernel, peers),
        "sends",
        [shape((share * reps, columns, width), BF16)]
        + [shape((columns, 2 * CAP * width + keep.shape[1]), BF16)] * (peers - 1)
        + [shape((columns, CAP * width), F32), shape(keep.shape, BF16)],
        [smem()] * peers + [vmem()] * 4,
        [pltpu.VMEM((columns, slots * width), F32)],
        flops=2 ** 28,
        moved=2 ** 21,
    )(*ids, mine, came, keep, operator)


def terms_kernel(peers, at, *refs):
    out_ref, terms = refs[peers], refs[peers + 1]
    me = lax.axis_index("graph")
    terms[0] = refs[0][...].astype(F32)
    for k in range(1, peers):
        terms[k] = refs[k][:, at:].astype(F32)
    total = terms[lax.rem(me, peers)]
    for p in range(1, peers):
        total = total + terms[lax.rem(me - p + peers, peers)]
    out_ref[...] = total


def sum_terms(terms, at):
    peers = len(terms)
    return call(
        functools.partial(terms_kernel, peers, at),
        "terms",
        shape(terms[0].shape, F32),
        [vmem()] * peers,
        [pltpu.VMEM((peers,) + terms[0].shape, F32)],
    )(*terms)


def join_kernel(mine_ref, came_ref, out_ref):
    half = lax.axis_index("rep")
    share = mine_ref.shape[0]
    out_ref[pl.ds(half * share, share)] = mine_ref[...]
    out_ref[pl.ds((1 - half) * share, share)] = came_ref[...]


def join(mine, came):
    out = shape((2 * mine.shape[0],) + mine.shape[1:], BF16)
    return call(join_kernel, "join", out, [vmem(), vmem()])(mine, came)


def finish_kernel(mine_ref, other_ref, share_ref, other_share_ref, grad_ref, weight_ref):
    half = lax.axis_index("rep")
    share = share_ref.shape[1]
    grad_ref[...] = (mine_ref[...].astype(F32) + other_ref[...].astype(F32)).astype(BF16)
    weight_ref[pl.ds(pl.multiple_of(half * share, share), share), :] = share_ref[...].T
    weight_ref[pl.ds(pl.multiple_of((1 - half) * share, share), share), :] = other_share_ref[...].T


def finish(mine, other, share, other_share):
    columns, width = share.shape
    return call(
        finish_kernel,
        "finish",
        [shape(mine.shape, BF16), shape((2 * width, columns), F32)],
        [vmem()] * 4,
    )(mine, other, share, other_share)


def ahead(value, axis, size, k):
    return lax.ppermute(value, axis, [(i, (i + k) % size) for i in range(size)])


def after(value, first):
    return lax.optimization_barrier((value, first))[0]


def shifts(peers):
    return sorted(range(1, peers), key=lambda k: (abs(2 * k - peers), k))


def local(features, weight, cotangent, tiles, tile_row, tile_col, tile_count):
    peers = lax.axis_size("graph")
    feats = lax.axis_size("feat")
    reps = lax.axis_size("rep")
    order = shifts(peers)

    operator, mirrors, own_mirror, own_ids = list_operator(
        features, tiles, tile_row, tile_col, tile_count, peers
    )
    came, ids, fars = [None] * peers, [own_ids] + [None] * (peers - 1), [None] * peers
    for k in order:
        came[k] = ahead(mirrors[k - 1], "graph", peers, k)
    for k in order:
        packed, ids[peers - k] = far_of(came[peers - k], features)
        fars[peers - k] = ahead(packed, "graph", peers, k)
    cots = [cotangent]
    if feats > 1:
        held = after(cotangent, mirrors[0])
        cots += [ahead(held, "feat", feats, feats - q) for q in range(1, feats)]
        cots, fars = lax.optimization_barrier((cots, fars))
    give, keep = rows_of(features, operator, ids, came[1:], fars[1:], 0, own_mirror, peers, reps, True)

    mine = add_up(keep, ahead(give, "rep", reps, 1))
    sums = [mine] + [ahead(mine, "feat", feats, feats - q) for q in range(1, feats)]
    act, give, spread, keep = dense(sums, cots, weight, feats, reps)
    outs = sends_of(spread, ahead(give, "rep", reps, 1), keep, operator, ids, peers, reps)
    values, sends, own_mirror, term = outs[0], outs[1:peers], outs[peers], outs[peers + 1]

    came, fars = [None] * peers, [None] * peers
    for k in order:
        came[k] = ahead(sends[k - 1], "graph", peers, k)
        fars[peers - k] = came[k]
    activated = join(act, ahead(act, "rep", reps, 1))
    (part,) = rows_of(
        values, operator, ids, came[1:], fars[1:], CAP * values.shape[2], own_mirror, peers, reps, False
    )
    share = sum_terms([term] + came[1:], 2 * CAP * values.shape[2])
    input_grad, weight_grad = finish(
        part, ahead(part, "rep", reps, 1), share, ahead(share, "rep", reps, 1)
    )
    return (activated, input_grad, weight_grad)


def solution(mesh):
    placed = (
        P(("parts", "graph"), "feat", None),
        P(),
        P(("parts", "graph"), "feat", None),
        P(("parts", "graph", "rep"), None, None),
        P(("parts", "graph", "rep")),
        P(("parts", "graph", "rep")),
        P(("parts", "graph", "rep")),
    )
    return jax.shard_map(
        local,
        mesh=mesh,
        in_specs=placed,
        out_specs=(
            P(("parts", "graph"), "feat", None),
            P(("parts", "graph"), "feat", None),
            P("parts", "feat"),
        ),
        check_vma=False,
    )
```

```python
import functools

import jax
import jax.numpy as jnp
from jax import lax
from jax.experimental import pallas as pl
from jax.experimental.pallas import tpu as pltpu
from jax.sharding import PartitionSpec as P

CAP = 2
GROUP = 8
CHUNK = 16
SIDES = 2
VMEM_LIMIT = 40 * 2 ** 20
VMEM_MOST = 50 * 2 ** 20

NT = (((1,), (1,)), ((), ()))
TN = (((0,), (0,)), ((), ()))
F32 = jnp.float32
BF16 = jnp.bfloat16


def vmem():
    return pl.BlockSpec(memory_space=pltpu.VMEM)


def smem():
    return pl.BlockSpec(memory_space=pltpu.SMEM)


def hbm():
    return pl.BlockSpec(memory_space=pltpu.HBM)


def shape(dims, dtype):
    return jax.ShapeDtypeStruct(tuple(dims), dtype)


def dot(a, b, dims=None):
    if dims is None:
        return jnp.dot(a, b, preferred_element_type=F32)
    return lax.dot_general(a, b, dims, preferred_element_type=F32)


def call(kernel, name, outs, in_specs, scratch=(), flops=0, moved=2 ** 18, limit=VMEM_LIMIT, **kwargs):
    return pl.pallas_call(
        kernel,
        out_shape=outs,
        in_specs=in_specs,
        scratch_shapes=list(scratch),
        compiler_params=pltpu.CompilerParams(vmem_limit_bytes=limit),
        cost_estimate=pl.CostEstimate(flops=flops, bytes_accessed=moved, transcendentals=0),
        name=name,
        **kwargs,
    )


def lanes(x3):
    return jnp.concatenate([x3[b] for b in range(x3.shape[0])], axis=1)


def request_kernel(peers, blocks_dev, count_ref, row_ref, col_ref, place_ref, *ask_refs):
    me = lax.axis_index("graph")
    col = col_ref[...]
    lane = lax.broadcasted_iota(jnp.int32, col.shape, 1)
    live = lane < count_ref[0]
    place = jnp.full(col.shape, peers * CAP * blocks_dev, jnp.int32)
    for k in range(peers):
        local = col - lax.rem(me + k, peers) * blocks_dev
        inside = live & (local >= 0) & (local < blocks_dev)
        low = jnp.min(jnp.where(inside, local, blocks_dev - 1), axis=1, keepdims=True)
        high = jnp.max(jnp.where(inside, local, 0), axis=1, keepdims=True)
        ask_refs[k][...] = jnp.where(lane == 0, low, high)
        slot = k * CAP + (local != low).astype(jnp.int32)
        place = jnp.where(inside, slot * blocks_dev + row_ref[...], place)
    place_ref[...] = place


def request(tile_row, tile_col, tile_count, peers, blocks_dev):
    per = tile_col.shape[0]
    outs = call(
        functools.partial(request_kernel, peers, blocks_dev),
        "request",
        [shape((1, per), jnp.int32)] * (peers + 1),
        [smem(), vmem(), vmem()],
        limit=VMEM_MOST,
    )(tile_count, tile_row.reshape(1, per), tile_col.reshape(1, per))
    return outs[0], list(outs[1:])


def operator_kernel(blocks_dev, slots_here, groups, place_ref, tiles_ref, m_ref, tiles, acc, sems):
    step = pl.program_id(0)
    per, width = tiles.shape[0], tiles.shape[1]
    chunks = per // CHUNK
    spare = slots_here * blocks_dev

    def chunk_copy(c):
        part = pl.ds(c * CHUNK, CHUNK)
        return pltpu.make_async_copy(tiles_ref.at[part], tiles.at[part], sems.at[c])

    @pl.when(step == 0)
    def _():
        for c in range(chunks):
            chunk_copy(c).start()

    acc[...] = jnp.zeros_like(acc)

    def add_chunk(c, carry):
        @pl.when(step == 0)
        def _():
            chunk_copy(c).wait()

        for u in range(CHUNK):
            t = c * CHUNK + u
            place = place_ref[0, t]
            if groups > 1:
                place = place - step * spare
                place = jnp.where((place >= 0) & (place < spare), place, spare)
            side = u % SIDES
            acc[side, place] = acc[side, place] + tiles[t].astype(F32)
        return carry

    lax.fori_loop(0, chunks, add_chunk, 0)
    for s in range(slots_here):
        for r in range(blocks_dev):
            total = acc[0, s * blocks_dev + r]
            for side in range(1, SIDES):
                total = total + acc[side, s * blocks_dev + r]
            m_ref[r * width : (r + 1) * width, s * width : (s + 1) * width] = total.astype(BF16)


def list_operator(tiles, place, peers, blocks_dev):
    per, width = tiles.shape[0], tiles.shape[1]
    slots = peers * CAP
    slots_here = min(slots, GROUP)
    groups = slots // slots_here
    return call(
        functools.partial(operator_kernel, blocks_dev, slots_here, groups),
        "operator",
        shape((blocks_dev * width, slots * width), BF16),
        [smem(), hbm()],
        [
            pltpu.VMEM((per, width, width), BF16),
            pltpu.VMEM((SIDES, slots_here * blocks_dev + 1, width, width), F32),
            pltpu.SemaphoreType.DMA((per // CHUNK,)),
        ],
        moved=2 ** 24,
        limit=VMEM_MOST,
        grid=(groups,),
        out_specs=pl.BlockSpec((blocks_dev * width, slots_here * width), lambda i: (0, i)),
    )(place, tiles)


def fill_sends(peers, x3, m_ref, ids_refs, mir, send_refs, self_ref, extra):
    blocks_dev, _, width = x3.shape
    slots = peers * CAP
    both = CAP * width
    near = lanes(x3)
    if slots <= GROUP:
        mir[...] = dot(near, m_ref[...])
    else:
        part = GROUP * width

        @pl.loop(0, slots // GROUP)
        def _(i):
            where = pl.ds(pl.multiple_of(i * part, part), part)
            mir[:, where] = dot(near, m_ref[:, where])

    self_ref[...] = mir[:, :both]
    for k in range(1, peers):
        out = send_refs[k - 1]
        out[:, :both] = mir[:, k * both : (k + 1) * both].astype(BF16)
        for s in range(CAP):
            at = (CAP + s) * width
            out[:, at : at + width] = x3[ids_refs[peers - k][0, s]]
        if extra is not None:
            out[:, 2 * both :] = extra


def first_sends_kernel(peers, *refs):
    ids_refs, refs = refs[:peers], refs[peers:]
    x3, cot, m_ref, refs = refs[0], refs[1], refs[2], refs[3:]
    cot_ref, mir = refs[peers:]
    share = cot_ref.shape[0]
    cot_ref[...] = cot[pl.ds(lax.axis_index("rep") * share, share)]
    fill_sends(peers, x3, m_ref, ids_refs, mir, refs[: peers - 1], refs[peers - 1], None)


def first_sends(values, cotangent, operator, ids, peers, reps):
    blocks_dev, columns, width = values.shape
    outs = call(
        functools.partial(first_sends_kernel, peers),
        "first_sends",
        [shape((columns, 2 * CAP * width), BF16)] * (peers - 1)
        + [shape((columns, CAP * width), F32), shape((blocks_dev // reps, columns, width), BF16)],
        [smem()] * peers + [vmem()] * 3,
        [pltpu.VMEM((columns, peers * CAP * width), F32)],
        flops=2 ** 28,
        moved=2 ** 21,
    )(*ids, values, cotangent, operator)
    return outs[: peers - 1], outs[peers - 1], outs[peers]


def add_blocks(acc, ids_ref, sums):
    width = acc.shape[2]
    for s in range(CAP):
        block = ids_ref[0, s]
        acc[block] = acc[block] + sums[:, s * width : (s + 1) * width].astype(F32)


def rows_kernel(peers, k, first, last, *refs):
    at = 0
    if first:
        own_ids, x3, self_ref = refs[:3]
        at = 3
    else:
        before = refs[0]
        at = 1
    ids_ref, came_ref, m_ref = refs[at : at + 3]
    outs = refs[at + 3 :]
    acc = outs[-1] if last else outs[0]
    blocks_dev, columns, width = acc.shape
    both = CAP * width
    there = (peers - k) * both
    own = dot(came_ref[:, both : 2 * both], m_ref[:, there : there + both], NT)
    if first:
        far = jnp.concatenate([x3[own_ids[0, s]] for s in range(CAP)], axis=1)
        own = own + dot(far, m_ref[:, :both], NT)
    for b in range(blocks_dev):
        add = own[:, b * width : (b + 1) * width]
        acc[b] = add if first else before[b] + add
    if first:
        add_blocks(acc, own_ids, self_ref)
    add_blocks(acc, ids_ref, came_ref[:, :both])
    if last == "split":
        give_ref, keep_ref = outs[:2]
        half = lax.axis_index("rep")
        share = give_ref.shape[0]
        give_ref[...] = acc[pl.ds((1 - half) * share, share)].astype(BF16)
        keep_ref[...] = acc[pl.ds(half * share, share)]
    elif last:
        outs[0][...] = acc[...].astype(BF16)


def rows_of(values, operator, ids, came, own_mirror, order, peers, reps, how):
    blocks_dev, columns, width = values.shape
    acc = None
    for k in order:
        first, last = k == order[0], how if k == order[-1] else ""
        if last == "split":
            share = (blocks_dev // reps, columns, width)
            outs = [shape(share, BF16), shape(share, F32)]
        else:
            outs = [shape(values.shape, BF16 if last else F32)]
        head = [ids[0], values, own_mirror] if first else [acc]
        specs = [smem(), vmem(), vmem()] if first else [vmem()]
        made = call(
            functools.partial(rows_kernel, peers, k, first, last),
            "rows",
            outs,
            specs + [smem(), vmem(), vmem()],
            [pltpu.VMEM(values.shape, F32)] if last else [],
            flops=2 ** 27,
            moved=2 ** 20,
            input_output_aliases={} if first or last else {0: 0},
        )(*head, ids[k], came[k], operator)
        acc = made[0]
    return made


def add_kernel(keep_ref, came_ref, out_ref):
    out_ref[...] = (keep_ref[...] + came_ref[...].astype(F32)).astype(BF16)


def add_up(keep, came):
    return call(add_kernel, "add_up", shape(came.shape, BF16), [vmem(), vmem()])(keep, came)


def dense_kernel(feats, *refs):
    sums, cots, refs = refs[:feats], refs[feats : 2 * feats], refs[2 * feats :]
    w_ref, act_ref, give_ref, spread_ref, keep_ref, wide, wide_cot, pre_scr, grad, term = refs
    share, columns, width = act_ref.shape
    me = lax.axis_index("feat")
    half = lax.axis_index("rep")
    rows = [pl.ds(pl.multiple_of(lax.rem(me + q, feats) * columns, columns), columns) for q in range(feats)]
    for q in range(feats):
        for b in range(share):
            wide[rows[q], b * width : (b + 1) * width] = sums[q][b]
            wide_cot[rows[q], b * width : (b + 1) * width] = cots[q][b]
    pre = dot(w_ref[...], wide[...], TN)
    pre_scr[...] = pre
    sig = jax.nn.sigmoid(pre)
    factor = wide_cot[...].astype(F32) * sig * (1.0 + pre * (1.0 - sig))
    grad[...] = factor.astype(BF16)
    spread = dot(w_ref[rows[0], :], grad[...]).astype(BF16)
    term[...] = dot(grad[rows[0], :], wide[...], NT)
    part = keep_ref.shape[1]
    wide_share = share * width
    give_ref[:, :wide_share] = spread
    give_ref[:, 2 * wide_share :] = term[:, pl.ds(pl.multiple_of((1 - half) * part, part), part)].astype(BF16)
    keep_ref[...] = term[:, pl.ds(pl.multiple_of(half * part, part), part)]
    for b in range(share):
        spread_ref[b] = spread[:, b * width : (b + 1) * width]
    own = pre_scr[rows[0], :]
    act = (own * jax.nn.sigmoid(own)).astype(BF16)
    give_ref[:, wide_share : 2 * wide_share] = act
    for b in range(share):
        act_ref[b] = act[:, b * width : (b + 1) * width]


def dense(sums, cots, weight, feats, reps):
    share, columns, width = sums[0].shape
    features = weight.shape[0]
    part = features // reps
    return call(
        functools.partial(dense_kernel, feats),
        "dense",
        [
            shape((share, columns, width), BF16),
            shape((columns, 2 * share * width + part), BF16),
            shape((share, columns, width), BF16),
            shape((columns, part), F32),
        ],
        [vmem()] * (2 * feats + 1),
        [
            pltpu.VMEM((features, share * width), BF16),
            pltpu.VMEM((features, share * width), BF16),
            pltpu.VMEM((features, share * width), F32),
            pltpu.VMEM((features, share * width), BF16),
            pltpu.VMEM((columns, features), F32),
        ],
        flops=2 ** 28,
        moved=2 ** 20,
    )(*sums, *cots, weight)


def send_kernel(peers, *refs):
    ids_refs, refs = refs[:peers], refs[peers:]
    mine_ref, act_ref, came_ref, keep_ref, m_ref, refs = refs[0], refs[1], refs[2], refs[3], refs[4], refs[5:]
    x3, joined, refs = refs[0], refs[1], refs[2:]
    send_refs, refs = refs[: peers - 1], refs[peers - 1 :]
    self_ref, term_ref, mir = refs
    share, _, width = mine_ref.shape
    wide_share = share * width
    half = lax.axis_index("rep")
    x3[pl.ds(half * share, share)] = mine_ref[...]
    joined[pl.ds(half * share, share)] = act_ref[...]
    for b in range(share):
        x3[(1 - half) * share + b] = came_ref[:, b * width : (b + 1) * width]
        joined[(1 - half) * share + b] = came_ref[:, wide_share + b * width : wide_share + (b + 1) * width]
    term = (keep_ref[...] + came_ref[:, 2 * wide_share :].astype(F32)).astype(BF16)
    term_ref[...] = term
    fill_sends(peers, x3, m_ref, ids_refs, mir, send_refs, self_ref, term)


def sends_of(mine, act, came, keep, operator, ids, peers, reps):
    share, columns, width = mine.shape
    whole = shape((share * reps, columns, width), BF16)
    return call(
        functools.partial(send_kernel, peers),
        "sends",
        [whole, whole]
        + [shape((columns, 2 * CAP * width + keep.shape[1]), BF16)] * (peers - 1)
        + [shape((columns, CAP * width), F32), shape(keep.shape, BF16)],
        [smem()] * peers + [vmem()] * 5,
        [pltpu.VMEM((columns, peers * CAP * width), F32)],
        flops=2 ** 28,
        moved=2 ** 21,
    )(*ids, mine, act, came, keep, operator)


def terms_kernel(peers, at, *refs):
    out_ref, terms = refs[peers], refs[peers + 1]
    me = lax.axis_index("graph")
    terms[0] = refs[0][...].astype(F32)
    for k in range(1, peers):
        terms[k] = refs[k][:, at:].astype(F32)
    total = terms[lax.rem(me, peers)]
    for p in range(1, peers):
        total = total + terms[lax.rem(me - p + peers, peers)]
    out_ref[...] = total


def sum_terms(terms, at):
    peers = len(terms)
    return call(
        functools.partial(terms_kernel, peers, at),
        "terms",
        shape(terms[0].shape, F32),
        [vmem()] * peers,
        [pltpu.VMEM((peers,) + terms[0].shape, F32)],
    )(*terms)


def finish_kernel(mine_ref, other_ref, share_ref, other_share_ref, grad_ref, weight_ref):
    half = lax.axis_index("rep")
    share = share_ref.shape[1]
    grad_ref[...] = (mine_ref[...].astype(F32) + other_ref[...].astype(F32)).astype(BF16)
    weight_ref[pl.ds(pl.multiple_of(half * share, share), share), :] = share_ref[...].T
    weight_ref[pl.ds(pl.multiple_of((1 - half) * share, share), share), :] = other_share_ref[...].T


def finish(mine, other, share, other_share):
    columns, width = share.shape
    return call(
        finish_kernel,
        "finish",
        [shape(mine.shape, BF16), shape((2 * width, columns), F32)],
        [vmem()] * 4,
    )(mine, other, share, other_share)


def ahead(value, axis, size, k):
    return lax.ppermute(value, axis, [(i, (i + k) % size) for i in range(size)])


def after(value, first):
    return lax.optimization_barrier((value, first))[0]


def shifts(peers):
    return sorted(range(1, peers), key=lambda k: (abs(2 * k - peers), k))


def local(features, weight, cotangent, tiles, tile_row, tile_col, tile_count):
    blocks_dev = features.shape[0]
    peers = lax.axis_size("graph")
    feats = lax.axis_size("feat")
    reps = lax.axis_size("rep")
    order = shifts(peers)

    place, wanted = request(tile_row, tile_col, tile_count, peers, blocks_dev)
    ids = [wanted[0]] + [ahead(wanted[k], "graph", peers, k) for k in range(1, peers)]
    place, ids = lax.optimization_barrier((place, ids))
    operator = list_operator(tiles, place, peers, blocks_dev)
    sends, own_mirror, own_cot = first_sends(features, cotangent, operator, ids, peers, reps)
    came = [None] * peers
    for k in order:
        came[k] = ahead(sends[k - 1], "graph", peers, k)
    cots = [own_cot]
    if feats > 1:
        held = after(own_cot, came[order[0]])
        cots += [ahead(held, "feat", feats, feats - q) for q in range(1, feats)]
    give, keep = rows_of(features, operator, ids, came, own_mirror, order, peers, reps, "split")

    given, cots = lax.optimization_barrier((ahead(give, "rep", reps, 1), cots))
    mine = add_up(keep, given)
    sums = [mine] + [ahead(mine, "feat", feats, feats - q) for q in range(1, feats)]
    act, give, spread, keep = dense(sums, cots, weight, feats, reps)
    outs = sends_of(spread, act, ahead(give, "rep", reps, 1), keep, operator, ids, peers, reps)
    values, activated, sends, own_mirror, term = outs[0], outs[1], outs[2 : peers + 1], outs[peers + 1], outs[peers + 2]

    came = [None] * peers
    for k in order:
        came[k] = ahead(sends[k - 1], "graph", peers, k)
    (part,) = rows_of(values, operator, ids, came, own_mirror, order, peers, reps, "whole")
    share = sum_terms([term] + came[1:], 2 * CAP * values.shape[2])
    input_grad, weight_grad = finish(
        part, ahead(part, "rep", reps, 1), share, ahead(share, "rep", reps, 1)
    )
    return (activated, input_grad, weight_grad)


def solution(mesh):
    placed = (
        P(("parts", "graph"), "feat", None),
        P(),
        P(("parts", "graph"), "feat", None),
        P(("parts", "graph", "rep"), None, None),
        P(("parts", "graph", "rep")),
        P(("parts", "graph", "rep")),
        P(("parts", "graph", "rep")),
    )
    return jax.shard_map(
        local,
        mesh=mesh,
        in_specs=placed,
        out_specs=(
            P(("parts", "graph"), "feat", None),
            P(("parts", "graph"), "feat", None),
            P("parts", "feat"),
        ),
        check_vma=False,
    )
```

```python
import functools

import jax
import jax.numpy as jnp
from jax import lax
from jax.experimental import pallas as pl
from jax.experimental.pallas import tpu as pltpu
from jax.sharding import PartitionSpec as P

CAP = 2
GROUP = 8
CHUNK = 16
SIDES = 2
TAIL = 16
VMEM_LIMIT = 40 * 2 ** 20
VMEM_MOST = 50 * 2 ** 20
VMEM_ALL = 58 * 2 ** 20

NT = (((1,), (1,)), ((), ()))
TN = (((0,), (0,)), ((), ()))
F32 = jnp.float32
BF16 = jnp.bfloat16


def vmem():
    return pl.BlockSpec(memory_space=pltpu.VMEM)


def smem():
    return pl.BlockSpec(memory_space=pltpu.SMEM)


def hbm():
    return pl.BlockSpec(memory_space=pltpu.HBM)


def shape(dims, dtype):
    return jax.ShapeDtypeStruct(tuple(dims), dtype)


def dot(a, b, dims=None):
    if dims is None:
        return jnp.dot(a, b, preferred_element_type=F32)
    return lax.dot_general(a, b, dims, preferred_element_type=F32)


def call(kernel, name, outs, in_specs, scratch=(), flops=0, moved=2 ** 18, limit=VMEM_LIMIT, **kwargs):
    return pl.pallas_call(
        kernel,
        out_shape=outs,
        in_specs=in_specs,
        scratch_shapes=list(scratch),
        compiler_params=pltpu.CompilerParams(vmem_limit_bytes=limit),
        cost_estimate=pl.CostEstimate(flops=flops, bytes_accessed=moved, transcendentals=0),
        name=name,
        **kwargs,
    )


def lanes(x3):
    return jnp.concatenate([x3[b] for b in range(x3.shape[0])], axis=1)


def prepare_kernel(peers, count_ref, row_ref, col_ref, x3, cot, place_ref, half_ref, cot_ref, *ask_refs):
    blocks_dev = x3.shape[0]
    share = half_ref.shape[0]
    mine = pl.ds(lax.axis_index("rep") * share, share)
    half_ref[...] = x3[mine]
    cot_ref[...] = cot[mine]
    me = lax.axis_index("graph")
    col = col_ref[...]
    lane = lax.broadcasted_iota(jnp.int32, col.shape, 1)
    live = lane < count_ref[0]
    place = jnp.full(col.shape, peers * CAP * blocks_dev, jnp.int32)
    for k in range(peers):
        local = col - jnp.bitwise_xor(me, k) * blocks_dev
        inside = live & (local >= 0) & (local < blocks_dev)
        low = jnp.min(jnp.where(inside, local, blocks_dev - 1), axis=1, keepdims=True)
        high = jnp.max(jnp.where(inside, local, 0), axis=1, keepdims=True)
        ask_refs[k][...] = jnp.where(lane == 0, low, high)
        slot = k * CAP + (local != low).astype(jnp.int32)
        place = jnp.where(inside, slot * blocks_dev + row_ref[...], place)
    place_ref[...] = place


def prepare(features, cotangent, tile_row, tile_col, tile_count, peers, reps):
    per = tile_col.shape[0]
    blocks_dev, columns, width = features.shape
    share = shape((blocks_dev // reps, columns, width), BF16)
    outs = call(
        functools.partial(prepare_kernel, peers),
        "prepare",
        [shape((1, per), jnp.int32), share, share] + [shape((1, per), jnp.int32)] * peers,
        [smem()] + [vmem()] * 4,
        limit=VMEM_ALL,
    )(tile_count, tile_row.reshape(1, per), tile_col.reshape(1, per), features, cotangent)
    return outs[0], outs[1], outs[2], list(outs[3:])


def pick(ids_ref, lane):
    ids = ids_ref[...].astype(F32)
    at = lax.broadcasted_iota(jnp.int32, ids.shape, 1)
    return jnp.max(jnp.where(at == lane, ids, 0.0)).astype(jnp.int32)


def operator_kernel(blocks_dev, slots_here, groups, place_in, tiles_ref, m_ref, tiles, acc, place_ref, sems, sem):
    step = pl.program_id(0)
    per, width = tiles.shape[0], tiles.shape[1]
    chunks = per // CHUNK
    spare = slots_here * blocks_dev

    def chunk_copy(c):
        part = pl.ds(c * CHUNK, CHUNK)
        return pltpu.make_async_copy(tiles_ref.at[part], tiles.at[part], sems.at[c])

    @pl.when(step == 0)
    def _():
        placed = pltpu.make_async_copy(place_in, place_ref, sem)
        placed.start()
        for c in range(chunks):
            chunk_copy(c).start()
        placed.wait()

    acc[...] = jnp.zeros_like(acc)

    def add_chunk(c, carry):
        @pl.when(step == 0)
        def _():
            chunk_copy(c).wait()

        for u in range(CHUNK):
            t = c * CHUNK + u
            place = place_ref[0, t]
            if groups > 1:
                place = place - step * spare
                place = jnp.where((place >= 0) & (place < spare), place, spare)
            side = u % SIDES
            acc[side, place] = acc[side, place] + tiles[t].astype(F32)
        return carry

    lax.fori_loop(0, chunks, add_chunk, 0)
    for s in range(slots_here):
        for r in range(blocks_dev):
            total = acc[0, s * blocks_dev + r]
            for side in range(1, SIDES):
                total = total + acc[side, s * blocks_dev + r]
            m_ref[r * width : (r + 1) * width, s * width : (s + 1) * width] = total.astype(BF16)


def list_operator(tiles, place, peers, blocks_dev):
    per, width = tiles.shape[0], tiles.shape[1]
    slots = peers * CAP
    slots_here = min(slots, GROUP)
    groups = slots // slots_here
    return call(
        functools.partial(operator_kernel, blocks_dev, slots_here, groups),
        "operator",
        shape((blocks_dev * width, slots * width), BF16),
        [pl.BlockSpec(memory_space=pl.ANY), hbm()],
        [
            pltpu.VMEM((per, width, width), BF16),
            pltpu.VMEM((SIDES, slots_here * blocks_dev + 1, width, width), F32),
            pltpu.SMEM((1, per), jnp.int32),
            pltpu.SemaphoreType.DMA((per // CHUNK,)),
            pltpu.SemaphoreType.DMA,
        ],
        moved=2 ** 24,
        limit=VMEM_MOST,
        grid=(groups,),
        out_specs=pl.BlockSpec((blocks_dev * width, slots_here * width), lambda i: (0, i)),
    )(place, tiles)


def mirrored(near, m_ref, mir, slots, width):
    if slots <= GROUP:
        mir[...] = dot(near, m_ref[...])
    else:
        part = GROUP * width

        @pl.loop(0, slots // GROUP)
        def _(i):
            where = pl.ds(pl.multiple_of(i * part, part), part)
            mir[:, where] = dot(near, m_ref[:, where])


def first_sends_kernel(peers, *refs):
    ask_refs, refs = refs[: peers - 1], refs[peers - 1 :]
    x3, m_ref, refs = refs[0], refs[1], refs[2:]
    send_refs, self_ref, mir = refs[: peers - 1], refs[peers - 1], refs[peers]
    _, columns, width = x3.shape
    both = CAP * width
    mirrored(lanes(x3), m_ref, mir, peers * CAP, width)
    self_ref[...] = mir[:, :both]
    lane = lax.broadcasted_iota(jnp.int32, (TAIL, both), 1)
    for k in range(1, peers):
        out = send_refs[k - 1]
        out[:columns, :] = mir[:, k * both : (k + 1) * both].astype(BF16)
        low, high = ask_refs[k - 1][:, :1], ask_refs[k - 1][:, 1:2]
        out[columns:, :] = jnp.where(lane < width, low, high).astype(F32).astype(BF16)


def first_sends(values, operator, asks, peers):
    _, columns, width = values.shape
    outs = call(
        functools.partial(first_sends_kernel, peers),
        "first_sends",
        [shape((columns + TAIL, CAP * width), BF16)] * (peers - 1) + [shape((columns, CAP * width), F32)],
        [vmem()] * (peers + 1),
        [pltpu.VMEM((columns, peers * CAP * width), F32)],
        flops=2 ** 28,
        moved=2 ** 21,
    )(*asks, values, operator)
    return [None] + list(outs[: peers - 1]), outs[peers - 1]


def add_sums(acc, block, sums):
    acc[block] = acc[block] + sums.astype(F32)


def own_rows(far, m_ref, k):
    both = far.shape[1]
    return dot(far, m_ref[:, k * both : (k + 1) * both], NT)


def put_rows(acc, own, before=None):
    blocks_dev, _, width = acc.shape
    for b in range(blocks_dev):
        add = own[:, b * width : (b + 1) * width]
        acc[b] = add if before is None else before[b] + add


def split_rows(acc, give_ref, keep_ref):
    half = lax.axis_index("rep")
    share = give_ref.shape[0]
    give_ref[...] = acc[pl.ds((1 - half) * share, share)].astype(BF16)
    keep_ref[...] = acc[pl.ds(half * share, share)]


def self_rows(x3, m_ref, ask_ref):
    far = jnp.concatenate([x3[pick(ask_ref, s)] for s in range(CAP)], axis=1)
    return own_rows(far, m_ref, 0)


def far_of(block, mine_ref, other_ref, ask_ref, at=0):
    half = lax.axis_index("rep")
    share = block.shape[0] // 2
    block[pl.ds(half * share, share)] = mine_ref[at * share : (at + 1) * share]
    block[pl.ds((1 - half) * share, share)] = other_ref[at * share : (at + 1) * share]
    return jnp.concatenate([block[pick(ask_ref, s)] for s in range(CAP)], axis=1)


def first_rows_kernel(peers, *refs):
    ask_ref, refs = refs[0], refs[1:]
    came_refs, refs = refs[: peers - 1], refs[peers - 1 :]
    x3, m_ref, self_ref, acc, ids_refs = refs[0], refs[1], refs[2], refs[3], refs[4:]
    _, columns, width = x3.shape
    put_rows(acc, self_rows(x3, m_ref, ask_ref))
    for s in range(CAP):
        add_sums(acc, pick(ask_ref, s), self_ref[:, s * width : (s + 1) * width])
    lane = lax.broadcasted_iota(jnp.int32, ids_refs[0].shape, 1)
    for k in range(1, peers):
        came = came_refs[k - 1]
        ids = jnp.zeros(lane.shape, jnp.int32)
        for s in range(CAP):
            here = slice(s * width, (s + 1) * width)
            asked = jnp.max(came[columns:, here].astype(F32)).astype(jnp.int32)
            ids = jnp.where(lane == s, asked, ids)
            add_sums(acc, asked, came[:columns, here])
        ids_refs[k - 1][...] = ids


def first_rows(values, operator, ask, came, own_mirror, peers):
    _, columns, width = values.shape
    outs = call(
        functools.partial(first_rows_kernel, peers),
        "first_rows",
        [shape(values.shape, F32)] + [shape((1, width), jnp.int32)] * (peers - 1),
        [vmem()] * (peers + 3),
        flops=2 ** 27,
        moved=2 ** 20,
    )(ask, *came[1:], values, operator, own_mirror)
    return outs[0], [None] + list(outs[1:])


def stack_kernel(*refs):
    share = refs[0].shape[0]
    for i, ref in enumerate(refs[:-1]):
        refs[-1][i * share : (i + 1) * share] = ref[...]


def stack(pieces):
    share, columns, width = pieces[0].shape
    out = shape((len(pieces) * share, columns, width), BF16)
    return call(stack_kernel, "stack", out, [vmem()] * len(pieces))(*pieces)


def far_rows_kernel(peers, *refs):
    ask_refs, refs = refs[: peers - 1], refs[peers - 1 :]
    before, mine_ref, other_ref, m_ref, give_ref, keep_ref, acc, block, far = refs
    both = CAP * acc.shape[2]
    for k in range(1, peers):
        far[:, k * both : (k + 1) * both] = far_of(block, mine_ref, other_ref, ask_refs[k - 1], k - 1)
    if peers * CAP <= GROUP:
        own = dot(far[:, both:], m_ref[:, both:], NT)
    else:

        def add_peer(k, total):
            here = pl.ds(pl.multiple_of(k * both, both), both)
            return total + dot(far[:, here], m_ref[:, here], NT)

        own = lax.fori_loop(1, peers, add_peer, jnp.zeros((acc.shape[1], m_ref.shape[0]), F32))
    put_rows(acc, own, before)
    split_rows(acc, give_ref, keep_ref)


def far_rows(before, asks, mine, other, operator, peers, reps):
    blocks_dev, columns, width = before.shape
    share = (blocks_dev // reps, columns, width)
    return call(
        functools.partial(far_rows_kernel, peers),
        "far_rows",
        [shape(share, BF16), shape(share, F32)],
        [vmem()] * (peers + 3),
        [
            pltpu.VMEM(before.shape, F32),
            pltpu.VMEM(before.shape, BF16),
            pltpu.VMEM((columns, peers * CAP * width), BF16),
        ],
        flops=2 ** 28,
        moved=2 ** 21,
    )(*asks[1:], before, mine, other, operator)


def late_rows_kernel(ks, first, last, *refs):
    if first:
        ask_ref, x3, self_ref = refs[:3]
    else:
        before = refs[0]
    refs = refs[3 if first else 1 :]
    ids_refs, refs = refs[: len(ks)], refs[len(ks) :]
    came_refs, refs = refs[: len(ks)], refs[len(ks) :]
    m_ref, out_ref = refs[:2]
    acc = refs[2] if last else out_ref
    width = acc.shape[2]
    both = CAP * width
    own = self_rows(x3, m_ref, ask_ref) if first else None
    for i, k in enumerate(ks):
        add = own_rows(came_refs[i][:, both : 2 * both], m_ref, k)
        own = add if own is None else own + add
    put_rows(acc, own, None if first else before)
    if first:
        for s in range(CAP):
            add_sums(acc, pick(ask_ref, s), self_ref[:, s * width : (s + 1) * width])
    for i in range(len(ks)):
        for s in range(CAP):
            add_sums(acc, pick(ids_refs[i], s), came_refs[i][:, s * width : (s + 1) * width])
    if last:
        out_ref[...] = acc[...].astype(BF16)


def late_rows(head, ids, came, ks, operator, first, last):
    values = head[1] if first else head[0]
    return call(
        functools.partial(late_rows_kernel, ks, first, last),
        "late_rows",
        shape(values.shape, BF16 if last else F32),
        [vmem()] * (len(head) + 2 * len(ks) + 1),
        [pltpu.VMEM(values.shape, F32)] if last else [],
        flops=2 ** 27,
        moved=2 ** 20,
    )(*head, *[ids[k] for k in ks], *[came[k] for k in ks], operator)


def add_kernel(keep_ref, came_ref, out_ref):
    out_ref[...] = (keep_ref[...] + came_ref[...].astype(F32)).astype(BF16)


def add_up(keep, came):
    return call(add_kernel, "add_up", shape(came.shape, BF16), [vmem(), vmem()])(keep, came)


def dense_kernel(feats, *refs):
    sums, cots, refs = refs[:feats], refs[feats : 2 * feats], refs[2 * feats :]
    w_ref, act_ref, give_ref, spread_ref, keep_ref, wide, wide_cot, pre_scr, grad, term = refs
    share, columns, width = act_ref.shape
    me = lax.axis_index("feat")
    half = lax.axis_index("rep")
    rows = [pl.ds(pl.multiple_of(lax.rem(me + q, feats) * columns, columns), columns) for q in range(feats)]
    for q in range(feats):
        for b in range(share):
            wide[rows[q], b * width : (b + 1) * width] = sums[q][b]
            wide_cot[rows[q], b * width : (b + 1) * width] = cots[q][b]
    pre = dot(w_ref[...], wide[...], TN)
    pre_scr[...] = pre
    sig = jax.nn.sigmoid(pre)
    factor = wide_cot[...].astype(F32) * sig * (1.0 + pre * (1.0 - sig))
    grad[...] = factor.astype(BF16)
    spread = dot(w_ref[rows[0], :], grad[...]).astype(BF16)
    term[...] = dot(grad[rows[0], :], wide[...], NT)
    part = keep_ref.shape[1]
    wide_share = share * width
    give_ref[:, :wide_share] = spread
    give_ref[:, 2 * wide_share :] = term[:, pl.ds(pl.multiple_of((1 - half) * part, part), part)].astype(BF16)
    keep_ref[...] = term[:, pl.ds(pl.multiple_of(half * part, part), part)]
    for b in range(share):
        spread_ref[b] = spread[:, b * width : (b + 1) * width]
    own = pre_scr[rows[0], :]
    act = (own * jax.nn.sigmoid(own)).astype(BF16)
    give_ref[:, wide_share : 2 * wide_share] = act
    for b in range(share):
        act_ref[b] = act[:, b * width : (b + 1) * width]


def dense(sums, cots, weight, feats, reps):
    share, columns, width = sums[0].shape
    features = weight.shape[0]
    part = features // reps
    return call(
        functools.partial(dense_kernel, feats),
        "dense",
        [
            shape((share, columns, width), BF16),
            shape((columns, 2 * share * width + part), BF16),
            shape((share, columns, width), BF16),
            shape((columns, part), F32),
        ],
        [vmem()] * (2 * feats + 1),
        [
            pltpu.VMEM((features, share * width), BF16),
            pltpu.VMEM((features, share * width), BF16),
            pltpu.VMEM((features, share * width), F32),
            pltpu.VMEM((features, share * width), BF16),
            pltpu.VMEM((columns, features), F32),
        ],
        flops=2 ** 28,
        moved=2 ** 20,
    )(*sums, *cots, weight)


def send_kernel(peers, *refs):
    ids_refs, refs = refs[: peers - 1], refs[peers - 1 :]
    mine_ref, came_ref, keep_ref, m_ref, refs = refs[0], refs[1], refs[2], refs[3], refs[4:]
    x3, refs = refs[0], refs[1:]
    send_refs, refs = refs[: peers - 1], refs[peers - 1 :]
    self_ref, term_ref, mir = refs
    share, _, width = mine_ref.shape
    both = CAP * width
    half = lax.axis_index("rep")
    x3[pl.ds(half * share, share)] = mine_ref[...]
    for b in range(share):
        x3[(1 - half) * share + b] = came_ref[:, b * width : (b + 1) * width]
    term = (keep_ref[...] + came_ref[:, 2 * share * width :].astype(F32)).astype(BF16)
    term_ref[...] = term
    mirrored(lanes(x3), m_ref, mir, peers * CAP, width)
    self_ref[...] = mir[:, :both]
    for k in range(1, peers):
        out = send_refs[k - 1]
        out[:, :both] = mir[:, k * both : (k + 1) * both].astype(BF16)
        for s in range(CAP):
            at = (CAP + s) * width
            out[:, at : at + width] = x3[pick(ids_refs[k - 1], s)]
    send_refs[0][:, 2 * both :] = term


def sends_of(mine, came, keep, operator, ids, peers, reps):
    share, columns, width = mine.shape
    chunk = 2 * CAP * width
    outs = call(
        functools.partial(send_kernel, peers),
        "sends",
        [shape((share * reps, columns, width), BF16), shape((columns, chunk + keep.shape[1]), BF16)]
        + [shape((columns, chunk), BF16)] * (peers - 2)
        + [shape((columns, CAP * width), F32), shape(keep.shape, BF16)],
        [vmem()] * (peers + 3),
        [pltpu.VMEM((columns, peers * CAP * width), F32)],
        flops=2 ** 28,
        moved=2 ** 21,
    )(*ids[1:], mine, came, keep, operator)
    return outs[0], [None] + list(outs[1:peers]), outs[peers], outs[peers + 1]


def pair_kernel(at, mine_ref, came_ref, out_ref):
    total = mine_ref[...].astype(F32) + came_ref[:, at:].astype(F32)
    out_ref[...] = total.astype(out_ref.dtype)


def pair_sum(mine, came, at, dtype):
    return call(functools.partial(pair_kernel, at), "pair_sum", shape(mine.shape, dtype), [vmem(), vmem()])(
        mine, came
    )


def finish_kernel(mine_ref, other_ref, share_ref, other_share_ref, act_ref, came_ref, grad_ref, weight_ref, out_ref):
    half = lax.axis_index("rep")
    share = share_ref.shape[1]
    grad_ref[...] = (mine_ref[...].astype(F32) + other_ref[...].astype(F32)).astype(BF16)
    weight_ref[pl.ds(pl.multiple_of(half * share, share), share), :] = share_ref[...].T
    weight_ref[pl.ds(pl.multiple_of((1 - half) * share, share), share), :] = other_share_ref[...].T
    blocks, _, width = act_ref.shape
    out_ref[pl.ds(half * blocks, blocks)] = act_ref[...]
    for b in range(blocks):
        at = (blocks + b) * width
        out_ref[(1 - half) * blocks + b] = came_ref[:, at : at + width]


def finish(mine, other, share, other_share, act, came):
    columns, width = share.shape
    return call(
        finish_kernel,
        "finish",
        [shape(mine.shape, BF16), shape((2 * width, columns), F32), shape(mine.shape, BF16)],
        [vmem()] * 6,
    )(mine, other, share, other_share, act, came)


def ahead(value, axis, size, k):
    return lax.ppermute(value, axis, [(i, (i + k) % size) for i in range(size)])


def across(value, peers, k):
    return lax.ppermute(value, "graph", [(i, i ^ k) for i in range(peers)])


def after(value, first):
    return lax.optimization_barrier((value, first))[0]


def local(features, weight, cotangent, tiles, tile_row, tile_col, tile_count):
    blocks_dev, _, width = features.shape
    peers = lax.axis_size("graph")
    feats = lax.axis_size("feat")
    reps = lax.axis_size("rep")
    far_first = sorted(range(1, peers), key=lambda k: (-(k & (peers // 2)), k))

    place, half, own_cot, asks = prepare(features, cotangent, tile_row, tile_col, tile_count, peers, reps)
    operator = list_operator(tiles, place, peers, blocks_dev)
    sends, own_mirror = first_sends(features, operator, asks[1:], peers)
    pieces, held = {0: half}, [0]
    bit = peers // 2
    while bit:
        for k in held:
            piece = after(pieces[k], sends[1]) if k else half
            pieces[k ^ bit] = across(piece, peers, bit)
        held = held + [k ^ bit for k in held]
        bit //= 2
    came = [None] * peers
    for k in far_first:
        came[k] = across(sends[k], peers, k)
    cots = [own_cot]
    if feats > 1:
        waited = after(own_cot, pieces[peers // 2])
        cots += [ahead(waited, "feat", feats, feats - q) for q in range(1, feats)]
    arrived = [pieces[k] for k in range(1, peers)]
    arrived, came, cots = lax.optimization_barrier((arrived, came, cots))
    stacked = stack(arrived)
    swapped = ahead(stacked, "rep", reps, 1)
    acc, ids = first_rows(features, operator, asks[0], came, own_mirror, peers)
    give, keep = far_rows(acc, asks, stacked, swapped, operator, peers, reps)

    mine = add_up(keep, ahead(give, "rep", reps, 1))
    sums = [mine] + [ahead(mine, "feat", feats, feats - q) for q in range(1, feats)]
    act, give, spread, keep = dense(sums, cots, weight, feats, reps)
    shared = ahead(give, "rep", reps, 1)
    values, sends, own_mirror, term = sends_of(spread, shared, keep, operator, ids, peers, reps)

    came = [None] * peers
    for k in far_first:
        came[k] = across(sends[k], peers, k)
    total = pair_sum(term, came[1], 2 * CAP * width, F32 if peers == 2 else BF16)
    bit = 2
    while bit < peers:
        total = pair_sum(total, across(total, peers, bit), 0, F32 if 2 * bit == peers else BF16)
        bit *= 2
    ends = [peers // 2]
    acc = late_rows([asks[0], values, own_mirror], ids, came, [k for k in range(1, peers) if k not in ends], operator, True, False)
    acc, total = lax.optimization_barrier((acc, total))
    part = late_rows([acc], ids, came, ends, operator, False, True)
    input_grad, weight_grad, activated = finish(
        part, ahead(part, "rep", reps, 1), total, ahead(total, "rep", reps, 1), act, shared
    )
    return (activated, input_grad, weight_grad)


def solution(mesh):
    placed = (
        P(("parts", "graph"), "feat", None),
        P(),
        P(("parts", "graph"), "feat", None),
        P(("parts", "graph", "rep"), None, None),
        P(("parts", "graph", "rep")),
        P(("parts", "graph", "rep")),
        P(("parts", "graph", "rep")),
    )
    return jax.shard_map(
        local,
        mesh=mesh,
        in_specs=placed,
        out_specs=(
            P(("parts", "graph"), "feat", None),
            P(("parts", "graph"), "feat", None),
            P("parts", "feat"),
        ),
        check_vma=False,
    )
```

```python
import functools

import jax
import jax.numpy as jnp
from jax import lax
from jax.experimental import pallas as pl
from jax.experimental.pallas import tpu as pltpu
from jax.sharding import PartitionSpec as P

CAP = 2
GROUP = 8
CHUNK = 16
SIDES = 2
TAIL = 16
VMEM_LIMIT = 40 * 2 ** 20
VMEM_MOST = 50 * 2 ** 20
VMEM_ALL = 58 * 2 ** 20

NT = (((1,), (1,)), ((), ()))
TN = (((0,), (0,)), ((), ()))
F32 = jnp.float32
BF16 = jnp.bfloat16


def vmem():
    return pl.BlockSpec(memory_space=pltpu.VMEM)


def smem():
    return pl.BlockSpec(memory_space=pltpu.SMEM)


def hbm():
    return pl.BlockSpec(memory_space=pltpu.HBM)


def shape(dims, dtype):
    return jax.ShapeDtypeStruct(tuple(dims), dtype)


def dot(a, b, dims=None):
    if dims is None:
        return jnp.dot(a, b, preferred_element_type=F32)
    return lax.dot_general(a, b, dims, preferred_element_type=F32)


def call(kernel, name, outs, in_specs, scratch=(), flops=0, moved=2 ** 18, limit=VMEM_LIMIT, **kwargs):
    return pl.pallas_call(
        kernel,
        out_shape=outs,
        in_specs=in_specs,
        scratch_shapes=list(scratch),
        compiler_params=pltpu.CompilerParams(vmem_limit_bytes=limit),
        cost_estimate=pl.CostEstimate(flops=flops, bytes_accessed=moved, transcendentals=0),
        name=name,
        **kwargs,
    )


def lanes(x3):
    return jnp.concatenate([x3[b] for b in range(x3.shape[0])], axis=1)


def half_kernel(x3, half_ref, sem):
    share = half_ref.shape[0]
    copy = pltpu.make_async_copy(x3.at[pl.ds(lax.axis_index("rep") * share, share)], half_ref, sem)
    copy.start()
    copy.wait()


def half_of(values, reps):
    blocks_dev, columns, width = values.shape
    anywhere = pl.BlockSpec(memory_space=pl.ANY)
    return call(
        half_kernel,
        "half",
        shape((blocks_dev // reps, columns, width), BF16),
        [anywhere],
        [pltpu.SemaphoreType.DMA],
        limit=VMEM_ALL,
        out_specs=anywhere,
    )(values)


def places(peers, blocks_dev, count, row, col, ask_refs):
    me = lax.axis_index("graph")
    lane = lax.broadcasted_iota(jnp.int32, col.shape, 1)
    live = lane < count
    place = jnp.full(col.shape, peers * CAP * blocks_dev, jnp.int32)
    for k in range(peers):
        local = col - jnp.bitwise_xor(me, k) * blocks_dev
        inside = live & (local >= 0) & (local < blocks_dev)
        low = jnp.min(jnp.where(inside, local, blocks_dev - 1), axis=1, keepdims=True)
        high = jnp.max(jnp.where(inside, local, 0), axis=1, keepdims=True)
        ask_refs[k][...] = jnp.where(lane == 0, low, high)
        slot = k * CAP + (local != low).astype(jnp.int32)
        place = jnp.where(inside, slot * blocks_dev + row, place)
    return place


def pick(ids_ref, lane):
    ids = ids_ref[...].astype(F32)
    at = lax.broadcasted_iota(jnp.int32, ids.shape, 1)
    return jnp.max(jnp.where(at == lane, ids, 0.0)).astype(jnp.int32)


def operator_kernel(peers, blocks_dev, slots_here, groups, *refs):
    count_ref, row_ref, col_ref, tiles_ref, m_ref = refs[:5]
    ask_refs, refs = refs[5 : 5 + peers], refs[5 + peers :]
    tiles, acc, place_lanes, place_ref, sems, sem = refs
    step = pl.program_id(0)
    per, width = tiles.shape[0], tiles.shape[1]
    chunks = per // CHUNK
    spare = slots_here * blocks_dev

    def chunk_copy(c):
        part = pl.ds(c * CHUNK, CHUNK)
        return pltpu.make_async_copy(tiles_ref.at[part], tiles.at[part], sems.at[c])

    @pl.when(step == 0)
    def _():
        for c in range(chunks):
            chunk_copy(c).start()
        place_lanes[...] = places(peers, blocks_dev, count_ref[...], row_ref[...], col_ref[...], ask_refs)
        placed = pltpu.make_async_copy(place_lanes, place_ref, sem)
        placed.start()
        placed.wait()

    acc[...] = jnp.zeros_like(acc)

    def add_chunk(c, carry):
        @pl.when(step == 0)
        def _():
            chunk_copy(c).wait()

        for u in range(CHUNK):
            t = c * CHUNK + u
            place = place_ref[0, t]
            if groups > 1:
                place = place - step * spare
                place = jnp.where((place >= 0) & (place < spare), place, spare)
            side = u % SIDES
            acc[side, place] = acc[side, place] + tiles[t].astype(F32)
        return carry

    lax.fori_loop(0, chunks, add_chunk, 0)
    for s in range(slots_here):
        for r in range(blocks_dev):
            total = acc[0, s * blocks_dev + r]
            for side in range(1, SIDES):
                total = total + acc[side, s * blocks_dev + r]
            m_ref[r * width : (r + 1) * width, s * width : (s + 1) * width] = total.astype(BF16)


def list_operator(tiles, tile_row, tile_col, tile_count, peers, blocks_dev):
    per, width = tiles.shape[0], tiles.shape[1]
    slots = peers * CAP
    slots_here = min(slots, GROUP)
    groups = slots // slots_here
    outs = call(
        functools.partial(operator_kernel, peers, blocks_dev, slots_here, groups),
        "operator",
        [shape((blocks_dev * width, slots * width), BF16)] + [shape((1, per), jnp.int32)] * peers,
        [vmem(), vmem(), vmem(), hbm()],
        [
            pltpu.VMEM((per, width, width), BF16),
            pltpu.VMEM((SIDES, slots_here * blocks_dev + 1, width, width), F32),
            pltpu.VMEM((1, per), jnp.int32),
            pltpu.SMEM((1, per), jnp.int32),
            pltpu.SemaphoreType.DMA((per // CHUNK,)),
            pltpu.SemaphoreType.DMA,
        ],
        moved=2 ** 24,
        limit=VMEM_MOST,
        grid=(groups,),
        out_specs=[pl.BlockSpec((blocks_dev * width, slots_here * width), lambda i: (0, i))] + [vmem()] * peers,
    )(tile_count.reshape(1, 1), tile_row.reshape(1, per), tile_col.reshape(1, per), tiles)
    return outs[0], list(outs[1:])


def mirrored(near, m_ref, mir, slots, width):
    if slots <= GROUP:
        mir[...] = dot(near, m_ref[...])
    else:
        part = GROUP * width

        @pl.loop(0, slots // GROUP)
        def _(i):
            where = pl.ds(pl.multiple_of(i * part, part), part)
            mir[:, where] = dot(near, m_ref[:, where])


def first_sends_kernel(peers, *refs):
    ask_refs, refs = refs[: peers - 1], refs[peers - 1 :]
    x3, m_ref, refs = refs[0], refs[1], refs[2:]
    send_refs, self_ref, mir = refs[: peers - 1], refs[peers - 1], refs[peers]
    _, columns, width = x3.shape
    both = CAP * width
    mirrored(lanes(x3), m_ref, mir, peers * CAP, width)
    self_ref[...] = mir[:, :both]
    lane = lax.broadcasted_iota(jnp.int32, (TAIL, both), 1)
    for k in range(1, peers):
        out = send_refs[k - 1]
        out[:columns, :] = mir[:, k * both : (k + 1) * both].astype(BF16)
        low, high = ask_refs[k - 1][:, :1], ask_refs[k - 1][:, 1:2]
        out[columns:, :] = jnp.where(lane < width, low, high).astype(F32).astype(BF16)


def first_sends(values, operator, asks, peers):
    _, columns, width = values.shape
    outs = call(
        functools.partial(first_sends_kernel, peers),
        "first_sends",
        [shape((columns + TAIL, CAP * width), BF16)] * (peers - 1) + [shape((columns, CAP * width), F32)],
        [vmem()] * (peers + 1),
        [pltpu.VMEM((columns, peers * CAP * width), F32)],
        flops=2 ** 28,
        moved=2 ** 21,
    )(*asks, values, operator)
    return [None] + list(outs[: peers - 1]), outs[peers - 1]


def add_sums(acc, block, sums):
    acc[block] = acc[block] + sums.astype(F32)


def own_rows(far, m_ref, k):
    both = far.shape[1]
    return dot(far, m_ref[:, k * both : (k + 1) * both], NT)


def put_rows(acc, own, before=None):
    blocks_dev, _, width = acc.shape
    for b in range(blocks_dev):
        add = own[:, b * width : (b + 1) * width]
        acc[b] = add if before is None else before[b] + add


def split_rows(acc, give_ref, keep_ref):
    half = lax.axis_index("rep")
    share = give_ref.shape[0]
    give_ref[...] = acc[pl.ds((1 - half) * share, share)].astype(BF16)
    keep_ref[...] = acc[pl.ds(half * share, share)]


def self_rows(x3, m_ref, ask_ref):
    far = jnp.concatenate([x3[pick(ask_ref, s)] for s in range(CAP)], axis=1)
    return own_rows(far, m_ref, 0)


def far_of(block, mine_ref, other_ref, ask_ref, at=0):
    half = lax.axis_index("rep")
    share = block.shape[0] // 2
    block[pl.ds(half * share, share)] = mine_ref[at * share : (at + 1) * share]
    block[pl.ds((1 - half) * share, share)] = other_ref[at * share : (at + 1) * share]
    return jnp.concatenate([block[pick(ask_ref, s)] for s in range(CAP)], axis=1)


def first_rows_kernel(peers, *refs):
    ask_ref, refs = refs[0], refs[1:]
    came_refs, refs = refs[: peers - 1], refs[peers - 1 :]
    x3, m_ref, self_ref, acc, ids_refs = refs[0], refs[1], refs[2], refs[3], refs[4:]
    _, columns, width = x3.shape
    put_rows(acc, self_rows(x3, m_ref, ask_ref))
    for s in range(CAP):
        add_sums(acc, pick(ask_ref, s), self_ref[:, s * width : (s + 1) * width])
    lane = lax.broadcasted_iota(jnp.int32, ids_refs[0].shape, 1)
    for k in range(1, peers):
        came = came_refs[k - 1]
        ids = jnp.zeros(lane.shape, jnp.int32)
        for s in range(CAP):
            here = slice(s * width, (s + 1) * width)
            asked = jnp.max(came[columns:, here].astype(F32)).astype(jnp.int32)
            ids = jnp.where(lane == s, asked, ids)
            add_sums(acc, asked, came[:columns, here])
        ids_refs[k - 1][...] = ids


def first_rows(values, operator, ask, came, own_mirror, peers):
    _, columns, width = values.shape
    outs = call(
        functools.partial(first_rows_kernel, peers),
        "first_rows",
        [shape(values.shape, F32)] + [shape((1, width), jnp.int32)] * (peers - 1),
        [vmem()] * (peers + 3),
        flops=2 ** 27,
        moved=2 ** 20,
    )(ask, *came[1:], values, operator, own_mirror)
    return outs[0], [None] + list(outs[1:])


def stack_kernel(*refs):
    at = 0
    for ref in refs[:-1]:
        share = ref.shape[0]
        refs[-1][at : at + share] = ref[...]
        at += share


def halves_kernel(in_ref, low_ref, high_ref):
    share = low_ref.shape[0]
    low_ref[...] = in_ref[:share]
    high_ref[...] = in_ref[share:]


def halves(parts):
    if len(parts) > 1:
        return parts
    share, columns, width = parts[0].shape
    part = shape((share // 2, columns, width), BF16)
    return list(call(halves_kernel, "halves", [part, part], [vmem()])(*parts))


def stack(pieces):
    _, columns, width = pieces[0].shape
    out = shape((sum(piece.shape[0] for piece in pieces), columns, width), BF16)
    return call(stack_kernel, "stack", out, [vmem()] * len(pieces))(*pieces)


def far_rows_kernel(peers, *refs):
    ask_refs, refs = refs[: peers - 1], refs[peers - 1 :]
    before, mine_ref, other_ref, m_ref, give_ref, keep_ref, acc, block, far = refs
    both = CAP * acc.shape[2]
    for k in range(1, peers):
        far[:, k * both : (k + 1) * both] = far_of(block, mine_ref, other_ref, ask_refs[k - 1], k - 1)
    if peers * CAP <= GROUP:
        own = dot(far[:, both:], m_ref[:, both:], NT)
    else:

        def add_peer(k, total):
            here = pl.ds(pl.multiple_of(k * both, both), both)
            return total + dot(far[:, here], m_ref[:, here], NT)

        own = lax.fori_loop(1, peers, add_peer, jnp.zeros((acc.shape[1], m_ref.shape[0]), F32))
    put_rows(acc, own, before)
    split_rows(acc, give_ref, keep_ref)


def far_rows(before, asks, mine, other, operator, peers, reps):
    blocks_dev, columns, width = before.shape
    share = (blocks_dev // reps, columns, width)
    return call(
        functools.partial(far_rows_kernel, peers),
        "far_rows",
        [shape(share, BF16), shape(share, F32)],
        [vmem()] * (peers + 3),
        [
            pltpu.VMEM(before.shape, F32),
            pltpu.VMEM(before.shape, BF16),
            pltpu.VMEM((columns, peers * CAP * width), BF16),
        ],
        flops=2 ** 28,
        moved=2 ** 21,
    )(*asks[1:], before, mine, other, operator)


def late_rows_kernel(ks, first, last, *refs):
    if first:
        ask_ref, x3, self_ref = refs[:3]
    else:
        before = refs[0]
    refs = refs[3 if first else 1 :]
    ids_refs, refs = refs[: len(ks)], refs[len(ks) :]
    came_refs, refs = refs[: len(ks)], refs[len(ks) :]
    m_ref, out_ref = refs[:2]
    acc = refs[2] if last else out_ref
    width = acc.shape[2]
    both = CAP * width
    own = self_rows(x3, m_ref, ask_ref) if first else None
    for i, k in enumerate(ks):
        add = own_rows(came_refs[i][:, both : 2 * both], m_ref, k)
        own = add if own is None else own + add
    put_rows(acc, own, None if first else before)
    if first:
        for s in range(CAP):
            add_sums(acc, pick(ask_ref, s), self_ref[:, s * width : (s + 1) * width])
    for i in range(len(ks)):
        for s in range(CAP):
            add_sums(acc, pick(ids_refs[i], s), came_refs[i][:, s * width : (s + 1) * width])
    if last:
        out_ref[...] = acc[...].astype(BF16)


def late_rows(head, ids, came, ks, operator, first, last):
    values = head[1] if first else head[0]
    return call(
        functools.partial(late_rows_kernel, ks, first, last),
        "late_rows",
        shape(values.shape, BF16 if last else F32),
        [vmem()] * (len(head) + 2 * len(ks) + 1),
        [pltpu.VMEM(values.shape, F32)] if last else [],
        flops=2 ** 27,
        moved=2 ** 20,
    )(*head, *[ids[k] for k in ks], *[came[k] for k in ks], operator)


def add_kernel(keep_ref, came_ref, out_ref):
    out_ref[...] = (keep_ref[...] + came_ref[...].astype(F32)).astype(BF16)


def add_up(keep, came):
    return call(add_kernel, "add_up", shape(came.shape, BF16), [vmem(), vmem()])(keep, came)


def dense_kernel(feats, *refs):
    sums, cots, refs = refs[:feats], refs[feats : 2 * feats], refs[2 * feats :]
    w_ref, act_ref, give_ref, spread_ref, keep_ref, wide, wide_cot, pre_scr, grad, term = refs
    share, columns, width = act_ref.shape
    me = lax.axis_index("feat")
    half = lax.axis_index("rep")
    rows = [pl.ds(pl.multiple_of(lax.rem(me + q, feats) * columns, columns), columns) for q in range(feats)]
    for q in range(feats):
        for b in range(share):
            wide[rows[q], b * width : (b + 1) * width] = sums[q][b]
            wide_cot[rows[q], b * width : (b + 1) * width] = cots[q][b]
    pre = dot(w_ref[...], wide[...], TN)
    pre_scr[...] = pre
    sig = jax.nn.sigmoid(pre)
    factor = wide_cot[...].astype(F32) * sig * (1.0 + pre * (1.0 - sig))
    grad[...] = factor.astype(BF16)
    spread = dot(w_ref[rows[0], :], grad[...]).astype(BF16)
    term[...] = dot(grad[rows[0], :], wide[...], NT)
    part = keep_ref.shape[1]
    wide_share = share * width
    give_ref[:, :wide_share] = spread
    give_ref[:, 2 * wide_share :] = term[:, pl.ds(pl.multiple_of((1 - half) * part, part), part)].astype(BF16)
    keep_ref[...] = term[:, pl.ds(pl.multiple_of(half * part, part), part)]
    for b in range(share):
        spread_ref[b] = spread[:, b * width : (b + 1) * width]
    own = pre_scr[rows[0], :]
    act = (own * jax.nn.sigmoid(own)).astype(BF16)
    give_ref[:, wide_share : 2 * wide_share] = act
    for b in range(share):
        act_ref[b] = act[:, b * width : (b + 1) * width]


def dense(sums, cots, weight, feats, reps):
    share, columns, width = sums[0].shape
    features = weight.shape[0]
    part = features // reps
    return call(
        functools.partial(dense_kernel, feats),
        "dense",
        [
            shape((share, columns, width), BF16),
            shape((columns, 2 * share * width + part), BF16),
            shape((share, columns, width), BF16),
            shape((columns, part), F32),
        ],
        [vmem()] * (2 * feats + 1),
        [
            pltpu.VMEM((features, share * width), BF16),
            pltpu.VMEM((features, share * width), BF16),
            pltpu.VMEM((features, share * width), F32),
            pltpu.VMEM((features, share * width), BF16),
            pltpu.VMEM((columns, features), F32),
        ],
        flops=2 ** 28,
        moved=2 ** 20,
    )(*sums, *cots, weight)


def send_kernel(peers, *refs):
    ids_refs, refs = refs[: peers - 1], refs[peers - 1 :]
    mine_ref, came_ref, keep_ref, m_ref, refs = refs[0], refs[1], refs[2], refs[3], refs[4:]
    x3, refs = refs[0], refs[1:]
    send_refs, refs = refs[: peers - 1], refs[peers - 1 :]
    self_ref, term_ref, mir = refs
    share, _, width = mine_ref.shape
    both = CAP * width
    half = lax.axis_index("rep")
    x3[pl.ds(half * share, share)] = mine_ref[...]
    for b in range(share):
        x3[(1 - half) * share + b] = came_ref[:, b * width : (b + 1) * width]
    term = (keep_ref[...] + came_ref[:, 2 * share * width :].astype(F32)).astype(BF16)
    term_ref[...] = term
    mirrored(lanes(x3), m_ref, mir, peers * CAP, width)
    self_ref[...] = mir[:, :both]
    for k in range(1, peers):
        out = send_refs[k - 1]
        out[:, :both] = mir[:, k * both : (k + 1) * both].astype(BF16)
        for s in range(CAP):
            at = (CAP + s) * width
            out[:, at : at + width] = x3[pick(ids_refs[k - 1], s)]
    send_refs[0][:, 2 * both :] = term


def sends_of(mine, came, keep, operator, ids, peers, reps):
    share, columns, width = mine.shape
    chunk = 2 * CAP * width
    outs = call(
        functools.partial(send_kernel, peers),
        "sends",
        [shape((share * reps, columns, width), BF16), shape((columns, chunk + keep.shape[1]), BF16)]
        + [shape((columns, chunk), BF16)] * (peers - 2)
        + [shape((columns, CAP * width), F32), shape(keep.shape, BF16)],
        [vmem()] * (peers + 3),
        [pltpu.VMEM((columns, peers * CAP * width), F32)],
        flops=2 ** 28,
        moved=2 ** 21,
    )(*ids[1:], mine, came, keep, operator)
    return outs[0], [None] + list(outs[1:peers]), outs[peers], outs[peers + 1]


def pair_kernel(at, mine_ref, came_ref, out_ref):
    total = mine_ref[...].astype(F32) + came_ref[:, at:].astype(F32)
    out_ref[...] = total.astype(out_ref.dtype)


def pair_sum(mine, came, at, dtype):
    return call(functools.partial(pair_kernel, at), "pair_sum", shape(mine.shape, dtype), [vmem(), vmem()])(
        mine, came
    )


def finish_kernel(mine_ref, other_ref, share_ref, other_share_ref, act_ref, came_ref, grad_ref, weight_ref, out_ref):
    half = lax.axis_index("rep")
    share = share_ref.shape[1]
    grad_ref[...] = (mine_ref[...].astype(F32) + other_ref[...].astype(F32)).astype(BF16)
    weight_ref[pl.ds(pl.multiple_of(half * share, share), share), :] = share_ref[...].T
    weight_ref[pl.ds(pl.multiple_of((1 - half) * share, share), share), :] = other_share_ref[...].T
    blocks, _, width = act_ref.shape
    out_ref[pl.ds(half * blocks, blocks)] = act_ref[...]
    for b in range(blocks):
        at = (blocks + b) * width
        out_ref[(1 - half) * blocks + b] = came_ref[:, at : at + width]


def finish(mine, other, share, other_share, act, came):
    columns, width = share.shape
    return call(
        finish_kernel,
        "finish",
        [shape(mine.shape, BF16), shape((2 * width, columns), F32), shape(mine.shape, BF16)],
        [vmem()] * 6,
    )(mine, other, share, other_share, act, came)


def ahead(value, axis, size, k):
    return lax.ppermute(value, axis, [(i, (i + k) % size) for i in range(size)])


def across(value, peers, k):
    return lax.ppermute(value, "graph", [(i, i ^ k) for i in range(peers)])


def after(value, first):
    return lax.optimization_barrier((value, first))[0]


def local(features, weight, cotangent, tiles, tile_row, tile_col, tile_count):
    blocks_dev, _, width = features.shape
    peers = lax.axis_size("graph")
    feats = lax.axis_size("feat")
    reps = lax.axis_size("rep")
    far_first = sorted(range(1, peers), key=lambda k: (-(k & (peers // 2)), k))

    half = half_of(features, reps)
    operator, asks = list_operator(tiles, tile_row, tile_col, tile_count, peers, blocks_dev)
    sends, own_mirror = first_sends(features, operator, asks[1:], peers)
    pieces, held = {0: [half]}, [0]
    bit = peers // 2
    while bit:
        for k in held:
            parts = pieces[k]
            if k:
                parts = after(halves(after(parts, sends[1])), pieces.get(1, half))
            pieces[k ^ bit] = [across(part, peers, bit) for part in parts]
        held = held + [k ^ bit for k in held]
        bit //= 2
    came = [None] * peers
    for k in far_first:
        came[k] = across(sends[k], peers, k)
    arrived = [pieces[k] for k in range(1, peers)]
    ordered, arrived = lax.optimization_barrier(([came[k] for k in far_first], arrived))
    came = [None] + [ordered[far_first.index(k)] for k in range(1, peers)]
    stacked = stack([part for parts in arrived for part in parts])
    swapped = ahead(stacked, "rep", reps, 1)
    cots = [half_of(cotangent, reps)]
    if feats > 1:
        waited = after(cots[0], stacked)
        cots += [ahead(waited, "feat", feats, feats - q) for q in range(1, feats)]
    acc, ids = first_rows(features, operator, asks[0], came, own_mirror, peers)
    give, keep = far_rows(acc, asks, stacked, swapped, operator, peers, reps)

    given, cots = lax.optimization_barrier((ahead(give, "rep", reps, 1), cots))
    mine = add_up(keep, given)
    sums = [mine] + [ahead(mine, "feat", feats, feats - q) for q in range(1, feats)]
    act, give, spread, keep = dense(sums, cots, weight, feats, reps)
    shared = ahead(give, "rep", reps, 1)
    values, sends, own_mirror, term = sends_of(spread, shared, keep, operator, ids, peers, reps)

    came = [None] * peers
    for k in far_first:
        came[k] = across(sends[k], peers, k)
    total = pair_sum(term, came[1], 2 * CAP * width, F32 if peers == 2 else BF16)
    bit = 2
    while bit < peers:
        total = pair_sum(total, across(total, peers, bit), 0, F32 if 2 * bit == peers else BF16)
        bit *= 2
    came, total = lax.optimization_barrier((came, total))
    part = late_rows([asks[0], values, own_mirror], ids, came, far_first, operator, True, True)
    input_grad, weight_grad, activated = finish(
        part, ahead(part, "rep", reps, 1), total, ahead(total, "rep", reps, 1), act, shared
    )
    return (activated, input_grad, weight_grad)


def solution(mesh):
    placed = (
        P(("parts", "graph"), "feat", None),
        P(),
        P(("parts", "graph"), "feat", None),
        P(("parts", "graph", "rep"), None, None),
        P(("parts", "graph", "rep")),
        P(("parts", "graph", "rep")),
        P(("parts", "graph", "rep")),
    )
    return jax.shard_map(
        local,
        mesh=mesh,
        in_specs=placed,
        out_specs=(
            P(("parts", "graph"), "feat", None),
            P(("parts", "graph"), "feat", None),
            P("parts", "feat"),
        ),
        check_vma=False,
    )
```

```python
import functools

import jax
import jax.numpy as jnp
from jax import lax
from jax.experimental import pallas as pl
from jax.experimental.pallas import tpu as pltpu
from jax.sharding import PartitionSpec as P

CAP = 2
GROUP = 8
CHUNK = 16
SIDES = 2
TAIL = 16
VMEM_LIMIT = 40 * 2 ** 20
VMEM_MOST = 50 * 2 ** 20
VMEM_ALL = 58 * 2 ** 20

NT = (((1,), (1,)), ((), ()))
TN = (((0,), (0,)), ((), ()))
F32 = jnp.float32
BF16 = jnp.bfloat16


def vmem():
    return pl.BlockSpec(memory_space=pltpu.VMEM)


def smem():
    return pl.BlockSpec(memory_space=pltpu.SMEM)


def hbm():
    return pl.BlockSpec(memory_space=pltpu.HBM)


def shape(dims, dtype):
    return jax.ShapeDtypeStruct(tuple(dims), dtype)


def dot(a, b, dims=None):
    if dims is None:
        return jnp.dot(a, b, preferred_element_type=F32)
    return lax.dot_general(a, b, dims, preferred_element_type=F32)


def call(kernel, name, outs, in_specs, scratch=(), flops=0, moved=2 ** 18, limit=VMEM_LIMIT, **kwargs):
    return pl.pallas_call(
        kernel,
        out_shape=outs,
        in_specs=in_specs,
        scratch_shapes=list(scratch),
        compiler_params=pltpu.CompilerParams(vmem_limit_bytes=limit),
        cost_estimate=pl.CostEstimate(flops=flops, bytes_accessed=moved, transcendentals=0),
        name=name,
        **kwargs,
    )


def lanes(x3):
    return jnp.concatenate([x3[b] for b in range(x3.shape[0])], axis=1)


def places(peers, blocks_dev, count, row, col, ask_refs):
    me = lax.axis_index("graph")
    lane = lax.broadcasted_iota(jnp.int32, col.shape, 1)
    live = lane < count
    place = jnp.full(col.shape, peers * CAP * blocks_dev, jnp.int32)
    for k in range(peers):
        local = col - jnp.bitwise_xor(me, k) * blocks_dev
        inside = live & (local >= 0) & (local < blocks_dev)
        low = jnp.min(jnp.where(inside, local, blocks_dev - 1), axis=1, keepdims=True)
        high = jnp.max(jnp.where(inside, local, 0), axis=1, keepdims=True)
        ask_refs[k][...] = jnp.where(lane == 0, low, high)
        slot = k * CAP + (local != low).astype(jnp.int32)
        place = jnp.where(inside, slot * blocks_dev + row, place)
    return place


def prepare_kernel(peers, count_ref, row_ref, col_ref, x3, half_ref, place_ref, *ask_refs):
    share = half_ref.shape[0]
    half_ref[...] = x3[pl.ds(lax.axis_index("rep") * share, share)]
    count = jnp.broadcast_to(count_ref[...], (1, 1))
    place_ref[...] = places(peers, x3.shape[0], count, row_ref[...], col_ref[...], ask_refs)


def prepare(features, tile_row, tile_col, tile_count, peers, reps):
    per = tile_col.shape[0]
    blocks_dev, columns, width = features.shape
    outs = call(
        functools.partial(prepare_kernel, peers),
        "prepare",
        [shape((blocks_dev // reps, columns, width), BF16)] + [shape((1, per), jnp.int32)] * (peers + 1),
        [vmem()] * 4,
        limit=VMEM_ALL,
    )(tile_count, tile_row.reshape(1, per), tile_col.reshape(1, per), features)
    return outs[0], outs[1], list(outs[2:])


def pick(ids_ref, lane):
    ids = ids_ref[...].astype(F32)
    at = lax.broadcasted_iota(jnp.int32, ids.shape, 1)
    return jnp.max(jnp.where(at == lane, ids, 0.0)).astype(jnp.int32)


def operator_kernel(blocks_dev, slots_here, groups, place_in, tiles_ref, m_ref, tiles, acc, place_ref, sems, sem):
    step = pl.program_id(0)
    per, width = tiles.shape[0], tiles.shape[1]
    chunks = per // CHUNK
    spare = slots_here * blocks_dev

    def chunk_copy(c):
        part = pl.ds(c * CHUNK, CHUNK)
        return pltpu.make_async_copy(tiles_ref.at[part], tiles.at[part], sems.at[c])

    @pl.when(step == 0)
    def _():
        placed = pltpu.make_async_copy(place_in, place_ref, sem)
        placed.start()
        for c in range(chunks):
            chunk_copy(c).start()
        placed.wait()

    acc[...] = jnp.zeros_like(acc)

    def add_chunk(c, carry):
        @pl.when(step == 0)
        def _():
            chunk_copy(c).wait()

        for u in range(CHUNK):
            t = c * CHUNK + u
            place = place_ref[0, t]
            if groups > 1:
                place = place - step * spare
                place = jnp.where((place >= 0) & (place < spare), place, spare)
            side = u % SIDES
            acc[side, place] = acc[side, place] + tiles[t].astype(F32)
        return carry

    lax.fori_loop(0, chunks, add_chunk, 0)
    for s in range(slots_here):
        for r in range(blocks_dev):
            total = acc[0, s * blocks_dev + r]
            for side in range(1, SIDES):
                total = total + acc[side, s * blocks_dev + r]
            m_ref[r * width : (r + 1) * width, s * width : (s + 1) * width] = total.astype(BF16)


def list_operator(tiles, place, peers, blocks_dev):
    per, width = tiles.shape[0], tiles.shape[1]
    slots = peers * CAP
    slots_here = min(slots, GROUP)
    groups = slots // slots_here
    return call(
        functools.partial(operator_kernel, blocks_dev, slots_here, groups),
        "operator",
        shape((blocks_dev * width, slots * width), BF16),
        [pl.BlockSpec(memory_space=pl.ANY), hbm()],
        [
            pltpu.VMEM((per, width, width), BF16),
            pltpu.VMEM((SIDES, slots_here * blocks_dev + 1, width, width), F32),
            pltpu.SMEM((1, per), jnp.int32),
            pltpu.SemaphoreType.DMA((per // CHUNK,)),
            pltpu.SemaphoreType.DMA,
        ],
        moved=2 ** 24,
        limit=VMEM_MOST,
        grid=(groups,),
        out_specs=pl.BlockSpec((blocks_dev * width, slots_here * width), lambda i: (0, i)),
    )(place, tiles)


def mirrored(near, m_ref, mir, slots, width):
    if slots <= GROUP:
        mir[...] = dot(near, m_ref[...])
    else:
        part = GROUP * width

        @pl.loop(0, slots // GROUP)
        def _(i):
            where = pl.ds(pl.multiple_of(i * part, part), part)
            mir[:, where] = dot(near, m_ref[:, where])


def first_sends_kernel(peers, *refs):
    ask_refs, refs = refs[: peers - 1], refs[peers - 1 :]
    x3, cot, m_ref, refs = refs[0], refs[1], refs[2], refs[3:]
    send_refs, self_ref, cot_ref, mir = refs[: peers - 1], refs[peers - 1], refs[peers], refs[peers + 1]
    _, columns, width = x3.shape
    share = cot_ref.shape[0]
    both = CAP * width
    half = lax.axis_index("rep")
    mirrored(lanes(x3), m_ref, mir, peers * CAP, width)
    self_ref[...] = mir[:, :both]
    lane = lax.broadcasted_iota(jnp.int32, (TAIL, both), 1)
    for k in range(1, peers):
        out = send_refs[k - 1]
        out[:columns, :] = mir[:, k * both : (k + 1) * both].astype(BF16)
        low, high = ask_refs[k - 1][:, :1], ask_refs[k - 1][:, 1:2]
        out[columns:, :] = jnp.where(lane < width, low, high).astype(F32).astype(BF16)
    cot_ref[...] = cot[pl.ds(half * share, share)]


def first_sends(values, cotangent, operator, asks, peers, reps):
    blocks_dev, columns, width = values.shape
    share = blocks_dev // reps
    outs = call(
        functools.partial(first_sends_kernel, peers),
        "first_sends",
        [shape((columns + TAIL, CAP * width), BF16)] * (peers - 1)
        + [shape((columns, CAP * width), F32), shape((share, columns, width), BF16)],
        [vmem()] * (peers + 2),
        [pltpu.VMEM((columns, peers * CAP * width), F32)],
        flops=2 ** 28,
        moved=2 ** 21,
    )(*asks, values, cotangent, operator)
    return [None] + list(outs[: peers - 1]), outs[peers - 1], outs[peers]


def add_sums(acc, block, sums):
    acc[block] = acc[block] + sums.astype(F32)


def own_rows(far, m_ref, k):
    both = far.shape[1]
    return dot(far, m_ref[:, k * both : (k + 1) * both], NT)


def put_rows(acc, own, before=None):
    blocks_dev, _, width = acc.shape
    for b in range(blocks_dev):
        add = own[:, b * width : (b + 1) * width]
        acc[b] = add if before is None else before[b] + add


def split_rows(acc, give_ref, keep_ref):
    half = lax.axis_index("rep")
    share = give_ref.shape[0]
    give_ref[...] = acc[pl.ds((1 - half) * share, share)].astype(BF16)
    keep_ref[...] = acc[pl.ds(half * share, share)]


def self_rows(x3, m_ref, ask_ref):
    far = jnp.concatenate([x3[pick(ask_ref, s)] for s in range(CAP)], axis=1)
    return own_rows(far, m_ref, 0)


def far_of(block, mine_ref, other_ref, ask_ref, at=0):
    half = lax.axis_index("rep")
    share = block.shape[0] // 2
    block[pl.ds(half * share, share)] = mine_ref[at * share : (at + 1) * share]
    block[pl.ds((1 - half) * share, share)] = other_ref[at * share : (at + 1) * share]
    return jnp.concatenate([block[pick(ask_ref, s)] for s in range(CAP)], axis=1)


def first_rows_kernel(peers, *refs):
    ask_ref, refs = refs[0], refs[1:]
    came_refs, refs = refs[: peers - 1], refs[peers - 1 :]
    x3, m_ref, self_ref, acc, ids_refs = refs[0], refs[1], refs[2], refs[3], refs[4:]
    _, columns, width = x3.shape
    put_rows(acc, self_rows(x3, m_ref, ask_ref))
    for s in range(CAP):
        add_sums(acc, pick(ask_ref, s), self_ref[:, s * width : (s + 1) * width])
    lane = lax.broadcasted_iota(jnp.int32, ids_refs[0].shape, 1)
    for k in range(1, peers):
        came = came_refs[k - 1]
        ids = jnp.zeros(lane.shape, jnp.int32)
        for s in range(CAP):
            here = slice(s * width, (s + 1) * width)
            asked = jnp.max(came[columns:, here].astype(F32)).astype(jnp.int32)
            ids = jnp.where(lane == s, asked, ids)
            add_sums(acc, asked, came[:columns, here])
        ids_refs[k - 1][...] = ids


def first_rows(values, operator, ask, came, own_mirror, peers):
    _, columns, width = values.shape
    outs = call(
        functools.partial(first_rows_kernel, peers),
        "first_rows",
        [shape(values.shape, F32)] + [shape((1, width), jnp.int32)] * (peers - 1),
        [vmem()] * (peers + 3),
        flops=2 ** 27,
        moved=2 ** 20,
    )(ask, *came[1:], values, operator, own_mirror)
    return outs[0], [None] + list(outs[1:])


def stack_kernel(*refs):
    at = 0
    for ref in refs[:-1]:
        share = ref.shape[0]
        refs[-1][at : at + share] = ref[...]
        at += share


def halves_kernel(in_ref, low_ref, high_ref):
    share = low_ref.shape[0]
    low_ref[...] = in_ref[:share]
    high_ref[...] = in_ref[share:]


def halves(parts):
    if len(parts) > 1:
        return parts
    share, columns, width = parts[0].shape
    part = shape((share // 2, columns, width), BF16)
    return list(call(halves_kernel, "halves", [part, part], [vmem()])(*parts))


def stack(pieces):
    _, columns, width = pieces[0].shape
    out = shape((sum(piece.shape[0] for piece in pieces), columns, width), BF16)
    return call(stack_kernel, "stack", out, [vmem()] * len(pieces))(*pieces)


def far_rows_kernel(peers, *refs):
    ask_refs, refs = refs[: peers - 1], refs[peers - 1 :]
    before, mine_ref, other_ref, m_ref, give_ref, keep_ref, acc, block, far = refs
    both = CAP * acc.shape[2]
    for k in range(1, peers):
        far[:, k * both : (k + 1) * both] = far_of(block, mine_ref, other_ref, ask_refs[k - 1], k - 1)
    if peers * CAP <= GROUP:
        own = dot(far[:, both:], m_ref[:, both:], NT)
    else:

        def add_peer(k, total):
            here = pl.ds(pl.multiple_of(k * both, both), both)
            return total + dot(far[:, here], m_ref[:, here], NT)

        own = lax.fori_loop(1, peers, add_peer, jnp.zeros((acc.shape[1], m_ref.shape[0]), F32))
    put_rows(acc, own, before)
    split_rows(acc, give_ref, keep_ref)


def far_rows(before, asks, mine, other, operator, peers, reps):
    blocks_dev, columns, width = before.shape
    share = (blocks_dev // reps, columns, width)
    return call(
        functools.partial(far_rows_kernel, peers),
        "far_rows",
        [shape(share, BF16), shape(share, F32)],
        [vmem()] * (peers + 3),
        [
            pltpu.VMEM(before.shape, F32),
            pltpu.VMEM(before.shape, BF16),
            pltpu.VMEM((columns, peers * CAP * width), BF16),
        ],
        flops=2 ** 28,
        moved=2 ** 21,
    )(*asks[1:], before, mine, other, operator)


def late_rows_kernel(ks, first, last, *refs):
    if first:
        ask_ref, x3, self_ref = refs[:3]
    else:
        before = refs[0]
    refs = refs[3 if first else 1 :]
    ids_refs, refs = refs[: len(ks)], refs[len(ks) :]
    came_refs, refs = refs[: len(ks)], refs[len(ks) :]
    m_ref, out_ref = refs[:2]
    acc = refs[2] if last else out_ref
    width = acc.shape[2]
    both = CAP * width
    own = self_rows(x3, m_ref, ask_ref) if first else None
    for i, k in enumerate(ks):
        add = own_rows(came_refs[i][:, both : 2 * both], m_ref, k)
        own = add if own is None else own + add
    put_rows(acc, own, None if first else before)
    if first:
        for s in range(CAP):
            add_sums(acc, pick(ask_ref, s), self_ref[:, s * width : (s + 1) * width])
    for i in range(len(ks)):
        for s in range(CAP):
            add_sums(acc, pick(ids_refs[i], s), came_refs[i][:, s * width : (s + 1) * width])
    if last:
        out_ref[...] = acc[...].astype(BF16)


def late_rows(head, ids, came, ks, operator, first, last):
    values = head[1] if first else head[0]
    return call(
        functools.partial(late_rows_kernel, ks, first, last),
        "late_rows",
        shape(values.shape, BF16 if last else F32),
        [vmem()] * (len(head) + 2 * len(ks) + 1),
        [pltpu.VMEM(values.shape, F32)] if last else [],
        flops=2 ** 27,
        moved=2 ** 20,
    )(*head, *[ids[k] for k in ks], *[came[k] for k in ks], operator)


def add_kernel(keep_ref, came_ref, out_ref):
    out_ref[...] = (keep_ref[...] + came_ref[...].astype(F32)).astype(BF16)


def add_up(keep, came):
    return call(add_kernel, "add_up", shape(came.shape, BF16), [vmem(), vmem()])(keep, came)


def dense_kernel(feats, *refs):
    sums, cots, refs = refs[:feats], refs[feats : 2 * feats], refs[2 * feats :]
    w_ref, act_ref, give_ref, spread_ref, keep_ref, wide, wide_cot, pre_scr, grad, term = refs
    share, columns, width = act_ref.shape
    me = lax.axis_index("feat")
    half = lax.axis_index("rep")
    rows = [pl.ds(pl.multiple_of(lax.rem(me + q, feats) * columns, columns), columns) for q in range(feats)]
    for q in range(feats):
        for b in range(share):
            wide[rows[q], b * width : (b + 1) * width] = sums[q][b]
            wide_cot[rows[q], b * width : (b + 1) * width] = cots[q][b]
    pre = dot(w_ref[...], wide[...], TN)
    pre_scr[...] = pre
    sig = jax.nn.sigmoid(pre)
    factor = wide_cot[...].astype(F32) * sig * (1.0 + pre * (1.0 - sig))
    grad[...] = factor.astype(BF16)
    spread = dot(w_ref[rows[0], :], grad[...]).astype(BF16)
    term[...] = dot(grad[rows[0], :], wide[...], NT)
    part = keep_ref.shape[1]
    wide_share = share * width
    give_ref[:, :wide_share] = spread
    give_ref[:, 2 * wide_share :] = term[:, pl.ds(pl.multiple_of((1 - half) * part, part), part)].astype(BF16)
    keep_ref[...] = term[:, pl.ds(pl.multiple_of(half * part, part), part)]
    for b in range(share):
        spread_ref[b] = spread[:, b * width : (b + 1) * width]
    own = pre_scr[rows[0], :]
    act = (own * jax.nn.sigmoid(own)).astype(BF16)
    give_ref[:, wide_share : 2 * wide_share] = act
    for b in range(share):
        act_ref[b] = act[:, b * width : (b + 1) * width]


def dense(sums, cots, weight, feats, reps):
    share, columns, width = sums[0].shape
    features = weight.shape[0]
    part = features // reps
    return call(
        functools.partial(dense_kernel, feats),
        "dense",
        [
            shape((share, columns, width), BF16),
            shape((columns, 2 * share * width + part), BF16),
            shape((share, columns, width), BF16),
            shape((columns, part), F32),
        ],
        [vmem()] * (2 * feats + 1),
        [
            pltpu.VMEM((features, share * width), BF16),
            pltpu.VMEM((features, share * width), BF16),
            pltpu.VMEM((features, share * width), F32),
            pltpu.VMEM((features, share * width), BF16),
            pltpu.VMEM((columns, features), F32),
        ],
        flops=2 ** 28,
        moved=2 ** 20,
    )(*sums, *cots, weight)


def send_kernel(peers, *refs):
    ids_refs, refs = refs[: peers - 1], refs[peers - 1 :]
    mine_ref, came_ref, keep_ref, m_ref, refs = refs[0], refs[1], refs[2], refs[3], refs[4:]
    x3, refs = refs[0], refs[1:]
    send_refs, refs = refs[: peers - 1], refs[peers - 1 :]
    self_ref, term_ref, mir = refs
    share, _, width = mine_ref.shape
    both = CAP * width
    half = lax.axis_index("rep")
    x3[pl.ds(half * share, share)] = mine_ref[...]
    for b in range(share):
        x3[(1 - half) * share + b] = came_ref[:, b * width : (b + 1) * width]
    term = (keep_ref[...] + came_ref[:, 2 * share * width :].astype(F32)).astype(BF16)
    term_ref[...] = term
    mirrored(lanes(x3), m_ref, mir, peers * CAP, width)
    self_ref[...] = mir[:, :both]
    for k in range(1, peers):
        out = send_refs[k - 1]
        out[:, :both] = mir[:, k * both : (k + 1) * both].astype(BF16)
        for s in range(CAP):
            at = (CAP + s) * width
            out[:, at : at + width] = x3[pick(ids_refs[k - 1], s)]


def sends_of(mine, came, keep, operator, ids, peers, reps):
    share, columns, width = mine.shape
    chunk = 2 * CAP * width
    outs = call(
        functools.partial(send_kernel, peers),
        "sends",
        [shape((share * reps, columns, width), BF16)]
        + [shape((columns, chunk), BF16)] * (peers - 1)
        + [shape((columns, CAP * width), F32), shape(keep.shape, BF16)],
        [vmem()] * (peers + 3),
        [pltpu.VMEM((columns, peers * CAP * width), F32)],
        flops=2 ** 28,
        moved=2 ** 21,
    )(*ids[1:], mine, came, keep, operator)
    return outs[0], [None] + list(outs[1:peers]), outs[peers], outs[peers + 1]


def pair_kernel(mine_ref, came_ref, out_ref):
    out_ref[...] = (mine_ref[...].astype(F32) + came_ref[...].astype(F32)).astype(out_ref.dtype)


def pair_sum(mine, came, dtype):
    return call(pair_kernel, "pair_sum", shape(mine.shape, dtype), [vmem(), vmem()])(mine, came)


def finish_kernel(mine_ref, other_ref, share_ref, other_share_ref, act_ref, came_ref, grad_ref, weight_ref, out_ref):
    half = lax.axis_index("rep")
    share = share_ref.shape[1]
    grad_ref[...] = (mine_ref[...].astype(F32) + other_ref[...].astype(F32)).astype(BF16)
    weight_ref[pl.ds(pl.multiple_of(half * share, share), share), :] = share_ref[...].T
    weight_ref[pl.ds(pl.multiple_of((1 - half) * share, share), share), :] = other_share_ref[...].T
    blocks, _, width = act_ref.shape
    out_ref[pl.ds(half * blocks, blocks)] = act_ref[...]
    for b in range(blocks):
        at = (blocks + b) * width
        out_ref[(1 - half) * blocks + b] = came_ref[:, at : at + width]


def finish(mine, other, share, other_share, act, came):
    columns, width = share.shape
    return call(
        finish_kernel,
        "finish",
        [shape(mine.shape, BF16), shape((2 * width, columns), F32), shape(mine.shape, BF16)],
        [vmem()] * 6,
    )(mine, other, share, other_share, act, came)


def ahead(value, axis, size, k):
    return lax.ppermute(value, axis, [(i, (i + k) % size) for i in range(size)])


def across(value, peers, k):
    return lax.ppermute(value, "graph", [(i, i ^ k) for i in range(peers)])


def after(value, first):
    return lax.optimization_barrier((value, first))[0]


def local(features, weight, cotangent, tiles, tile_row, tile_col, tile_count):
    blocks_dev, _, width = features.shape
    peers = lax.axis_size("graph")
    feats = lax.axis_size("feat")
    reps = lax.axis_size("rep")
    far_first = sorted(range(1, peers), key=lambda k: (-(k & (peers // 2)), k))

    half, place, asks = prepare(features, tile_row, tile_col, tile_count, peers, reps)
    operator = list_operator(tiles, place, peers, blocks_dev)
    sends, own_mirror, own_cot = first_sends(features, cotangent, operator, asks[1:], peers, reps)
    pieces, held = {0: [half]}, [0]
    bit = peers // 2
    while bit:
        for k in held:
            parts = pieces[k]
            if k:
                parts = after(halves(after(parts, sends[1])), pieces.get(1, half))
            pieces[k ^ bit] = [across(part, peers, bit) for part in parts]
        held = held + [k ^ bit for k in held]
        bit //= 2
    came = [None] * peers
    for k in far_first:
        came[k] = across(sends[k], peers, k)
    arrived = [part for k in range(1, peers) for part in pieces[k]]
    ordered, arrived = lax.optimization_barrier(([came[k] for k in far_first], arrived))
    came = [None] + [ordered[far_first.index(k)] for k in range(1, peers)]
    stacked = stack(arrived)
    swapped = ahead(stacked, "rep", reps, 1)
    cots = [own_cot]
    if feats > 1:
        waited = after(own_cot, stacked)
        cots += [ahead(waited, "feat", feats, feats - q) for q in range(1, feats)]
    acc, ids = first_rows(features, operator, asks[0], came, own_mirror, peers)
    give, keep = far_rows(acc, asks, stacked, swapped, operator, peers, reps)

    given, cots = lax.optimization_barrier((ahead(give, "rep", reps, 1), cots))
    mine = add_up(keep, given)
    sums = [mine] + [ahead(mine, "feat", feats, feats - q) for q in range(1, feats)]
    act, give, spread, keep = dense(sums, cots, weight, feats, reps)
    shared = ahead(give, "rep", reps, 1)
    values, sends, own_mirror, term = sends_of(spread, shared, keep, operator, ids, peers, reps)

    came = [None] * peers
    for k in far_first:
        came[k] = across(sends[k], peers, k)
    total, bit = term, 1
    while bit < peers:
        total = pair_sum(total, across(total, peers, bit), F32 if 2 * bit == peers else BF16)
        bit *= 2
    ordered, total = lax.optimization_barrier(([came[k] for k in far_first], total))
    came = [None] + [ordered[far_first.index(k)] for k in range(1, peers)]
    part = late_rows([asks[0], values, own_mirror], ids, came, far_first, operator, True, True)
    input_grad, weight_grad, activated = finish(
        part, ahead(part, "rep", reps, 1), total, ahead(total, "rep", reps, 1), act, shared
    )
    return (activated, input_grad, weight_grad)


def solution(mesh):
    placed = (
        P(("parts", "graph"), "feat", None),
        P(),
        P(("parts", "graph"), "feat", None),
        P(("parts", "graph", "rep"), None, None),
        P(("parts", "graph", "rep")),
        P(("parts", "graph", "rep")),
        P(("parts", "graph", "rep")),
    )
    return jax.shard_map(
        local,
        mesh=mesh,
        in_specs=placed,
        out_specs=(
            P(("parts", "graph"), "feat", None),
            P(("parts", "graph"), "feat", None),
            P("parts", "feat"),
        ),
        check_vma=False,
    )
```

```python
import functools

import jax
import jax.numpy as jnp
from jax import lax
from jax.experimental import pallas as pl
from jax.experimental.pallas import tpu as pltpu
from jax.sharding import PartitionSpec as P

CAP = 2
GROUP = 8
CHUNK = 16
SIDES = 2
TAIL = 16
VMEM_LIMIT = 40 * 2 ** 20
VMEM_MOST = 50 * 2 ** 20
VMEM_ALL = 58 * 2 ** 20

NT = (((1,), (1,)), ((), ()))
TN = (((0,), (0,)), ((), ()))
F32 = jnp.float32
BF16 = jnp.bfloat16


def vmem():
    return pl.BlockSpec(memory_space=pltpu.VMEM)


def smem():
    return pl.BlockSpec(memory_space=pltpu.SMEM)


def hbm():
    return pl.BlockSpec(memory_space=pltpu.HBM)


def shape(dims, dtype):
    return jax.ShapeDtypeStruct(tuple(dims), dtype)


def dot(a, b, dims=None):
    if dims is None:
        return jnp.dot(a, b, preferred_element_type=F32)
    return lax.dot_general(a, b, dims, preferred_element_type=F32)


def call(kernel, name, outs, in_specs, scratch=(), flops=0, moved=2 ** 18, limit=VMEM_LIMIT, **kwargs):
    return pl.pallas_call(
        kernel,
        out_shape=outs,
        in_specs=in_specs,
        scratch_shapes=list(scratch),
        compiler_params=pltpu.CompilerParams(vmem_limit_bytes=limit),
        cost_estimate=pl.CostEstimate(flops=flops, bytes_accessed=moved, transcendentals=0),
        name=name,
        **kwargs,
    )


def lanes(x3):
    return jnp.concatenate([x3[b] for b in range(x3.shape[0])], axis=1)


def places(peers, blocks_dev, count, row, col, ask_refs):
    me = lax.axis_index("graph")
    lane = lax.broadcasted_iota(jnp.int32, col.shape, 1)
    live = lane < count
    place = jnp.full(col.shape, peers * CAP * blocks_dev, jnp.int32)
    for k in range(peers):
        local = col - jnp.bitwise_xor(me, k) * blocks_dev
        inside = live & (local >= 0) & (local < blocks_dev)
        low = jnp.min(jnp.where(inside, local, blocks_dev - 1), axis=1, keepdims=True)
        high = jnp.max(jnp.where(inside, local, 0), axis=1, keepdims=True)
        ask_refs[k][...] = jnp.where(lane == 0, low, high)
        slot = k * CAP + (local != low).astype(jnp.int32)
        place = jnp.where(inside, slot * blocks_dev + row, place)
    return place


def prepare_kernel(peers, count_ref, row_ref, col_ref, x3, half_ref, place_ref, *ask_refs):
    share = half_ref.shape[0]
    half_ref[...] = x3[pl.ds(lax.axis_index("rep") * share, share)]
    count = jnp.broadcast_to(count_ref[...], (1, 1))
    place_ref[...] = places(peers, x3.shape[0], count, row_ref[...], col_ref[...], ask_refs)


def prepare(features, tile_row, tile_col, tile_count, peers, reps):
    per = tile_col.shape[0]
    blocks_dev, columns, width = features.shape
    outs = call(
        functools.partial(prepare_kernel, peers),
        "prepare",
        [shape((blocks_dev // reps, columns, width), BF16)] + [shape((1, per), jnp.int32)] * (peers + 1),
        [vmem()] * 4,
        limit=VMEM_ALL,
    )(tile_count, tile_row.reshape(1, per), tile_col.reshape(1, per), features)
    return outs[0], outs[1], list(outs[2:])


def pick(ids_ref, lane):
    ids = ids_ref[...].astype(F32)
    at = lax.broadcasted_iota(jnp.int32, ids.shape, 1)
    return jnp.max(jnp.where(at == lane, ids, 0.0)).astype(jnp.int32)


def operator_kernel(blocks_dev, slots_here, groups, place_in, tiles_ref, m_ref, tiles, acc, place_ref, sems, sem):
    step = pl.program_id(0)
    per, width = tiles.shape[0], tiles.shape[1]
    chunks = per // CHUNK
    spare = slots_here * blocks_dev

    def chunk_copy(c):
        part = pl.ds(c * CHUNK, CHUNK)
        return pltpu.make_async_copy(tiles_ref.at[part], tiles.at[part], sems.at[c])

    @pl.when(step == 0)
    def _():
        placed = pltpu.make_async_copy(place_in, place_ref, sem)
        placed.start()
        for c in range(chunks):
            chunk_copy(c).start()
        placed.wait()

    acc[...] = jnp.zeros_like(acc)

    def add_chunk(c, carry):
        @pl.when(step == 0)
        def _():
            chunk_copy(c).wait()

        for u in range(CHUNK):
            t = c * CHUNK + u
            place = place_ref[0, t]
            if groups > 1:
                place = place - step * spare
                place = jnp.where((place >= 0) & (place < spare), place, spare)
            side = u % SIDES
            acc[side, place] = acc[side, place] + tiles[t].astype(F32)
        return carry

    lax.fori_loop(0, chunks, add_chunk, 0)
    for s in range(slots_here):
        for r in range(blocks_dev):
            total = acc[0, s * blocks_dev + r]
            for side in range(1, SIDES):
                total = total + acc[side, s * blocks_dev + r]
            m_ref[r * width : (r + 1) * width, s * width : (s + 1) * width] = total.astype(BF16)


def list_operator(tiles, place, peers, blocks_dev):
    per, width = tiles.shape[0], tiles.shape[1]
    slots = peers * CAP
    slots_here = min(slots, GROUP)
    groups = slots // slots_here
    return call(
        functools.partial(operator_kernel, blocks_dev, slots_here, groups),
        "operator",
        shape((blocks_dev * width, slots * width), BF16),
        [pl.BlockSpec(memory_space=pl.ANY), hbm()],
        [
            pltpu.VMEM((per, width, width), BF16),
            pltpu.VMEM((SIDES, slots_here * blocks_dev + 1, width, width), F32),
            pltpu.SMEM((1, per), jnp.int32),
            pltpu.SemaphoreType.DMA((per // CHUNK,)),
            pltpu.SemaphoreType.DMA,
        ],
        moved=2 ** 24,
        limit=VMEM_MOST,
        grid=(groups,),
        out_specs=pl.BlockSpec((blocks_dev * width, slots_here * width), lambda i: (0, i)),
    )(place, tiles)


def mirrored(near, m_ref, mir, slots, width):
    if slots <= GROUP:
        mir[...] = dot(near, m_ref[...])
    else:
        part = GROUP * width

        @pl.loop(0, slots // GROUP)
        def _(i):
            where = pl.ds(pl.multiple_of(i * part, part), part)
            mir[:, where] = dot(near, m_ref[:, where])


def first_sends_kernel(peers, *refs):
    ask_refs, refs = refs[: peers - 1], refs[peers - 1 :]
    x3, cot, m_ref, refs = refs[0], refs[1], refs[2], refs[3:]
    send_refs, self_ref, cot_ref, mir = refs[: peers - 1], refs[peers - 1], refs[peers], refs[peers + 1]
    _, columns, width = x3.shape
    share = cot_ref.shape[0]
    both = CAP * width
    half = lax.axis_index("rep")
    mirrored(lanes(x3), m_ref, mir, peers * CAP, width)
    self_ref[...] = mir[:, :both]
    lane = lax.broadcasted_iota(jnp.int32, (TAIL, both), 1)
    for k in range(1, peers):
        out = send_refs[k - 1]
        out[:columns, :] = mir[:, k * both : (k + 1) * both].astype(BF16)
        low, high = ask_refs[k - 1][:, :1], ask_refs[k - 1][:, 1:2]
        out[columns:, :] = jnp.where(lane < width, low, high).astype(F32).astype(BF16)
    cot_ref[...] = cot[pl.ds(half * share, share)]


def first_sends(values, cotangent, operator, asks, peers, reps):
    blocks_dev, columns, width = values.shape
    share = blocks_dev // reps
    outs = call(
        functools.partial(first_sends_kernel, peers),
        "first_sends",
        [shape((columns + TAIL, CAP * width), BF16)] * (peers - 1)
        + [shape((columns, CAP * width), F32), shape((share, columns, width), BF16)],
        [vmem()] * (peers + 2),
        [pltpu.VMEM((columns, peers * CAP * width), F32)],
        flops=2 ** 28,
        moved=2 ** 21,
    )(*asks, values, cotangent, operator)
    return [None] + list(outs[: peers - 1]), outs[peers - 1], outs[peers]


def add_sums(acc, block, sums):
    acc[block] = acc[block] + sums.astype(F32)


def own_rows(far, m_ref, k):
    both = far.shape[1]
    return dot(far, m_ref[:, k * both : (k + 1) * both], NT)


def put_rows(acc, own, before=None):
    blocks_dev, _, width = acc.shape
    for b in range(blocks_dev):
        add = own[:, b * width : (b + 1) * width]
        acc[b] = add if before is None else before[b] + add


def split_rows(acc, give_ref, keep_ref):
    half = lax.axis_index("rep")
    share = give_ref.shape[0]
    give_ref[...] = acc[pl.ds((1 - half) * share, share)].astype(BF16)
    keep_ref[...] = acc[pl.ds(half * share, share)]


def self_rows(x3, m_ref, ask_ref):
    far = jnp.concatenate([x3[pick(ask_ref, s)] for s in range(CAP)], axis=1)
    return own_rows(far, m_ref, 0)


def far_of(block, mine_ref, other_ref, ask_ref, at=0):
    half = lax.axis_index("rep")
    share = block.shape[0] // 2
    block[pl.ds(half * share, share)] = mine_ref[at * share : (at + 1) * share]
    block[pl.ds((1 - half) * share, share)] = other_ref[at * share : (at + 1) * share]
    return jnp.concatenate([block[pick(ask_ref, s)] for s in range(CAP)], axis=1)


def first_rows_kernel(peers, *refs):
    ask_ref, refs = refs[0], refs[1:]
    came_refs, refs = refs[: peers - 1], refs[peers - 1 :]
    x3, m_ref, self_ref, acc, ids_refs = refs[0], refs[1], refs[2], refs[3], refs[4:]
    _, columns, width = x3.shape
    put_rows(acc, self_rows(x3, m_ref, ask_ref))
    for s in range(CAP):
        add_sums(acc, pick(ask_ref, s), self_ref[:, s * width : (s + 1) * width])
    lane = lax.broadcasted_iota(jnp.int32, ids_refs[0].shape, 1)
    for k in range(1, peers):
        came = came_refs[k - 1]
        ids = jnp.zeros(lane.shape, jnp.int32)
        for s in range(CAP):
            here = slice(s * width, (s + 1) * width)
            asked = jnp.max(came[columns:, here].astype(F32)).astype(jnp.int32)
            ids = jnp.where(lane == s, asked, ids)
            add_sums(acc, asked, came[:columns, here])
        ids_refs[k - 1][...] = ids


def first_rows(values, operator, ask, came, own_mirror, peers):
    _, columns, width = values.shape
    outs = call(
        functools.partial(first_rows_kernel, peers),
        "first_rows",
        [shape(values.shape, F32)] + [shape((1, width), jnp.int32)] * (peers - 1),
        [vmem()] * (peers + 3),
        flops=2 ** 27,
        moved=2 ** 20,
    )(ask, *came[1:], values, operator, own_mirror)
    return outs[0], [None] + list(outs[1:])


def stack_kernel(*refs):
    at = 0
    for ref in refs[:-1]:
        share = ref.shape[0]
        refs[-1][at : at + share] = ref[...]
        at += share


def halves_kernel(in_ref, low_ref, high_ref):
    share = low_ref.shape[0]
    low_ref[...] = in_ref[:share]
    high_ref[...] = in_ref[share:]


def halves(parts):
    if len(parts) > 1:
        return parts
    share, columns, width = parts[0].shape
    part = shape((share // 2, columns, width), BF16)
    return list(call(halves_kernel, "halves", [part, part], [vmem()])(*parts))


def stack(pieces):
    _, columns, width = pieces[0].shape
    out = shape((sum(piece.shape[0] for piece in pieces), columns, width), BF16)
    return call(stack_kernel, "stack", out, [vmem()] * len(pieces))(*pieces)


def far_rows_kernel(peers, *refs):
    ask_refs, refs = refs[: peers - 1], refs[peers - 1 :]
    before, mine_ref, other_ref, m_ref, give_ref, keep_ref, acc, block, far = refs
    both = CAP * acc.shape[2]
    for k in range(1, peers):
        far[:, k * both : (k + 1) * both] = far_of(block, mine_ref, other_ref, ask_refs[k - 1], k - 1)
    if peers * CAP <= GROUP:
        own = dot(far[:, both:], m_ref[:, both:], NT)
    else:

        def add_peer(k, total):
            here = pl.ds(pl.multiple_of(k * both, both), both)
            return total + dot(far[:, here], m_ref[:, here], NT)

        own = lax.fori_loop(1, peers, add_peer, jnp.zeros((acc.shape[1], m_ref.shape[0]), F32))
    put_rows(acc, own, before)
    split_rows(acc, give_ref, keep_ref)


def far_rows(before, asks, mine, other, operator, peers, reps):
    blocks_dev, columns, width = before.shape
    share = (blocks_dev // reps, columns, width)
    return call(
        functools.partial(far_rows_kernel, peers),
        "far_rows",
        [shape(share, BF16), shape(share, F32)],
        [vmem()] * (peers + 3),
        [
            pltpu.VMEM(before.shape, F32),
            pltpu.VMEM(before.shape, BF16),
            pltpu.VMEM((columns, peers * CAP * width), BF16),
        ],
        flops=2 ** 28,
        moved=2 ** 21,
    )(*asks[1:], before, mine, other, operator)


def late_rows_kernel(ks, first, last, *refs):
    if first:
        ask_ref, x3, self_ref = refs[:3]
    else:
        before = refs[0]
    refs = refs[3 if first else 1 :]
    ids_refs, refs = refs[: len(ks)], refs[len(ks) :]
    came_refs, refs = refs[: len(ks)], refs[len(ks) :]
    m_ref, out_ref = refs[:2]
    acc = refs[2] if last else out_ref
    width = acc.shape[2]
    both = CAP * width
    own = self_rows(x3, m_ref, ask_ref) if first else None
    for i, k in enumerate(ks):
        add = own_rows(came_refs[i][:, both : 2 * both], m_ref, k)
        own = add if own is None else own + add
    put_rows(acc, own, None if first else before)
    if first:
        for s in range(CAP):
            add_sums(acc, pick(ask_ref, s), self_ref[:, s * width : (s + 1) * width])
    for i in range(len(ks)):
        for s in range(CAP):
            add_sums(acc, pick(ids_refs[i], s), came_refs[i][:, s * width : (s + 1) * width])
    if last:
        out_ref[...] = acc[...].astype(BF16)


def late_rows(head, ids, came, ks, operator, first, last):
    values = head[1] if first else head[0]
    return call(
        functools.partial(late_rows_kernel, ks, first, last),
        "late_rows",
        shape(values.shape, BF16 if last else F32),
        [vmem()] * (len(head) + 2 * len(ks) + 1),
        [pltpu.VMEM(values.shape, F32)] if last else [],
        flops=2 ** 27,
        moved=2 ** 20,
    )(*head, *[ids[k] for k in ks], *[came[k] for k in ks], operator)


def add_kernel(keep_ref, came_ref, out_ref):
    out_ref[...] = (keep_ref[...] + came_ref[...].astype(F32)).astype(BF16)


def add_up(keep, came):
    return call(add_kernel, "add_up", shape(came.shape, BF16), [vmem(), vmem()])(keep, came)


def dense_kernel(feats, *refs):
    sums, cots, refs = refs[:feats], refs[feats : 2 * feats], refs[2 * feats :]
    w_ref, act_ref, give_ref, spread_ref, keep_ref, wide, wide_cot, pre_scr, grad, term = refs
    share, columns, width = act_ref.shape
    me = lax.axis_index("feat")
    half = lax.axis_index("rep")
    rows = [pl.ds(pl.multiple_of(lax.rem(me + q, feats) * columns, columns), columns) for q in range(feats)]
    for q in range(feats):
        for b in range(share):
            wide[rows[q], b * width : (b + 1) * width] = sums[q][b]
            wide_cot[rows[q], b * width : (b + 1) * width] = cots[q][b]
    pre = dot(w_ref[...], wide[...], TN)
    pre_scr[...] = pre
    sig = jax.nn.sigmoid(pre)
    factor = wide_cot[...].astype(F32) * sig * (1.0 + pre * (1.0 - sig))
    grad[...] = factor.astype(BF16)
    spread = dot(w_ref[rows[0], :], grad[...]).astype(BF16)
    term[...] = dot(grad[rows[0], :], wide[...], NT)
    part = keep_ref.shape[1]
    wide_share = share * width
    give_ref[:, :wide_share] = spread
    give_ref[:, 2 * wide_share :] = term[:, pl.ds(pl.multiple_of((1 - half) * part, part), part)].astype(BF16)
    keep_ref[...] = term[:, pl.ds(pl.multiple_of(half * part, part), part)]
    for b in range(share):
        spread_ref[b] = spread[:, b * width : (b + 1) * width]
    own = pre_scr[rows[0], :]
    act = (own * jax.nn.sigmoid(own)).astype(BF16)
    give_ref[:, wide_share : 2 * wide_share] = act
    for b in range(share):
        act_ref[b] = act[:, b * width : (b + 1) * width]


def dense(sums, cots, weight, feats, reps):
    share, columns, width = sums[0].shape
    features = weight.shape[0]
    part = features // reps
    return call(
        functools.partial(dense_kernel, feats),
        "dense",
        [
            shape((share, columns, width), BF16),
            shape((columns, 2 * share * width + part), BF16),
            shape((share, columns, width), BF16),
            shape((columns, part), F32),
        ],
        [vmem()] * (2 * feats + 1),
        [
            pltpu.VMEM((features, share * width), BF16),
            pltpu.VMEM((features, share * width), BF16),
            pltpu.VMEM((features, share * width), F32),
            pltpu.VMEM((features, share * width), BF16),
            pltpu.VMEM((columns, features), F32),
        ],
        flops=2 ** 28,
        moved=2 ** 20,
    )(*sums, *cots, weight)


def send_kernel(peers, *refs):
    ids_refs, refs = refs[: peers - 1], refs[peers - 1 :]
    mine_ref, came_ref, keep_ref, m_ref, refs = refs[0], refs[1], refs[2], refs[3], refs[4:]
    x3, refs = refs[0], refs[1:]
    send_refs, refs = refs[: peers - 1], refs[peers - 1 :]
    self_ref, term_ref, mir = refs
    share, _, width = mine_ref.shape
    both = CAP * width
    half = lax.axis_index("rep")
    x3[pl.ds(half * share, share)] = mine_ref[...]
    for b in range(share):
        x3[(1 - half) * share + b] = came_ref[:, b * width : (b + 1) * width]
    term = (keep_ref[...] + came_ref[:, 2 * share * width :].astype(F32)).astype(BF16)
    term_ref[...] = term
    mirrored(lanes(x3), m_ref, mir, peers * CAP, width)
    self_ref[...] = mir[:, :both]
    for k in range(1, peers):
        out = send_refs[k - 1]
        out[:, :both] = mir[:, k * both : (k + 1) * both].astype(BF16)
        for s in range(CAP):
            at = (CAP + s) * width
            out[:, at : at + width] = x3[pick(ids_refs[k - 1], s)]
    send_refs[peers // 2 - 1][:, 2 * both :] = term


def sends_of(mine, came, keep, operator, ids, peers, reps):
    share, columns, width = mine.shape
    chunk = 2 * CAP * width
    outs = call(
        functools.partial(send_kernel, peers),
        "sends",
        [shape((share * reps, columns, width), BF16)]
        + [shape((columns, chunk + (keep.shape[1] if 2 * k == peers else 0)), BF16) for k in range(1, peers)]
        + [shape((columns, CAP * width), F32), shape(keep.shape, BF16)],
        [vmem()] * (peers + 3),
        [pltpu.VMEM((columns, peers * CAP * width), F32)],
        flops=2 ** 28,
        moved=2 ** 21,
    )(*ids[1:], mine, came, keep, operator)
    return outs[0], [None] + list(outs[1:peers]), outs[peers], outs[peers + 1]


def pair_kernel(at, mine_ref, came_ref, out_ref):
    out_ref[...] = (mine_ref[...].astype(F32) + came_ref[:, at:].astype(F32)).astype(out_ref.dtype)


def pair_sum(mine, came, at, dtype):
    kernel = functools.partial(pair_kernel, at)
    return call(kernel, "pair_sum", shape(mine.shape, dtype), [vmem(), vmem()])(mine, came)


def finish_kernel(mine_ref, other_ref, share_ref, other_share_ref, act_ref, came_ref, grad_ref, weight_ref, out_ref):
    half = lax.axis_index("rep")
    share = share_ref.shape[1]
    grad_ref[...] = (mine_ref[...].astype(F32) + other_ref[...].astype(F32)).astype(BF16)
    weight_ref[pl.ds(pl.multiple_of(half * share, share), share), :] = share_ref[...].T
    weight_ref[pl.ds(pl.multiple_of((1 - half) * share, share), share), :] = other_share_ref[...].T
    blocks, _, width = act_ref.shape
    out_ref[pl.ds(half * blocks, blocks)] = act_ref[...]
    for b in range(blocks):
        at = (blocks + b) * width
        out_ref[(1 - half) * blocks + b] = came_ref[:, at : at + width]


def finish(mine, other, share, other_share, act, came):
    columns, width = share.shape
    return call(
        finish_kernel,
        "finish",
        [shape(mine.shape, BF16), shape((2 * width, columns), F32), shape(mine.shape, BF16)],
        [vmem()] * 6,
    )(mine, other, share, other_share, act, came)


def ahead(value, axis, size, k):
    return lax.ppermute(value, axis, [(i, (i + k) % size) for i in range(size)])


def across(value, peers, k):
    return lax.ppermute(value, "graph", [(i, i ^ k) for i in range(peers)])


def after(value, first):
    return lax.optimization_barrier((value, first))[0]


def local(features, weight, cotangent, tiles, tile_row, tile_col, tile_count):
    blocks_dev, _, width = features.shape
    peers = lax.axis_size("graph")
    feats = lax.axis_size("feat")
    reps = lax.axis_size("rep")
    far_first = sorted(range(1, peers), key=lambda k: (-(k & (peers // 2)), k))

    half, place, asks = prepare(features, tile_row, tile_col, tile_count, peers, reps)
    operator = list_operator(tiles, place, peers, blocks_dev)
    sends, own_mirror, own_cot = first_sends(features, cotangent, operator, asks[1:], peers, reps)
    pieces, held = {0: [half]}, [0]
    bit = peers // 2
    while bit:
        for k in held:
            parts = pieces[k]
            if k:
                parts = after(halves(after(parts, sends[1])), pieces.get(1, half))
            pieces[k ^ bit] = [across(part, peers, bit) for part in parts]
        held = held + [k ^ bit for k in held]
        bit //= 2
    came = [None] * peers
    for k in far_first:
        came[k] = across(sends[k], peers, k)
    arrived = [part for k in range(1, peers) for part in pieces[k]]
    ordered, arrived = lax.optimization_barrier(([came[k] for k in far_first], arrived))
    came = [None] + [ordered[far_first.index(k)] for k in range(1, peers)]
    stacked = stack(arrived)
    swapped = ahead(stacked, "rep", reps, 1)
    cots = [own_cot]
    if feats > 1:
        waited = after(own_cot, stacked)
        cots += [ahead(waited, "feat", feats, feats - q) for q in range(1, feats)]
    acc, ids = first_rows(features, operator, asks[0], came, own_mirror, peers)
    give, keep = far_rows(acc, asks, stacked, swapped, operator, peers, reps)

    mine = add_up(keep, ahead(give, "rep", reps, 1))
    sums = [mine] + [ahead(mine, "feat", feats, feats - q) for q in range(1, feats)]
    act, give, spread, keep = dense(sums, cots, weight, feats, reps)
    shared = ahead(give, "rep", reps, 1)
    values, sends, own_mirror, term = sends_of(spread, shared, keep, operator, ids, peers, reps)

    came = [None] * peers
    for k in far_first:
        came[k] = across(sends[k], peers, k)
    middle = peers // 2
    total = pair_sum(term, came[middle], 2 * CAP * width, F32 if middle == 1 else BF16)
    bit = middle // 2
    while bit:
        total = pair_sum(total, across(total, peers, bit), 0, F32 if bit == 1 else BF16)
        bit //= 2
    late = far_first[-2]
    acc = late_rows([asks[0], values, own_mirror], ids, came, [k for k in far_first if k != late], operator, True, False)
    acc, total = lax.optimization_barrier((acc, total))
    part = late_rows([acc], ids, came, [late], operator, False, True)
    input_grad, weight_grad, activated = finish(
        part, ahead(part, "rep", reps, 1), total, ahead(total, "rep", reps, 1), act, shared
    )
    return (activated, input_grad, weight_grad)


def solution(mesh):
    placed = (
        P(("parts", "graph"), "feat", None),
        P(),
        P(("parts", "graph"), "feat", None),
        P(("parts", "graph", "rep"), None, None),
        P(("parts", "graph", "rep")),
        P(("parts", "graph", "rep")),
        P(("parts", "graph", "rep")),
    )
    return jax.shard_map(
        local,
        mesh=mesh,
        in_specs=placed,
        out_specs=(
            P(("parts", "graph"), "feat", None),
            P(("parts", "graph"), "feat", None),
            P("parts", "feat"),
        ),
        check_vma=False,
    )
```

```python
import functools

import jax
import jax.numpy as jnp
from jax import lax
from jax.experimental import pallas as pl
from jax.experimental.pallas import tpu as pltpu
from jax.sharding import PartitionSpec as P

CAP = 2
GROUP = 8
CHUNK = 16
SIDES = 2
TAIL = 16
VMEM_LIMIT = 40 * 2 ** 20
VMEM_MOST = 50 * 2 ** 20
VMEM_ALL = 58 * 2 ** 20

NT = (((1,), (1,)), ((), ()))
TN = (((0,), (0,)), ((), ()))
F32 = jnp.float32
BF16 = jnp.bfloat16


def vmem():
    return pl.BlockSpec(memory_space=pltpu.VMEM)


def smem():
    return pl.BlockSpec(memory_space=pltpu.SMEM)


def hbm():
    return pl.BlockSpec(memory_space=pltpu.HBM)


def shape(dims, dtype):
    return jax.ShapeDtypeStruct(tuple(dims), dtype)


def dot(a, b, dims=None):
    if dims is None:
        return jnp.dot(a, b, preferred_element_type=F32)
    return lax.dot_general(a, b, dims, preferred_element_type=F32)


def call(kernel, name, outs, in_specs, scratch=(), flops=0, moved=2 ** 18, limit=VMEM_LIMIT, **kwargs):
    return pl.pallas_call(
        kernel,
        out_shape=outs,
        in_specs=in_specs,
        scratch_shapes=list(scratch),
        compiler_params=pltpu.CompilerParams(vmem_limit_bytes=limit),
        cost_estimate=pl.CostEstimate(flops=flops, bytes_accessed=moved, transcendentals=0),
        name=name,
        **kwargs,
    )


def lanes(x3):
    return jnp.concatenate([x3[b] for b in range(x3.shape[0])], axis=1)


def places(peers, blocks_dev, count, row, col, ask_refs):
    me = lax.axis_index("graph")
    lane = lax.broadcasted_iota(jnp.int32, col.shape, 1)
    live = lane < count
    place = jnp.full(col.shape, peers * CAP * blocks_dev, jnp.int32)
    for k in range(peers):
        local = col - jnp.bitwise_xor(me, k) * blocks_dev
        inside = live & (local >= 0) & (local < blocks_dev)
        low = jnp.min(jnp.where(inside, local, blocks_dev - 1), axis=1, keepdims=True)
        high = jnp.max(jnp.where(inside, local, 0), axis=1, keepdims=True)
        ask_refs[k][...] = jnp.where(lane == 0, low, high)
        slot = k * CAP + (local != low).astype(jnp.int32)
        place = jnp.where(inside, slot * blocks_dev + row, place)
    return place


def prepare_kernel(peers, count_ref, row_ref, col_ref, x3, half_ref, place_ref, *ask_refs):
    share = half_ref.shape[0]
    half_ref[...] = x3[pl.ds(lax.axis_index("rep") * share, share)]
    count = jnp.broadcast_to(count_ref[...], (1, 1))
    place_ref[...] = places(peers, x3.shape[0], count, row_ref[...], col_ref[...], ask_refs)


def prepare(features, tile_row, tile_col, tile_count, peers, reps):
    per = tile_col.shape[0]
    blocks_dev, columns, width = features.shape
    outs = call(
        functools.partial(prepare_kernel, peers),
        "prepare",
        [shape((blocks_dev // reps, columns, width), BF16)] + [shape((1, per), jnp.int32)] * (peers + 1),
        [vmem()] * 4,
        limit=VMEM_ALL,
    )(tile_count, tile_row.reshape(1, per), tile_col.reshape(1, per), features)
    return outs[0], outs[1], list(outs[2:])


def pick(ids_ref, lane):
    ids = ids_ref[...].astype(F32)
    at = lax.broadcasted_iota(jnp.int32, ids.shape, 1)
    return jnp.max(jnp.where(at == lane, ids, 0.0)).astype(jnp.int32)


def operator_kernel(blocks_dev, slots_here, groups, place_in, tiles_ref, m_ref, tiles, acc, place_ref, sems, sem):
    step = pl.program_id(0)
    per, width = tiles.shape[0], tiles.shape[1]
    chunks = per // CHUNK
    spare = slots_here * blocks_dev

    def chunk_copy(c):
        part = pl.ds(c * CHUNK, CHUNK)
        return pltpu.make_async_copy(tiles_ref.at[part], tiles.at[part], sems.at[c])

    @pl.when(step == 0)
    def _():
        placed = pltpu.make_async_copy(place_in, place_ref, sem)
        placed.start()
        for c in range(chunks):
            chunk_copy(c).start()
        placed.wait()

    acc[...] = jnp.zeros_like(acc)

    def add_chunk(c, carry):
        @pl.when(step == 0)
        def _():
            chunk_copy(c).wait()

        for u in range(CHUNK):
            t = c * CHUNK + u
            place = place_ref[0, t]
            if groups > 1:
                place = place - step * spare
                place = jnp.where((place >= 0) & (place < spare), place, spare)
            side = u % SIDES
            acc[side, place] = acc[side, place] + tiles[t].astype(F32)
        return carry

    lax.fori_loop(0, chunks, add_chunk, 0)
    for s in range(slots_here):
        for r in range(blocks_dev):
            total = acc[0, s * blocks_dev + r]
            for side in range(1, SIDES):
                total = total + acc[side, s * blocks_dev + r]
            m_ref[r * width : (r + 1) * width, s * width : (s + 1) * width] = total.astype(BF16)


def list_operator(tiles, place, peers, blocks_dev):
    per, width = tiles.shape[0], tiles.shape[1]
    slots = peers * CAP
    slots_here = min(slots, GROUP)
    groups = slots // slots_here
    return call(
        functools.partial(operator_kernel, blocks_dev, slots_here, groups),
        "operator",
        shape((blocks_dev * width, slots * width), BF16),
        [pl.BlockSpec(memory_space=pl.ANY), hbm()],
        [
            pltpu.VMEM((per, width, width), BF16),
            pltpu.VMEM((SIDES, slots_here * blocks_dev + 1, width, width), F32),
            pltpu.SMEM((1, per), jnp.int32),
            pltpu.SemaphoreType.DMA((per // CHUNK,)),
            pltpu.SemaphoreType.DMA,
        ],
        moved=2 ** 24,
        limit=VMEM_MOST,
        grid=(groups,),
        out_specs=pl.BlockSpec((blocks_dev * width, slots_here * width), lambda i: (0, i)),
    )(place, tiles)


def mirrored(near, m_ref, mir, slots, width):
    if slots <= GROUP:
        mir[...] = dot(near, m_ref[...])
    else:
        part = GROUP * width

        @pl.loop(0, slots // GROUP)
        def _(i):
            where = pl.ds(pl.multiple_of(i * part, part), part)
            mir[:, where] = dot(near, m_ref[:, where])


def first_sends_kernel(peers, *refs):
    ask_refs, refs = refs[: peers - 1], refs[peers - 1 :]
    x3, cot, m_ref, refs = refs[0], refs[1], refs[2], refs[3:]
    send_refs, self_ref, cot_ref, mir = refs[: peers - 1], refs[peers - 1], refs[peers], refs[peers + 1]
    _, columns, width = x3.shape
    share = cot_ref.shape[0]
    both = CAP * width
    half = lax.axis_index("rep")
    mirrored(lanes(x3), m_ref, mir, peers * CAP, width)
    self_ref[...] = mir[:, :both]
    lane = lax.broadcasted_iota(jnp.int32, (TAIL, both), 1)
    for k in range(1, peers):
        out = send_refs[k - 1]
        out[:columns, :] = mir[:, k * both : (k + 1) * both].astype(BF16)
        low, high = ask_refs[k - 1][:, :1], ask_refs[k - 1][:, 1:2]
        out[columns : columns + TAIL, :] = jnp.where(lane < width, low, high).astype(F32).astype(BF16)
    for b in range(share):
        top = columns + TAIL + b // CAP * columns
        left = b % CAP * width
        send_refs[0][top : top + columns, left : left + width] = x3[half * share + b]
    cot_ref[...] = cot[pl.ds(half * share, share)]


def first_sends(values, cotangent, operator, asks, peers, reps):
    blocks_dev, columns, width = values.shape
    share = blocks_dev // reps
    outs = call(
        functools.partial(first_sends_kernel, peers),
        "first_sends",
        [shape((columns + TAIL + share // CAP * columns, CAP * width), BF16)]
        + [shape((columns + TAIL, CAP * width), BF16)] * (peers - 2)
        + [shape((columns, CAP * width), F32), shape((share, columns, width), BF16)],
        [vmem()] * (peers + 2),
        [pltpu.VMEM((columns, peers * CAP * width), F32)],
        flops=2 ** 28,
        moved=2 ** 21,
    )(*asks, values, cotangent, operator)
    return [None] + list(outs[: peers - 1]), outs[peers - 1], outs[peers]


def add_sums(acc, block, sums):
    acc[block] = acc[block] + sums.astype(F32)


def own_rows(far, m_ref, k):
    both = far.shape[1]
    return dot(far, m_ref[:, k * both : (k + 1) * both], NT)


def put_rows(acc, own, before=None):
    blocks_dev, _, width = acc.shape
    for b in range(blocks_dev):
        add = own[:, b * width : (b + 1) * width]
        acc[b] = add if before is None else before[b] + add


def split_rows(acc, give_ref, keep_ref):
    half = lax.axis_index("rep")
    share = give_ref.shape[0]
    give_ref[...] = acc[pl.ds((1 - half) * share, share)].astype(BF16)
    keep_ref[...] = acc[pl.ds(half * share, share)]


def self_rows(x3, m_ref, ask_ref):
    far = jnp.concatenate([x3[pick(ask_ref, s)] for s in range(CAP)], axis=1)
    return own_rows(far, m_ref, 0)


def far_of(block, mine_ref, other_ref, ask_ref, at=0):
    half = lax.axis_index("rep")
    share = block.shape[0] // 2
    block[pl.ds(half * share, share)] = mine_ref[at * share : (at + 1) * share]
    block[pl.ds((1 - half) * share, share)] = other_ref[at * share : (at + 1) * share]
    return jnp.concatenate([block[pick(ask_ref, s)] for s in range(CAP)], axis=1)


def first_rows_kernel(peers, *refs):
    ask_ref, refs = refs[0], refs[1:]
    came_refs, refs = refs[: peers - 1], refs[peers - 1 :]
    x3, m_ref, self_ref, acc, ids_refs = refs[0], refs[1], refs[2], refs[3], refs[4:]
    _, columns, width = x3.shape
    put_rows(acc, self_rows(x3, m_ref, ask_ref))
    for s in range(CAP):
        add_sums(acc, pick(ask_ref, s), self_ref[:, s * width : (s + 1) * width])
    lane = lax.broadcasted_iota(jnp.int32, ids_refs[0].shape, 1)
    for k in range(1, peers):
        came = came_refs[k - 1]
        ids = jnp.zeros(lane.shape, jnp.int32)
        for s in range(CAP):
            here = slice(s * width, (s + 1) * width)
            asked = jnp.max(came[columns : columns + TAIL, here].astype(F32)).astype(jnp.int32)
            ids = jnp.where(lane == s, asked, ids)
            add_sums(acc, asked, came[:columns, here])
        ids_refs[k - 1][...] = ids


def first_rows(values, operator, ask, came, own_mirror, peers):
    _, columns, width = values.shape
    outs = call(
        functools.partial(first_rows_kernel, peers),
        "first_rows",
        [shape(values.shape, F32)] + [shape((1, width), jnp.int32)] * (peers - 1),
        [vmem()] * (peers + 3),
        flops=2 ** 27,
        moved=2 ** 20,
    )(ask, *came[1:], values, operator, own_mirror)
    return outs[0], [None] + list(outs[1:])


def stack_kernel(below_ref, *refs):
    out_ref = refs[-1]
    _, columns, width = out_ref.shape
    at = (below_ref.shape[0] - TAIL) // columns * CAP - CAP
    for b in range(at):
        top = columns + TAIL + b // CAP * columns
        left = b % CAP * width
        out_ref[b] = below_ref[top : top + columns, left : left + width]
    for ref in refs[:-1]:
        share = ref.shape[0]
        out_ref[at : at + share] = ref[...]
        at += share


def halves_kernel(in_ref, low_ref, high_ref):
    share = low_ref.shape[0]
    low_ref[...] = in_ref[:share]
    high_ref[...] = in_ref[share:]


def halves(parts):
    if len(parts) > 1:
        return parts
    share, columns, width = parts[0].shape
    part = shape((share // 2, columns, width), BF16)
    return list(call(halves_kernel, "halves", [part, part], [vmem()])(*parts))


def stack(below, pieces):
    _, columns, width = pieces[0].shape
    count = (below.shape[0] - TAIL) // columns * CAP - CAP + sum(piece.shape[0] for piece in pieces)
    out = shape((count, columns, width), BF16)
    return call(stack_kernel, "stack", out, [vmem()] * (len(pieces) + 1))(below, *pieces)


def far_rows_kernel(peers, *refs):
    ask_refs, refs = refs[: peers - 1], refs[peers - 1 :]
    before, mine_ref, other_ref, m_ref, give_ref, keep_ref, acc, block, far = refs
    both = CAP * acc.shape[2]
    for k in range(1, peers):
        far[:, k * both : (k + 1) * both] = far_of(block, mine_ref, other_ref, ask_refs[k - 1], k - 1)
    if peers * CAP <= GROUP:
        own = dot(far[:, both:], m_ref[:, both:], NT)
    else:

        def add_peer(k, total):
            here = pl.ds(pl.multiple_of(k * both, both), both)
            return total + dot(far[:, here], m_ref[:, here], NT)

        own = lax.fori_loop(1, peers, add_peer, jnp.zeros((acc.shape[1], m_ref.shape[0]), F32))
    put_rows(acc, own, before)
    split_rows(acc, give_ref, keep_ref)


def far_rows(before, asks, mine, other, operator, peers, reps):
    blocks_dev, columns, width = before.shape
    share = (blocks_dev // reps, columns, width)
    return call(
        functools.partial(far_rows_kernel, peers),
        "far_rows",
        [shape(share, BF16), shape(share, F32)],
        [vmem()] * (peers + 3),
        [
            pltpu.VMEM(before.shape, F32),
            pltpu.VMEM(before.shape, BF16),
            pltpu.VMEM((columns, peers * CAP * width), BF16),
        ],
        flops=2 ** 28,
        moved=2 ** 21,
    )(*asks[1:], before, mine, other, operator)


def late_rows_kernel(ks, first, last, *refs):
    if first:
        ask_ref, x3, self_ref = refs[:3]
    else:
        before = refs[0]
    refs = refs[3 if first else 1 :]
    ids_refs, refs = refs[: len(ks)], refs[len(ks) :]
    came_refs, refs = refs[: len(ks)], refs[len(ks) :]
    m_ref, out_ref = refs[:2]
    acc = refs[2] if last else out_ref
    width = acc.shape[2]
    both = CAP * width
    own = self_rows(x3, m_ref, ask_ref) if first else None
    for i, k in enumerate(ks):
        add = own_rows(came_refs[i][:, both : 2 * both], m_ref, k)
        own = add if own is None else own + add
    put_rows(acc, own, None if first else before)
    if first:
        for s in range(CAP):
            add_sums(acc, pick(ask_ref, s), self_ref[:, s * width : (s + 1) * width])
    for i in range(len(ks)):
        for s in range(CAP):
            add_sums(acc, pick(ids_refs[i], s), came_refs[i][:, s * width : (s + 1) * width])
    if last:
        out_ref[...] = acc[...].astype(BF16)


def late_rows(head, ids, came, ks, operator, first, last):
    values = head[1] if first else head[0]
    return call(
        functools.partial(late_rows_kernel, ks, first, last),
        "late_rows",
        shape(values.shape, BF16 if last else F32),
        [vmem()] * (len(head) + 2 * len(ks) + 1),
        [pltpu.VMEM(values.shape, F32)] if last else [],
        flops=2 ** 27,
        moved=2 ** 20,
    )(*head, *[ids[k] for k in ks], *[came[k] for k in ks], operator)


def add_kernel(keep_ref, came_ref, out_ref):
    out_ref[...] = (keep_ref[...] + came_ref[...].astype(F32)).astype(BF16)


def add_up(keep, came):
    return call(add_kernel, "add_up", shape(came.shape, BF16), [vmem(), vmem()])(keep, came)


def widen_kernel(feats, *refs):
    out_ref = refs[feats]
    share, columns, width = refs[0].shape
    me = lax.axis_index("feat")
    for q in range(feats):
        rows = pl.ds(pl.multiple_of(lax.rem(me + q, feats) * columns, columns), columns)
        for b in range(share):
            out_ref[rows, b * width : (b + 1) * width] = refs[q][b]


def widen(parts):
    share, columns, width = parts[0].shape
    out = shape((len(parts) * columns, share * width), BF16)
    kernel = functools.partial(widen_kernel, len(parts))
    return call(kernel, "widen", out, [vmem()] * len(parts))(*parts)


def dense_kernel(feats, *refs):
    sums, wide_cot, refs = refs[:feats], refs[feats], refs[feats + 1 :]
    w_ref, act_ref, give_ref, spread_ref, keep_ref, wide, pre_scr, grad, term = refs
    share, columns, width = act_ref.shape
    me = lax.axis_index("feat")
    half = lax.axis_index("rep")
    rows = [pl.ds(pl.multiple_of(lax.rem(me + q, feats) * columns, columns), columns) for q in range(feats)]
    for q in range(feats):
        for b in range(share):
            wide[rows[q], b * width : (b + 1) * width] = sums[q][b]
    pre = dot(w_ref[...], wide[...], TN)
    pre_scr[...] = pre
    sig = jax.nn.sigmoid(pre)
    factor = wide_cot[...].astype(F32) * sig * (1.0 + pre * (1.0 - sig))
    grad[...] = factor.astype(BF16)
    spread = dot(w_ref[rows[0], :], grad[...]).astype(BF16)
    term[...] = dot(grad[rows[0], :], wide[...], NT)
    part = keep_ref.shape[1]
    wide_share = share * width
    give_ref[:, :wide_share] = spread
    give_ref[:, 2 * wide_share :] = term[:, pl.ds(pl.multiple_of((1 - half) * part, part), part)].astype(BF16)
    keep_ref[...] = term[:, pl.ds(pl.multiple_of(half * part, part), part)]
    for b in range(share):
        spread_ref[b] = spread[:, b * width : (b + 1) * width]
    own = pre_scr[rows[0], :]
    act = (own * jax.nn.sigmoid(own)).astype(BF16)
    give_ref[:, wide_share : 2 * wide_share] = act
    for b in range(share):
        act_ref[b] = act[:, b * width : (b + 1) * width]


def dense(sums, cot, weight, feats, reps):
    share, columns, width = sums[0].shape
    features = weight.shape[0]
    part = features // reps
    return call(
        functools.partial(dense_kernel, feats),
        "dense",
        [
            shape((share, columns, width), BF16),
            shape((columns, 2 * share * width + part), BF16),
            shape((share, columns, width), BF16),
            shape((columns, part), F32),
        ],
        [vmem()] * (feats + 2),
        [
            pltpu.VMEM((features, share * width), BF16),
            pltpu.VMEM((features, share * width), F32),
            pltpu.VMEM((features, share * width), BF16),
            pltpu.VMEM((columns, features), F32),
        ],
        flops=2 ** 28,
        moved=2 ** 20,
    )(*sums, cot, weight)


def send_kernel(peers, *refs):
    ids_refs, refs = refs[: peers - 1], refs[peers - 1 :]
    mine_ref, came_ref, keep_ref, m_ref, refs = refs[0], refs[1], refs[2], refs[3], refs[4:]
    x3, refs = refs[0], refs[1:]
    send_refs, refs = refs[: peers - 1], refs[peers - 1 :]
    self_ref, term_ref, mir = refs
    share, _, width = mine_ref.shape
    both = CAP * width
    half = lax.axis_index("rep")
    x3[pl.ds(half * share, share)] = mine_ref[...]
    for b in range(share):
        x3[(1 - half) * share + b] = came_ref[:, b * width : (b + 1) * width]
    term = (keep_ref[...] + came_ref[:, 2 * share * width :].astype(F32)).astype(BF16)
    term_ref[...] = term
    mirrored(lanes(x3), m_ref, mir, peers * CAP, width)
    self_ref[...] = mir[:, :both]
    for k in range(1, peers):
        out = send_refs[k - 1]
        out[:, :both] = mir[:, k * both : (k + 1) * both].astype(BF16)
        for s in range(CAP):
            at = (CAP + s) * width
            out[:, at : at + width] = x3[pick(ids_refs[k - 1], s)]
        out[:, 2 * both :] = term


def sends_of(mine, came, keep, operator, ids, peers, reps):
    share, columns, width = mine.shape
    chunk = 2 * CAP * width
    outs = call(
        functools.partial(send_kernel, peers),
        "sends",
        [shape((share * reps, columns, width), BF16)]
        + [shape((columns, chunk + keep.shape[1]), BF16)] * (peers - 1)
        + [shape((columns, CAP * width), F32), shape(keep.shape, BF16)],
        [vmem()] * (peers + 3),
        [pltpu.VMEM((columns, peers * CAP * width), F32)],
        flops=2 ** 28,
        moved=2 ** 21,
    )(*ids[1:], mine, came, keep, operator)
    return outs[0], [None] + list(outs[1:peers]), outs[peers], outs[peers + 1]


def terms_kernel(peers, at, *refs):
    out_ref, terms = refs[peers], refs[peers + 1]
    me = lax.axis_index("graph")
    terms[0] = refs[0][...].astype(F32)
    for k in range(1, peers):
        terms[k] = refs[k][:, at:].astype(F32)
    total = terms[me]
    for p in range(1, peers):
        total = total + terms[jnp.bitwise_xor(me, p)]
    out_ref[...] = total


def sum_terms(term, came, at):
    peers = len(came)
    return call(
        functools.partial(terms_kernel, peers, at),
        "terms",
        shape(term.shape, F32),
        [vmem()] * peers,
        [pltpu.VMEM((peers,) + term.shape, F32)],
    )(term, *came[1:])


def finish_kernel(mine_ref, other_ref, share_ref, other_share_ref, act_ref, came_ref, grad_ref, weight_ref, out_ref):
    half = lax.axis_index("rep")
    share = share_ref.shape[1]
    grad_ref[...] = (mine_ref[...].astype(F32) + other_ref[...].astype(F32)).astype(BF16)
    weight_ref[pl.ds(pl.multiple_of(half * share, share), share), :] = share_ref[...].T
    weight_ref[pl.ds(pl.multiple_of((1 - half) * share, share), share), :] = other_share_ref[...].T
    blocks, _, width = act_ref.shape
    out_ref[pl.ds(half * blocks, blocks)] = act_ref[...]
    for b in range(blocks):
        at = (blocks + b) * width
        out_ref[(1 - half) * blocks + b] = came_ref[:, at : at + width]


def finish(mine, other, share, other_share, act, came):
    columns, width = share.shape
    return call(
        finish_kernel,
        "finish",
        [shape(mine.shape, BF16), shape((2 * width, columns), F32), shape(mine.shape, BF16)],
        [vmem()] * 6,
    )(mine, other, share, other_share, act, came)


def ahead(value, axis, size, k):
    return lax.ppermute(value, axis, [(i, (i + k) % size) for i in range(size)])


def across(value, peers, k):
    return lax.ppermute(value, "graph", [(i, i ^ k) for i in range(peers)])


def after(value, first):
    return lax.optimization_barrier((value, first))[0]


def local(features, weight, cotangent, tiles, tile_row, tile_col, tile_count):
    blocks_dev, _, width = features.shape
    peers = lax.axis_size("graph")
    feats = lax.axis_size("feat")
    reps = lax.axis_size("rep")
    far_first = sorted(range(1, peers), key=lambda k: (-(k & (peers // 2)), k))

    half, place, asks = prepare(features, tile_row, tile_col, tile_count, peers, reps)
    operator = list_operator(tiles, place, peers, blocks_dev)
    sends, own_mirror, own_cot = first_sends(features, cotangent, operator, asks[1:], peers, reps)
    pieces, held = {0: [half]}, [0]
    bit = peers // 2
    while bit:
        for k in held:
            if k ^ bit == 1:
                continue
            parts = halves(after(pieces[k], sends[1])) if k else pieces[k]
            pieces[k ^ bit] = [across(part, peers, bit) for part in parts]
        held = held + [k ^ bit for k in held]
        bit //= 2
    came = [None] * peers
    for k in far_first:
        send = after(sends[k], pieces[peers // 2]) if k == peers - 1 else sends[k]
        came[k] = across(send, peers, k)
    arrived = [part for k in range(2, peers) for part in pieces[k]]
    ordered, arrived = lax.optimization_barrier(([came[k] for k in far_first], arrived))
    came = [None] + [ordered[far_first.index(k)] for k in range(1, peers)]
    stacked = stack(came[1], arrived)
    swapped = ahead(stacked, "rep", reps, 1)
    cots = [own_cot]
    if feats > 1:
        waited = after(own_cot, stacked)
        cots += [ahead(waited, "feat", feats, feats - q) for q in range(1, feats)]
    acc, ids = first_rows(features, operator, asks[0], came, own_mirror, peers)
    give, keep = far_rows(acc, asks, stacked, swapped, operator, peers, reps)

    mine = add_up(keep, ahead(give, "rep", reps, 1))
    cot = widen(cots)
    sums = [mine] + [ahead(mine, "feat", feats, feats - q) for q in range(1, feats)]
    act, give, spread, keep = dense(sums, cot, weight, feats, reps)
    shared = ahead(give, "rep", reps, 1)
    values, sends, own_mirror, term = sends_of(spread, shared, keep, operator, ids, peers, reps)

    came = [None] * peers
    for k in far_first:
        came[k] = across(sends[k], peers, k)
    ordered = lax.optimization_barrier([came[k] for k in far_first])
    came = [None] + [ordered[far_first.index(k)] for k in range(1, peers)]
    part = late_rows([asks[0], values, own_mirror], ids, came, far_first, operator, True, True)
    total = sum_terms(term, came, 2 * CAP * width)
    input_grad, weight_grad, activated = finish(
        part, ahead(part, "rep", reps, 1), total, ahead(total, "rep", reps, 1), act, shared
    )
    return (activated, input_grad, weight_grad)


def solution(mesh):
    placed = (
        P(("parts", "graph"), "feat", None),
        P(),
        P(("parts", "graph"), "feat", None),
        P(("parts", "graph", "rep"), None, None),
        P(("parts", "graph", "rep")),
        P(("parts", "graph", "rep")),
        P(("parts", "graph", "rep")),
    )
    return jax.shard_map(
        local,
        mesh=mesh,
        in_specs=placed,
        out_specs=(
            P(("parts", "graph"), "feat", None),
            P(("parts", "graph"), "feat", None),
            P("parts", "feat"),
        ),
        check_vma=False,
    )
```

```python
import functools

import jax
import jax.numpy as jnp
from jax import lax
from jax.experimental import pallas as pl
from jax.experimental.pallas import tpu as pltpu
from jax.sharding import PartitionSpec as P

CAP = 2
GROUP = 8
CHUNK = 16
SIDES = 2
TAIL = 16
VMEM_LIMIT = 40 * 2 ** 20
VMEM_MOST = 50 * 2 ** 20
VMEM_ALL = 58 * 2 ** 20

NT = (((1,), (1,)), ((), ()))
TN = (((0,), (0,)), ((), ()))
F32 = jnp.float32
BF16 = jnp.bfloat16


def vmem():
    return pl.BlockSpec(memory_space=pltpu.VMEM)


def smem():
    return pl.BlockSpec(memory_space=pltpu.SMEM)


def hbm():
    return pl.BlockSpec(memory_space=pltpu.HBM)


def shape(dims, dtype):
    return jax.ShapeDtypeStruct(tuple(dims), dtype)


def dot(a, b, dims=None):
    if dims is None:
        return jnp.dot(a, b, preferred_element_type=F32)
    return lax.dot_general(a, b, dims, preferred_element_type=F32)


def call(kernel, name, outs, in_specs, scratch=(), flops=0, moved=2 ** 18, limit=VMEM_LIMIT, **kwargs):
    return pl.pallas_call(
        kernel,
        out_shape=outs,
        in_specs=in_specs,
        scratch_shapes=list(scratch),
        compiler_params=pltpu.CompilerParams(vmem_limit_bytes=limit),
        cost_estimate=pl.CostEstimate(flops=flops, bytes_accessed=moved, transcendentals=0),
        name=name,
        **kwargs,
    )


def lanes(x3):
    return jnp.concatenate([x3[b] for b in range(x3.shape[0])], axis=1)


def places(peers, blocks_dev, count, row, col, ask_refs):
    me = lax.axis_index("graph")
    lane = lax.broadcasted_iota(jnp.int32, col.shape, 1)
    live = lane < count
    place = jnp.full(col.shape, peers * CAP * blocks_dev, jnp.int32)
    for k in range(peers):
        local = col - jnp.bitwise_xor(me, k) * blocks_dev
        inside = live & (local >= 0) & (local < blocks_dev)
        low = jnp.min(jnp.where(inside, local, blocks_dev - 1), axis=1, keepdims=True)
        high = jnp.max(jnp.where(inside, local, 0), axis=1, keepdims=True)
        ask_refs[k][...] = jnp.where(lane == 0, low, high)
        slot = k * CAP + (local != low).astype(jnp.int32)
        place = jnp.where(inside, slot * blocks_dev + row, place)
    return place


def prepare_kernel(peers, count_ref, row_ref, col_ref, x3, half_ref, place_ref, *ask_refs):
    share = half_ref.shape[0]
    half_ref[...] = x3[pl.ds(lax.axis_index("rep") * share, share)]
    count = jnp.broadcast_to(count_ref[...], (1, 1))
    place_ref[...] = places(peers, x3.shape[0], count, row_ref[...], col_ref[...], ask_refs)


def prepare(features, tile_row, tile_col, tile_count, peers, reps):
    per = tile_col.shape[0]
    blocks_dev, columns, width = features.shape
    outs = call(
        functools.partial(prepare_kernel, peers),
        "prepare",
        [shape((blocks_dev // reps, columns, width), BF16)] + [shape((1, per), jnp.int32)] * (peers + 1),
        [vmem()] * 4,
        limit=VMEM_ALL,
    )(tile_count, tile_row.reshape(1, per), tile_col.reshape(1, per), features)
    return outs[0], outs[1], list(outs[2:])


def pick(ids_ref, lane):
    ids = ids_ref[...].astype(F32)
    at = lax.broadcasted_iota(jnp.int32, ids.shape, 1)
    return jnp.max(jnp.where(at == lane, ids, 0.0)).astype(jnp.int32)


def operator_kernel(blocks_dev, slots_here, groups, place_in, tiles_ref, m_ref, tiles, acc, place_ref, sems, sem):
    step = pl.program_id(0)
    per, width = tiles.shape[0], tiles.shape[1]
    chunks = per // CHUNK
    spare = slots_here * blocks_dev

    def chunk_copy(c):
        part = pl.ds(c * CHUNK, CHUNK)
        return pltpu.make_async_copy(tiles_ref.at[part], tiles.at[part], sems.at[c])

    @pl.when(step == 0)
    def _():
        placed = pltpu.make_async_copy(place_in, place_ref, sem)
        placed.start()
        for c in range(chunks):
            chunk_copy(c).start()
        placed.wait()

    acc[...] = jnp.zeros_like(acc)

    def add_chunk(c, carry):
        @pl.when(step == 0)
        def _():
            chunk_copy(c).wait()

        for u in range(CHUNK):
            t = c * CHUNK + u
            place = place_ref[0, t]
            if groups > 1:
                place = place - step * spare
                place = jnp.where((place >= 0) & (place < spare), place, spare)
            side = u % SIDES
            acc[side, place] = acc[side, place] + tiles[t].astype(F32)
        return carry

    lax.fori_loop(0, chunks, add_chunk, 0)
    for s in range(slots_here):
        for r in range(blocks_dev):
            total = acc[0, s * blocks_dev + r]
            for side in range(1, SIDES):
                total = total + acc[side, s * blocks_dev + r]
            m_ref[r * width : (r + 1) * width, s * width : (s + 1) * width] = total.astype(BF16)


def list_operator(tiles, place, peers, blocks_dev):
    per, width = tiles.shape[0], tiles.shape[1]
    slots = peers * CAP
    slots_here = min(slots, GROUP)
    groups = slots // slots_here
    return call(
        functools.partial(operator_kernel, blocks_dev, slots_here, groups),
        "operator",
        shape((blocks_dev * width, slots * width), BF16),
        [pl.BlockSpec(memory_space=pl.ANY), hbm()],
        [
            pltpu.VMEM((per, width, width), BF16),
            pltpu.VMEM((SIDES, slots_here * blocks_dev + 1, width, width), F32),
            pltpu.SMEM((1, per), jnp.int32),
            pltpu.SemaphoreType.DMA((per // CHUNK,)),
            pltpu.SemaphoreType.DMA,
        ],
        moved=2 ** 24,
        limit=VMEM_MOST,
        grid=(groups,),
        out_specs=pl.BlockSpec((blocks_dev * width, slots_here * width), lambda i: (0, i)),
    )(place, tiles)


def mirrored(near, m_ref, mir, slots, width):
    if slots <= GROUP:
        mir[...] = dot(near, m_ref[...])
    else:
        part = GROUP * width

        @pl.loop(0, slots // GROUP)
        def _(i):
            where = pl.ds(pl.multiple_of(i * part, part), part)
            mir[:, where] = dot(near, m_ref[:, where])


def first_sends_kernel(peers, *refs):
    ask_refs, refs = refs[: peers - 1], refs[peers - 1 :]
    x3, cot, m_ref, refs = refs[0], refs[1], refs[2], refs[3:]
    send_refs, self_ref, cot_ref, mir = refs[: peers - 1], refs[peers - 1], refs[peers], refs[peers + 1]
    _, columns, width = x3.shape
    share = cot_ref.shape[0]
    both = CAP * width
    half = lax.axis_index("rep")
    mirrored(lanes(x3), m_ref, mir, peers * CAP, width)
    self_ref[...] = mir[:, :both]
    lane = lax.broadcasted_iota(jnp.int32, (TAIL, both), 1)
    for k in range(1, peers):
        out = send_refs[k - 1]
        out[:columns, :] = mir[:, k * both : (k + 1) * both].astype(BF16)
        low, high = ask_refs[k - 1][:, :1], ask_refs[k - 1][:, 1:2]
        out[columns : columns + TAIL, :] = jnp.where(lane < width, low, high).astype(F32).astype(BF16)
    for b in range(share):
        top = columns + TAIL + b // CAP * columns
        left = b % CAP * width
        send_refs[0][top : top + columns, left : left + width] = x3[half * share + b]
    cot_ref[...] = cot[pl.ds(half * share, share)]


def first_sends(values, cotangent, operator, asks, peers, reps):
    blocks_dev, columns, width = values.shape
    share = blocks_dev // reps
    outs = call(
        functools.partial(first_sends_kernel, peers),
        "first_sends",
        [shape((columns + TAIL + share // CAP * columns, CAP * width), BF16)]
        + [shape((columns + TAIL, CAP * width), BF16)] * (peers - 2)
        + [shape((columns, CAP * width), F32), shape((share, columns, width), BF16)],
        [vmem()] * (peers + 2),
        [pltpu.VMEM((columns, peers * CAP * width), F32)],
        flops=2 ** 28,
        moved=2 ** 21,
    )(*asks, values, cotangent, operator)
    return [None] + list(outs[: peers - 1]), outs[peers - 1], outs[peers]


def add_sums(acc, block, sums):
    acc[block] = acc[block] + sums.astype(F32)


def own_rows(far, m_ref, k):
    both = far.shape[1]
    return dot(far, m_ref[:, k * both : (k + 1) * both], NT)


def put_rows(acc, own, before=None):
    blocks_dev, _, width = acc.shape
    for b in range(blocks_dev):
        add = own[:, b * width : (b + 1) * width]
        acc[b] = add if before is None else before[b] + add


def split_rows(acc, give_ref, keep_ref):
    half = lax.axis_index("rep")
    share = give_ref.shape[0]
    give_ref[...] = acc[pl.ds((1 - half) * share, share)].astype(BF16)
    keep_ref[...] = acc[pl.ds(half * share, share)]


def self_rows(x3, m_ref, ask_ref):
    far = jnp.concatenate([x3[pick(ask_ref, s)] for s in range(CAP)], axis=1)
    return own_rows(far, m_ref, 0)


def far_of(block, mine_ref, other_ref, ask_ref, at=0):
    half = lax.axis_index("rep")
    share = block.shape[0] // 2
    block[pl.ds(half * share, share)] = mine_ref[at * share : (at + 1) * share]
    block[pl.ds((1 - half) * share, share)] = other_ref[at * share : (at + 1) * share]
    return jnp.concatenate([block[pick(ask_ref, s)] for s in range(CAP)], axis=1)


def first_rows_kernel(peers, *refs):
    ask_ref, refs = refs[0], refs[1:]
    came_refs, refs = refs[: peers - 1], refs[peers - 1 :]
    x3, m_ref, self_ref, acc, ids_refs = refs[0], refs[1], refs[2], refs[3], refs[4:]
    _, columns, width = x3.shape
    put_rows(acc, self_rows(x3, m_ref, ask_ref))
    for s in range(CAP):
        add_sums(acc, pick(ask_ref, s), self_ref[:, s * width : (s + 1) * width])
    lane = lax.broadcasted_iota(jnp.int32, ids_refs[0].shape, 1)
    for k in range(1, peers):
        came = came_refs[k - 1]
        ids = jnp.zeros(lane.shape, jnp.int32)
        for s in range(CAP):
            here = slice(s * width, (s + 1) * width)
            asked = jnp.max(came[columns : columns + TAIL, here].astype(F32)).astype(jnp.int32)
            ids = jnp.where(lane == s, asked, ids)
            add_sums(acc, asked, came[:columns, here])
        ids_refs[k - 1][...] = ids


def first_rows(values, operator, ask, came, own_mirror, peers):
    _, columns, width = values.shape
    outs = call(
        functools.partial(first_rows_kernel, peers),
        "first_rows",
        [shape(values.shape, F32)] + [shape((1, width), jnp.int32)] * (peers - 1),
        [vmem()] * (peers + 3),
        flops=2 ** 27,
        moved=2 ** 20,
    )(ask, *came[1:], values, operator, own_mirror)
    return outs[0], [None] + list(outs[1:])


def stack_kernel(below_ref, *refs):
    out_ref = refs[-1]
    _, columns, width = out_ref.shape
    at = (below_ref.shape[0] - TAIL) // columns * CAP - CAP
    for b in range(at):
        top = columns + TAIL + b // CAP * columns
        left = b % CAP * width
        out_ref[b] = below_ref[top : top + columns, left : left + width]
    for ref in refs[:-1]:
        share = ref.shape[0]
        out_ref[at : at + share] = ref[...]
        at += share


def cut_kernel(in_ref, low_ref, high_ref):
    share = low_ref.shape[0]
    low_ref[...] = in_ref[:share]
    high_ref[...] = in_ref[share:]


def cut(parts):
    if len(parts) > 1:
        return parts
    share, columns, width = parts[0].shape
    low = share - share // 4
    outs = [shape((low, columns, width), BF16), shape((share - low, columns, width), BF16)]
    return list(call(cut_kernel, "cut", outs, [vmem()])(*parts))


def stack(below, pieces):
    _, columns, width = pieces[0].shape
    count = (below.shape[0] - TAIL) // columns * CAP - CAP + sum(piece.shape[0] for piece in pieces)
    out = shape((count, columns, width), BF16)
    return call(stack_kernel, "stack", out, [vmem()] * (len(pieces) + 1))(below, *pieces)


def far_rows_kernel(peers, *refs):
    ask_refs, refs = refs[: peers - 1], refs[peers - 1 :]
    before, mine_ref, other_ref, m_ref, give_ref, keep_ref, acc, block, far = refs
    both = CAP * acc.shape[2]
    for k in range(1, peers):
        far[:, k * both : (k + 1) * both] = far_of(block, mine_ref, other_ref, ask_refs[k - 1], k - 1)
    if peers * CAP <= GROUP:
        own = dot(far[:, both:], m_ref[:, both:], NT)
    else:

        def add_peer(k, total):
            here = pl.ds(pl.multiple_of(k * both, both), both)
            return total + dot(far[:, here], m_ref[:, here], NT)

        own = lax.fori_loop(1, peers, add_peer, jnp.zeros((acc.shape[1], m_ref.shape[0]), F32))
    put_rows(acc, own, before)
    split_rows(acc, give_ref, keep_ref)


def far_rows(before, asks, mine, other, operator, peers, reps):
    blocks_dev, columns, width = before.shape
    share = (blocks_dev // reps, columns, width)
    return call(
        functools.partial(far_rows_kernel, peers),
        "far_rows",
        [shape(share, BF16), shape(share, F32)],
        [vmem()] * (peers + 3),
        [
            pltpu.VMEM(before.shape, F32),
            pltpu.VMEM(before.shape, BF16),
            pltpu.VMEM((columns, peers * CAP * width), BF16),
        ],
        flops=2 ** 28,
        moved=2 ** 21,
    )(*asks[1:], before, mine, other, operator)


def late_rows_kernel(ks, first, last, *refs):
    if first:
        ask_ref, x3, self_ref = refs[:3]
    else:
        before = refs[0]
    refs = refs[3 if first else 1 :]
    ids_refs, refs = refs[: len(ks)], refs[len(ks) :]
    came_refs, refs = refs[: len(ks)], refs[len(ks) :]
    m_ref, out_ref = refs[:2]
    acc = refs[2] if last else out_ref
    width = acc.shape[2]
    both = CAP * width
    own = self_rows(x3, m_ref, ask_ref) if first else None
    for i, k in enumerate(ks):
        add = own_rows(came_refs[i][:, both : 2 * both], m_ref, k)
        own = add if own is None else own + add
    put_rows(acc, own, None if first else before)
    if first:
        for s in range(CAP):
            add_sums(acc, pick(ask_ref, s), self_ref[:, s * width : (s + 1) * width])
    for i in range(len(ks)):
        for s in range(CAP):
            add_sums(acc, pick(ids_refs[i], s), came_refs[i][:, s * width : (s + 1) * width])
    if last:
        out_ref[...] = acc[...].astype(BF16)


def late_rows(head, ids, came, ks, operator, first, last):
    values = head[1] if first else head[0]
    return call(
        functools.partial(late_rows_kernel, ks, first, last),
        "late_rows",
        shape(values.shape, BF16 if last else F32),
        [vmem()] * (len(head) + 2 * len(ks) + 1),
        [pltpu.VMEM(values.shape, F32)] if last else [],
        flops=2 ** 27,
        moved=2 ** 20,
    )(*head, *[ids[k] for k in ks], *[came[k] for k in ks], operator)


def add_kernel(keep_ref, came_ref, out_ref):
    out_ref[...] = (keep_ref[...] + came_ref[...].astype(F32)).astype(BF16)


def add_up(keep, came):
    return call(add_kernel, "add_up", shape(came.shape, BF16), [vmem(), vmem()])(keep, came)


def widen_kernel(feats, *refs):
    out_ref = refs[feats]
    share, columns, width = refs[0].shape
    me = lax.axis_index("feat")
    for q in range(feats):
        rows = pl.ds(pl.multiple_of(lax.rem(me + q, feats) * columns, columns), columns)
        for b in range(share):
            out_ref[rows, b * width : (b + 1) * width] = refs[q][b]


def widen(parts):
    share, columns, width = parts[0].shape
    out = shape((len(parts) * columns, share * width), BF16)
    kernel = functools.partial(widen_kernel, len(parts))
    return call(kernel, "widen", out, [vmem()] * len(parts))(*parts)


def dense_kernel(feats, *refs):
    sums, wide_cot, refs = refs[:feats], refs[feats], refs[feats + 1 :]
    w_ref, act_ref, give_ref, spread_ref, term_ref, wide, pre_scr, grad = refs
    share, columns, width = act_ref.shape
    me = lax.axis_index("feat")
    rows = [pl.ds(pl.multiple_of(lax.rem(me + q, feats) * columns, columns), columns) for q in range(feats)]
    for q in range(feats):
        for b in range(share):
            wide[rows[q], b * width : (b + 1) * width] = sums[q][b]
    pre = dot(w_ref[...], wide[...], TN)
    pre_scr[...] = pre
    sig = jax.nn.sigmoid(pre)
    factor = wide_cot[...].astype(F32) * sig * (1.0 + pre * (1.0 - sig))
    grad[...] = factor.astype(BF16)
    spread = dot(w_ref[rows[0], :], grad[...]).astype(BF16)
    term_ref[...] = dot(grad[rows[0], :], wide[...], NT).astype(BF16)
    wide_share = share * width
    give_ref[:, :wide_share] = spread
    for b in range(share):
        spread_ref[b] = spread[:, b * width : (b + 1) * width]
    own = pre_scr[rows[0], :]
    act = (own * jax.nn.sigmoid(own)).astype(BF16)
    give_ref[:, wide_share:] = act
    for b in range(share):
        act_ref[b] = act[:, b * width : (b + 1) * width]


def dense(sums, cot, weight, feats):
    share, columns, width = sums[0].shape
    features = weight.shape[0]
    return call(
        functools.partial(dense_kernel, feats),
        "dense",
        [
            shape((share, columns, width), BF16),
            shape((columns, 2 * share * width), BF16),
            shape((share, columns, width), BF16),
            shape((columns, features), BF16),
        ],
        [vmem()] * (feats + 2),
        [
            pltpu.VMEM((features, share * width), BF16),
            pltpu.VMEM((features, share * width), F32),
            pltpu.VMEM((features, share * width), BF16),
        ],
        flops=2 ** 28,
        moved=2 ** 20,
    )(*sums, cot, weight)


def send_kernel(peers, *refs):
    ids_refs, refs = refs[: peers - 1], refs[peers - 1 :]
    mine_ref, came_ref, m_ref, refs = refs[0], refs[1], refs[2], refs[3:]
    x3, refs = refs[0], refs[1:]
    send_refs, refs = refs[: peers - 1], refs[peers - 1 :]
    self_ref, mir = refs
    share, _, width = mine_ref.shape
    both = CAP * width
    half = lax.axis_index("rep")
    x3[pl.ds(half * share, share)] = mine_ref[...]
    for b in range(share):
        x3[(1 - half) * share + b] = came_ref[:, b * width : (b + 1) * width]
    mirrored(lanes(x3), m_ref, mir, peers * CAP, width)
    self_ref[...] = mir[:, :both]
    for k in range(1, peers):
        out = send_refs[k - 1]
        out[:, :both] = mir[:, k * both : (k + 1) * both].astype(BF16)
        for s in range(CAP):
            at = (CAP + s) * width
            out[:, at : at + width] = x3[pick(ids_refs[k - 1], s)]


def sends_of(mine, came, operator, ids, peers, reps):
    share, columns, width = mine.shape
    chunk = 2 * CAP * width
    outs = call(
        functools.partial(send_kernel, peers),
        "sends",
        [shape((share * reps, columns, width), BF16)]
        + [shape((columns, chunk), BF16)] * (peers - 1)
        + [shape((columns, CAP * width), F32)],
        [vmem()] * (peers + 2),
        [pltpu.VMEM((columns, peers * CAP * width), F32)],
        flops=2 ** 28,
        moved=2 ** 21,
    )(*ids[1:], mine, came, operator)
    return outs[0], [None] + list(outs[1:peers]), outs[peers]


def pair_kernel(mine_ref, came_ref, out_ref):
    out_ref[...] = (mine_ref[...].astype(F32) + came_ref[...].astype(F32)).astype(out_ref.dtype)


def pair_sum(mine, came, dtype):
    return call(pair_kernel, "pair_sum", shape(mine.shape, dtype), [vmem(), vmem()])(mine, came)


def split_kernel(mine_ref, came_ref, give_ref, keep_ref, total):
    half = lax.axis_index("rep")
    part = keep_ref.shape[1]
    total[...] = mine_ref[...].astype(F32) + came_ref[...].astype(F32)
    give_ref[...] = total[:, pl.ds(pl.multiple_of((1 - half) * part, part), part)].astype(BF16)
    keep_ref[...] = total[:, pl.ds(pl.multiple_of(half * part, part), part)]


def split_sum(mine, came, reps):
    columns, features = mine.shape
    part = (columns, features // reps)
    return call(
        split_kernel,
        "split_sum",
        [shape(part, BF16), shape(part, F32)],
        [vmem(), vmem()],
        [pltpu.VMEM(mine.shape, F32)],
    )(mine, came)


def total_term(term, peers, reps):
    bit = peers // 2
    give, total = split_sum(term, across(term, peers, bit), reps)
    total = pair_sum(total, ahead(give, "rep", reps, 1), F32 if bit == 1 else BF16)
    while bit > 1:
        bit //= 2
        total = pair_sum(total, across(total, peers, bit), F32 if bit == 1 else BF16)
    return total


def finish_kernel(mine_ref, other_ref, share_ref, other_share_ref, act_ref, came_ref, grad_ref, weight_ref, out_ref):
    half = lax.axis_index("rep")
    share = share_ref.shape[1]
    grad_ref[...] = (mine_ref[...].astype(F32) + other_ref[...].astype(F32)).astype(BF16)
    weight_ref[pl.ds(pl.multiple_of(half * share, share), share), :] = share_ref[...].T
    weight_ref[pl.ds(pl.multiple_of((1 - half) * share, share), share), :] = other_share_ref[...].T
    blocks, _, width = act_ref.shape
    out_ref[pl.ds(half * blocks, blocks)] = act_ref[...]
    for b in range(blocks):
        at = (blocks + b) * width
        out_ref[(1 - half) * blocks + b] = came_ref[:, at : at + width]


def finish(mine, other, share, other_share, act, came):
    columns, width = share.shape
    return call(
        finish_kernel,
        "finish",
        [shape(mine.shape, BF16), shape((2 * width, columns), F32), shape(mine.shape, BF16)],
        [vmem()] * 6,
    )(mine, other, share, other_share, act, came)


def ahead(value, axis, size, k):
    return lax.ppermute(value, axis, [(i, (i + k) % size) for i in range(size)])


def across(value, peers, k):
    return lax.ppermute(value, "graph", [(i, i ^ k) for i in range(peers)])


def after(value, first):
    return lax.optimization_barrier((value, first))[0]


def local(features, weight, cotangent, tiles, tile_row, tile_col, tile_count):
    blocks_dev, _, width = features.shape
    peers = lax.axis_size("graph")
    feats = lax.axis_size("feat")
    reps = lax.axis_size("rep")
    far_first = sorted(range(1, peers), key=lambda k: (-(k & (peers // 2)), k))

    half, place, asks = prepare(features, tile_row, tile_col, tile_count, peers, reps)
    operator = list_operator(tiles, place, peers, blocks_dev)
    sends, own_mirror, own_cot = first_sends(features, cotangent, operator, asks[1:], peers, reps)
    middle = peers // 2
    came = [None] * peers
    came[middle] = across(sends[middle], peers, middle)
    pieces, held = {0: [half]}, [0]
    bit = middle
    while bit:
        for k in held:
            if k ^ bit == 1:
                continue
            parts = pieces[k]
            if k:
                parts = cut(after(parts, sends[1]))
                parts[-1] = after(parts[-1], came[middle])
            pieces[k ^ bit] = [across(part, peers, bit) for part in parts]
        held = held + [k ^ bit for k in held]
        bit //= 2
    for k in far_first[1:]:
        send = after(sends[k], pieces[middle]) if k == peers - 1 else sends[k]
        came[k] = across(send, peers, k)
    cots = [own_cot] + [ahead(own_cot, "feat", feats, feats - q) for q in range(1, feats)]
    arrived = [part for k in range(2, peers) for part in pieces[k]]
    ordered, arrived, cots = lax.optimization_barrier(([came[k] for k in far_first], arrived, cots))
    came = [None] + [ordered[far_first.index(k)] for k in range(1, peers)]
    stacked = stack(came[1], arrived)
    swapped = ahead(stacked, "rep", reps, 1)
    acc, ids = first_rows(features, operator, asks[0], came, own_mirror, peers)
    give, keep = far_rows(acc, asks, stacked, swapped, operator, peers, reps)

    mine = add_up(keep, ahead(give, "rep", reps, 1))
    cot = widen(cots)
    sums = [mine] + [ahead(mine, "feat", feats, feats - q) for q in range(1, feats)]
    act, give, spread, term = dense(sums, cot, weight, feats)
    total = total_term(term, peers, reps)
    shared = ahead(give, "rep", reps, 1)
    values, sends, own_mirror = sends_of(spread, shared, operator, ids, peers, reps)

    came = [None] * peers
    for k in far_first:
        came[k] = across(sends[k], peers, k)
    ordered, total = lax.optimization_barrier(([came[k] for k in far_first], total))
    came = [None] + [ordered[far_first.index(k)] for k in range(1, peers)]
    part = late_rows([asks[0], values, own_mirror], ids, came, far_first, operator, True, True)
    input_grad, weight_grad, activated = finish(
        part, ahead(part, "rep", reps, 1), total, ahead(total, "rep", reps, 1), act, shared
    )
    return (activated, input_grad, weight_grad)


def solution(mesh):
    placed = (
        P(("parts", "graph"), "feat", None),
        P(),
        P(("parts", "graph"), "feat", None),
        P(("parts", "graph", "rep"), None, None),
        P(("parts", "graph", "rep")),
        P(("parts", "graph", "rep")),
        P(("parts", "graph", "rep")),
    )
    return jax.shard_map(
        local,
        mesh=mesh,
        in_specs=placed,
        out_specs=(
            P(("parts", "graph"), "feat", None),
            P(("parts", "graph"), "feat", None),
            P("parts", "feat"),
        ),
        check_vma=False,
    )
```

```python
import functools

import jax
import jax.numpy as jnp
from jax import lax
from jax.experimental import pallas as pl
from jax.experimental.pallas import tpu as pltpu
from jax.sharding import PartitionSpec as P

CAP = 2
GROUP = 8
CHUNK = 16
SIDES = 2
TAIL = 16
VMEM_LIMIT = 40 * 2 ** 20
VMEM_MOST = 50 * 2 ** 20
VMEM_ALL = 58 * 2 ** 20

NT = (((1,), (1,)), ((), ()))
TN = (((0,), (0,)), ((), ()))
F32 = jnp.float32
BF16 = jnp.bfloat16


def vmem():
    return pl.BlockSpec(memory_space=pltpu.VMEM)


def smem():
    return pl.BlockSpec(memory_space=pltpu.SMEM)


def hbm():
    return pl.BlockSpec(memory_space=pltpu.HBM)


def shape(dims, dtype):
    return jax.ShapeDtypeStruct(tuple(dims), dtype)


def dot(a, b, dims=None):
    if dims is None:
        return jnp.dot(a, b, preferred_element_type=F32)
    return lax.dot_general(a, b, dims, preferred_element_type=F32)


def call(kernel, name, outs, in_specs, scratch=(), flops=0, moved=2 ** 18, limit=VMEM_LIMIT, **kwargs):
    return pl.pallas_call(
        kernel,
        out_shape=outs,
        in_specs=in_specs,
        scratch_shapes=list(scratch),
        compiler_params=pltpu.CompilerParams(vmem_limit_bytes=limit),
        cost_estimate=pl.CostEstimate(flops=flops, bytes_accessed=moved, transcendentals=0),
        name=name,
        **kwargs,
    )


def lanes(x3):
    return jnp.concatenate([x3[b] for b in range(x3.shape[0])], axis=1)


def places(peers, blocks_dev, count, row, col, ask_refs):
    me = lax.axis_index("graph")
    lane = lax.broadcasted_iota(jnp.int32, col.shape, 1)
    live = lane < count
    place = jnp.full(col.shape, peers * CAP * blocks_dev, jnp.int32)
    for k in range(peers):
        local = col - jnp.bitwise_xor(me, k) * blocks_dev
        inside = live & (local >= 0) & (local < blocks_dev)
        low = jnp.min(jnp.where(inside, local, blocks_dev - 1), axis=1, keepdims=True)
        high = jnp.max(jnp.where(inside, local, 0), axis=1, keepdims=True)
        ask_refs[k][...] = jnp.where(lane == 0, low, high)
        slot = k * CAP + (local != low).astype(jnp.int32)
        place = jnp.where(inside, slot * blocks_dev + row, place)
    return place


def prepare_kernel(peers, count_ref, row_ref, col_ref, x3, half_ref, place_ref, *ask_refs):
    share = half_ref.shape[0]
    half_ref[...] = x3[pl.ds(lax.axis_index("rep") * share, share)]
    count = jnp.broadcast_to(count_ref[...], (1, 1))
    place_ref[...] = places(peers, x3.shape[0], count, row_ref[...], col_ref[...], ask_refs)


def prepare(features, tile_row, tile_col, tile_count, peers, reps):
    per = tile_col.shape[0]
    blocks_dev, columns, width = features.shape
    outs = call(
        functools.partial(prepare_kernel, peers),
        "prepare",
        [shape((blocks_dev // reps, columns, width), BF16)] + [shape((1, per), jnp.int32)] * (peers + 1),
        [vmem()] * 4,
        limit=VMEM_ALL,
    )(tile_count, tile_row.reshape(1, per), tile_col.reshape(1, per), features)
    return outs[0], outs[1], list(outs[2:])


def pick(ids_ref, lane):
    ids = ids_ref[...].astype(F32)
    at = lax.broadcasted_iota(jnp.int32, ids.shape, 1)
    return jnp.max(jnp.where(at == lane, ids, 0.0)).astype(jnp.int32)


def operator_kernel(blocks_dev, slots_here, groups, place_in, tiles_ref, m_ref, tiles, acc, place_ref, sems, sem):
    step = pl.program_id(0)
    per, width = tiles.shape[0], tiles.shape[1]
    chunks = per // CHUNK
    spare = slots_here * blocks_dev

    def chunk_copy(c):
        part = pl.ds(c * CHUNK, CHUNK)
        return pltpu.make_async_copy(tiles_ref.at[part], tiles.at[part], sems.at[c])

    @pl.when(step == 0)
    def _():
        placed = pltpu.make_async_copy(place_in, place_ref, sem)
        placed.start()
        for c in range(chunks):
            chunk_copy(c).start()
        placed.wait()

    acc[...] = jnp.zeros_like(acc)

    def add_chunk(c, carry):
        @pl.when(step == 0)
        def _():
            chunk_copy(c).wait()

        for u in range(CHUNK):
            t = c * CHUNK + u
            place = place_ref[0, t]
            if groups > 1:
                place = place - step * spare
                place = jnp.where((place >= 0) & (place < spare), place, spare)
            side = u % SIDES
            acc[side, place] = acc[side, place] + tiles[t].astype(F32)
        return carry

    lax.fori_loop(0, chunks, add_chunk, 0)
    for s in range(slots_here):
        for r in range(blocks_dev):
            total = acc[0, s * blocks_dev + r]
            for side in range(1, SIDES):
                total = total + acc[side, s * blocks_dev + r]
            m_ref[r * width : (r + 1) * width, s * width : (s + 1) * width] = total.astype(BF16)


def list_operator(tiles, place, peers, blocks_dev):
    per, width = tiles.shape[0], tiles.shape[1]
    slots = peers * CAP
    slots_here = min(slots, GROUP)
    groups = slots // slots_here
    return call(
        functools.partial(operator_kernel, blocks_dev, slots_here, groups),
        "operator",
        shape((blocks_dev * width, slots * width), BF16),
        [pl.BlockSpec(memory_space=pl.ANY), hbm()],
        [
            pltpu.VMEM((per, width, width), BF16),
            pltpu.VMEM((SIDES, slots_here * blocks_dev + 1, width, width), F32),
            pltpu.SMEM((1, per), jnp.int32),
            pltpu.SemaphoreType.DMA((per // CHUNK,)),
            pltpu.SemaphoreType.DMA,
        ],
        moved=2 ** 24,
        limit=VMEM_MOST,
        grid=(groups,),
        out_specs=pl.BlockSpec((blocks_dev * width, slots_here * width), lambda i: (0, i)),
    )(place, tiles)


def mirrored(near, m_ref, mir, slots, width):
    if slots <= GROUP:
        mir[...] = dot(near, m_ref[...])
    else:
        part = GROUP * width

        @pl.loop(0, slots // GROUP)
        def _(i):
            where = pl.ds(pl.multiple_of(i * part, part), part)
            mir[:, where] = dot(near, m_ref[:, where])


def first_sends_kernel(peers, *refs):
    ask_refs, refs = refs[: peers - 1], refs[peers - 1 :]
    x3, cot, m_ref, refs = refs[0], refs[1], refs[2], refs[3:]
    middle = peers // 2
    far_ref, near_refs, refs = refs[0], refs[1:middle], refs[middle:]
    self_ref, cot_ref, mir = refs
    _, columns, width = x3.shape
    share = cot_ref.shape[0]
    both = CAP * width
    mirrored(lanes(x3), m_ref, mir, peers * CAP, width)
    self_ref[...] = mir[:, :both]
    lane = lax.broadcasted_iota(jnp.int32, (TAIL, both), 1)
    for k in range(1, peers):
        out, left = (near_refs[k - 1], 0) if k < middle else (far_ref, (k - middle) * both)
        out[:columns, left : left + both] = mir[:, k * both : (k + 1) * both].astype(BF16)
        low, high = ask_refs[k - 1][:, :1], ask_refs[k - 1][:, 1:2]
        out[columns:, left : left + both] = jnp.where(lane < width, low, high).astype(F32).astype(BF16)
    cot_ref[...] = cot[pl.ds(lax.axis_index("rep") * share, share)]


def first_sends(values, cotangent, operator, asks, peers, reps):
    blocks_dev, columns, width = values.shape
    middle = peers // 2
    outs = call(
        functools.partial(first_sends_kernel, peers),
        "first_sends",
        [shape((columns + TAIL, middle * CAP * width), BF16)]
        + [shape((columns + TAIL, CAP * width), BF16)] * (middle - 1)
        + [shape((columns, CAP * width), F32), shape((blocks_dev // reps, columns, width), BF16)],
        [vmem()] * (peers + 2),
        [pltpu.VMEM((columns, peers * CAP * width), F32)],
        flops=2 ** 28,
        moved=2 ** 21,
    )(*asks, values, cotangent, operator)
    return outs[0], [None] + list(outs[1:middle]), outs[middle], outs[middle + 1]


def below_kernel(sums_ref, half_ref, out_ref):
    top = sums_ref.shape[0]
    share, columns, width = half_ref.shape
    out_ref[:top, :] = sums_ref[...]
    for b in range(share):
        row, left = top + b // CAP * columns, b % CAP * width
        out_ref[row : row + columns, left : left + width] = half_ref[b]


def below(sums, half):
    share, columns, width = half.shape
    out = shape((sums.shape[0] + share // CAP * columns, sums.shape[1]), BF16)
    return call(below_kernel, "below", out, [vmem(), vmem()])(sums, half)


def pass_kernel(j, came_ref, out_ref):
    both = out_ref.shape[1]
    out_ref[...] = came_ref[:, j * both : (j + 1) * both]


def pass_on(came, j, middle):
    out = shape((came.shape[0], came.shape[1] // middle), BF16)
    return call(functools.partial(pass_kernel, j), "pass_on", out, [vmem()])(came)


def add_sums(acc, block, sums):
    acc[block] = acc[block] + sums.astype(F32)


def own_rows(far, m_ref, k):
    both = far.shape[1]
    return dot(far, m_ref[:, k * both : (k + 1) * both], NT)


def put_rows(acc, own, before=None):
    blocks_dev, _, width = acc.shape
    for b in range(blocks_dev):
        add = own[:, b * width : (b + 1) * width]
        acc[b] = add if before is None else before[b] + add


def split_rows(acc, give_ref, keep_ref):
    half = lax.axis_index("rep")
    share = give_ref.shape[0]
    give_ref[...] = acc[pl.ds((1 - half) * share, share)].astype(BF16)
    keep_ref[...] = acc[pl.ds(half * share, share)]


def self_rows(x3, m_ref, ask_ref):
    far = jnp.concatenate([x3[pick(ask_ref, s)] for s in range(CAP)], axis=1)
    return own_rows(far, m_ref, 0)


def far_of(block, mine_ref, other_ref, ask_ref, at=0):
    half = lax.axis_index("rep")
    share = block.shape[0] // 2
    block[pl.ds(half * share, share)] = mine_ref[at * share : (at + 1) * share]
    block[pl.ds((1 - half) * share, share)] = other_ref[at * share : (at + 1) * share]
    return jnp.concatenate([block[pick(ask_ref, s)] for s in range(CAP)], axis=1)


def first_rows_kernel(peers, *refs):
    ask_ref, refs = refs[0], refs[1:]
    came_refs, refs = refs[: peers - 1], refs[peers - 1 :]
    x3, m_ref, self_ref, acc, ids_refs = refs[0], refs[1], refs[2], refs[3], refs[4:]
    _, columns, width = x3.shape
    put_rows(acc, self_rows(x3, m_ref, ask_ref))
    for s in range(CAP):
        add_sums(acc, pick(ask_ref, s), self_ref[:, s * width : (s + 1) * width])
    lane = lax.broadcasted_iota(jnp.int32, ids_refs[0].shape, 1)
    for k in range(1, peers):
        came = came_refs[k - 1]
        ids = jnp.zeros(lane.shape, jnp.int32)
        for s in range(CAP):
            here = slice(s * width, (s + 1) * width)
            asked = jnp.max(came[columns : columns + TAIL, here].astype(F32)).astype(jnp.int32)
            ids = jnp.where(lane == s, asked, ids)
            add_sums(acc, asked, came[:columns, here])
        ids_refs[k - 1][...] = ids


def first_rows(values, operator, ask, came, own_mirror, peers):
    _, columns, width = values.shape
    outs = call(
        functools.partial(first_rows_kernel, peers),
        "first_rows",
        [shape(values.shape, F32)] + [shape((1, width), jnp.int32)] * (peers - 1),
        [vmem()] * (peers + 3),
        flops=2 ** 27,
        moved=2 ** 20,
    )(ask, *came[1:], values, operator, own_mirror)
    return outs[0], [None] + list(outs[1:])


def stack_kernel(middle, *refs):
    out_ref = refs[-1]
    share, columns, width = refs[0].shape
    for k in range(1, middle + 1):
        out_ref[(k - 1) * share : k * share] = refs[k - 1][...]
    for k in range(middle + 1, 2 * middle):
        ref = refs[k - 1]
        for b in range(share):
            row, left = columns + TAIL + b // CAP * columns, b % CAP * width
            out_ref[(k - 1) * share + b] = ref[row : row + columns, left : left + width]


def stack(pieces, chunks):
    share, columns, width = pieces[0].shape
    out = shape(((len(pieces) + len(chunks)) * share, columns, width), BF16)
    kernel = functools.partial(stack_kernel, len(pieces))
    return call(kernel, "stack", out, [vmem()] * (len(pieces) + len(chunks)))(*pieces, *chunks)


def far_rows_kernel(peers, *refs):
    ask_refs, refs = refs[: peers - 1], refs[peers - 1 :]
    before, mine_ref, other_ref, m_ref, give_ref, keep_ref, acc, block, far = refs
    both = CAP * acc.shape[2]
    for k in range(1, peers):
        far[:, k * both : (k + 1) * both] = far_of(block, mine_ref, other_ref, ask_refs[k - 1], k - 1)
    if peers * CAP <= GROUP:
        own = dot(far[:, both:], m_ref[:, both:], NT)
    else:

        def add_peer(k, total):
            here = pl.ds(pl.multiple_of(k * both, both), both)
            return total + dot(far[:, here], m_ref[:, here], NT)

        own = lax.fori_loop(1, peers, add_peer, jnp.zeros((acc.shape[1], m_ref.shape[0]), F32))
    put_rows(acc, own, before)
    split_rows(acc, give_ref, keep_ref)


def far_rows(before, asks, mine, other, operator, peers, reps):
    blocks_dev, columns, width = before.shape
    share = (blocks_dev // reps, columns, width)
    return call(
        functools.partial(far_rows_kernel, peers),
        "far_rows",
        [shape(share, BF16), shape(share, F32)],
        [vmem()] * (peers + 3),
        [
            pltpu.VMEM(before.shape, F32),
            pltpu.VMEM(before.shape, BF16),
            pltpu.VMEM((columns, peers * CAP * width), BF16),
        ],
        flops=2 ** 28,
        moved=2 ** 21,
    )(*asks[1:], before, mine, other, operator)


def late_rows_kernel(ks, first, last, *refs):
    if first:
        ask_ref, x3, self_ref = refs[:3]
    else:
        before = refs[0]
    refs = refs[3 if first else 1 :]
    ids_refs, refs = refs[: len(ks)], refs[len(ks) :]
    came_refs, refs = refs[: len(ks)], refs[len(ks) :]
    m_ref, out_ref = refs[:2]
    acc = refs[2] if last else out_ref
    width = acc.shape[2]
    both = CAP * width
    own = self_rows(x3, m_ref, ask_ref) if first else None
    for i, k in enumerate(ks):
        add = own_rows(came_refs[i][:, both : 2 * both], m_ref, k)
        own = add if own is None else own + add
    put_rows(acc, own, None if first else before)
    if first:
        for s in range(CAP):
            add_sums(acc, pick(ask_ref, s), self_ref[:, s * width : (s + 1) * width])
    for i in range(len(ks)):
        for s in range(CAP):
            add_sums(acc, pick(ids_refs[i], s), came_refs[i][:, s * width : (s + 1) * width])
    if last:
        out_ref[...] = acc[...].astype(BF16)


def late_rows(head, ids, came, ks, operator, first, last):
    values = head[1] if first else head[0]
    return call(
        functools.partial(late_rows_kernel, ks, first, last),
        "late_rows",
        shape(values.shape, BF16 if last else F32),
        [vmem()] * (len(head) + 2 * len(ks) + 1),
        [pltpu.VMEM(values.shape, F32)] if last else [],
        flops=2 ** 27,
        moved=2 ** 20,
    )(*head, *[ids[k] for k in ks], *[came[k] for k in ks], operator)


def add_kernel(keep_ref, came_ref, out_ref):
    out_ref[...] = (keep_ref[...] + came_ref[...].astype(F32)).astype(BF16)


def add_up(keep, came):
    return call(add_kernel, "add_up", shape(came.shape, BF16), [vmem(), vmem()])(keep, came)


def widen_kernel(feats, *refs):
    out_ref = refs[feats]
    share, columns, width = refs[0].shape
    me = lax.axis_index("feat")
    for q in range(feats):
        rows = pl.ds(pl.multiple_of(lax.rem(me + q, feats) * columns, columns), columns)
        for b in range(share):
            out_ref[rows, b * width : (b + 1) * width] = refs[q][b]


def widen(parts):
    share, columns, width = parts[0].shape
    out = shape((len(parts) * columns, share * width), BF16)
    kernel = functools.partial(widen_kernel, len(parts))
    return call(kernel, "widen", out, [vmem()] * len(parts))(*parts)


def dense_kernel(feats, *refs):
    sums, wide_cot, refs = refs[:feats], refs[feats], refs[feats + 1 :]
    w_ref, act_ref, give_ref, spread_ref, term_ref, wide, pre_scr, grad = refs
    share, columns, width = act_ref.shape
    me = lax.axis_index("feat")
    rows = [pl.ds(pl.multiple_of(lax.rem(me + q, feats) * columns, columns), columns) for q in range(feats)]
    for q in range(feats):
        for b in range(share):
            wide[rows[q], b * width : (b + 1) * width] = sums[q][b]
    pre = dot(w_ref[...], wide[...], TN)
    pre_scr[...] = pre
    sig = jax.nn.sigmoid(pre)
    factor = wide_cot[...].astype(F32) * sig * (1.0 + pre * (1.0 - sig))
    grad[...] = factor.astype(BF16)
    spread = dot(w_ref[rows[0], :], grad[...]).astype(BF16)
    term_ref[...] = dot(grad[rows[0], :], wide[...], NT).astype(BF16)
    wide_share = share * width
    give_ref[:, :wide_share] = spread
    for b in range(share):
        spread_ref[b] = spread[:, b * width : (b + 1) * width]
    own = pre_scr[rows[0], :]
    act = (own * jax.nn.sigmoid(own)).astype(BF16)
    give_ref[:, wide_share:] = act
    for b in range(share):
        act_ref[b] = act[:, b * width : (b + 1) * width]


def dense(sums, cot, weight, feats):
    share, columns, width = sums[0].shape
    features = weight.shape[0]
    return call(
        functools.partial(dense_kernel, feats),
        "dense",
        [
            shape((share, columns, width), BF16),
            shape((columns, 2 * share * width), BF16),
            shape((share, columns, width), BF16),
            shape((columns, features), BF16),
        ],
        [vmem()] * (feats + 2),
        [
            pltpu.VMEM((features, share * width), BF16),
            pltpu.VMEM((features, share * width), F32),
            pltpu.VMEM((features, share * width), BF16),
        ],
        flops=2 ** 28,
        moved=2 ** 20,
    )(*sums, cot, weight)


def send_kernel(peers, *refs):
    ids_refs, refs = refs[: peers - 1], refs[peers - 1 :]
    mine_ref, came_ref, m_ref, refs = refs[0], refs[1], refs[2], refs[3:]
    x3, refs = refs[0], refs[1:]
    send_refs, refs = refs[: peers - 1], refs[peers - 1 :]
    self_ref, mir = refs
    share, _, width = mine_ref.shape
    both = CAP * width
    half = lax.axis_index("rep")
    x3[pl.ds(half * share, share)] = mine_ref[...]
    for b in range(share):
        x3[(1 - half) * share + b] = came_ref[:, b * width : (b + 1) * width]
    mirrored(lanes(x3), m_ref, mir, peers * CAP, width)
    self_ref[...] = mir[:, :both]
    for k in range(1, peers):
        out = send_refs[k - 1]
        out[:, :both] = mir[:, k * both : (k + 1) * both].astype(BF16)
        for s in range(CAP):
            at = (CAP + s) * width
            out[:, at : at + width] = x3[pick(ids_refs[k - 1], s)]


def sends_of(mine, came, operator, ids, peers, reps):
    share, columns, width = mine.shape
    chunk = 2 * CAP * width
    outs = call(
        functools.partial(send_kernel, peers),
        "sends",
        [shape((share * reps, columns, width), BF16)]
        + [shape((columns, chunk), BF16)] * (peers - 1)
        + [shape((columns, CAP * width), F32)],
        [vmem()] * (peers + 2),
        [pltpu.VMEM((columns, peers * CAP * width), F32)],
        flops=2 ** 28,
        moved=2 ** 21,
    )(*ids[1:], mine, came, operator)
    return outs[0], [None] + list(outs[1:peers]), outs[peers]


def pair_kernel(mine_ref, came_ref, out_ref):
    out_ref[...] = (mine_ref[...].astype(F32) + came_ref[...].astype(F32)).astype(out_ref.dtype)


def pair_sum(mine, came, dtype):
    return call(pair_kernel, "pair_sum", shape(mine.shape, dtype), [vmem(), vmem()])(mine, came)


def split_kernel(mine_ref, came_ref, give_ref, keep_ref, total):
    half = lax.axis_index("rep")
    part = keep_ref.shape[1]
    total[...] = mine_ref[...].astype(F32) + came_ref[...].astype(F32)
    give_ref[...] = total[:, pl.ds(pl.multiple_of((1 - half) * part, part), part)].astype(BF16)
    keep_ref[...] = total[:, pl.ds(pl.multiple_of(half * part, part), part)]


def split_sum(mine, came, reps):
    columns, features = mine.shape
    part = (columns, features // reps)
    return call(
        split_kernel,
        "split_sum",
        [shape(part, BF16), shape(part, F32)],
        [vmem(), vmem()],
        [pltpu.VMEM(mine.shape, F32)],
    )(mine, came)


def total_term(term, peers, reps):
    bit = peers // 2
    give, total = split_sum(term, across(term, peers, bit), reps)
    total = pair_sum(total, ahead(give, "rep", reps, 1), F32 if bit == 1 else BF16)
    while bit > 1:
        bit //= 2
        total = pair_sum(total, across(total, peers, bit), F32 if bit == 1 else BF16)
    return total


def finish_kernel(mine_ref, other_ref, share_ref, other_share_ref, act_ref, came_ref, grad_ref, weight_ref, out_ref):
    half = lax.axis_index("rep")
    share = share_ref.shape[1]
    grad_ref[...] = (mine_ref[...].astype(F32) + other_ref[...].astype(F32)).astype(BF16)
    weight_ref[pl.ds(pl.multiple_of(half * share, share), share), :] = share_ref[...].T
    weight_ref[pl.ds(pl.multiple_of((1 - half) * share, share), share), :] = other_share_ref[...].T
    blocks, _, width = act_ref.shape
    out_ref[pl.ds(half * blocks, blocks)] = act_ref[...]
    for b in range(blocks):
        at = (blocks + b) * width
        out_ref[(1 - half) * blocks + b] = came_ref[:, at : at + width]


def finish(mine, other, share, other_share, act, came):
    columns, width = share.shape
    return call(
        finish_kernel,
        "finish",
        [shape(mine.shape, BF16), shape((2 * width, columns), F32), shape(mine.shape, BF16)],
        [vmem()] * 6,
    )(mine, other, share, other_share, act, came)


def ahead(value, axis, size, k):
    return lax.ppermute(value, axis, [(i, (i + k) % size) for i in range(size)])


def across(value, peers, k):
    return lax.ppermute(value, "graph", [(i, i ^ k) for i in range(peers)])


def after(value, first):
    return lax.optimization_barrier((value, first))[0]


def local(features, weight, cotangent, tiles, tile_row, tile_col, tile_count):
    blocks_dev, _, width = features.shape
    peers = lax.axis_size("graph")
    feats = lax.axis_size("feat")
    reps = lax.axis_size("rep")
    far_first = sorted(range(1, peers), key=lambda k: (-(k & (peers // 2)), k))

    half, place, asks = prepare(features, tile_row, tile_col, tile_count, peers, reps)
    operator = list_operator(tiles, place, peers, blocks_dev)
    far, near, own_mirror, own_cot = first_sends(features, cotangent, operator, asks[1:], peers, reps)
    middle = peers // 2
    pieces = [across(half, peers, j) for j in range(1, middle)]
    crossed = across(half, peers, middle)
    sums = across(far, peers, middle)
    chunks = []
    for j in range(1, middle):
        chunk, pieces[j - 1] = lax.optimization_barrier((below(near[j], crossed), pieces[j - 1]))
        chunks.append(across(chunk, peers, j))
    passed = [across(pass_on(sums, j, middle), peers, j) for j in range(1, middle)]
    cots = [own_cot] + [ahead(own_cot, "feat", feats, feats - q) for q in range(1, feats)]
    chunks, passed, cots = lax.optimization_barrier((chunks, passed, cots))
    came = [None] + chunks + [sums] + passed
    stacked = stack(pieces + [crossed], chunks)
    swapped = ahead(stacked, "rep", reps, 1)
    acc, ids = first_rows(features, operator, asks[0], came, own_mirror, peers)
    give, keep = far_rows(acc, asks, stacked, swapped, operator, peers, reps)

    mine = add_up(keep, ahead(give, "rep", reps, 1))
    cot = widen(cots)
    sums = [mine] + [ahead(mine, "feat", feats, feats - q) for q in range(1, feats)]
    act, give, spread, term = dense(sums, cot, weight, feats)
    total = total_term(term, peers, reps)
    shared = ahead(give, "rep", reps, 1)
    values, sends, own_mirror = sends_of(spread, shared, operator, ids, peers, reps)

    came = [None] * peers
    for k in far_first:
        came[k] = across(sends[k], peers, k)
    ordered, total = lax.optimization_barrier(([came[k] for k in far_first], total))
    came = [None] + [ordered[far_first.index(k)] for k in range(1, peers)]
    part = late_rows([asks[0], values, own_mirror], ids, came, far_first, operator, True, True)
    input_grad, weight_grad, activated = finish(
        part, ahead(part, "rep", reps, 1), total, ahead(total, "rep", reps, 1), act, shared
    )
    return (activated, input_grad, weight_grad)


def solution(mesh):
    placed = (
        P(("parts", "graph"), "feat", None),
        P(),
        P(("parts", "graph"), "feat", None),
        P(("parts", "graph", "rep"), None, None),
        P(("parts", "graph", "rep")),
        P(("parts", "graph", "rep")),
        P(("parts", "graph", "rep")),
    )
    return jax.shard_map(
        local,
        mesh=mesh,
        in_specs=placed,
        out_specs=(
            P(("parts", "graph"), "feat", None),
            P(("parts", "graph"), "feat", None),
            P("parts", "feat"),
        ),
        check_vma=False,
    )
```

```python
import functools

import jax
import jax.numpy as jnp
from jax import lax
from jax.experimental import pallas as pl
from jax.experimental.pallas import tpu as pltpu
from jax.sharding import PartitionSpec as P

CAP = 2
GROUP = 8
CHUNK = 16
SIDES = 2
TAIL = 16
VMEM_LIMIT = 40 * 2 ** 20
VMEM_MOST = 50 * 2 ** 20
VMEM_ALL = 58 * 2 ** 20

NT = (((1,), (1,)), ((), ()))
TN = (((0,), (0,)), ((), ()))
F32 = jnp.float32
BF16 = jnp.bfloat16


def vmem():
    return pl.BlockSpec(memory_space=pltpu.VMEM)


def smem():
    return pl.BlockSpec(memory_space=pltpu.SMEM)


def hbm():
    return pl.BlockSpec(memory_space=pltpu.HBM)


def shape(dims, dtype):
    return jax.ShapeDtypeStruct(tuple(dims), dtype)


def dot(a, b, dims=None):
    if dims is None:
        return jnp.dot(a, b, preferred_element_type=F32)
    return lax.dot_general(a, b, dims, preferred_element_type=F32)


def call(kernel, name, outs, in_specs, scratch=(), flops=0, moved=2 ** 18, limit=VMEM_LIMIT, **kwargs):
    return pl.pallas_call(
        kernel,
        out_shape=outs,
        in_specs=in_specs,
        scratch_shapes=list(scratch),
        compiler_params=pltpu.CompilerParams(vmem_limit_bytes=limit),
        cost_estimate=pl.CostEstimate(flops=flops, bytes_accessed=moved, transcendentals=0),
        name=name,
        **kwargs,
    )


def lanes(x3):
    return jnp.concatenate([x3[b] for b in range(x3.shape[0])], axis=1)


def places(peers, blocks_dev, count, row, col, ask_refs):
    me = lax.axis_index("graph")
    lane = lax.broadcasted_iota(jnp.int32, col.shape, 1)
    live = lane < count
    place = jnp.full(col.shape, peers * CAP * blocks_dev, jnp.int32)
    for k in range(peers):
        local = col - jnp.bitwise_xor(me, k) * blocks_dev
        inside = live & (local >= 0) & (local < blocks_dev)
        low = jnp.min(jnp.where(inside, local, blocks_dev - 1), axis=1, keepdims=True)
        high = jnp.max(jnp.where(inside, local, 0), axis=1, keepdims=True)
        ask_refs[k][...] = jnp.where(lane == 0, low, high)
        slot = k * CAP + (local != low).astype(jnp.int32)
        place = jnp.where(inside, slot * blocks_dev + row, place)
    return place


def prepare_kernel(peers, count_ref, row_ref, col_ref, x3, half_ref, place_ref, *ask_refs):
    share = half_ref.shape[0]
    half_ref[...] = x3[pl.ds(lax.axis_index("rep") * share, share)]
    count = jnp.broadcast_to(count_ref[...], (1, 1))
    place_ref[...] = places(peers, x3.shape[0], count, row_ref[...], col_ref[...], ask_refs)


def prepare(features, tile_row, tile_col, tile_count, peers, reps):
    per = tile_col.shape[0]
    blocks_dev, columns, width = features.shape
    outs = call(
        functools.partial(prepare_kernel, peers),
        "prepare",
        [shape((blocks_dev // reps, columns, width), BF16)] + [shape((1, per), jnp.int32)] * (peers + 1),
        [vmem()] * 4,
        limit=VMEM_ALL,
    )(tile_count, tile_row.reshape(1, per), tile_col.reshape(1, per), features)
    return outs[0], outs[1], list(outs[2:])


def pick(ids_ref, lane):
    ids = ids_ref[...].astype(F32)
    at = lax.broadcasted_iota(jnp.int32, ids.shape, 1)
    return jnp.max(jnp.where(at == lane, ids, 0.0)).astype(jnp.int32)


def operator_kernel(blocks_dev, slots_here, groups, place_in, tiles_ref, m_ref, tiles, acc, place_ref, sems, sem):
    step = pl.program_id(0)
    per, width = tiles.shape[0], tiles.shape[1]
    chunks = per // CHUNK
    spare = slots_here * blocks_dev

    def chunk_copy(c):
        part = pl.ds(c * CHUNK, CHUNK)
        return pltpu.make_async_copy(tiles_ref.at[part], tiles.at[part], sems.at[c])

    @pl.when(step == 0)
    def _():
        placed = pltpu.make_async_copy(place_in, place_ref, sem)
        placed.start()
        for c in range(chunks):
            chunk_copy(c).start()

    acc[...] = jnp.zeros_like(acc)

    @pl.when(step == 0)
    def _():
        pltpu.make_async_copy(place_in, place_ref, sem).wait()

    def add_chunk(c, carry):
        @pl.when(step == 0)
        def _():
            chunk_copy(c).wait()

        for u in range(CHUNK):
            t = c * CHUNK + u
            place = place_ref[0, t]
            if groups > 1:
                place = place - step * spare
                place = jnp.where((place >= 0) & (place < spare), place, spare)
            side = u % SIDES
            acc[side, place] = acc[side, place] + tiles[t].astype(F32)
        return carry

    lax.fori_loop(0, chunks, add_chunk, 0)
    for s in range(slots_here):
        for r in range(blocks_dev):
            total = acc[0, s * blocks_dev + r]
            for side in range(1, SIDES):
                total = total + acc[side, s * blocks_dev + r]
            m_ref[r * width : (r + 1) * width, s * width : (s + 1) * width] = total.astype(BF16)


def list_operator(tiles, place, peers, blocks_dev):
    per, width = tiles.shape[0], tiles.shape[1]
    slots = peers * CAP
    slots_here = min(slots, GROUP)
    groups = slots // slots_here
    return call(
        functools.partial(operator_kernel, blocks_dev, slots_here, groups),
        "operator",
        shape((blocks_dev * width, slots * width), BF16),
        [pl.BlockSpec(memory_space=pl.ANY), hbm()],
        [
            pltpu.VMEM((per, width, width), BF16),
            pltpu.VMEM((SIDES, slots_here * blocks_dev + 1, width, width), F32),
            pltpu.SMEM((1, per), jnp.int32),
            pltpu.SemaphoreType.DMA((per // CHUNK,)),
            pltpu.SemaphoreType.DMA,
        ],
        moved=2 ** 24,
        limit=VMEM_MOST,
        grid=(groups,),
        out_specs=pl.BlockSpec((blocks_dev * width, slots_here * width), lambda i: (0, i)),
    )(place, tiles)


def mirrored(near, m_ref, mir, slots, width):
    if slots <= GROUP:
        mir[...] = dot(near, m_ref[...])
    else:
        part = GROUP * width

        @pl.loop(0, slots // GROUP)
        def _(i):
            where = pl.ds(pl.multiple_of(i * part, part), part)
            mir[:, where] = dot(near, m_ref[:, where])


def first_sends_kernel(peers, *refs):
    ask_refs, refs = refs[: peers - 1], refs[peers - 1 :]
    x3, m_ref, refs = refs[0], refs[1], refs[2:]
    send_refs, self_ref, mir = refs[: peers - 1], refs[peers - 1], refs[peers]
    _, columns, width = x3.shape
    both = CAP * width
    mirrored(lanes(x3), m_ref, mir, peers * CAP, width)
    self_ref[...] = mir[:, :both]
    lane = lax.broadcasted_iota(jnp.int32, (TAIL, both), 1)
    for k in range(1, peers):
        out = send_refs[k - 1]
        out[:columns, :] = mir[:, k * both : (k + 1) * both].astype(BF16)
        low, high = ask_refs[k - 1][:, :1], ask_refs[k - 1][:, 1:2]
        out[columns:, :] = jnp.where(lane < width, low, high).astype(F32).astype(BF16)


def first_sends(values, operator, asks, peers):
    _, columns, width = values.shape
    outs = call(
        functools.partial(first_sends_kernel, peers),
        "first_sends",
        [shape((columns + TAIL, CAP * width), BF16)] * (peers - 1)
        + [shape((columns, CAP * width), F32)],
        [vmem()] * (peers + 1),
        [pltpu.VMEM((columns, peers * CAP * width), F32)],
        flops=2 ** 28,
        moved=2 ** 21,
    )(*asks, values, operator)
    return [None] + list(outs[: peers - 1]), outs[peers - 1]


def add_sums(acc, block, sums):
    acc[block] = acc[block] + sums.astype(F32)


def own_rows(far, m_ref, k):
    both = far.shape[1]
    return dot(far, m_ref[:, k * both : (k + 1) * both], NT)


def put_rows(acc, own, before=None):
    blocks_dev, _, width = acc.shape
    for b in range(blocks_dev):
        add = own[:, b * width : (b + 1) * width]
        acc[b] = add if before is None else before[b] + add


def split_rows(acc, give_ref, keep_ref):
    half = lax.axis_index("rep")
    share = give_ref.shape[0]
    give_ref[...] = acc[pl.ds((1 - half) * share, share)].astype(BF16)
    keep_ref[...] = acc[pl.ds(half * share, share)]


def self_rows(x3, m_ref, ask_ref):
    far = jnp.concatenate([x3[pick(ask_ref, s)] for s in range(CAP)], axis=1)
    return own_rows(far, m_ref, 0)


def far_of(block, mine_ref, other_ref, ask_ref, at=0):
    half = lax.axis_index("rep")
    share = block.shape[0] // 2
    block[pl.ds(half * share, share)] = mine_ref[at * share : (at + 1) * share]
    block[pl.ds((1 - half) * share, share)] = other_ref[at * share : (at + 1) * share]
    return jnp.concatenate([block[pick(ask_ref, s)] for s in range(CAP)], axis=1)


def first_rows_kernel(peers, *refs):
    ask_ref, refs = refs[0], refs[1:]
    came_refs, refs = refs[: peers - 1], refs[peers - 1 :]
    x3, m_ref, self_ref, acc, ids_refs = refs[0], refs[1], refs[2], refs[3], refs[4:]
    _, columns, width = x3.shape
    put_rows(acc, self_rows(x3, m_ref, ask_ref))
    for s in range(CAP):
        add_sums(acc, pick(ask_ref, s), self_ref[:, s * width : (s + 1) * width])
    lane = lax.broadcasted_iota(jnp.int32, ids_refs[0].shape, 1)
    for k in range(1, peers):
        came = came_refs[k - 1]
        ids = jnp.zeros(lane.shape, jnp.int32)
        for s in range(CAP):
            here = slice(s * width, (s + 1) * width)
            asked = jnp.max(came[columns : columns + TAIL, here].astype(F32)).astype(jnp.int32)
            ids = jnp.where(lane == s, asked, ids)
            add_sums(acc, asked, came[:columns, here])
        ids_refs[k - 1][...] = ids


def first_rows(values, operator, ask, came, own_mirror, peers):
    _, columns, width = values.shape
    outs = call(
        functools.partial(first_rows_kernel, peers),
        "first_rows",
        [shape(values.shape, F32)] + [shape((1, width), jnp.int32)] * (peers - 1),
        [vmem()] * (peers + 3),
        flops=2 ** 27,
        moved=2 ** 20,
    )(ask, *came[1:], values, operator, own_mirror)
    return outs[0], [None] + list(outs[1:])


def stack_kernel(*refs):
    at = 0
    for ref in refs[:-1]:
        share = ref.shape[0]
        refs[-1][at : at + share] = ref[...]
        at += share


def halves_kernel(in_ref, low_ref, high_ref):
    share = low_ref.shape[0]
    low_ref[...] = in_ref[:share]
    high_ref[...] = in_ref[share:]


def halves(parts):
    if len(parts) > 1:
        return parts
    share, columns, width = parts[0].shape
    part = shape((share // 2, columns, width), BF16)
    return list(call(halves_kernel, "halves", [part, part], [vmem()])(*parts))


def stack(pieces):
    _, columns, width = pieces[0].shape
    out = shape((sum(piece.shape[0] for piece in pieces), columns, width), BF16)
    return call(stack_kernel, "stack", out, [vmem()] * len(pieces))(*pieces)


def far_rows_kernel(peers, *refs):
    ask_refs, refs = refs[: peers - 1], refs[peers - 1 :]
    before, mine_ref, other_ref, m_ref, give_ref, keep_ref, acc, block, far = refs
    both = CAP * acc.shape[2]
    for k in range(1, peers):
        far[:, k * both : (k + 1) * both] = far_of(block, mine_ref, other_ref, ask_refs[k - 1], k - 1)
    if peers * CAP <= GROUP:
        own = dot(far[:, both:], m_ref[:, both:], NT)
    else:

        def add_peer(k, total):
            here = pl.ds(pl.multiple_of(k * both, both), both)
            return total + dot(far[:, here], m_ref[:, here], NT)

        own = lax.fori_loop(1, peers, add_peer, jnp.zeros((acc.shape[1], m_ref.shape[0]), F32))
    put_rows(acc, own, before)
    split_rows(acc, give_ref, keep_ref)


def far_rows(before, asks, mine, other, operator, peers, reps):
    blocks_dev, columns, width = before.shape
    share = (blocks_dev // reps, columns, width)
    return call(
        functools.partial(far_rows_kernel, peers),
        "far_rows",
        [shape(share, BF16), shape(share, F32)],
        [vmem()] * (peers + 3),
        [
            pltpu.VMEM(before.shape, F32),
            pltpu.VMEM(before.shape, BF16),
            pltpu.VMEM((columns, peers * CAP * width), BF16),
        ],
        flops=2 ** 28,
        moved=2 ** 21,
    )(*asks[1:], before, mine, other, operator)


def late_rows_kernel(ks, first, last, *refs):
    if first:
        ask_ref, x3, self_ref = refs[:3]
    else:
        before = refs[0]
    refs = refs[3 if first else 1 :]
    ids_refs, refs = refs[: len(ks)], refs[len(ks) :]
    came_refs, refs = refs[: len(ks)], refs[len(ks) :]
    m_ref, out_ref = refs[:2]
    acc = refs[2] if last else out_ref
    width = acc.shape[2]
    both = CAP * width
    own = self_rows(x3, m_ref, ask_ref) if first else None
    for i, k in enumerate(ks):
        add = own_rows(came_refs[i][:, both : 2 * both], m_ref, k)
        own = add if own is None else own + add
    put_rows(acc, own, None if first else before)
    if first:
        for s in range(CAP):
            add_sums(acc, pick(ask_ref, s), self_ref[:, s * width : (s + 1) * width])
    for i in range(len(ks)):
        for s in range(CAP):
            add_sums(acc, pick(ids_refs[i], s), came_refs[i][:, s * width : (s + 1) * width])
    if last:
        out_ref[...] = acc[...].astype(BF16)


def late_rows(head, ids, came, ks, operator, first, last):
    values = head[1] if first else head[0]
    return call(
        functools.partial(late_rows_kernel, ks, first, last),
        "late_rows",
        shape(values.shape, BF16 if last else F32),
        [vmem()] * (len(head) + 2 * len(ks) + 1),
        [pltpu.VMEM(values.shape, F32)] if last else [],
        flops=2 ** 27,
        moved=2 ** 20,
    )(*head, *[ids[k] for k in ks], *[came[k] for k in ks], operator)


def add_kernel(keep_ref, came_ref, out_ref):
    out_ref[...] = (keep_ref[...] + came_ref[...].astype(F32)).astype(BF16)


def add_up(keep, came):
    return call(add_kernel, "add_up", shape(came.shape, BF16), [vmem(), vmem()])(keep, came)


def widen_kernel(feats, *refs):
    out_ref = refs[feats]
    _, columns, width = refs[0].shape
    share = out_ref.shape[1] // width
    first = lax.axis_index("rep") * share
    me = lax.axis_index("feat")
    for q in range(feats):
        rows = pl.ds(pl.multiple_of(lax.rem(me + q, feats) * columns, columns), columns)
        for b in range(share):
            out_ref[rows, b * width : (b + 1) * width] = refs[q][first + b]


def widen(parts, reps):
    blocks_dev, columns, width = parts[0].shape
    out = shape((len(parts) * columns, blocks_dev // reps * width), BF16)
    kernel = functools.partial(widen_kernel, len(parts))
    return call(kernel, "widen", out, [vmem()] * len(parts))(*parts)


def dense_kernel(feats, *refs):
    sums, wide_cot, refs = refs[:feats], refs[feats], refs[feats + 1 :]
    w_ref, act_ref, give_ref, spread_ref, term_ref, wide, pre_scr, grad = refs
    share, columns, width = act_ref.shape
    me = lax.axis_index("feat")
    rows = [pl.ds(pl.multiple_of(lax.rem(me + q, feats) * columns, columns), columns) for q in range(feats)]
    for q in range(feats):
        for b in range(share):
            wide[rows[q], b * width : (b + 1) * width] = sums[q][b]
    pre = dot(w_ref[...], wide[...], TN)
    pre_scr[...] = pre
    sig = jax.nn.sigmoid(pre)
    factor = wide_cot[...].astype(F32) * sig * (1.0 + pre * (1.0 - sig))
    grad[...] = factor.astype(BF16)
    spread = dot(w_ref[rows[0], :], grad[...]).astype(BF16)
    term_ref[...] = dot(grad[rows[0], :], wide[...], NT).astype(BF16)
    wide_share = share * width
    give_ref[:, :wide_share] = spread
    for b in range(share):
        spread_ref[b] = spread[:, b * width : (b + 1) * width]
    own = pre_scr[rows[0], :]
    act = (own * jax.nn.sigmoid(own)).astype(BF16)
    give_ref[:, wide_share:] = act
    for b in range(share):
        act_ref[b] = act[:, b * width : (b + 1) * width]


def dense(sums, cot, weight, feats):
    share, columns, width = sums[0].shape
    features = weight.shape[0]
    return call(
        functools.partial(dense_kernel, feats),
        "dense",
        [
            shape((share, columns, width), BF16),
            shape((columns, 2 * share * width), BF16),
            shape((share, columns, width), BF16),
            shape((columns, features), BF16),
        ],
        [vmem()] * (feats + 2),
        [
            pltpu.VMEM((features, share * width), BF16),
            pltpu.VMEM((features, share * width), F32),
            pltpu.VMEM((features, share * width), BF16),
        ],
        flops=2 ** 28,
        moved=2 ** 20,
    )(*sums, cot, weight)


def send_kernel(peers, *refs):
    ids_refs, refs = refs[: peers - 1], refs[peers - 1 :]
    mine_ref, came_ref, m_ref, refs = refs[0], refs[1], refs[2], refs[3:]
    x3, refs = refs[0], refs[1:]
    send_refs, refs = refs[: peers - 1], refs[peers - 1 :]
    self_ref, mir = refs
    share, _, width = mine_ref.shape
    both = CAP * width
    half = lax.axis_index("rep")
    x3[pl.ds(half * share, share)] = mine_ref[...]
    for b in range(share):
        x3[(1 - half) * share + b] = came_ref[:, b * width : (b + 1) * width]
    mirrored(lanes(x3), m_ref, mir, peers * CAP, width)
    self_ref[...] = mir[:, :both]
    for k in range(1, peers):
        out = send_refs[k - 1]
        out[:, :both] = mir[:, k * both : (k + 1) * both].astype(BF16)
        for s in range(CAP):
            at = (CAP + s) * width
            out[:, at : at + width] = x3[pick(ids_refs[k - 1], s)]


def sends_of(mine, came, operator, ids, peers, reps):
    share, columns, width = mine.shape
    chunk = 2 * CAP * width
    outs = call(
        functools.partial(send_kernel, peers),
        "sends",
        [shape((share * reps, columns, width), BF16)]
        + [shape((columns, chunk), BF16)] * (peers - 1)
        + [shape((columns, CAP * width), F32)],
        [vmem()] * (peers + 2),
        [pltpu.VMEM((columns, peers * CAP * width), F32)],
        flops=2 ** 28,
        moved=2 ** 21,
    )(*ids[1:], mine, came, operator)
    return outs[0], [None] + list(outs[1:peers]), outs[peers]


def pair_kernel(mine_ref, came_ref, out_ref):
    out_ref[...] = (mine_ref[...].astype(F32) + came_ref[...].astype(F32)).astype(out_ref.dtype)


def pair_sum(mine, came, dtype):
    return call(pair_kernel, "pair_sum", shape(mine.shape, dtype), [vmem(), vmem()])(mine, came)


def split_kernel(mine_ref, came_ref, give_ref, keep_ref, total):
    half = lax.axis_index("rep")
    part = keep_ref.shape[1]
    total[...] = mine_ref[...].astype(F32) + came_ref[...].astype(F32)
    give_ref[...] = total[:, pl.ds(pl.multiple_of((1 - half) * part, part), part)].astype(BF16)
    keep_ref[...] = total[:, pl.ds(pl.multiple_of(half * part, part), part)]


def split_sum(mine, came, reps):
    columns, features = mine.shape
    part = (columns, features // reps)
    return call(
        split_kernel,
        "split_sum",
        [shape(part, BF16), shape(part, F32)],
        [vmem(), vmem()],
        [pltpu.VMEM(mine.shape, F32)],
    )(mine, came)


def total_term(term, peers, reps):
    bit = peers // 2
    give, total = split_sum(term, across(term, peers, bit), reps)
    total = pair_sum(total, ahead(give, "rep", reps, 1), F32 if bit == 1 else BF16)
    while bit > 1:
        bit //= 2
        total = pair_sum(total, across(total, peers, bit), F32 if bit == 1 else BF16)
    return total


def finish_kernel(mine_ref, other_ref, share_ref, other_share_ref, act_ref, came_ref, grad_ref, weight_ref, out_ref):
    half = lax.axis_index("rep")
    share = share_ref.shape[1]
    grad_ref[...] = (mine_ref[...].astype(F32) + other_ref[...].astype(F32)).astype(BF16)
    weight_ref[pl.ds(pl.multiple_of(half * share, share), share), :] = share_ref[...].T
    weight_ref[pl.ds(pl.multiple_of((1 - half) * share, share), share), :] = other_share_ref[...].T
    blocks, _, width = act_ref.shape
    out_ref[pl.ds(half * blocks, blocks)] = act_ref[...]
    for b in range(blocks):
        at = (blocks + b) * width
        out_ref[(1 - half) * blocks + b] = came_ref[:, at : at + width]


def finish(mine, other, share, other_share, act, came):
    columns, width = share.shape
    return call(
        finish_kernel,
        "finish",
        [shape(mine.shape, BF16), shape((2 * width, columns), F32), shape(mine.shape, BF16)],
        [vmem()] * 6,
    )(mine, other, share, other_share, act, came)


def ahead(value, axis, size, k):
    return lax.ppermute(value, axis, [(i, (i + k) % size) for i in range(size)])


def across(value, peers, k):
    return lax.ppermute(value, "graph", [(i, i ^ k) for i in range(peers)])


def after(value, first):
    return lax.optimization_barrier((value, first))[0]


def local(features, weight, cotangent, tiles, tile_row, tile_col, tile_count):
    blocks_dev, _, width = features.shape
    peers = lax.axis_size("graph")
    feats = lax.axis_size("feat")
    reps = lax.axis_size("rep")
    far_first = sorted(range(1, peers), key=lambda k: (-(k & (peers // 2)), k))

    half, place, asks = prepare(features, tile_row, tile_col, tile_count, peers, reps)
    operator = list_operator(tiles, place, peers, blocks_dev)
    sends, own_mirror = first_sends(features, operator, asks[1:], peers)
    cots = [cotangent] + [ahead(cotangent, "feat", feats, feats - q) for q in range(1, feats)]
    pieces, held = {0: [half]}, [0]
    bit = peers // 2
    while bit:
        for k in held:
            parts = pieces[k]
            if k:
                parts, cots, _ = lax.optimization_barrier(
                    (halves(after(parts, sends[1])), cots, pieces.get(1, half))
                )
            pieces[k ^ bit] = [across(part, peers, bit) for part in parts]
        held = held + [k ^ bit for k in held]
        bit //= 2
    came = [None] * peers
    for k in far_first:
        came[k] = across(sends[k], peers, k)
    arrived = [part for k in range(1, peers) for part in pieces[k]]
    ordered, arrived = lax.optimization_barrier(([came[k] for k in far_first], arrived))
    came = [None] + [ordered[far_first.index(k)] for k in range(1, peers)]
    stacked = stack(arrived)
    swapped = ahead(stacked, "rep", reps, 1)
    acc, ids = first_rows(features, operator, asks[0], came, own_mirror, peers)
    give, keep = far_rows(acc, asks, stacked, swapped, operator, peers, reps)

    mine = add_up(keep, ahead(give, "rep", reps, 1))
    cot = widen(cots, reps)
    sums = [mine] + [ahead(mine, "feat", feats, feats - q) for q in range(1, feats)]
    act, give, spread, term = dense(sums, cot, weight, feats)
    total = total_term(term, peers, reps)
    shared = ahead(give, "rep", reps, 1)
    values, sends, own_mirror = sends_of(spread, shared, operator, ids, peers, reps)

    came = [None] * peers
    for k in far_first:
        came[k] = across(sends[k], peers, k)
    ordered, total = lax.optimization_barrier(([came[k] for k in far_first], total))
    came = [None] + [ordered[far_first.index(k)] for k in range(1, peers)]
    part = late_rows([asks[0], values, own_mirror], ids, came, far_first, operator, True, True)
    input_grad, weight_grad, activated = finish(
        part, ahead(part, "rep", reps, 1), total, ahead(total, "rep", reps, 1), act, shared
    )
    return (activated, input_grad, weight_grad)


def solution(mesh):
    placed = (
        P(("parts", "graph"), "feat", None),
        P(),
        P(("parts", "graph"), "feat", None),
        P(("parts", "graph", "rep"), None, None),
        P(("parts", "graph", "rep")),
        P(("parts", "graph", "rep")),
        P(("parts", "graph", "rep")),
    )
    return jax.shard_map(
        local,
        mesh=mesh,
        in_specs=placed,
        out_specs=(
            P(("parts", "graph"), "feat", None),
            P(("parts", "graph"), "feat", None),
            P("parts", "feat"),
        ),
        check_vma=False,
    )
```

```python
import functools

import jax
import jax.numpy as jnp
from jax import lax
from jax.experimental import pallas as pl
from jax.experimental.pallas import tpu as pltpu
from jax.sharding import PartitionSpec as P

CAP = 2
GROUP = 8
CHUNK = 16
SIDES = 2
PLACE_ROWS = 8
PLACE_BUFFER = 2 ** 22
TAIL = 16
VMEM_LIMIT = 40 * 2 ** 20
VMEM_MOST = 50 * 2 ** 20
VMEM_ALL = 58 * 2 ** 20

NT = (((1,), (1,)), ((), ()))
TN = (((0,), (0,)), ((), ()))
F32 = jnp.float32
BF16 = jnp.bfloat16


def vmem():
    return pl.BlockSpec(memory_space=pltpu.VMEM)


def smem():
    return pl.BlockSpec(memory_space=pltpu.SMEM)


def hbm():
    return pl.BlockSpec(memory_space=pltpu.HBM)


def shape(dims, dtype):
    return jax.ShapeDtypeStruct(tuple(dims), dtype)


def dot(a, b, dims=None):
    if dims is None:
        return jnp.dot(a, b, preferred_element_type=F32)
    return lax.dot_general(a, b, dims, preferred_element_type=F32)


def call(kernel, name, outs, in_specs, scratch=(), flops=0, moved=2 ** 18, limit=VMEM_LIMIT, **kwargs):
    return pl.pallas_call(
        kernel,
        out_shape=outs,
        in_specs=in_specs,
        scratch_shapes=list(scratch),
        compiler_params=pltpu.CompilerParams(vmem_limit_bytes=limit),
        cost_estimate=pl.CostEstimate(flops=flops, bytes_accessed=moved, transcendentals=0),
        name=name,
        **kwargs,
    )


def lanes(x3):
    return jnp.concatenate([x3[b] for b in range(x3.shape[0])], axis=1)


def places(peers, blocks_dev, count, row, col, ask_refs):
    me = lax.axis_index("graph")
    lane = lax.broadcasted_iota(jnp.int32, col.shape, 1)
    live = lane < count
    place = jnp.full(col.shape, peers * CAP * blocks_dev, jnp.int32)
    for k in range(peers):
        local = col - jnp.bitwise_xor(me, k) * blocks_dev
        inside = live & (local >= 0) & (local < blocks_dev)
        low = jnp.min(jnp.where(inside, local, blocks_dev - 1), axis=1, keepdims=True)
        high = jnp.max(jnp.where(inside, local, 0), axis=1, keepdims=True)
        ask_refs[k][...] = jnp.where(lane == 0, low, high)
        slot = k * CAP + (local != low).astype(jnp.int32)
        place = jnp.where(inside, slot * blocks_dev + row, place)
    return place


def prepare_kernel(peers, count_ref, row_ref, col_ref, x3, half_ref, place_out, *refs):
    ask_refs, place_ref, sem = refs[:peers], refs[peers], refs[peers + 1]
    share = half_ref.shape[0]
    half_ref[...] = x3[pl.ds(lax.axis_index("rep") * share, share)]
    count = jnp.broadcast_to(count_ref[...], (1, 1))
    place = places(peers, x3.shape[0], count, row_ref[...], col_ref[...], ask_refs)
    place_ref[...] = jnp.broadcast_to(place, place_ref.shape)
    copy = pltpu.make_async_copy(place_ref, place_out.at[pl.ds(0, PLACE_ROWS)], sem)
    copy.start()
    copy.wait()


def prepare(features, tile_row, tile_col, tile_count, peers, reps):
    per = tile_col.shape[0]
    blocks_dev, columns, width = features.shape
    outs = call(
        functools.partial(prepare_kernel, peers),
        "prepare",
        [shape((blocks_dev // reps, columns, width), BF16), shape((PLACE_BUFFER // (4 * per), per), jnp.int32)]
        + [shape((1, per), jnp.int32)] * peers,
        [vmem()] * 4,
        [pltpu.VMEM((PLACE_ROWS, per), jnp.int32), pltpu.SemaphoreType.DMA],
        out_specs=[vmem(), hbm()] + [vmem()] * peers,
        limit=VMEM_ALL,
    )(tile_count, tile_row.reshape(1, per), tile_col.reshape(1, per), features)
    return outs[0], outs[1], list(outs[2:])


def pick(ids_ref, lane):
    ids = ids_ref[...].astype(F32)
    at = lax.broadcasted_iota(jnp.int32, ids.shape, 1)
    return jnp.max(jnp.where(at == lane, ids, 0.0)).astype(jnp.int32)


def operator_kernel(blocks_dev, slots_here, groups, place_in, tiles_ref, m_ref, tiles, acc, place_ref, sems, sem):
    step = pl.program_id(0)
    per, width = tiles.shape[0], tiles.shape[1]
    chunks = per // CHUNK
    spare = slots_here * blocks_dev

    def chunk_copy(c):
        part = pl.ds(c * CHUNK, CHUNK)
        return pltpu.make_async_copy(tiles_ref.at[part], tiles.at[part], sems.at[c])

    def place_copy():
        return pltpu.make_async_copy(place_in.at[pl.ds(0, PLACE_ROWS)], place_ref, sem)

    @pl.when(step == 0)
    def _():
        place_copy().start()
        for c in range(chunks):
            chunk_copy(c).start()

    acc[...] = jnp.zeros_like(acc)

    @pl.when(step == 0)
    def _():
        place_copy().wait()

    def add_chunk(c, carry):
        @pl.when(step == 0)
        def _():
            chunk_copy(c).wait()

        for u in range(CHUNK):
            t = c * CHUNK + u
            place = place_ref[0, t]
            if groups > 1:
                place = place - step * spare
                place = jnp.where((place >= 0) & (place < spare), place, spare)
            side = u % SIDES
            acc[side, place] = acc[side, place] + tiles[t].astype(F32)
        return carry

    lax.fori_loop(0, chunks, add_chunk, 0)
    for s in range(slots_here):
        for r in range(blocks_dev):
            total = acc[0, s * blocks_dev + r]
            for side in range(1, SIDES):
                total = total + acc[side, s * blocks_dev + r]
            m_ref[r * width : (r + 1) * width, s * width : (s + 1) * width] = total.astype(BF16)


def list_operator(tiles, place, peers, blocks_dev):
    per, width = tiles.shape[0], tiles.shape[1]
    slots = peers * CAP
    slots_here = min(slots, GROUP)
    groups = slots // slots_here
    return call(
        functools.partial(operator_kernel, blocks_dev, slots_here, groups),
        "operator",
        shape((blocks_dev * width, slots * width), BF16),
        [hbm(), hbm()],
        [
            pltpu.VMEM((per, width, width), BF16),
            pltpu.VMEM((SIDES, slots_here * blocks_dev + 1, width, width), F32),
            pltpu.SMEM((PLACE_ROWS, per), jnp.int32),
            pltpu.SemaphoreType.DMA((per // CHUNK,)),
            pltpu.SemaphoreType.DMA,
        ],
        moved=2 ** 24,
        limit=VMEM_MOST,
        grid=(groups,),
        out_specs=pl.BlockSpec((blocks_dev * width, slots_here * width), lambda i: (0, i)),
    )(place, tiles)


def mirrored(near, m_ref, mir, slots, width):
    if slots <= GROUP:
        mir[...] = dot(near, m_ref[...])
    else:
        part = GROUP * width

        @pl.loop(0, slots // GROUP)
        def _(i):
            where = pl.ds(pl.multiple_of(i * part, part), part)
            mir[:, where] = dot(near, m_ref[:, where])


def first_sends_kernel(peers, *refs):
    ask_refs, refs = refs[: peers - 1], refs[peers - 1 :]
    x3, m_ref, refs = refs[0], refs[1], refs[2:]
    send_refs, self_ref, mir = refs[: peers - 1], refs[peers - 1], refs[peers]
    _, columns, width = x3.shape
    both = CAP * width
    mirrored(lanes(x3), m_ref, mir, peers * CAP, width)
    self_ref[...] = mir[:, :both]
    lane = lax.broadcasted_iota(jnp.int32, (TAIL, both), 1)
    for k in range(1, peers):
        out = send_refs[k - 1]
        out[:columns, :] = mir[:, k * both : (k + 1) * both].astype(BF16)
        low, high = ask_refs[k - 1][:, :1], ask_refs[k - 1][:, 1:2]
        out[columns:, :] = jnp.where(lane < width, low, high).astype(F32).astype(BF16)


def first_sends(values, operator, asks, peers):
    _, columns, width = values.shape
    outs = call(
        functools.partial(first_sends_kernel, peers),
        "first_sends",
        [shape((columns + TAIL, CAP * width), BF16)] * (peers - 1)
        + [shape((columns, CAP * width), F32)],
        [vmem()] * (peers + 1),
        [pltpu.VMEM((columns, peers * CAP * width), F32)],
        flops=2 ** 28,
        moved=2 ** 21,
    )(*asks, values, operator)
    return [None] + list(outs[: peers - 1]), outs[peers - 1]


def add_sums(acc, block, sums):
    acc[block] = acc[block] + sums.astype(F32)


def own_rows(far, m_ref, k):
    both = far.shape[1]
    return dot(far, m_ref[:, k * both : (k + 1) * both], NT)


def put_rows(acc, own, before=None):
    blocks_dev, _, width = acc.shape
    for b in range(blocks_dev):
        add = own[:, b * width : (b + 1) * width]
        acc[b] = add if before is None else before[b] + add


def self_rows(x3, m_ref, ask_ref):
    far = jnp.concatenate([x3[pick(ask_ref, s)] for s in range(CAP)], axis=1)
    return own_rows(far, m_ref, 0)


def far_of(block, mine_ref, other_ref, ask_ref, at=0):
    half = lax.axis_index("rep")
    share = block.shape[0] // 2
    block[pl.ds(half * share, share)] = mine_ref[at * share : (at + 1) * share]
    block[pl.ds((1 - half) * share, share)] = other_ref[at * share : (at + 1) * share]
    return jnp.concatenate([block[pick(ask_ref, s)] for s in range(CAP)], axis=1)


def first_rows_kernel(peers, *refs):
    ask_ref, refs = refs[0], refs[1:]
    came_refs, refs = refs[: peers - 1], refs[peers - 1 :]
    x3, m_ref, self_ref, acc, ids_refs = refs[0], refs[1], refs[2], refs[3], refs[4:]
    _, columns, width = x3.shape
    put_rows(acc, self_rows(x3, m_ref, ask_ref))
    for s in range(CAP):
        add_sums(acc, pick(ask_ref, s), self_ref[:, s * width : (s + 1) * width])
    lane = lax.broadcasted_iota(jnp.int32, ids_refs[0].shape, 1)
    for k in range(1, peers):
        came = came_refs[k - 1]
        ids = jnp.zeros(lane.shape, jnp.int32)
        for s in range(CAP):
            here = slice(s * width, (s + 1) * width)
            asked = jnp.max(came[columns : columns + TAIL, here].astype(F32)).astype(jnp.int32)
            ids = jnp.where(lane == s, asked, ids)
            add_sums(acc, asked, came[:columns, here])
        ids_refs[k - 1][...] = ids


def first_rows(values, operator, ask, came, own_mirror, peers):
    _, columns, width = values.shape
    outs = call(
        functools.partial(first_rows_kernel, peers),
        "first_rows",
        [shape(values.shape, F32)] + [shape((1, width), jnp.int32)] * (peers - 1),
        [vmem()] * (peers + 3),
        flops=2 ** 27,
        moved=2 ** 20,
    )(ask, *came[1:], values, operator, own_mirror)
    return outs[0], [None] + list(outs[1:])


def stack_kernel(*refs):
    at = 0
    for ref in refs[:-1]:
        share = ref.shape[0]
        refs[-1][at : at + share] = ref[...]
        at += share


def halves_kernel(in_ref, low_ref, high_ref):
    share = low_ref.shape[0]
    low_ref[...] = in_ref[:share]
    high_ref[...] = in_ref[share:]


def halves(parts):
    if len(parts) > 1:
        return parts
    share, columns, width = parts[0].shape
    part = shape((share // 2, columns, width), BF16)
    return list(call(halves_kernel, "halves", [part, part], [vmem()])(*parts))


def stack(pieces):
    _, columns, width = pieces[0].shape
    out = shape((sum(piece.shape[0] for piece in pieces), columns, width), BF16)
    return call(stack_kernel, "stack", out, [vmem()] * len(pieces))(*pieces)


def half_rows(before, far_ref, m_ref, first, share):
    columns, width = before.shape[1:]
    both = CAP * width
    rows = pl.ds(pl.multiple_of(first * width, share * width), share * width)
    if m_ref.shape[1] <= GROUP * width:
        own = dot(far_ref[:, both:], m_ref[rows, both:], NT)
    else:

        def add_peer(k, total):
            here = pl.ds(pl.multiple_of(k * both, both), both)
            return total + dot(far_ref[:, here], m_ref[rows, here], NT)

        zeros = jnp.zeros((columns, share * width), F32)
        own = lax.fori_loop(1, m_ref.shape[1] // both, add_peer, zeros)
    return [before[first + b] + own[:, b * width : (b + 1) * width] for b in range(share)]


def give_rows_kernel(peers, *refs):
    ask_refs, refs = refs[: peers - 1], refs[peers - 1 :]
    before, mine_ref, other_ref, m_ref, give_ref, far_ref, block = refs
    both = CAP * before.shape[2]
    for k in range(1, peers):
        far_ref[:, k * both : (k + 1) * both] = far_of(block, mine_ref, other_ref, ask_refs[k - 1], k - 1)
    far_ref[:, :both] = jnp.zeros((far_ref.shape[0], both), BF16)
    share = give_ref.shape[0]
    rows = half_rows(before, far_ref, m_ref, (1 - lax.axis_index("rep")) * share, share)
    for b in range(share):
        give_ref[b] = rows[b].astype(BF16)


def give_rows(before, asks, mine, other, operator, peers, reps):
    blocks_dev, columns, width = before.shape
    return call(
        functools.partial(give_rows_kernel, peers),
        "give_rows",
        [shape((blocks_dev // reps, columns, width), BF16), shape((columns, peers * CAP * width), BF16)],
        [vmem()] * (peers + 3),
        [pltpu.VMEM(before.shape, BF16)],
        flops=2 ** 27,
        moved=2 ** 20,
    )(*asks[1:], before, mine, other, operator)


def keep_rows_kernel(before, far_ref, m_ref, keep_ref):
    share = keep_ref.shape[0]
    rows = half_rows(before, far_ref, m_ref, lax.axis_index("rep") * share, share)
    for b in range(share):
        keep_ref[b] = rows[b]


def keep_rows(before, far, operator, reps):
    blocks_dev, columns, width = before.shape
    return call(
        keep_rows_kernel,
        "keep_rows",
        shape((blocks_dev // reps, columns, width), F32),
        [vmem()] * 3,
        flops=2 ** 27,
        moved=2 ** 20,
    )(before, far, operator)


def late_rows_kernel(ks, first, last, *refs):
    if first:
        ask_ref, x3, self_ref = refs[:3]
    else:
        before = refs[0]
    refs = refs[3 if first else 1 :]
    ids_refs, refs = refs[: len(ks)], refs[len(ks) :]
    came_refs, refs = refs[: len(ks)], refs[len(ks) :]
    m_ref, out_ref = refs[:2]
    acc = refs[2] if last else out_ref
    width = acc.shape[2]
    both = CAP * width
    own = self_rows(x3, m_ref, ask_ref) if first else None
    for i, k in enumerate(ks):
        add = own_rows(came_refs[i][:, both : 2 * both], m_ref, k)
        own = add if own is None else own + add
    put_rows(acc, own, None if first else before)
    if first:
        for s in range(CAP):
            add_sums(acc, pick(ask_ref, s), self_ref[:, s * width : (s + 1) * width])
    for i in range(len(ks)):
        for s in range(CAP):
            add_sums(acc, pick(ids_refs[i], s), came_refs[i][:, s * width : (s + 1) * width])
    if last:
        out_ref[...] = acc[...].astype(BF16)


def late_rows(head, ids, came, ks, operator, first, last):
    values = head[1] if first else head[0]
    return call(
        functools.partial(late_rows_kernel, ks, first, last),
        "late_rows",
        shape(values.shape, BF16 if last else F32),
        [vmem()] * (len(head) + 2 * len(ks) + 1),
        [pltpu.VMEM(values.shape, F32)] if last else [],
        flops=2 ** 27,
        moved=2 ** 20,
    )(*head, *[ids[k] for k in ks], *[came[k] for k in ks], operator)


def add_kernel(keep_ref, came_ref, out_ref):
    out_ref[...] = (keep_ref[...] + came_ref[...].astype(F32)).astype(BF16)


def add_up(keep, came):
    return call(add_kernel, "add_up", shape(came.shape, BF16), [vmem(), vmem()])(keep, came)


def widen_kernel(feats, *refs):
    out_ref = refs[feats]
    _, columns, width = refs[0].shape
    share = out_ref.shape[1] // width
    first = lax.axis_index("rep") * share
    me = lax.axis_index("feat")
    for q in range(feats):
        rows = pl.ds(pl.multiple_of(lax.rem(me + q, feats) * columns, columns), columns)
        for b in range(share):
            out_ref[rows, b * width : (b + 1) * width] = refs[q][first + b]


def widen(parts, reps):
    blocks_dev, columns, width = parts[0].shape
    out = shape((len(parts) * columns, blocks_dev // reps * width), BF16)
    kernel = functools.partial(widen_kernel, len(parts))
    return call(kernel, "widen", out, [vmem()] * len(parts))(*parts)


def dense_kernel(feats, *refs):
    sums, wide_cot, refs = refs[:feats], refs[feats], refs[feats + 1 :]
    w_ref, act_ref, give_ref, spread_ref, term_ref, wide, pre_scr, grad = refs
    share, columns, width = act_ref.shape
    me = lax.axis_index("feat")
    rows = [pl.ds(pl.multiple_of(lax.rem(me + q, feats) * columns, columns), columns) for q in range(feats)]
    for q in range(feats):
        for b in range(share):
            wide[rows[q], b * width : (b + 1) * width] = sums[q][b]
    pre = dot(w_ref[...], wide[...], TN)
    pre_scr[...] = pre
    sig = jax.nn.sigmoid(pre)
    factor = wide_cot[...].astype(F32) * sig * (1.0 + pre * (1.0 - sig))
    grad[...] = factor.astype(BF16)
    spread = dot(w_ref[rows[0], :], grad[...]).astype(BF16)
    term_ref[...] = dot(grad[rows[0], :], wide[...], NT).astype(BF16)
    wide_share = share * width
    give_ref[:, :wide_share] = spread
    for b in range(share):
        spread_ref[b] = spread[:, b * width : (b + 1) * width]
    own = pre_scr[rows[0], :]
    act = (own * jax.nn.sigmoid(own)).astype(BF16)
    give_ref[:, wide_share:] = act
    for b in range(share):
        act_ref[b] = act[:, b * width : (b + 1) * width]


def dense(sums, cot, weight, feats):
    share, columns, width = sums[0].shape
    features = weight.shape[0]
    return call(
        functools.partial(dense_kernel, feats),
        "dense",
        [
            shape((share, columns, width), BF16),
            shape((columns, 2 * share * width), BF16),
            shape((share, columns, width), BF16),
            shape((columns, features), BF16),
        ],
        [vmem()] * (feats + 2),
        [
            pltpu.VMEM((features, share * width), BF16),
            pltpu.VMEM((features, share * width), F32),
            pltpu.VMEM((features, share * width), BF16),
        ],
        flops=2 ** 28,
        moved=2 ** 20,
    )(*sums, cot, weight)


def send_kernel(peers, *refs):
    ids_refs, refs = refs[: peers - 1], refs[peers - 1 :]
    mine_ref, came_ref, m_ref, refs = refs[0], refs[1], refs[2], refs[3:]
    x3, refs = refs[0], refs[1:]
    send_refs, refs = refs[: peers - 1], refs[peers - 1 :]
    self_ref, mir = refs
    share, _, width = mine_ref.shape
    both = CAP * width
    half = lax.axis_index("rep")
    x3[pl.ds(half * share, share)] = mine_ref[...]
    for b in range(share):
        x3[(1 - half) * share + b] = came_ref[:, b * width : (b + 1) * width]
    mirrored(lanes(x3), m_ref, mir, peers * CAP, width)
    self_ref[...] = mir[:, :both]
    for k in range(1, peers):
        out = send_refs[k - 1]
        out[:, :both] = mir[:, k * both : (k + 1) * both].astype(BF16)
        for s in range(CAP):
            at = (CAP + s) * width
            out[:, at : at + width] = x3[pick(ids_refs[k - 1], s)]


def sends_of(mine, came, operator, ids, peers, reps):
    share, columns, width = mine.shape
    chunk = 2 * CAP * width
    outs = call(
        functools.partial(send_kernel, peers),
        "sends",
        [shape((share * reps, columns, width), BF16)]
        + [shape((columns, chunk), BF16)] * (peers - 1)
        + [shape((columns, CAP * width), F32)],
        [vmem()] * (peers + 2),
        [pltpu.VMEM((columns, peers * CAP * width), F32)],
        flops=2 ** 28,
        moved=2 ** 21,
    )(*ids[1:], mine, came, operator)
    return outs[0], [None] + list(outs[1:peers]), outs[peers]


def pair_kernel(mine_ref, came_ref, out_ref):
    out_ref[...] = (mine_ref[...].astype(F32) + came_ref[...].astype(F32)).astype(out_ref.dtype)


def pair_sum(mine, came, dtype):
    return call(pair_kernel, "pair_sum", shape(mine.shape, dtype), [vmem(), vmem()])(mine, came)


def split_kernel(mine_ref, came_ref, act_ref, shared_ref, give_ref, keep_ref, out_ref, total):
    half = lax.axis_index("rep")
    blocks, _, width = act_ref.shape
    out_ref[pl.ds(half * blocks, blocks)] = act_ref[...]
    for b in range(blocks):
        at = (blocks + b) * width
        out_ref[(1 - half) * blocks + b] = shared_ref[:, at : at + width]
    part = keep_ref.shape[1]
    total[...] = mine_ref[...].astype(F32) + came_ref[...].astype(F32)
    give_ref[...] = total[:, pl.ds(pl.multiple_of((1 - half) * part, part), part)].astype(BF16)
    keep_ref[...] = total[:, pl.ds(pl.multiple_of(half * part, part), part)]


def split_sum(mine, came, act, shared, reps):
    columns, features = mine.shape
    part = (columns, features // reps)
    return call(
        split_kernel,
        "split_sum",
        [shape(part, BF16), shape(part, F32), shape((reps * act.shape[0],) + act.shape[1:], BF16)],
        [vmem()] * 4,
        [pltpu.VMEM(mine.shape, F32)],
    )(mine, came, act, shared)


def total_term(term, act, shared, peers, reps):
    bit = peers // 2
    give, total, activated = split_sum(term, across(term, peers, bit), act, shared, reps)
    total = pair_sum(total, ahead(give, "rep", reps, 1), F32 if bit == 1 else BF16)
    while bit > 1:
        bit //= 2
        total = pair_sum(total, across(total, peers, bit), F32 if bit == 1 else BF16)
    return total, activated


def finish_kernel(mine_ref, other_ref, share_ref, other_share_ref, grad_ref, weight_ref):
    half = lax.axis_index("rep")
    share = share_ref.shape[1]
    grad_ref[...] = (mine_ref[...].astype(F32) + other_ref[...].astype(F32)).astype(BF16)
    weight_ref[pl.ds(pl.multiple_of(half * share, share), share), :] = share_ref[...].T
    weight_ref[pl.ds(pl.multiple_of((1 - half) * share, share), share), :] = other_share_ref[...].T


def finish(mine, other, share, other_share):
    columns, width = share.shape
    return call(
        finish_kernel,
        "finish",
        [shape(mine.shape, BF16), shape((2 * width, columns), F32)],
        [vmem()] * 4,
    )(mine, other, share, other_share)


def ahead(value, axis, size, k):
    return lax.ppermute(value, axis, [(i, (i + k) % size) for i in range(size)])


def across(value, peers, k):
    return lax.ppermute(value, "graph", [(i, i ^ k) for i in range(peers)])


def after(value, first):
    return lax.optimization_barrier((value, first))[0]


def local(features, weight, cotangent, tiles, tile_row, tile_col, tile_count):
    blocks_dev, _, width = features.shape
    peers = lax.axis_size("graph")
    feats = lax.axis_size("feat")
    reps = lax.axis_size("rep")
    far_first = sorted(range(1, peers), key=lambda k: (-(k & (peers // 2)), k))

    half, place, asks = prepare(features, tile_row, tile_col, tile_count, peers, reps)
    operator = list_operator(tiles, place, peers, blocks_dev)
    sends, own_mirror = first_sends(features, operator, asks[1:], peers)
    cots = [cotangent] + [ahead(cotangent, "feat", feats, feats - q) for q in range(1, feats)]
    pieces, held = {0: [half]}, [0]
    bit = peers // 2
    while bit:
        for k in held:
            parts = pieces[k]
            if k:
                parts, cots, _ = lax.optimization_barrier(
                    (halves(after(parts, sends[1])), cots, pieces.get(1, half))
                )
            pieces[k ^ bit] = [across(part, peers, bit) for part in parts]
        held = held + [k ^ bit for k in held]
        bit //= 2
    came = [None] * peers
    for k in far_first:
        came[k] = across(sends[k], peers, k)
    arrived = [part for k in range(1, peers) for part in pieces[k]]
    middle = peers // 2
    came[middle:], arrived = lax.optimization_barrier((came[middle:], arrived))
    came[1:middle], arrived = lax.optimization_barrier((came[1:middle], arrived))
    stacked = stack(arrived)
    swapped = ahead(stacked, "rep", reps, 1)
    acc, ids = first_rows(features, operator, asks[0], came, own_mirror, peers)
    give, asked = give_rows(acc, asks, stacked, swapped, operator, peers, reps)
    keep = keep_rows(acc, asked, operator, reps)

    mine = add_up(keep, ahead(give, "rep", reps, 1))
    cot = widen(cots, reps)
    sums = [mine] + [ahead(mine, "feat", feats, feats - q) for q in range(1, feats)]
    act, give, spread, term = dense(sums, cot, weight, feats)
    shared = ahead(give, "rep", reps, 1)
    total, activated = total_term(term, act, shared, peers, reps)
    values, sends, own_mirror = sends_of(spread, shared, operator, ids, peers, reps)

    came = [None] * peers
    for k in far_first:
        came[k] = across(sends[k], peers, k)
    ordered, total = lax.optimization_barrier(([came[k] for k in far_first], total))
    came = [None] + [ordered[far_first.index(k)] for k in range(1, peers)]
    acc = late_rows([asks[0], values, own_mirror], ids, came, [], operator, True, False)
    part = late_rows([acc], ids, came, far_first, operator, False, True)
    input_grad, weight_grad = finish(
        part, ahead(part, "rep", reps, 1), total, ahead(total, "rep", reps, 1)
    )
    return (activated, input_grad, weight_grad)


def solution(mesh):
    placed = (
        P(("parts", "graph"), "feat", None),
        P(),
        P(("parts", "graph"), "feat", None),
        P(("parts", "graph", "rep"), None, None),
        P(("parts", "graph", "rep")),
        P(("parts", "graph", "rep")),
        P(("parts", "graph", "rep")),
    )
    return jax.shard_map(
        local,
        mesh=mesh,
        in_specs=placed,
        out_specs=(
            P(("parts", "graph"), "feat", None),
            P(("parts", "graph"), "feat", None),
            P("parts", "feat"),
        ),
        check_vma=False,
    )
```

```python
import functools

import jax
import jax.numpy as jnp
from jax import lax
from jax.experimental import pallas as pl
from jax.experimental.pallas import tpu as pltpu
from jax.sharding import PartitionSpec as P

CAP = 2
GROUP = 8
CHUNK = 16
SIDES = 2
PLACE_ROWS = 8
PLACE_BUFFER = 2 ** 22
TAIL = 16
VMEM_LIMIT = 40 * 2 ** 20
VMEM_MOST = 50 * 2 ** 20
VMEM_ALL = 58 * 2 ** 20

NT = (((1,), (1,)), ((), ()))
TN = (((0,), (0,)), ((), ()))
F32 = jnp.float32
BF16 = jnp.bfloat16


def vmem():
    return pl.BlockSpec(memory_space=pltpu.VMEM)


def smem():
    return pl.BlockSpec(memory_space=pltpu.SMEM)


def hbm():
    return pl.BlockSpec(memory_space=pltpu.HBM)


def shape(dims, dtype):
    return jax.ShapeDtypeStruct(tuple(dims), dtype)


def dot(a, b, dims=None):
    if dims is None:
        return jnp.dot(a, b, preferred_element_type=F32)
    return lax.dot_general(a, b, dims, preferred_element_type=F32)


def call(kernel, name, outs, in_specs, scratch=(), flops=0, moved=2 ** 18, limit=VMEM_LIMIT, **kwargs):
    return pl.pallas_call(
        kernel,
        out_shape=outs,
        in_specs=in_specs,
        scratch_shapes=list(scratch),
        compiler_params=pltpu.CompilerParams(vmem_limit_bytes=limit),
        cost_estimate=pl.CostEstimate(flops=flops, bytes_accessed=moved, transcendentals=0),
        name=name,
        **kwargs,
    )


def lanes(x3):
    return jnp.concatenate([x3[b] for b in range(x3.shape[0])], axis=1)


def places(peers, blocks_dev, count, row, col, table):
    me = lax.axis_index("graph")
    lane = lax.broadcasted_iota(jnp.int32, col.shape, 1)
    live = lane < count
    place = jnp.full(col.shape, peers * CAP * blocks_dev, jnp.int32)
    for k in range(peers):
        local = col - jnp.bitwise_xor(me, k) * blocks_dev
        inside = live & (local >= 0) & (local < blocks_dev)
        low = jnp.min(jnp.where(inside, local, blocks_dev - 1), axis=1, keepdims=True)
        high = jnp.max(jnp.where(inside, local, 0), axis=1, keepdims=True)
        table[PLACE_ROWS + k : PLACE_ROWS + k + 1, :] = jnp.where(lane == 0, low, high)
        slot = k * CAP + (local != low).astype(jnp.int32)
        place = jnp.where(inside, slot * blocks_dev + row, place)
    table[:PLACE_ROWS, :] = jnp.broadcast_to(place, (PLACE_ROWS, place.shape[1]))


def table_rows(peers):
    return PLACE_ROWS + -(-peers // 8) * 8


def prepare_kernel(peers, count_ref, row_ref, col_ref, x3, half_out, table_out, table, half_sem, sem):
    share = half_out.shape[0]
    mine = pl.ds(lax.axis_index("rep") * share, share)
    half_copy = pltpu.make_async_copy(x3.at[mine], half_out, half_sem)
    half_copy.start()
    count = jnp.broadcast_to(count_ref[...], (1, 1))
    if table.shape[0] > PLACE_ROWS + peers:
        table[...] = jnp.zeros(table.shape, jnp.int32)
    places(peers, x3.shape[0], count, row_ref[...], col_ref[...], table)
    copy = pltpu.make_async_copy(table, table_out.at[pl.ds(0, table.shape[0])], sem)
    copy.start()
    half_copy.wait()
    copy.wait()


def prepare(features, tile_row, tile_col, tile_count, peers, reps):
    per = tile_col.shape[0]
    blocks_dev, columns, width = features.shape
    return call(
        functools.partial(prepare_kernel, peers),
        "prepare",
        [shape((blocks_dev // reps, columns, width), BF16), shape((PLACE_BUFFER // (4 * per), per), jnp.int32)],
        [vmem()] * 4,
        [
            pltpu.VMEM((table_rows(peers), per), jnp.int32),
            pltpu.SemaphoreType.DMA,
            pltpu.SemaphoreType.DMA,
        ],
        limit=VMEM_ALL,
        out_specs=[hbm(), hbm()],
    )(tile_count, tile_row.reshape(1, per), tile_col.reshape(1, per), features)


def pick(ids_ref, lane):
    ids = ids_ref[...].astype(F32)
    at = lax.broadcasted_iota(jnp.int32, ids.shape, 1)
    return jnp.max(jnp.where(at == lane, ids, 0.0)).astype(jnp.int32)


def operator_kernel(blocks_dev, slots_here, groups, table_in, tiles_ref, m_ref, *refs):
    asks, (tiles, acc, place_ref, table, sems, sem, table_sem) = refs[:-7], refs[-7:]
    step = pl.program_id(0)
    per, width = tiles.shape[0], tiles.shape[1]
    chunks = per // CHUNK
    spare = slots_here * blocks_dev

    def chunk_copy(c):
        part = pl.ds(c * CHUNK, CHUNK)
        return pltpu.make_async_copy(tiles_ref.at[part], tiles.at[part], sems.at[c])

    def place_copy():
        return pltpu.make_async_copy(table_in.at[pl.ds(0, PLACE_ROWS)], place_ref, sem)

    def table_copy():
        return pltpu.make_async_copy(table_in.at[pl.ds(0, table.shape[0])], table, table_sem)

    @pl.when(step == 0)
    def _():
        place_copy().start()
        table_copy().start()
        for c in range(chunks):
            chunk_copy(c).start()

    acc[...] = jnp.zeros_like(acc)

    @pl.when(step == 0)
    def _():
        place_copy().wait()
        table_copy().wait()
        for k, ask_ref in enumerate(asks):
            ask_ref[...] = table[PLACE_ROWS + k : PLACE_ROWS + k + 1, :]

    def add_chunk(c, carry):
        @pl.when(step == 0)
        def _():
            chunk_copy(c).wait()

        for u in range(CHUNK):
            t = c * CHUNK + u
            place = place_ref[0, t]
            if groups > 1:
                place = place - step * spare
                place = jnp.where((place >= 0) & (place < spare), place, spare)
            side = u % SIDES
            acc[side, place] = acc[side, place] + tiles[t].astype(F32)
        return carry

    lax.fori_loop(0, chunks, add_chunk, 0)
    for s in range(slots_here):
        for r in range(blocks_dev):
            total = acc[0, s * blocks_dev + r]
            for side in range(1, SIDES):
                total = total + acc[side, s * blocks_dev + r]
            m_ref[r * width : (r + 1) * width, s * width : (s + 1) * width] = total.astype(BF16)


def list_operator(tiles, table, peers, blocks_dev):
    per, width = tiles.shape[0], tiles.shape[1]
    slots = peers * CAP
    slots_here = min(slots, GROUP)
    groups = slots // slots_here
    outs = call(
        functools.partial(operator_kernel, blocks_dev, slots_here, groups),
        "operator",
        [shape((blocks_dev * width, slots * width), BF16)] + [shape((1, per), jnp.int32)] * peers,
        [hbm(), hbm()],
        [
            pltpu.VMEM((per, width, width), BF16),
            pltpu.VMEM((SIDES, slots_here * blocks_dev + 1, width, width), F32),
            pltpu.SMEM((PLACE_ROWS, per), jnp.int32),
            pltpu.VMEM((table_rows(peers), per), jnp.int32),
            pltpu.SemaphoreType.DMA((per // CHUNK,)),
            pltpu.SemaphoreType.DMA,
            pltpu.SemaphoreType.DMA,
        ],
        moved=2 ** 24,
        limit=VMEM_MOST,
        grid=(groups,),
        out_specs=[pl.BlockSpec((blocks_dev * width, slots_here * width), lambda i: (0, i))] + [vmem()] * peers,
    )(table, tiles)
    return outs[0], list(outs[1:])


def mirrored(near, m_ref, mir, slots, width):
    if slots <= GROUP:
        mir[...] = dot(near, m_ref[...])
    else:
        part = GROUP * width

        @pl.loop(0, slots // GROUP)
        def _(i):
            where = pl.ds(pl.multiple_of(i * part, part), part)
            mir[:, where] = dot(near, m_ref[:, where])


def first_sends_kernel(peers, *refs):
    ask_refs, refs = refs[: peers - 1], refs[peers - 1 :]
    x3, m_ref, refs = refs[0], refs[1], refs[2:]
    send_refs, self_ref, mir = refs[: peers - 1], refs[peers - 1], refs[peers]
    _, columns, width = x3.shape
    both = CAP * width
    mirrored(lanes(x3), m_ref, mir, peers * CAP, width)
    self_ref[...] = mir[:, :both]
    lane = lax.broadcasted_iota(jnp.int32, (TAIL, both), 1)
    for k in range(1, peers):
        out = send_refs[k - 1]
        out[:columns, :] = mir[:, k * both : (k + 1) * both].astype(BF16)
        low, high = ask_refs[k - 1][:, :1], ask_refs[k - 1][:, 1:2]
        out[columns:, :] = jnp.where(lane < width, low, high).astype(F32).astype(BF16)


def first_sends(values, operator, asks, peers):
    _, columns, width = values.shape
    outs = call(
        functools.partial(first_sends_kernel, peers),
        "first_sends",
        [shape((columns + TAIL, CAP * width), BF16)] * (peers - 1)
        + [shape((columns, CAP * width), F32)],
        [vmem()] * (peers + 1),
        [pltpu.VMEM((columns, peers * CAP * width), F32)],
        flops=2 ** 28,
        moved=2 ** 21,
    )(*asks, values, operator)
    return [None] + list(outs[: peers - 1]), outs[peers - 1]


def add_sums(acc, block, sums):
    acc[block] = acc[block] + sums.astype(F32)


def own_rows(far, m_ref, k):
    both = far.shape[1]
    return dot(far, m_ref[:, k * both : (k + 1) * both], NT)


def put_rows(acc, own, before=None):
    blocks_dev, _, width = acc.shape
    for b in range(blocks_dev):
        add = own[:, b * width : (b + 1) * width]
        acc[b] = add if before is None else before[b] + add


def self_rows(x3, m_ref, ask_ref):
    far = jnp.concatenate([x3[pick(ask_ref, s)] for s in range(CAP)], axis=1)
    return own_rows(far, m_ref, 0)


def far_of(block, mine_ref, other_ref, ask_ref, at=0):
    half = lax.axis_index("rep")
    share = block.shape[0] // 2
    block[pl.ds(half * share, share)] = mine_ref[at * share : (at + 1) * share]
    block[pl.ds((1 - half) * share, share)] = other_ref[at * share : (at + 1) * share]
    return jnp.concatenate([block[pick(ask_ref, s)] for s in range(CAP)], axis=1)


def first_rows_kernel(peers, *refs):
    ask_ref, refs = refs[0], refs[1:]
    came_refs, refs = refs[: peers - 1], refs[peers - 1 :]
    x3, m_ref, self_ref, acc, ids_refs = refs[0], refs[1], refs[2], refs[3], refs[4:]
    _, columns, width = x3.shape
    put_rows(acc, self_rows(x3, m_ref, ask_ref))
    for s in range(CAP):
        add_sums(acc, pick(ask_ref, s), self_ref[:, s * width : (s + 1) * width])
    lane = lax.broadcasted_iota(jnp.int32, ids_refs[0].shape, 1)
    for k in range(1, peers):
        came = came_refs[k - 1]
        ids = jnp.zeros(lane.shape, jnp.int32)
        for s in range(CAP):
            here = slice(s * width, (s + 1) * width)
            asked = jnp.max(came[columns : columns + TAIL, here].astype(F32)).astype(jnp.int32)
            ids = jnp.where(lane == s, asked, ids)
            add_sums(acc, asked, came[:columns, here])
        ids_refs[k - 1][...] = ids


def first_rows(values, operator, ask, came, own_mirror, peers):
    _, columns, width = values.shape
    outs = call(
        functools.partial(first_rows_kernel, peers),
        "first_rows",
        [shape(values.shape, F32)] + [shape((1, width), jnp.int32)] * (peers - 1),
        [vmem()] * (peers + 3),
        flops=2 ** 27,
        moved=2 ** 20,
    )(ask, *came[1:], values, operator, own_mirror)
    return outs[0], [None] + list(outs[1:])


def stack_kernel(*refs):
    at = 0
    for ref in refs[:-1]:
        share = ref.shape[0]
        refs[-1][at : at + share] = ref[...]
        at += share


def halves_kernel(in_ref, low_ref, high_ref):
    share = low_ref.shape[0]
    low_ref[...] = in_ref[:share]
    high_ref[...] = in_ref[share:]


def halves(parts):
    if len(parts) > 1:
        return parts
    share, columns, width = parts[0].shape
    part = shape((share // 2, columns, width), BF16)
    return list(call(halves_kernel, "halves", [part, part], [vmem()])(*parts))


def stack(pieces):
    _, columns, width = pieces[0].shape
    out = shape((sum(piece.shape[0] for piece in pieces), columns, width), BF16)
    return call(stack_kernel, "stack", out, [vmem()] * len(pieces))(*pieces)


def half_rows(before, far_ref, m_ref, first, share):
    columns, width = before.shape[1:]
    both = CAP * width
    rows = pl.ds(pl.multiple_of(first * width, share * width), share * width)
    if m_ref.shape[1] <= GROUP * width:
        own = dot(far_ref[:, both:], m_ref[rows, both:], NT)
    else:

        def add_peer(k, total):
            here = pl.ds(pl.multiple_of(k * both, both), both)
            return total + dot(far_ref[:, here], m_ref[rows, here], NT)

        zeros = jnp.zeros((columns, share * width), F32)
        own = lax.fori_loop(1, m_ref.shape[1] // both, add_peer, zeros)
    return [before[first + b] + own[:, b * width : (b + 1) * width] for b in range(share)]


def give_rows_kernel(peers, *refs):
    ask_refs, refs = refs[: peers - 1], refs[peers - 1 :]
    before, mine_ref, other_ref, m_ref, give_ref, far_ref, block = refs
    both = CAP * before.shape[2]
    for k in range(1, peers):
        far_ref[:, k * both : (k + 1) * both] = far_of(block, mine_ref, other_ref, ask_refs[k - 1], k - 1)
    far_ref[:, :both] = jnp.zeros((far_ref.shape[0], both), BF16)
    share = give_ref.shape[0]
    rows = half_rows(before, far_ref, m_ref, (1 - lax.axis_index("rep")) * share, share)
    for b in range(share):
        give_ref[b] = rows[b].astype(BF16)


def give_rows(before, asks, mine, other, operator, peers, reps):
    blocks_dev, columns, width = before.shape
    return call(
        functools.partial(give_rows_kernel, peers),
        "give_rows",
        [shape((blocks_dev // reps, columns, width), BF16), shape((columns, peers * CAP * width), BF16)],
        [vmem()] * (peers + 3),
        [pltpu.VMEM(before.shape, BF16)],
        flops=2 ** 27,
        moved=2 ** 20,
    )(*asks[1:], before, mine, other, operator)


def keep_rows_kernel(before, far_ref, m_ref, keep_ref):
    share = keep_ref.shape[0]
    rows = half_rows(before, far_ref, m_ref, lax.axis_index("rep") * share, share)
    for b in range(share):
        keep_ref[b] = rows[b]


def keep_rows(before, far, operator, reps):
    blocks_dev, columns, width = before.shape
    return call(
        keep_rows_kernel,
        "keep_rows",
        shape((blocks_dev // reps, columns, width), F32),
        [vmem()] * 3,
        flops=2 ** 27,
        moved=2 ** 20,
    )(before, far, operator)


def late_rows_kernel(ks, first, last, *refs):
    if first:
        ask_ref, x3, self_ref = refs[:3]
    else:
        before = refs[0]
    refs = refs[3 if first else 1 :]
    ids_refs, refs = refs[: len(ks)], refs[len(ks) :]
    came_refs, refs = refs[: len(ks)], refs[len(ks) :]
    m_ref, out_ref = refs[:2]
    acc = refs[2] if last else out_ref
    width = acc.shape[2]
    both = CAP * width
    own = self_rows(x3, m_ref, ask_ref) if first else None
    for i, k in enumerate(ks):
        add = own_rows(came_refs[i][:, both : 2 * both], m_ref, k)
        own = add if own is None else own + add
    put_rows(acc, own, None if first else before)
    if first:
        for s in range(CAP):
            add_sums(acc, pick(ask_ref, s), self_ref[:, s * width : (s + 1) * width])
    for i in range(len(ks)):
        for s in range(CAP):
            add_sums(acc, pick(ids_refs[i], s), came_refs[i][:, s * width : (s + 1) * width])
    if last:
        out_ref[...] = acc[...].astype(BF16)


def late_rows(head, ids, came, ks, operator, first, last):
    values = head[1] if first else head[0]
    return call(
        functools.partial(late_rows_kernel, ks, first, last),
        "late_rows",
        shape(values.shape, BF16 if last else F32),
        [vmem()] * (len(head) + 2 * len(ks) + 1),
        [pltpu.VMEM(values.shape, F32)] if last else [],
        flops=2 ** 27,
        moved=2 ** 20,
    )(*head, *[ids[k] for k in ks], *[came[k] for k in ks], operator)


def add_kernel(keep_ref, came_ref, out_ref):
    out_ref[...] = (keep_ref[...] + came_ref[...].astype(F32)).astype(BF16)


def add_up(keep, came):
    return call(add_kernel, "add_up", shape(came.shape, BF16), [vmem(), vmem()])(keep, came)


def widen_kernel(feats, in_ref, out_ref):
    blocks, columns, width = in_ref.shape
    share = out_ref.shape[1] // width
    first = lax.axis_index("rep") * share
    for f in range(feats):
        for b in range(share):
            out_ref[f * columns : (f + 1) * columns, b * width : (b + 1) * width] = in_ref[
                f * (blocks // feats) + first + b
            ]


def widen(parts, feats, reps):
    blocks, columns, width = parts.shape
    out = shape((feats * columns, blocks // feats // reps * width), BF16)
    return call(functools.partial(widen_kernel, feats), "widen", out, [vmem()])(parts)


def dense_kernel(feats, *refs):
    sums, wide_cot, refs = refs[:feats], refs[feats], refs[feats + 1 :]
    w_ref, act_ref, give_ref, spread_ref, term_ref, wide, pre_scr, grad = refs
    share, columns, width = act_ref.shape
    me = lax.axis_index("feat")
    rows = [pl.ds(pl.multiple_of(lax.rem(me + q, feats) * columns, columns), columns) for q in range(feats)]
    for q in range(feats):
        for b in range(share):
            wide[rows[q], b * width : (b + 1) * width] = sums[q][b]
    pre = dot(w_ref[...], wide[...], TN)
    pre_scr[...] = pre
    sig = jax.nn.sigmoid(pre)
    factor = wide_cot[...].astype(F32) * sig * (1.0 + pre * (1.0 - sig))
    grad[...] = factor.astype(BF16)
    spread = dot(w_ref[rows[0], :], grad[...]).astype(BF16)
    term_ref[...] = dot(grad[rows[0], :], wide[...], NT).astype(BF16)
    wide_share = share * width
    give_ref[:, :wide_share] = spread
    for b in range(share):
        spread_ref[b] = spread[:, b * width : (b + 1) * width]
    own = pre_scr[rows[0], :]
    act = (own * jax.nn.sigmoid(own)).astype(BF16)
    give_ref[:, wide_share:] = act
    for b in range(share):
        act_ref[b] = act[:, b * width : (b + 1) * width]


def dense(sums, cot, weight, feats):
    share, columns, width = sums[0].shape
    features = weight.shape[0]
    return call(
        functools.partial(dense_kernel, feats),
        "dense",
        [
            shape((share, columns, width), BF16),
            shape((columns, 2 * share * width), BF16),
            shape((share, columns, width), BF16),
            shape((columns, features), BF16),
        ],
        [vmem()] * (feats + 2),
        [
            pltpu.VMEM((features, share * width), BF16),
            pltpu.VMEM((features, share * width), F32),
            pltpu.VMEM((features, share * width), BF16),
        ],
        flops=2 ** 28,
        moved=2 ** 20,
    )(*sums, cot, weight)


def send_kernel(peers, *refs):
    ids_refs, refs = refs[: peers - 1], refs[peers - 1 :]
    mine_ref, came_ref, m_ref, refs = refs[0], refs[1], refs[2], refs[3:]
    x3, refs = refs[0], refs[1:]
    send_refs, refs = refs[: peers - 1], refs[peers - 1 :]
    self_ref, mir = refs
    share, _, width = mine_ref.shape
    both = CAP * width
    half = lax.axis_index("rep")
    x3[pl.ds(half * share, share)] = mine_ref[...]
    for b in range(share):
        x3[(1 - half) * share + b] = came_ref[:, b * width : (b + 1) * width]
    mirrored(lanes(x3), m_ref, mir, peers * CAP, width)
    self_ref[...] = mir[:, :both]
    for k in range(1, peers):
        out = send_refs[k - 1]
        out[:, :both] = mir[:, k * both : (k + 1) * both].astype(BF16)
        for s in range(CAP):
            at = (CAP + s) * width
            out[:, at : at + width] = x3[pick(ids_refs[k - 1], s)]


def sends_of(mine, came, operator, ids, peers, reps):
    share, columns, width = mine.shape
    chunk = 2 * CAP * width
    outs = call(
        functools.partial(send_kernel, peers),
        "sends",
        [shape((share * reps, columns, width), BF16)]
        + [shape((columns, chunk), BF16)] * (peers - 1)
        + [shape((columns, CAP * width), F32)],
        [vmem()] * (peers + 2),
        [pltpu.VMEM((columns, peers * CAP * width), F32)],
        flops=2 ** 28,
        moved=2 ** 21,
    )(*ids[1:], mine, came, operator)
    return outs[0], [None] + list(outs[1:peers]), outs[peers]


def pair_kernel(mine_ref, came_ref, out_ref):
    out_ref[...] = (mine_ref[...].astype(F32) + came_ref[...].astype(F32)).astype(out_ref.dtype)


def pair_sum(mine, came, dtype):
    return call(pair_kernel, "pair_sum", shape(mine.shape, dtype), [vmem(), vmem()])(mine, came)


def split_kernel(mine_ref, came_ref, act_ref, shared_ref, give_ref, keep_ref, out_ref, total):
    half = lax.axis_index("rep")
    blocks, _, width = act_ref.shape
    out_ref[pl.ds(half * blocks, blocks)] = act_ref[...]
    for b in range(blocks):
        at = (blocks + b) * width
        out_ref[(1 - half) * blocks + b] = shared_ref[:, at : at + width]
    part = keep_ref.shape[1]
    total[...] = mine_ref[...].astype(F32) + came_ref[...].astype(F32)
    give_ref[...] = total[:, pl.ds(pl.multiple_of((1 - half) * part, part), part)].astype(BF16)
    keep_ref[...] = total[:, pl.ds(pl.multiple_of(half * part, part), part)]


def split_sum(mine, came, act, shared, reps):
    columns, features = mine.shape
    part = (columns, features // reps)
    return call(
        split_kernel,
        "split_sum",
        [shape(part, BF16), shape(part, F32), shape((reps * act.shape[0],) + act.shape[1:], BF16)],
        [vmem()] * 4,
        [pltpu.VMEM(mine.shape, F32)],
    )(mine, came, act, shared)


def total_term(term, act, shared, peers, reps):
    bit = peers // 2
    give, total, activated = split_sum(term, across(term, peers, bit), act, shared, reps)
    total = pair_sum(total, ahead(give, "rep", reps, 1), F32 if bit == 1 else BF16)
    while bit > 1:
        bit //= 2
        total = pair_sum(total, across(total, peers, bit), F32 if bit == 1 else BF16)
    return total, activated


def finish_kernel(mine_ref, other_ref, share_ref, other_share_ref, grad_ref, weight_ref):
    half = lax.axis_index("rep")
    share = share_ref.shape[1]
    grad_ref[...] = (mine_ref[...].astype(F32) + other_ref[...].astype(F32)).astype(BF16)
    weight_ref[pl.ds(pl.multiple_of(half * share, share), share), :] = share_ref[...].T
    weight_ref[pl.ds(pl.multiple_of((1 - half) * share, share), share), :] = other_share_ref[...].T


def finish(mine, other, share, other_share):
    columns, width = share.shape
    return call(
        finish_kernel,
        "finish",
        [shape(mine.shape, BF16), shape((2 * width, columns), F32)],
        [vmem()] * 4,
    )(mine, other, share, other_share)


def ahead(value, axis, size, k):
    return lax.ppermute(value, axis, [(i, (i + k) % size) for i in range(size)])


def across(value, peers, k):
    return lax.ppermute(value, "graph", [(i, i ^ k) for i in range(peers)])


def after(value, first):
    return lax.optimization_barrier((value, first))[0]


def local(features, weight, cotangent, tiles, tile_row, tile_col, tile_count):
    blocks_dev, _, width = features.shape
    peers = lax.axis_size("graph")
    feats = lax.axis_size("feat")
    reps = lax.axis_size("rep")
    far_first = sorted(range(1, peers), key=lambda k: (-(k & (peers // 2)), k))

    half, table = prepare(features, tile_row, tile_col, tile_count, peers, reps)
    operator, asks = list_operator(tiles, table, peers, blocks_dev)
    sends, own_mirror = first_sends(features, operator, asks[1:], peers)
    cots = lax.all_gather(cotangent, "feat", axis=0, tiled=True)
    pieces, held = {0: [half]}, [0]
    bit = peers // 2
    while bit:
        for k in held:
            parts = pieces[k]
            if k:
                parts = after(halves(after(parts, sends[1])), pieces.get(1, half))
            pieces[k ^ bit] = [across(part, peers, bit) for part in parts]
        held = held + [k ^ bit for k in held]
        bit //= 2
    came = [None] * peers
    for k in far_first:
        came[k] = across(sends[k], peers, k)
    arrived = [part for k in range(1, peers) for part in pieces[k]]
    middle = peers // 2
    came[middle:], arrived, cots = lax.optimization_barrier((came[middle:], arrived, cots))
    came[1:middle], arrived = lax.optimization_barrier((came[1:middle], arrived))
    stacked = stack(arrived)
    swapped = ahead(stacked, "rep", reps, 1)
    acc, ids = first_rows(features, operator, asks[0], came, own_mirror, peers)
    give, asked = give_rows(acc, asks, stacked, swapped, operator, peers, reps)
    keep = keep_rows(acc, asked, operator, reps)

    mine = add_up(keep, ahead(give, "rep", reps, 1))
    cot = widen(cots, feats, reps)
    sums = [mine] + [ahead(mine, "feat", feats, feats - q) for q in range(1, feats)]
    act, give, spread, term = dense(sums, cot, weight, feats)
    shared = ahead(give, "rep", reps, 1)
    total, activated = total_term(term, act, shared, peers, reps)
    values, sends, own_mirror = sends_of(spread, shared, operator, ids, peers, reps)

    came = [None] * peers
    for k in far_first:
        came[k] = across(sends[k], peers, k)
    ordered, total = lax.optimization_barrier(([came[k] for k in far_first], total))
    came = [None] + [ordered[far_first.index(k)] for k in range(1, peers)]
    acc = late_rows([asks[0], values, own_mirror], ids, came, [], operator, True, False)
    part = late_rows([acc], ids, came, far_first, operator, False, True)
    input_grad, weight_grad = finish(
        part, ahead(part, "rep", reps, 1), total, ahead(total, "rep", reps, 1)
    )
    return (activated, input_grad, weight_grad)


def solution(mesh):
    placed = (
        P(("parts", "graph"), "feat", None),
        P(),
        P(("parts", "graph"), "feat", None),
        P(("parts", "graph", "rep"), None, None),
        P(("parts", "graph", "rep")),
        P(("parts", "graph", "rep")),
        P(("parts", "graph", "rep")),
    )
    return jax.shard_map(
        local,
        mesh=mesh,
        in_specs=placed,
        out_specs=(
            P(("parts", "graph"), "feat", None),
            P(("parts", "graph"), "feat", None),
            P("parts", "feat"),
        ),
        check_vma=False,
    )
```

```python
import functools

import jax
import jax.numpy as jnp
from jax import lax
from jax.experimental import pallas as pl
from jax.experimental.pallas import tpu as pltpu
from jax.sharding import PartitionSpec as P

CAP = 2
GROUP = 8
CHUNK = 16
SIDES = 2
PLACE_ROWS = 8
PLACE_BUFFER = 2 ** 22
TAIL = 16
VMEM_LIMIT = 40 * 2 ** 20
VMEM_MOST = 50 * 2 ** 20
VMEM_ALL = 58 * 2 ** 20

NT = (((1,), (1,)), ((), ()))
TN = (((0,), (0,)), ((), ()))
F32 = jnp.float32
BF16 = jnp.bfloat16


def vmem():
    return pl.BlockSpec(memory_space=pltpu.VMEM)


def smem():
    return pl.BlockSpec(memory_space=pltpu.SMEM)


def hbm():
    return pl.BlockSpec(memory_space=pltpu.HBM)


def shape(dims, dtype):
    return jax.ShapeDtypeStruct(tuple(dims), dtype)


def dot(a, b, dims=None):
    if dims is None:
        return jnp.dot(a, b, preferred_element_type=F32)
    return lax.dot_general(a, b, dims, preferred_element_type=F32)


def call(kernel, name, outs, in_specs, scratch=(), flops=0, moved=2 ** 18, limit=VMEM_LIMIT, **kwargs):
    return pl.pallas_call(
        kernel,
        out_shape=outs,
        in_specs=in_specs,
        scratch_shapes=list(scratch),
        compiler_params=pltpu.CompilerParams(vmem_limit_bytes=limit),
        cost_estimate=pl.CostEstimate(flops=flops, bytes_accessed=moved, transcendentals=0),
        name=name,
        **kwargs,
    )


def lanes(x3):
    return jnp.concatenate([x3[b] for b in range(x3.shape[0])], axis=1)


def places(peers, blocks_dev, count, row, col, table):
    me = lax.axis_index("graph")
    lane = lax.broadcasted_iota(jnp.int32, col.shape, 1)
    live = lane < count
    place = jnp.full(col.shape, peers * CAP * blocks_dev, jnp.int32)
    for k in range(peers):
        local = col - jnp.bitwise_xor(me, k) * blocks_dev
        inside = live & (local >= 0) & (local < blocks_dev)
        low = jnp.min(jnp.where(inside, local, blocks_dev - 1), axis=1, keepdims=True)
        high = jnp.max(jnp.where(inside, local, 0), axis=1, keepdims=True)
        table[PLACE_ROWS + k : PLACE_ROWS + k + 1, :] = jnp.where(lane == 0, low, high)
        slot = k * CAP + (local != low).astype(jnp.int32)
        place = jnp.where(inside, slot * blocks_dev + row, place)
    table[:PLACE_ROWS, :] = jnp.broadcast_to(place, (PLACE_ROWS, place.shape[1]))


def table_rows(peers):
    return PLACE_ROWS + -(-peers // 8) * 8


def prepare_kernel(peers, count_ref, row_ref, col_ref, x3, half_out, table_out, table, half_sem, sem):
    share = half_out.shape[0]
    mine = pl.ds(lax.axis_index("rep") * share, share)
    half_copy = pltpu.make_async_copy(x3.at[mine], half_out, half_sem)
    half_copy.start()
    count = jnp.broadcast_to(count_ref[...], (1, 1))
    if table.shape[0] > PLACE_ROWS + peers:
        table[...] = jnp.zeros(table.shape, jnp.int32)
    places(peers, x3.shape[0], count, row_ref[...], col_ref[...], table)
    copy = pltpu.make_async_copy(table, table_out.at[pl.ds(0, table.shape[0])], sem)
    copy.start()
    half_copy.wait()
    copy.wait()


def prepare(features, tile_row, tile_col, tile_count, peers, reps):
    per = tile_col.shape[0]
    blocks_dev, columns, width = features.shape
    return call(
        functools.partial(prepare_kernel, peers),
        "prepare",
        [shape((blocks_dev // reps, columns, width), BF16), shape((PLACE_BUFFER // (4 * per), per), jnp.int32)],
        [vmem()] * 4,
        [
            pltpu.VMEM((table_rows(peers), per), jnp.int32),
            pltpu.SemaphoreType.DMA,
            pltpu.SemaphoreType.DMA,
        ],
        limit=VMEM_ALL,
        out_specs=[hbm(), hbm()],
    )(tile_count, tile_row.reshape(1, per), tile_col.reshape(1, per), features)


def pick(ids_ref, lane):
    ids = ids_ref[...].astype(F32)
    at = lax.broadcasted_iota(jnp.int32, ids.shape, 1)
    return jnp.max(jnp.where(at == lane, ids, 0.0)).astype(jnp.int32)


def operator_kernel(blocks_dev, slots_here, groups, table_in, tiles_ref, m_ref, *refs):
    asks, (tiles, acc, place_ref, table, sems, sem, table_sem) = refs[:-7], refs[-7:]
    step = pl.program_id(0)
    per, width = tiles.shape[0], tiles.shape[1]
    chunks = per // CHUNK
    spare = slots_here * blocks_dev

    def chunk_copy(c):
        part = pl.ds(c * CHUNK, CHUNK)
        return pltpu.make_async_copy(tiles_ref.at[part], tiles.at[part], sems.at[c])

    def place_copy():
        return pltpu.make_async_copy(table_in.at[pl.ds(0, PLACE_ROWS)], place_ref, sem)

    def table_copy():
        return pltpu.make_async_copy(table_in.at[pl.ds(0, table.shape[0])], table, table_sem)

    @pl.when(step == 0)
    def _():
        place_copy().start()
        table_copy().start()
        for c in range(chunks):
            chunk_copy(c).start()

    acc[...] = jnp.zeros_like(acc)

    @pl.when(step == 0)
    def _():
        place_copy().wait()

    def add_chunk(c, carry):
        @pl.when(step == 0)
        def _():
            chunk_copy(c).wait()

        for u in range(CHUNK):
            t = c * CHUNK + u
            place = place_ref[0, t]
            if groups > 1:
                place = place - step * spare
                place = jnp.where((place >= 0) & (place < spare), place, spare)
            side = u % SIDES
            acc[side, place] = acc[side, place] + tiles[t].astype(F32)
        return carry

    lax.fori_loop(0, chunks, add_chunk, 0)
    for s in range(slots_here):
        for r in range(blocks_dev):
            total = acc[0, s * blocks_dev + r]
            for side in range(1, SIDES):
                total = total + acc[side, s * blocks_dev + r]
            m_ref[r * width : (r + 1) * width, s * width : (s + 1) * width] = total.astype(BF16)

    @pl.when(step == 0)
    def _():
        table_copy().wait()
        for k, ask_ref in enumerate(asks):
            ask_ref[...] = table[PLACE_ROWS + k : PLACE_ROWS + k + 1, :]


def list_operator(tiles, table, peers, blocks_dev):
    per, width = tiles.shape[0], tiles.shape[1]
    slots = peers * CAP
    slots_here = min(slots, GROUP)
    groups = slots // slots_here
    outs = call(
        functools.partial(operator_kernel, blocks_dev, slots_here, groups),
        "operator",
        [shape((blocks_dev * width, slots * width), BF16)] + [shape((1, per), jnp.int32)] * peers,
        [hbm(), hbm()],
        [
            pltpu.VMEM((per, width, width), BF16),
            pltpu.VMEM((SIDES, slots_here * blocks_dev + 1, width, width), F32),
            pltpu.SMEM((PLACE_ROWS, per), jnp.int32),
            pltpu.VMEM((table_rows(peers), per), jnp.int32),
            pltpu.SemaphoreType.DMA((per // CHUNK,)),
            pltpu.SemaphoreType.DMA,
            pltpu.SemaphoreType.DMA,
        ],
        moved=2 ** 24,
        limit=VMEM_MOST,
        grid=(groups,),
        out_specs=[pl.BlockSpec((blocks_dev * width, slots_here * width), lambda i: (0, i))] + [vmem()] * peers,
    )(table, tiles)
    return outs[0], list(outs[1:])


def mirrored(near, m_ref, mir, slots, width):
    if slots <= GROUP:
        mir[...] = dot(near, m_ref[...])
    else:
        part = GROUP * width

        @pl.loop(0, slots // GROUP)
        def _(i):
            where = pl.ds(pl.multiple_of(i * part, part), part)
            mir[:, where] = dot(near, m_ref[:, where])


def first_sends_kernel(peers, *refs):
    ask_refs, refs = refs[: peers - 1], refs[peers - 1 :]
    x3, cot, m_ref, refs = refs[0], refs[1], refs[2], refs[3:]
    send_refs, self_ref, cot_ref, mir = refs[: peers - 1], refs[peers - 1], refs[peers], refs[peers + 1]
    _, columns, width = x3.shape
    share = cot_ref.shape[0]
    cot_ref[...] = cot[pl.ds(lax.axis_index("rep") * share, share)]
    both = CAP * width
    mirrored(lanes(x3), m_ref, mir, peers * CAP, width)
    self_ref[...] = mir[:, :both]
    lane = lax.broadcasted_iota(jnp.int32, (TAIL, both), 1)
    for k in range(1, peers):
        out = send_refs[k - 1]
        out[:columns, :] = mir[:, k * both : (k + 1) * both].astype(BF16)
        low, high = ask_refs[k - 1][:, :1], ask_refs[k - 1][:, 1:2]
        out[columns:, :] = jnp.where(lane < width, low, high).astype(F32).astype(BF16)


def first_sends(values, cotangent, operator, asks, peers, reps):
    blocks_dev, columns, width = values.shape
    outs = call(
        functools.partial(first_sends_kernel, peers),
        "first_sends",
        [shape((columns + TAIL, CAP * width), BF16)] * (peers - 1)
        + [shape((columns, CAP * width), F32), shape((blocks_dev // reps, columns, width), BF16)],
        [vmem()] * (peers + 2),
        [pltpu.VMEM((columns, peers * CAP * width), F32)],
        flops=2 ** 28,
        moved=2 ** 21,
    )(*asks, values, cotangent, operator)
    return [None] + list(outs[: peers - 1]), outs[peers - 1], outs[peers]


def add_sums(acc, block, sums):
    acc[block] = acc[block] + sums.astype(F32)


def own_rows(far, m_ref, k):
    both = far.shape[1]
    return dot(far, m_ref[:, k * both : (k + 1) * both], NT)


def put_rows(acc, own, before=None):
    blocks_dev, _, width = acc.shape
    for b in range(blocks_dev):
        add = own[:, b * width : (b + 1) * width]
        acc[b] = add if before is None else before[b] + add


def self_rows(x3, m_ref, ask_ref):
    far = jnp.concatenate([x3[pick(ask_ref, s)] for s in range(CAP)], axis=1)
    return own_rows(far, m_ref, 0)


def far_of(block, mine_ref, other_ref, ask_ref, at=0):
    half = lax.axis_index("rep")
    share = block.shape[0] // 2
    block[pl.ds(half * share, share)] = mine_ref[at * share : (at + 1) * share]
    block[pl.ds((1 - half) * share, share)] = other_ref[at * share : (at + 1) * share]
    return jnp.concatenate([block[pick(ask_ref, s)] for s in range(CAP)], axis=1)


def first_rows_kernel(peers, *refs):
    ask_ref, refs = refs[0], refs[1:]
    came_refs, refs = refs[: peers - 1], refs[peers - 1 :]
    x3, m_ref, self_ref, acc, ids_refs = refs[0], refs[1], refs[2], refs[3], refs[4:]
    _, columns, width = x3.shape
    put_rows(acc, self_rows(x3, m_ref, ask_ref))
    for s in range(CAP):
        add_sums(acc, pick(ask_ref, s), self_ref[:, s * width : (s + 1) * width])
    lane = lax.broadcasted_iota(jnp.int32, ids_refs[0].shape, 1)
    for k in range(1, peers):
        came = came_refs[k - 1]
        ids = jnp.zeros(lane.shape, jnp.int32)
        for s in range(CAP):
            here = slice(s * width, (s + 1) * width)
            asked = jnp.max(came[columns : columns + TAIL, here].astype(F32)).astype(jnp.int32)
            ids = jnp.where(lane == s, asked, ids)
            add_sums(acc, asked, came[:columns, here])
        ids_refs[k - 1][...] = ids


def first_rows(values, operator, ask, came, own_mirror, peers):
    _, columns, width = values.shape
    outs = call(
        functools.partial(first_rows_kernel, peers),
        "first_rows",
        [shape(values.shape, F32)] + [shape((1, width), jnp.int32)] * (peers - 1),
        [vmem()] * (peers + 3),
        flops=2 ** 27,
        moved=2 ** 20,
    )(ask, *came[1:], values, operator, own_mirror)
    return outs[0], [None] + list(outs[1:])


def stack_kernel(*refs):
    at = 0
    for ref in refs[:-1]:
        share = ref.shape[0]
        refs[-1][at : at + share] = ref[...]
        at += share


def halves_kernel(in_ref, low_ref, high_ref):
    share = low_ref.shape[0]
    low_ref[...] = in_ref[:share]
    high_ref[...] = in_ref[share:]


def halves(parts):
    if len(parts) > 1:
        return parts
    share, columns, width = parts[0].shape
    part = shape((share // 2, columns, width), BF16)
    return list(call(halves_kernel, "halves", [part, part], [vmem()])(*parts))


def stack(pieces):
    _, columns, width = pieces[0].shape
    out = shape((sum(piece.shape[0] for piece in pieces), columns, width), BF16)
    return call(stack_kernel, "stack", out, [vmem()] * len(pieces))(*pieces)


def half_rows(before, far_ref, m_ref, first, share):
    columns, width = before.shape[1:]
    both = CAP * width
    rows = pl.ds(pl.multiple_of(first * width, share * width), share * width)
    if m_ref.shape[1] <= GROUP * width:
        own = dot(far_ref[:, both:], m_ref[rows, both:], NT)
    else:

        def add_peer(k, total):
            here = pl.ds(pl.multiple_of(k * both, both), both)
            return total + dot(far_ref[:, here], m_ref[rows, here], NT)

        zeros = jnp.zeros((columns, share * width), F32)
        own = lax.fori_loop(1, m_ref.shape[1] // both, add_peer, zeros)
    return [before[first + b] + own[:, b * width : (b + 1) * width] for b in range(share)]


def give_rows_kernel(peers, *refs):
    ask_refs, refs = refs[: peers - 1], refs[peers - 1 :]
    before, mine_ref, other_ref, m_ref, give_ref, far_ref, block = refs
    both = CAP * before.shape[2]
    for k in range(1, peers):
        far_ref[:, k * both : (k + 1) * both] = far_of(block, mine_ref, other_ref, ask_refs[k - 1], k - 1)
    far_ref[:, :both] = jnp.zeros((far_ref.shape[0], both), BF16)
    share = give_ref.shape[0]
    rows = half_rows(before, far_ref, m_ref, (1 - lax.axis_index("rep")) * share, share)
    for b in range(share):
        give_ref[b] = rows[b].astype(BF16)


def give_rows(before, asks, mine, other, operator, peers, reps):
    blocks_dev, columns, width = before.shape
    return call(
        functools.partial(give_rows_kernel, peers),
        "give_rows",
        [shape((blocks_dev // reps, columns, width), BF16), shape((columns, peers * CAP * width), BF16)],
        [vmem()] * (peers + 3),
        [pltpu.VMEM(before.shape, BF16)],
        flops=2 ** 27,
        moved=2 ** 20,
    )(*asks[1:], before, mine, other, operator)


def keep_rows_kernel(before, far_ref, m_ref, keep_ref):
    share = keep_ref.shape[0]
    rows = half_rows(before, far_ref, m_ref, lax.axis_index("rep") * share, share)
    for b in range(share):
        keep_ref[b] = rows[b]


def keep_rows(before, far, operator, reps):
    blocks_dev, columns, width = before.shape
    return call(
        keep_rows_kernel,
        "keep_rows",
        shape((blocks_dev // reps, columns, width), F32),
        [vmem()] * 3,
        flops=2 ** 27,
        moved=2 ** 20,
    )(before, far, operator)


def late_rows_kernel(ks, first, last, *refs):
    if first:
        ask_ref, x3, self_ref = refs[:3]
    else:
        before = refs[0]
    refs = refs[3 if first else 1 :]
    ids_refs, refs = refs[: len(ks)], refs[len(ks) :]
    came_refs, refs = refs[: len(ks)], refs[len(ks) :]
    m_ref, out_ref = refs[:2]
    acc = refs[2] if last else out_ref
    width = acc.shape[2]
    both = CAP * width
    own = self_rows(x3, m_ref, ask_ref) if first else None
    for i, k in enumerate(ks):
        add = own_rows(came_refs[i][:, both : 2 * both], m_ref, k)
        own = add if own is None else own + add
    put_rows(acc, own, None if first else before)
    if first:
        for s in range(CAP):
            add_sums(acc, pick(ask_ref, s), self_ref[:, s * width : (s + 1) * width])
    for i in range(len(ks)):
        for s in range(CAP):
            add_sums(acc, pick(ids_refs[i], s), came_refs[i][:, s * width : (s + 1) * width])
    if last:
        out_ref[...] = acc[...].astype(BF16)


def late_rows(head, ids, came, ks, operator, first, last):
    values = head[1] if first else head[0]
    return call(
        functools.partial(late_rows_kernel, ks, first, last),
        "late_rows",
        shape(values.shape, BF16 if last else F32),
        [vmem()] * (len(head) + 2 * len(ks) + 1),
        [pltpu.VMEM(values.shape, F32)] if last else [],
        flops=2 ** 27,
        moved=2 ** 20,
    )(*head, *[ids[k] for k in ks], *[came[k] for k in ks], operator)


def add_kernel(keep_ref, came_ref, out_ref):
    out_ref[...] = (keep_ref[...] + came_ref[...].astype(F32)).astype(BF16)


def add_up(keep, came):
    return call(add_kernel, "add_up", shape(came.shape, BF16), [vmem(), vmem()])(keep, came)


def widen_kernel(feats, in_ref, out_ref):
    _, columns, width = in_ref.shape
    share = out_ref.shape[1] // width
    for f in range(feats):
        for b in range(share):
            out_ref[f * columns : (f + 1) * columns, b * width : (b + 1) * width] = in_ref[f * share + b]


def widen(parts, feats):
    blocks, columns, width = parts.shape
    out = shape((feats * columns, blocks // feats * width), BF16)
    return call(functools.partial(widen_kernel, feats), "widen", out, [vmem()])(parts)


def dense_kernel(feats, *refs):
    sums, wide_cot, refs = refs[:feats], refs[feats], refs[feats + 1 :]
    w_ref, act_ref, give_ref, spread_ref, term_ref, wide, pre_scr, grad = refs
    share, columns, width = act_ref.shape
    me = lax.axis_index("feat")
    rows = [pl.ds(pl.multiple_of(lax.rem(me + q, feats) * columns, columns), columns) for q in range(feats)]
    for q in range(feats):
        for b in range(share):
            wide[rows[q], b * width : (b + 1) * width] = sums[q][b]
    pre = dot(w_ref[...], wide[...], TN)
    pre_scr[...] = pre
    sig = jax.nn.sigmoid(pre)
    factor = wide_cot[...].astype(F32) * sig * (1.0 + pre * (1.0 - sig))
    grad[...] = factor.astype(BF16)
    spread = dot(w_ref[rows[0], :], grad[...]).astype(BF16)
    term_ref[...] = dot(grad[rows[0], :], wide[...], NT).astype(BF16)
    wide_share = share * width
    give_ref[:, :wide_share] = spread
    for b in range(share):
        spread_ref[b] = spread[:, b * width : (b + 1) * width]
    own = pre_scr[rows[0], :]
    act = (own * jax.nn.sigmoid(own)).astype(BF16)
    give_ref[:, wide_share:] = act
    for b in range(share):
        act_ref[b] = act[:, b * width : (b + 1) * width]


def dense(sums, cot, weight, feats):
    share, columns, width = sums[0].shape
    features = weight.shape[0]
    return call(
        functools.partial(dense_kernel, feats),
        "dense",
        [
            shape((share, columns, width), BF16),
            shape((columns, 2 * share * width), BF16),
            shape((share, columns, width), BF16),
            shape((columns, features), BF16),
        ],
        [vmem()] * (feats + 2),
        [
            pltpu.VMEM((features, share * width), BF16),
            pltpu.VMEM((features, share * width), F32),
            pltpu.VMEM((features, share * width), BF16),
        ],
        flops=2 ** 28,
        moved=2 ** 20,
    )(*sums, cot, weight)


def send_kernel(peers, *refs):
    ids_refs, refs = refs[: peers - 1], refs[peers - 1 :]
    mine_ref, came_ref, m_ref, refs = refs[0], refs[1], refs[2], refs[3:]
    x3, refs = refs[0], refs[1:]
    send_refs, refs = refs[: peers - 1], refs[peers - 1 :]
    self_ref, mir = refs
    share, _, width = mine_ref.shape
    both = CAP * width
    half = lax.axis_index("rep")
    x3[pl.ds(half * share, share)] = mine_ref[...]
    for b in range(share):
        x3[(1 - half) * share + b] = came_ref[:, b * width : (b + 1) * width]
    mirrored(lanes(x3), m_ref, mir, peers * CAP, width)
    self_ref[...] = mir[:, :both]
    for k in range(1, peers):
        out = send_refs[k - 1]
        out[:, :both] = mir[:, k * both : (k + 1) * both].astype(BF16)
        for s in range(CAP):
            at = (CAP + s) * width
            out[:, at : at + width] = x3[pick(ids_refs[k - 1], s)]


def sends_of(mine, came, operator, ids, peers, reps):
    share, columns, width = mine.shape
    chunk = 2 * CAP * width
    outs = call(
        functools.partial(send_kernel, peers),
        "sends",
        [shape((share * reps, columns, width), BF16)]
        + [shape((columns, chunk), BF16)] * (peers - 1)
        + [shape((columns, CAP * width), F32)],
        [vmem()] * (peers + 2),
        [pltpu.VMEM((columns, peers * CAP * width), F32)],
        flops=2 ** 28,
        moved=2 ** 21,
    )(*ids[1:], mine, came, operator)
    return outs[0], [None] + list(outs[1:peers]), outs[peers]


def pair_kernel(mine_ref, came_ref, out_ref):
    out_ref[...] = (mine_ref[...].astype(F32) + came_ref[...].astype(F32)).astype(out_ref.dtype)


def pair_sum(mine, came, dtype):
    return call(pair_kernel, "pair_sum", shape(mine.shape, dtype), [vmem(), vmem()])(mine, came)


def split_kernel(mine_ref, came_ref, act_ref, shared_ref, give_ref, keep_ref, out_ref, total):
    half = lax.axis_index("rep")
    blocks, _, width = act_ref.shape
    out_ref[pl.ds(half * blocks, blocks)] = act_ref[...]
    for b in range(blocks):
        at = (blocks + b) * width
        out_ref[(1 - half) * blocks + b] = shared_ref[:, at : at + width]
    part = keep_ref.shape[1]
    total[...] = mine_ref[...].astype(F32) + came_ref[...].astype(F32)
    give_ref[...] = total[:, pl.ds(pl.multiple_of((1 - half) * part, part), part)].astype(BF16)
    keep_ref[...] = total[:, pl.ds(pl.multiple_of(half * part, part), part)]


def split_sum(mine, came, act, shared, reps):
    columns, features = mine.shape
    part = (columns, features // reps)
    return call(
        split_kernel,
        "split_sum",
        [shape(part, BF16), shape(part, F32), shape((reps * act.shape[0],) + act.shape[1:], BF16)],
        [vmem()] * 4,
        [pltpu.VMEM(mine.shape, F32)],
    )(mine, came, act, shared)


def total_term(term, act, shared, peers, reps):
    give, total, activated = split_sum(term, across(term, peers, 1), act, shared, reps)
    total = pair_sum(total, ahead(give, "rep", reps, 1), F32 if peers == 2 else BF16)
    bit = 2
    while bit < peers:
        total = pair_sum(total, across(total, peers, bit), F32 if 2 * bit == peers else BF16)
        bit *= 2
    return total, activated


def finish_kernel(mine_ref, other_ref, share_ref, other_share_ref, grad_ref, weight_ref):
    half = lax.axis_index("rep")
    share = share_ref.shape[1]
    grad_ref[...] = (mine_ref[...].astype(F32) + other_ref[...].astype(F32)).astype(BF16)
    weight_ref[pl.ds(pl.multiple_of(half * share, share), share), :] = share_ref[...].T
    weight_ref[pl.ds(pl.multiple_of((1 - half) * share, share), share), :] = other_share_ref[...].T


def finish(mine, other, share, other_share):
    columns, width = share.shape
    return call(
        finish_kernel,
        "finish",
        [shape(mine.shape, BF16), shape((2 * width, columns), F32)],
        [vmem()] * 4,
    )(mine, other, share, other_share)


def ahead(value, axis, size, k):
    return lax.ppermute(value, axis, [(i, (i + k) % size) for i in range(size)])


def across(value, peers, k):
    return lax.ppermute(value, "graph", [(i, i ^ k) for i in range(peers)])


def after(value, first):
    return lax.optimization_barrier((value, first))[0]


def local(features, weight, cotangent, tiles, tile_row, tile_col, tile_count):
    blocks_dev, _, width = features.shape
    peers = lax.axis_size("graph")
    feats = lax.axis_size("feat")
    reps = lax.axis_size("rep")
    far_first = sorted(range(1, peers), key=lambda k: (-(k & (peers // 2)), k))

    half, table = prepare(features, tile_row, tile_col, tile_count, peers, reps)
    operator, asks = list_operator(tiles, table, peers, blocks_dev)
    sends, own_mirror, own_cot = first_sends(features, cotangent, operator, asks[1:], peers, reps)
    cots = lax.all_gather(own_cot, "feat", axis=0, tiled=True)
    pieces, held = {0: [half]}, [0]
    bit = peers // 2
    while bit:
        for k in held:
            parts = pieces[k]
            if k:
                parts = after(halves(after(parts, sends[1])), pieces.get(1, half))
            pieces[k ^ bit] = [across(part, peers, bit) for part in parts]
        held = held + [k ^ bit for k in held]
        bit //= 2
    came = [None] * peers
    for k in far_first:
        came[k] = across(sends[k], peers, k)
    arrived = [part for k in range(1, peers) for part in pieces[k]]
    middle = peers // 2
    came[middle:], arrived, cots = lax.optimization_barrier((came[middle:], arrived, cots))
    came[1:middle], arrived = lax.optimization_barrier((came[1:middle], arrived))
    stacked = stack(arrived)
    swapped = ahead(stacked, "rep", reps, 1)
    acc, ids = first_rows(features, operator, asks[0], came, own_mirror, peers)
    give, asked = give_rows(acc, asks, stacked, swapped, operator, peers, reps)
    keep = keep_rows(acc, asked, operator, reps)

    mine = add_up(keep, ahead(give, "rep", reps, 1))
    cot = widen(cots, feats)
    sums = [mine] + [ahead(mine, "feat", feats, feats - q) for q in range(1, feats)]
    act, give, spread, term = dense(sums, cot, weight, feats)
    shared = ahead(give, "rep", reps, 1)
    total, activated = total_term(term, act, shared, peers, reps)
    values, sends, own_mirror = sends_of(spread, shared, operator, ids, peers, reps)

    came = [None] * peers
    for k in far_first:
        came[k] = across(sends[k], peers, k)
    ordered, total = lax.optimization_barrier(([came[k] for k in far_first], total))
    came = [None] + [ordered[far_first.index(k)] for k in range(1, peers)]
    acc = late_rows([asks[0], values, own_mirror], ids, came, [], operator, True, False)
    part = late_rows([acc], ids, came, far_first, operator, False, True)
    input_grad, weight_grad = finish(
        part, ahead(part, "rep", reps, 1), total, ahead(total, "rep", reps, 1)
    )
    return (activated, input_grad, weight_grad)


def solution(mesh):
    placed = (
        P(("parts", "graph"), "feat", None),
        P(),
        P(("parts", "graph"), "feat", None),
        P(("parts", "graph", "rep"), None, None),
        P(("parts", "graph", "rep")),
        P(("parts", "graph", "rep")),
        P(("parts", "graph", "rep")),
    )
    return jax.shard_map(
        local,
        mesh=mesh,
        in_specs=placed,
        out_specs=(
            P(("parts", "graph"), "feat", None),
            P(("parts", "graph"), "feat", None),
            P("parts", "feat"),
        ),
        check_vma=False,
    )
```

```python
import functools

import jax
import jax.numpy as jnp
from jax import lax
from jax.experimental import pallas as pl
from jax.experimental.pallas import tpu as pltpu
from jax.sharding import PartitionSpec as P

CAP = 2
GROUP = 8
CHUNK = 16
SIDES = 2
PLACE_ROWS = 8
PLACE_BUFFER = 2 ** 22
TAIL = 16
VMEM_LIMIT = 40 * 2 ** 20
VMEM_MOST = 50 * 2 ** 20
VMEM_ALL = 58 * 2 ** 20

NT = (((1,), (1,)), ((), ()))
TN = (((0,), (0,)), ((), ()))
F32 = jnp.float32
BF16 = jnp.bfloat16


def vmem():
    return pl.BlockSpec(memory_space=pltpu.VMEM)


def smem():
    return pl.BlockSpec(memory_space=pltpu.SMEM)


def hbm():
    return pl.BlockSpec(memory_space=pltpu.HBM)


def shape(dims, dtype):
    return jax.ShapeDtypeStruct(tuple(dims), dtype)


def dot(a, b, dims=None):
    if dims is None:
        return jnp.dot(a, b, preferred_element_type=F32)
    return lax.dot_general(a, b, dims, preferred_element_type=F32)


def call(kernel, name, outs, in_specs, scratch=(), flops=0, moved=2 ** 18, limit=VMEM_LIMIT, **kwargs):
    return pl.pallas_call(
        kernel,
        out_shape=outs,
        in_specs=in_specs,
        scratch_shapes=list(scratch),
        compiler_params=pltpu.CompilerParams(vmem_limit_bytes=limit),
        cost_estimate=pl.CostEstimate(flops=flops, bytes_accessed=moved, transcendentals=0),
        name=name,
        **kwargs,
    )


def lanes(x3):
    return jnp.concatenate([x3[b] for b in range(x3.shape[0])], axis=1)


def places(peers, blocks_dev, count, row, col, table):
    me = lax.axis_index("graph")
    lane = lax.broadcasted_iota(jnp.int32, col.shape, 1)
    live = lane < count
    place = jnp.full(col.shape, peers * CAP * blocks_dev, jnp.int32)
    for k in range(peers):
        local = col - jnp.bitwise_xor(me, k) * blocks_dev
        inside = live & (local >= 0) & (local < blocks_dev)
        low = jnp.min(jnp.where(inside, local, blocks_dev - 1), axis=1, keepdims=True)
        high = jnp.max(jnp.where(inside, local, 0), axis=1, keepdims=True)
        table[PLACE_ROWS + k : PLACE_ROWS + k + 1, :] = jnp.where(lane == 0, low, high)
        slot = k * CAP + (local != low).astype(jnp.int32)
        place = jnp.where(inside, slot * blocks_dev + row, place)
    table[:PLACE_ROWS, :] = jnp.broadcast_to(place, (PLACE_ROWS, place.shape[1]))


def table_rows(peers):
    return PLACE_ROWS + -(-peers // 8) * 8


def prepare_kernel(peers, count_ref, row_ref, col_ref, x3, half_out, table_out, table, half_sem, sem):
    share = half_out.shape[0]
    mine = pl.ds(lax.axis_index("rep") * share, share)
    half_copy = pltpu.make_async_copy(x3.at[mine], half_out, half_sem)
    half_copy.start()
    count = jnp.broadcast_to(count_ref[...], (1, 1))
    if table.shape[0] > PLACE_ROWS + peers:
        table[...] = jnp.zeros(table.shape, jnp.int32)
    places(peers, x3.shape[0], count, row_ref[...], col_ref[...], table)
    copy = pltpu.make_async_copy(table, table_out.at[pl.ds(0, table.shape[0])], sem)
    copy.start()
    half_copy.wait()
    copy.wait()


def prepare(features, tile_row, tile_col, tile_count, peers, reps):
    per = tile_col.shape[0]
    blocks_dev, columns, width = features.shape
    return call(
        functools.partial(prepare_kernel, peers),
        "prepare",
        [shape((blocks_dev // reps, columns, width), BF16), shape((PLACE_BUFFER // (4 * per), per), jnp.int32)],
        [vmem()] * 4,
        [
            pltpu.VMEM((table_rows(peers), per), jnp.int32),
            pltpu.SemaphoreType.DMA,
            pltpu.SemaphoreType.DMA,
        ],
        limit=VMEM_ALL,
        out_specs=[hbm(), hbm()],
    )(tile_count, tile_row.reshape(1, per), tile_col.reshape(1, per), features)


def pick(ids_ref, lane):
    ids = ids_ref[...].astype(F32)
    at = lax.broadcasted_iota(jnp.int32, ids.shape, 1)
    return jnp.max(jnp.where(at == lane, ids, 0.0)).astype(jnp.int32)


def operator_kernel(blocks_dev, slots_here, groups, table_in, tiles_ref, m_ref, *refs):
    asks, (tiles, acc, place_ref, table, sems, sem, table_sem) = refs[:-7], refs[-7:]
    step = pl.program_id(0)
    per, width = tiles.shape[0], tiles.shape[1]
    chunks = per // CHUNK
    spare = slots_here * blocks_dev

    def chunk_copy(c):
        part = pl.ds(c * CHUNK, CHUNK)
        return pltpu.make_async_copy(tiles_ref.at[part], tiles.at[part], sems.at[c])

    def place_copy():
        return pltpu.make_async_copy(table_in.at[pl.ds(0, PLACE_ROWS)], place_ref, sem)

    def table_copy():
        return pltpu.make_async_copy(table_in.at[pl.ds(0, table.shape[0])], table, table_sem)

    @pl.when(step == 0)
    def _():
        place_copy().start()
        table_copy().start()
        for c in range(chunks):
            chunk_copy(c).start()

    acc[...] = jnp.zeros_like(acc)

    @pl.when(step == 0)
    def _():
        place_copy().wait()

    def add_chunk(c, carry):
        @pl.when(step == 0)
        def _():
            chunk_copy(c).wait()

        for u in range(CHUNK):
            t = c * CHUNK + u
            place = place_ref[0, t]
            if groups > 1:
                place = place - step * spare
                place = jnp.where((place >= 0) & (place < spare), place, spare)
            side = u % SIDES
            acc[side, place] = acc[side, place] + tiles[t].astype(F32)
        return carry

    lax.fori_loop(0, chunks, add_chunk, 0)
    for s in range(slots_here):
        for r in range(blocks_dev):
            total = acc[0, s * blocks_dev + r]
            for side in range(1, SIDES):
                total = total + acc[side, s * blocks_dev + r]
            m_ref[r * width : (r + 1) * width, s * width : (s + 1) * width] = total.astype(BF16)

    @pl.when(step == 0)
    def _():
        table_copy().wait()
        for k, ask_ref in enumerate(asks):
            ask_ref[...] = table[PLACE_ROWS + k : PLACE_ROWS + k + 1, :]


def list_operator(tiles, table, peers, blocks_dev):
    per, width = tiles.shape[0], tiles.shape[1]
    slots = peers * CAP
    slots_here = min(slots, GROUP)
    groups = slots // slots_here
    outs = call(
        functools.partial(operator_kernel, blocks_dev, slots_here, groups),
        "operator",
        [shape((blocks_dev * width, slots * width), BF16)] + [shape((1, per), jnp.int32)] * peers,
        [hbm(), hbm()],
        [
            pltpu.VMEM((per, width, width), BF16),
            pltpu.VMEM((SIDES, slots_here * blocks_dev + 1, width, width), F32),
            pltpu.SMEM((PLACE_ROWS, per), jnp.int32),
            pltpu.VMEM((table_rows(peers), per), jnp.int32),
            pltpu.SemaphoreType.DMA((per // CHUNK,)),
            pltpu.SemaphoreType.DMA,
            pltpu.SemaphoreType.DMA,
        ],
        moved=2 ** 24,
        limit=VMEM_MOST,
        grid=(groups,),
        out_specs=[pl.BlockSpec((blocks_dev * width, slots_here * width), lambda i: (0, i))] + [vmem()] * peers,
    )(table, tiles)
    return outs[0], list(outs[1:])


def mirrored(near, m_ref, mir, slots, width):
    if slots <= GROUP:
        mir[...] = dot(near, m_ref[...])
    else:
        part = GROUP * width

        @pl.loop(0, slots // GROUP)
        def _(i):
            where = pl.ds(pl.multiple_of(i * part, part), part)
            mir[:, where] = dot(near, m_ref[:, where])


def first_sends_kernel(peers, *refs):
    ask_refs, refs = refs[: peers - 1], refs[peers - 1 :]
    x3, cot, m_ref, refs = refs[0], refs[1], refs[2], refs[3:]
    send_refs, self_ref, cot_refs, mir = refs[: peers - 1], refs[peers - 1], refs[peers : peers + 2], refs[peers + 2]
    _, columns, width = x3.shape
    first = lax.axis_index("rep") * (x3.shape[0] // 2)
    for cot_ref in cot_refs:
        part = cot_ref.shape[0]
        cot_ref[...] = cot[pl.ds(first, part)]
        first = first + part
    both = CAP * width
    mirrored(lanes(x3), m_ref, mir, peers * CAP, width)
    self_ref[...] = mir[:, :both]
    lane = lax.broadcasted_iota(jnp.int32, (TAIL, both), 1)
    for k in range(1, peers):
        out = send_refs[k - 1]
        out[:columns, :] = mir[:, k * both : (k + 1) * both].astype(BF16)
        low, high = ask_refs[k - 1][:, :1], ask_refs[k - 1][:, 1:2]
        out[columns:, :] = jnp.where(lane < width, low, high).astype(F32).astype(BF16)


def first_sends(values, cotangent, operator, asks, peers, reps):
    blocks_dev, columns, width = values.shape
    outs = call(
        functools.partial(first_sends_kernel, peers),
        "first_sends",
        [shape((columns + TAIL, CAP * width), BF16)] * (peers - 1)
        + [shape((columns, CAP * width), F32)]
        + [shape((blocks_dev // reps // 2, columns, width), BF16)] * 2,
        [vmem()] * (peers + 2),
        [pltpu.VMEM((columns, peers * CAP * width), F32)],
        flops=2 ** 28,
        moved=2 ** 21,
    )(*asks, values, cotangent, operator)
    return [None] + list(outs[: peers - 1]), outs[peers - 1], outs[peers], outs[peers + 1]


def add_sums(acc, block, sums):
    acc[block] = acc[block] + sums.astype(F32)


def own_rows(far, m_ref, k):
    both = far.shape[1]
    return dot(far, m_ref[:, k * both : (k + 1) * both], NT)


def put_rows(acc, own, before=None):
    blocks_dev, _, width = acc.shape
    for b in range(blocks_dev):
        add = own[:, b * width : (b + 1) * width]
        acc[b] = add if before is None else before[b] + add


def self_rows(x3, m_ref, ask_ref):
    far = jnp.concatenate([x3[pick(ask_ref, s)] for s in range(CAP)], axis=1)
    return own_rows(far, m_ref, 0)


def far_of(block, mine_ref, other_ref, ask_ref, at=0):
    half = lax.axis_index("rep")
    share = block.shape[0] // 2
    block[pl.ds(half * share, share)] = mine_ref[at * share : (at + 1) * share]
    block[pl.ds((1 - half) * share, share)] = other_ref[at * share : (at + 1) * share]
    return jnp.concatenate([block[pick(ask_ref, s)] for s in range(CAP)], axis=1)


def first_rows_kernel(peers, *refs):
    ask_ref, refs = refs[0], refs[1:]
    came_refs, refs = refs[: peers - 1], refs[peers - 1 :]
    x3, m_ref, self_ref, acc, ids_refs = refs[0], refs[1], refs[2], refs[3], refs[4:]
    _, columns, width = x3.shape
    put_rows(acc, self_rows(x3, m_ref, ask_ref))
    for s in range(CAP):
        add_sums(acc, pick(ask_ref, s), self_ref[:, s * width : (s + 1) * width])
    lane = lax.broadcasted_iota(jnp.int32, ids_refs[0].shape, 1)
    for k in range(1, peers):
        came = came_refs[k - 1]
        ids = jnp.zeros(lane.shape, jnp.int32)
        for s in range(CAP):
            here = slice(s * width, (s + 1) * width)
            asked = jnp.max(came[columns : columns + TAIL, here].astype(F32)).astype(jnp.int32)
            ids = jnp.where(lane == s, asked, ids)
            add_sums(acc, asked, came[:columns, here])
        ids_refs[k - 1][...] = ids


def first_rows(values, operator, ask, came, own_mirror, peers):
    _, columns, width = values.shape
    outs = call(
        functools.partial(first_rows_kernel, peers),
        "first_rows",
        [shape(values.shape, F32)] + [shape((1, width), jnp.int32)] * (peers - 1),
        [vmem()] * (peers + 3),
        flops=2 ** 27,
        moved=2 ** 20,
    )(ask, *came[1:], values, operator, own_mirror)
    return outs[0], [None] + list(outs[1:])


def stack_kernel(*refs):
    at = 0
    for ref in refs[:-1]:
        share = ref.shape[0]
        refs[-1][at : at + share] = ref[...]
        at += share


def halves_kernel(in_ref, low_ref, high_ref):
    share = low_ref.shape[0]
    low_ref[...] = in_ref[:share]
    high_ref[...] = in_ref[share:]


def halves(parts):
    if len(parts) > 1:
        return parts
    share, columns, width = parts[0].shape
    part = shape((share // 2, columns, width), BF16)
    return list(call(halves_kernel, "halves", [part, part], [vmem()])(*parts))


def stack(pieces):
    _, columns, width = pieces[0].shape
    out = shape((sum(piece.shape[0] for piece in pieces), columns, width), BF16)
    return call(stack_kernel, "stack", out, [vmem()] * len(pieces))(*pieces)


def half_rows(before, far_ref, m_ref, first, share):
    columns, width = before.shape[1:]
    both = CAP * width
    rows = pl.ds(pl.multiple_of(first * width, share * width), share * width)
    if m_ref.shape[1] <= GROUP * width:
        own = dot(far_ref[:, both:], m_ref[rows, both:], NT)
    else:

        def add_peer(k, total):
            here = pl.ds(pl.multiple_of(k * both, both), both)
            return total + dot(far_ref[:, here], m_ref[rows, here], NT)

        zeros = jnp.zeros((columns, share * width), F32)
        own = lax.fori_loop(1, m_ref.shape[1] // both, add_peer, zeros)
    return [before[first + b] + own[:, b * width : (b + 1) * width] for b in range(share)]


def give_rows_kernel(peers, *refs):
    ask_refs, refs = refs[: peers - 1], refs[peers - 1 :]
    before, mine_ref, other_ref, m_ref, give_ref, far_ref, block = refs
    both = CAP * before.shape[2]
    for k in range(1, peers):
        far_ref[:, k * both : (k + 1) * both] = far_of(block, mine_ref, other_ref, ask_refs[k - 1], k - 1)
    far_ref[:, :both] = jnp.zeros((far_ref.shape[0], both), BF16)
    share = give_ref.shape[0]
    rows = half_rows(before, far_ref, m_ref, (1 - lax.axis_index("rep")) * share, share)
    for b in range(share):
        give_ref[b] = rows[b].astype(BF16)


def give_rows(before, asks, mine, other, operator, peers, reps):
    blocks_dev, columns, width = before.shape
    return call(
        functools.partial(give_rows_kernel, peers),
        "give_rows",
        [shape((blocks_dev // reps, columns, width), BF16), shape((columns, peers * CAP * width), BF16)],
        [vmem()] * (peers + 3),
        [pltpu.VMEM(before.shape, BF16)],
        flops=2 ** 27,
        moved=2 ** 20,
    )(*asks[1:], before, mine, other, operator)


def keep_rows_kernel(before, far_ref, m_ref, keep_ref):
    share = keep_ref.shape[0]
    rows = half_rows(before, far_ref, m_ref, lax.axis_index("rep") * share, share)
    for b in range(share):
        keep_ref[b] = rows[b]


def keep_rows(before, far, operator, reps):
    blocks_dev, columns, width = before.shape
    return call(
        keep_rows_kernel,
        "keep_rows",
        shape((blocks_dev // reps, columns, width), F32),
        [vmem()] * 3,
        flops=2 ** 27,
        moved=2 ** 20,
    )(before, far, operator)


def late_rows_kernel(ks, first, last, *refs):
    if first:
        ask_ref, x3, self_ref = refs[:3]
    else:
        before = refs[0]
    refs = refs[3 if first else 1 :]
    ids_refs, refs = refs[: len(ks)], refs[len(ks) :]
    came_refs, refs = refs[: len(ks)], refs[len(ks) :]
    m_ref, out_ref = refs[:2]
    acc = refs[2] if last else out_ref
    width = acc.shape[2]
    both = CAP * width
    own = self_rows(x3, m_ref, ask_ref) if first else None
    for i, k in enumerate(ks):
        add = own_rows(came_refs[i][:, both : 2 * both], m_ref, k)
        own = add if own is None else own + add
    put_rows(acc, own, None if first else before)
    if first:
        for s in range(CAP):
            add_sums(acc, pick(ask_ref, s), self_ref[:, s * width : (s + 1) * width])
    for i in range(len(ks)):
        for s in range(CAP):
            add_sums(acc, pick(ids_refs[i], s), came_refs[i][:, s * width : (s + 1) * width])
    if last:
        out_ref[...] = acc[...].astype(BF16)


def late_rows(head, ids, came, ks, operator, first, last):
    values = head[1] if first else head[0]
    return call(
        functools.partial(late_rows_kernel, ks, first, last),
        "late_rows",
        shape(values.shape, BF16 if last else F32),
        [vmem()] * (len(head) + 2 * len(ks) + 1),
        [pltpu.VMEM(values.shape, F32)] if last else [],
        flops=2 ** 27,
        moved=2 ** 20,
    )(*head, *[ids[k] for k in ks], *[came[k] for k in ks], operator)


def add_kernel(keep_ref, came_ref, out_ref):
    out_ref[...] = (keep_ref[...] + came_ref[...].astype(F32)).astype(BF16)


def add_up(keep, came):
    return call(add_kernel, "add_up", shape(came.shape, BF16), [vmem(), vmem()])(keep, came)


def widen_kernel(feats, gathered, *refs):
    parts, out_ref = refs[:feats], refs[feats]
    share, columns, width = parts[0].shape
    me = lax.axis_index("feat")
    for f in range(feats):
        rows = pl.ds(pl.multiple_of(lax.rem(me + f, feats) * columns, columns), columns)
        for b in range(share):
            out_ref[f * columns : (f + 1) * columns, b * width : (b + 1) * width] = gathered[f * share + b]
            out_ref[rows, (share + b) * width : (share + b + 1) * width] = parts[f][b]


def widen(gathered, parts):
    share, columns, width = parts[0].shape
    feats = len(parts)
    out = shape((feats * columns, 2 * share * width), BF16)
    return call(functools.partial(widen_kernel, feats), "widen", out, [vmem()] * (feats + 1))(gathered, *parts)


def dense_kernel(feats, sums, wide_cot, *refs):
    w_ref, act_ref, give_ref, spread_ref, term_ref, wide, pre_scr, grad = refs
    share, columns, width = act_ref.shape
    me = lax.axis_index("feat")
    mine = pl.ds(pl.multiple_of(me * columns, columns), columns)
    for f in range(feats):
        for b in range(share):
            wide[f * columns : (f + 1) * columns, b * width : (b + 1) * width] = sums[f * share + b]
    pre = dot(w_ref[...], wide[...], TN)
    pre_scr[...] = pre
    sig = jax.nn.sigmoid(pre)
    factor = wide_cot[...].astype(F32) * sig * (1.0 + pre * (1.0 - sig))
    grad[...] = factor.astype(BF16)
    spread = dot(w_ref[mine, :], grad[...]).astype(BF16)
    term_ref[...] = dot(grad[mine, :], wide[...], NT).astype(BF16)
    wide_share = share * width
    give_ref[:, :wide_share] = spread
    for b in range(share):
        spread_ref[b] = spread[:, b * width : (b + 1) * width]
    own = pre_scr[mine, :]
    act = (own * jax.nn.sigmoid(own)).astype(BF16)
    give_ref[:, wide_share:] = act
    for b in range(share):
        act_ref[b] = act[:, b * width : (b + 1) * width]


def dense(sums, cot, weight, feats):
    blocks, columns, width = sums.shape
    share = blocks // feats
    features = weight.shape[0]
    return call(
        functools.partial(dense_kernel, feats),
        "dense",
        [
            shape((share, columns, width), BF16),
            shape((columns, 2 * share * width), BF16),
            shape((share, columns, width), BF16),
            shape((columns, features), BF16),
        ],
        [vmem()] * 3,
        [
            pltpu.VMEM((features, share * width), BF16),
            pltpu.VMEM((features, share * width), F32),
            pltpu.VMEM((features, share * width), BF16),
        ],
        flops=2 ** 28,
        moved=2 ** 20,
    )(sums, cot, weight)


def send_kernel(peers, *refs):
    ids_refs, refs = refs[: peers - 1], refs[peers - 1 :]
    mine_ref, came_ref, m_ref, refs = refs[0], refs[1], refs[2], refs[3:]
    x3, refs = refs[0], refs[1:]
    send_refs, refs = refs[: peers - 1], refs[peers - 1 :]
    self_ref, mir = refs
    share, _, width = mine_ref.shape
    both = CAP * width
    half = lax.axis_index("rep")
    x3[pl.ds(half * share, share)] = mine_ref[...]
    for b in range(share):
        x3[(1 - half) * share + b] = came_ref[:, b * width : (b + 1) * width]
    mirrored(lanes(x3), m_ref, mir, peers * CAP, width)
    self_ref[...] = mir[:, :both]
    for k in range(1, peers):
        out = send_refs[k - 1]
        out[:, :both] = mir[:, k * both : (k + 1) * both].astype(BF16)
        for s in range(CAP):
            at = (CAP + s) * width
            out[:, at : at + width] = x3[pick(ids_refs[k - 1], s)]


def sends_of(mine, came, operator, ids, peers, reps):
    share, columns, width = mine.shape
    chunk = 2 * CAP * width
    outs = call(
        functools.partial(send_kernel, peers),
        "sends",
        [shape((share * reps, columns, width), BF16)]
        + [shape((columns, chunk), BF16)] * (peers - 1)
        + [shape((columns, CAP * width), F32)],
        [vmem()] * (peers + 2),
        [pltpu.VMEM((columns, peers * CAP * width), F32)],
        flops=2 ** 28,
        moved=2 ** 21,
    )(*ids[1:], mine, came, operator)
    return outs[0], [None] + list(outs[1:peers]), outs[peers]


def pair_kernel(mine_ref, came_ref, out_ref):
    out_ref[...] = (mine_ref[...].astype(F32) + came_ref[...].astype(F32)).astype(out_ref.dtype)


def pair_sum(mine, came, dtype):
    return call(pair_kernel, "pair_sum", shape(mine.shape, dtype), [vmem(), vmem()])(mine, came)


def split_kernel(mine_ref, came_ref, act_ref, shared_ref, give_ref, keep_ref, out_ref, total):
    half = lax.axis_index("rep")
    blocks, _, width = act_ref.shape
    out_ref[pl.ds(half * blocks, blocks)] = act_ref[...]
    for b in range(blocks):
        at = (blocks + b) * width
        out_ref[(1 - half) * blocks + b] = shared_ref[:, at : at + width]
    part = keep_ref.shape[1]
    total[...] = mine_ref[...].astype(F32) + came_ref[...].astype(F32)
    give_ref[...] = total[:, pl.ds(pl.multiple_of((1 - half) * part, part), part)].astype(BF16)
    keep_ref[...] = total[:, pl.ds(pl.multiple_of(half * part, part), part)]


def split_sum(mine, came, act, shared, reps):
    columns, features = mine.shape
    part = (columns, features // reps)
    return call(
        split_kernel,
        "split_sum",
        [shape(part, BF16), shape(part, F32), shape((reps * act.shape[0],) + act.shape[1:], BF16)],
        [vmem()] * 4,
        [pltpu.VMEM(mine.shape, F32)],
    )(mine, came, act, shared)


def total_term(term, act, shared, peers, reps):
    give, total, activated = split_sum(term, across(term, peers, 1), act, shared, reps)
    total = pair_sum(total, ahead(give, "rep", reps, 1), F32 if peers == 2 else BF16)
    bit = 2
    while bit < peers:
        total = pair_sum(total, across(total, peers, bit), F32 if 2 * bit == peers else BF16)
        bit *= 2
    return total, activated


def finish_kernel(mine_ref, other_ref, share_ref, other_share_ref, grad_ref, weight_ref):
    half = lax.axis_index("rep")
    share = share_ref.shape[1]
    grad_ref[...] = (mine_ref[...].astype(F32) + other_ref[...].astype(F32)).astype(BF16)
    weight_ref[pl.ds(pl.multiple_of(half * share, share), share), :] = share_ref[...].T
    weight_ref[pl.ds(pl.multiple_of((1 - half) * share, share), share), :] = other_share_ref[...].T


def finish(mine, other, share, other_share):
    columns, width = share.shape
    return call(
        finish_kernel,
        "finish",
        [shape(mine.shape, BF16), shape((2 * width, columns), F32)],
        [vmem()] * 4,
    )(mine, other, share, other_share)


def ahead(value, axis, size, k):
    return lax.ppermute(value, axis, [(i, (i + k) % size) for i in range(size)])


def across(value, peers, k):
    return lax.ppermute(value, "graph", [(i, i ^ k) for i in range(peers)])


def after(value, first):
    return lax.optimization_barrier((value, first))[0]


def local(features, weight, cotangent, tiles, tile_row, tile_col, tile_count):
    blocks_dev, _, width = features.shape
    peers = lax.axis_size("graph")
    feats = lax.axis_size("feat")
    reps = lax.axis_size("rep")
    far_first = sorted(range(1, peers), key=lambda k: (-(k & (peers // 2)), k))

    half, table = prepare(features, tile_row, tile_col, tile_count, peers, reps)
    operator, asks = list_operator(tiles, table, peers, blocks_dev)
    sends, own_mirror, cot_a, cot_b = first_sends(features, cotangent, operator, asks[1:], peers, reps)
    cots = lax.all_gather(cot_a, "feat", axis=0, tiled=True)
    pieces, held = {0: [half]}, [0]
    bit = peers // 2
    while bit:
        for k in held:
            parts = pieces[k]
            if k:
                parts = after(halves(after(parts, sends[1])), pieces.get(1, half))
            pieces[k ^ bit] = [across(part, peers, bit) for part in parts]
        held = held + [k ^ bit for k in held]
        bit //= 2
    came = [None] * peers
    for k in far_first:
        came[k] = across(sends[k], peers, k)
    arrived = [part for k in range(1, peers) for part in pieces[k]]
    middle = peers // 2
    came[middle:], arrived, cots = lax.optimization_barrier((came[middle:], arrived, cots))
    came[1:middle], arrived = lax.optimization_barrier((came[1:middle], arrived))
    stacked = stack(arrived)
    swapped = ahead(stacked, "rep", reps, 1)
    acc, ids = first_rows(features, operator, asks[0], came, own_mirror, peers)
    give, asked = give_rows(acc, asks, stacked, swapped, operator, peers, reps)
    keep = keep_rows(acc, asked, operator, reps)

    mine = add_up(keep, ahead(give, "rep", reps, 1))
    waited = after(cot_b, stacked)
    cot = widen(cots, [cot_b] + [ahead(waited, "feat", feats, feats - q) for q in range(1, feats)])
    sums = lax.all_gather(mine, "feat", axis=0, tiled=True)
    act, give, spread, term = dense(sums, cot, weight, feats)
    shared = ahead(give, "rep", reps, 1)
    total, activated = total_term(term, act, shared, peers, reps)
    values, sends, own_mirror = sends_of(spread, shared, operator, ids, peers, reps)

    came = [None] * peers
    for k in far_first:
        came[k] = across(sends[k], peers, k)
    ordered, total = lax.optimization_barrier(([came[k] for k in far_first], total))
    came = [None] + [ordered[far_first.index(k)] for k in range(1, peers)]
    acc = late_rows([asks[0], values, own_mirror], ids, came, [], operator, True, False)
    part = late_rows([acc], ids, came, far_first, operator, False, True)
    input_grad, weight_grad = finish(
        part, ahead(part, "rep", reps, 1), total, ahead(total, "rep", reps, 1)
    )
    return (activated, input_grad, weight_grad)


def solution(mesh):
    placed = (
        P(("parts", "graph"), "feat", None),
        P(),
        P(("parts", "graph"), "feat", None),
        P(("parts", "graph", "rep"), None, None),
        P(("parts", "graph", "rep")),
        P(("parts", "graph", "rep")),
        P(("parts", "graph", "rep")),
    )
    return jax.shard_map(
        local,
        mesh=mesh,
        in_specs=placed,
        out_specs=(
            P(("parts", "graph"), "feat", None),
            P(("parts", "graph"), "feat", None),
            P("parts", "feat"),
        ),
        check_vma=False,
    )
```

```python
import functools

import jax
import jax.numpy as jnp
from jax import lax
from jax.experimental import pallas as pl
from jax.experimental.pallas import tpu as pltpu
from jax.sharding import PartitionSpec as P

CAP = 2
GROUP = 8
CHUNK = 16
SIDES = 1
PLACE_ROWS = 8
PLACE_BUFFER = 2 ** 22
TAIL = 16
VMEM_LIMIT = 40 * 2 ** 20
VMEM_MOST = 50 * 2 ** 20
VMEM_ALL = 58 * 2 ** 20

NT = (((1,), (1,)), ((), ()))
TN = (((0,), (0,)), ((), ()))
F32 = jnp.float32
BF16 = jnp.bfloat16


def vmem():
    return pl.BlockSpec(memory_space=pltpu.VMEM)


def smem():
    return pl.BlockSpec(memory_space=pltpu.SMEM)


def hbm():
    return pl.BlockSpec(memory_space=pltpu.HBM)


def shape(dims, dtype):
    return jax.ShapeDtypeStruct(tuple(dims), dtype)


def dot(a, b, dims=None):
    if dims is None:
        return jnp.dot(a, b, preferred_element_type=F32)
    return lax.dot_general(a, b, dims, preferred_element_type=F32)


def call(kernel, name, outs, in_specs, scratch=(), flops=0, moved=2 ** 18, limit=VMEM_LIMIT, **kwargs):
    return pl.pallas_call(
        kernel,
        out_shape=outs,
        in_specs=in_specs,
        scratch_shapes=list(scratch),
        compiler_params=pltpu.CompilerParams(vmem_limit_bytes=limit),
        cost_estimate=pl.CostEstimate(flops=flops, bytes_accessed=moved, transcendentals=0),
        name=name,
        **kwargs,
    )


def lanes(x3):
    return jnp.concatenate([x3[b] for b in range(x3.shape[0])], axis=1)


def places(peers, blocks_dev, row, col, table):
    me = lax.axis_index("graph")
    lane = lax.broadcasted_iota(jnp.int32, col.shape, 1)
    place = jnp.zeros(col.shape, jnp.int32)
    for k in range(peers):
        local = col - jnp.bitwise_xor(me, k) * blocks_dev
        inside = (local >= 0) & (local < blocks_dev)
        low = jnp.min(jnp.where(inside, local, blocks_dev - 1), axis=1, keepdims=True)
        high = jnp.max(jnp.where(inside, local, 0), axis=1, keepdims=True)
        table[PLACE_ROWS + k : PLACE_ROWS + k + 1, :] = jnp.where(lane == 0, low, high)
        slot = k * CAP + (local != low).astype(jnp.int32)
        place = jnp.where(inside, slot * blocks_dev + row, place)
    table[:PLACE_ROWS, :] = jnp.broadcast_to(place, (PLACE_ROWS, place.shape[1]))


def table_rows(peers):
    return PLACE_ROWS + -(-peers // 8) * 8


def prepare_kernel(peers, row_ref, col_ref, x3, half_out, table_out, table, half_sem, sem):
    share = half_out.shape[0]
    mine = pl.ds(lax.axis_index("rep") * share, share)
    half_copy = pltpu.make_async_copy(x3.at[mine], half_out, half_sem)
    half_copy.start()
    if table.shape[0] > PLACE_ROWS + peers:
        table[...] = jnp.zeros(table.shape, jnp.int32)
    places(peers, x3.shape[0], row_ref[...], col_ref[...], table)
    copy = pltpu.make_async_copy(table, table_out.at[pl.ds(0, table.shape[0])], sem)
    copy.start()
    half_copy.wait()
    copy.wait()


def prepare(features, tile_row, tile_col, peers, reps):
    per = tile_col.shape[0]
    blocks_dev, columns, width = features.shape
    return call(
        functools.partial(prepare_kernel, peers),
        "prepare",
        [shape((blocks_dev // reps, columns, width), BF16), shape((PLACE_BUFFER // (4 * per), per), jnp.int32)],
        [vmem()] * 3,
        [
            pltpu.VMEM((table_rows(peers), per), jnp.int32),
            pltpu.SemaphoreType.DMA,
            pltpu.SemaphoreType.DMA,
        ],
        limit=VMEM_ALL,
        out_specs=[hbm(), hbm()],
    )(tile_row.reshape(1, per), tile_col.reshape(1, per), features)


def pick(ids_ref, lane):
    ids = ids_ref[...].astype(F32)
    at = lax.broadcasted_iota(jnp.int32, ids.shape, 1)
    return jnp.max(jnp.where(at == lane, ids, 0.0)).astype(jnp.int32)


def operator_kernel(blocks_dev, slots_here, groups, count_ref, table_in, tiles_ref, m_ref, *refs):
    asks, (tiles, acc, place_ref, table, sems, sem, table_sem) = refs[:-7], refs[-7:]
    step = pl.program_id(0)
    per, width = tiles.shape[0], tiles.shape[1]
    chunks = per // CHUNK
    spare = slots_here * blocks_dev

    def chunk_copy(c):
        part = pl.ds(c * CHUNK, CHUNK)
        return pltpu.make_async_copy(tiles_ref.at[part], tiles.at[part], sems.at[c])

    def place_copy():
        return pltpu.make_async_copy(table_in.at[pl.ds(0, PLACE_ROWS)], place_ref, sem)

    def table_copy():
        return pltpu.make_async_copy(table_in.at[pl.ds(0, table.shape[0])], table, table_sem)

    @pl.when(step == 0)
    def _():
        place_copy().start()
        table_copy().start()
        for c in range(chunks):
            chunk_copy(c).start()

    acc[...] = jnp.zeros_like(acc)

    @pl.when(step == 0)
    def _():
        place_copy().wait()

    count = count_ref[0]

    def add_chunk(c, carry):
        @pl.when(step == 0)
        def _():
            chunk_copy(c).wait()

        for u in range(CHUNK):
            t = c * CHUNK + u
            place = place_ref[0, t]
            here = t < count
            if groups > 1:
                place = place - step * spare
                here = here & (place >= 0) & (place < spare)
            place = jnp.where(here, place, spare)
            side = u % SIDES
            acc[side, place] = acc[side, place] + tiles[t].astype(F32)
        return carry

    lax.fori_loop(0, chunks, add_chunk, 0)
    for s in range(slots_here):
        for r in range(blocks_dev):
            total = acc[0, s * blocks_dev + r]
            for side in range(1, SIDES):
                total = total + acc[side, s * blocks_dev + r]
            m_ref[r * width : (r + 1) * width, s * width : (s + 1) * width] = total.astype(BF16)

    @pl.when(step == 0)
    def _():
        table_copy().wait()
        for k, ask_ref in enumerate(asks):
            ask_ref[...] = table[PLACE_ROWS + k : PLACE_ROWS + k + 1, :]


def list_operator(tiles, table, tile_count, peers, blocks_dev):
    per, width = tiles.shape[0], tiles.shape[1]
    slots = peers * CAP
    slots_here = min(slots, GROUP)
    groups = slots // slots_here
    outs = call(
        functools.partial(operator_kernel, blocks_dev, slots_here, groups),
        "operator",
        [shape((blocks_dev * width, slots * width), BF16)] + [shape((1, per), jnp.int32)] * peers,
        [smem(), hbm(), hbm()],
        [
            pltpu.VMEM((per, width, width), BF16),
            pltpu.VMEM((SIDES, slots_here * blocks_dev + 1, width, width), F32),
            pltpu.SMEM((PLACE_ROWS, per), jnp.int32),
            pltpu.VMEM((table_rows(peers), per), jnp.int32),
            pltpu.SemaphoreType.DMA((per // CHUNK,)),
            pltpu.SemaphoreType.DMA,
            pltpu.SemaphoreType.DMA,
        ],
        moved=2 ** 24,
        limit=VMEM_MOST,
        grid=(groups,),
        out_specs=[pl.BlockSpec((blocks_dev * width, slots_here * width), lambda i: (0, i))] + [vmem()] * peers,
    )(tile_count, table, tiles)
    return outs[0], list(outs[1:])


def mirrored(near, m_ref, mir, slots, width):
    if slots <= GROUP:
        mir[...] = dot(near, m_ref[...])
    else:
        part = GROUP * width

        @pl.loop(0, slots // GROUP)
        def _(i):
            where = pl.ds(pl.multiple_of(i * part, part), part)
            mir[:, where] = dot(near, m_ref[:, where])


def first_sends_kernel(peers, *refs):
    ask_refs, refs = refs[: peers - 1], refs[peers - 1 :]
    x3, cot, m_ref, refs = refs[0], refs[1], refs[2], refs[3:]
    send_refs, self_ref, cot_ref, mir = refs[: peers - 1], refs[peers - 1], refs[peers], refs[peers + 1]
    _, columns, width = x3.shape
    share = cot_ref.shape[0]
    cot_ref[...] = cot[pl.ds(lax.axis_index("rep") * share, share)]
    both = CAP * width
    mirrored(lanes(x3), m_ref, mir, peers * CAP, width)
    self_ref[...] = mir[:, :both]
    lane = lax.broadcasted_iota(jnp.int32, (TAIL, both), 1)
    for k in range(1, peers):
        out = send_refs[k - 1]
        out[:columns, :] = mir[:, k * both : (k + 1) * both].astype(BF16)
        low, high = ask_refs[k - 1][:, :1], ask_refs[k - 1][:, 1:2]
        out[columns:, :] = jnp.where(lane < width, low, high).astype(F32).astype(BF16)


def first_sends(values, cotangent, operator, asks, peers, reps):
    blocks_dev, columns, width = values.shape
    outs = call(
        functools.partial(first_sends_kernel, peers),
        "first_sends",
        [shape((columns + TAIL, CAP * width), BF16)] * (peers - 1)
        + [shape((columns, CAP * width), F32), shape((blocks_dev // reps, columns, width), BF16)],
        [vmem()] * (peers + 2),
        [pltpu.VMEM((columns, peers * CAP * width), F32)],
        flops=2 ** 28,
        moved=2 ** 21,
    )(*asks, values, cotangent, operator)
    return [None] + list(outs[: peers - 1]), outs[peers - 1], outs[peers]


def add_sums(acc, block, sums):
    acc[block] = acc[block] + sums.astype(F32)


def own_rows(far, m_ref, k):
    both = far.shape[1]
    return dot(far, m_ref[:, k * both : (k + 1) * both], NT)


def put_rows(acc, own, before=None):
    blocks_dev, _, width = acc.shape
    for b in range(blocks_dev):
        add = own[:, b * width : (b + 1) * width]
        acc[b] = add if before is None else before[b] + add


def self_rows(x3, m_ref, ask_ref):
    far = jnp.concatenate([x3[pick(ask_ref, s)] for s in range(CAP)], axis=1)
    return own_rows(far, m_ref, 0)


def far_of(share, mine_ref, other_ref, ask_ref, at):
    first = lax.axis_index("rep") * share
    blocks = []
    for s in range(CAP):
        local = pick(ask_ref, s) - first
        own = (local >= 0) & (local < share)
        here = at * share + jnp.where(own, local, 0)
        there = at * share + jnp.where(own, 0, jnp.where(local < 0, local + share, local - share))
        blocks.append(jnp.where(own, mine_ref[here], other_ref[there]))
    return jnp.concatenate(blocks, axis=1)


def first_rows_kernel(peers, *refs):
    ask_ref, refs = refs[0], refs[1:]
    came_refs, refs = refs[: peers - 1], refs[peers - 1 :]
    x3, m_ref, self_ref, acc, ids_refs = refs[0], refs[1], refs[2], refs[3], refs[4:]
    _, columns, width = x3.shape
    put_rows(acc, self_rows(x3, m_ref, ask_ref))
    for s in range(CAP):
        add_sums(acc, pick(ask_ref, s), self_ref[:, s * width : (s + 1) * width])
    lane = lax.broadcasted_iota(jnp.int32, ids_refs[0].shape, 1)
    for k in range(1, peers):
        came = came_refs[k - 1]
        ids = jnp.zeros(lane.shape, jnp.int32)
        for s in range(CAP):
            here = slice(s * width, (s + 1) * width)
            asked = jnp.max(came[columns : columns + TAIL, here].astype(F32)).astype(jnp.int32)
            ids = jnp.where(lane == s, asked, ids)
            add_sums(acc, asked, came[:columns, here])
        ids_refs[k - 1][...] = ids


def first_rows(values, operator, ask, came, own_mirror, peers):
    _, columns, width = values.shape
    outs = call(
        functools.partial(first_rows_kernel, peers),
        "first_rows",
        [shape(values.shape, F32)] + [shape((1, width), jnp.int32)] * (peers - 1),
        [vmem()] * (peers + 3),
        flops=2 ** 27,
        moved=2 ** 20,
    )(ask, *came[1:], values, operator, own_mirror)
    return outs[0], [None] + list(outs[1:])


def stack_kernel(*refs):
    at = 0
    for ref in refs[:-1]:
        share = ref.shape[0]
        refs[-1][at : at + share] = ref[...]
        at += share


def halves_kernel(in_ref, low_ref, high_ref):
    share = low_ref.shape[0]
    low_ref[...] = in_ref[:share]
    high_ref[...] = in_ref[share:]


def halves(parts):
    if len(parts) > 1:
        return parts
    share, columns, width = parts[0].shape
    part = shape((share // 2, columns, width), BF16)
    return list(call(halves_kernel, "halves", [part, part], [vmem()])(*parts))


def stack(pieces):
    _, columns, width = pieces[0].shape
    out = shape((sum(piece.shape[0] for piece in pieces), columns, width), BF16)
    return call(stack_kernel, "stack", out, [vmem()] * len(pieces))(*pieces)


def half_rows(before, far_ref, m_ref, first, share):
    columns, width = before.shape[1:]
    both = CAP * width
    rows = pl.ds(pl.multiple_of(first * width, share * width), share * width)
    if m_ref.shape[1] <= GROUP * width:
        own = dot(far_ref[:, both:], m_ref[rows, both:], NT)
    else:

        def add_peer(k, total):
            here = pl.ds(pl.multiple_of(k * both, both), both)
            return total + dot(far_ref[:, here], m_ref[rows, here], NT)

        zeros = jnp.zeros((columns, share * width), F32)
        own = lax.fori_loop(1, m_ref.shape[1] // both, add_peer, zeros)
    return [before[first + b] + own[:, b * width : (b + 1) * width] for b in range(share)]


def give_rows_kernel(peers, *refs):
    ask_refs, refs = refs[: peers - 1], refs[peers - 1 :]
    before, mine_ref, other_ref, m_ref, give_ref, far_ref = refs
    share = give_ref.shape[0]
    both = CAP * before.shape[2]
    for k in range(1, peers):
        far_ref[:, k * both : (k + 1) * both] = far_of(share, mine_ref, other_ref, ask_refs[k - 1], k - 1)
    far_ref[:, :both] = jnp.zeros((far_ref.shape[0], both), BF16)
    rows = half_rows(before, far_ref, m_ref, (1 - lax.axis_index("rep")) * share, share)
    for b in range(share):
        give_ref[b] = rows[b].astype(BF16)


def give_rows(before, asks, mine, other, operator, peers, reps):
    blocks_dev, columns, width = before.shape
    return call(
        functools.partial(give_rows_kernel, peers),
        "give_rows",
        [shape((blocks_dev // reps, columns, width), BF16), shape((columns, peers * CAP * width), BF16)],
        [vmem()] * (peers + 3),
        flops=2 ** 27,
        moved=2 ** 20,
    )(*asks[1:], before, mine, other, operator)


def keep_rows_kernel(before, far_ref, m_ref, keep_ref):
    share = keep_ref.shape[0]
    rows = half_rows(before, far_ref, m_ref, lax.axis_index("rep") * share, share)
    for b in range(share):
        keep_ref[b] = rows[b]


def keep_rows(before, far, operator, reps):
    blocks_dev, columns, width = before.shape
    return call(
        keep_rows_kernel,
        "keep_rows",
        shape((blocks_dev // reps, columns, width), F32),
        [vmem()] * 3,
        flops=2 ** 27,
        moved=2 ** 20,
    )(before, far, operator)


def late_rows_kernel(ks, first, last, *refs):
    if first:
        ask_ref, x3, self_ref = refs[:3]
    else:
        before = refs[0]
    refs = refs[3 if first else 1 :]
    ids_refs, refs = refs[: len(ks)], refs[len(ks) :]
    came_refs, refs = refs[: len(ks)], refs[len(ks) :]
    m_ref, out_ref = refs[:2]
    acc = refs[2] if last else out_ref
    width = acc.shape[2]
    both = CAP * width
    own = self_rows(x3, m_ref, ask_ref) if first else None
    for i, k in enumerate(ks):
        add = own_rows(came_refs[i][:, both : 2 * both], m_ref, k)
        own = add if own is None else own + add
    put_rows(acc, own, None if first else before)
    if first:
        for s in range(CAP):
            add_sums(acc, pick(ask_ref, s), self_ref[:, s * width : (s + 1) * width])
    for i in range(len(ks)):
        for s in range(CAP):
            add_sums(acc, pick(ids_refs[i], s), came_refs[i][:, s * width : (s + 1) * width])
    if last:
        out_ref[...] = acc[...].astype(BF16)


def late_rows(head, ids, came, ks, operator, first, last):
    values = head[1] if first else head[0]
    return call(
        functools.partial(late_rows_kernel, ks, first, last),
        "late_rows",
        shape(values.shape, BF16 if last else F32),
        [vmem()] * (len(head) + 2 * len(ks) + 1),
        [pltpu.VMEM(values.shape, F32)] if last else [],
        flops=2 ** 27,
        moved=2 ** 20,
    )(*head, *[ids[k] for k in ks], *[came[k] for k in ks], operator)


def add_kernel(keep_ref, came_ref, out_ref):
    out_ref[...] = (keep_ref[...] + came_ref[...].astype(F32)).astype(BF16)


def add_up(keep, came):
    return call(add_kernel, "add_up", shape(came.shape, BF16), [vmem(), vmem()])(keep, came)


def widen_kernel(feats, in_ref, out_ref):
    _, columns, width = in_ref.shape
    share = out_ref.shape[1] // width
    for f in range(feats):
        for b in range(share):
            out_ref[f * columns : (f + 1) * columns, b * width : (b + 1) * width] = in_ref[f * share + b]


def widen(parts, feats):
    blocks, columns, width = parts.shape
    out = shape((feats * columns, blocks // feats * width), BF16)
    return call(functools.partial(widen_kernel, feats), "widen", out, [vmem()])(parts)


def dense_kernel(feats, *refs):
    sums, wide_cot, refs = refs[:feats], refs[feats], refs[feats + 1 :]
    w_ref, act_ref, give_ref, spread_ref, term_ref, wide, pre_scr, grad = refs
    share, columns, width = act_ref.shape
    me = lax.axis_index("feat")
    rows = [pl.ds(pl.multiple_of(lax.rem(me + q, feats) * columns, columns), columns) for q in range(feats)]
    for q in range(feats):
        for b in range(share):
            wide[rows[q], b * width : (b + 1) * width] = sums[q][b]
    pre = dot(w_ref[...], wide[...], TN)
    pre_scr[...] = pre
    sig = jax.nn.sigmoid(pre)
    factor = wide_cot[...].astype(F32) * sig * (1.0 + pre * (1.0 - sig))
    grad[...] = factor.astype(BF16)
    spread = dot(w_ref[rows[0], :], grad[...]).astype(BF16)
    term_ref[...] = dot(grad[rows[0], :], wide[...], NT).astype(BF16)
    wide_share = share * width
    give_ref[:, :wide_share] = spread
    for b in range(share):
        spread_ref[b] = spread[:, b * width : (b + 1) * width]
    own = pre_scr[rows[0], :]
    act = (own * jax.nn.sigmoid(own)).astype(BF16)
    give_ref[:, wide_share:] = act
    for b in range(share):
        act_ref[b] = act[:, b * width : (b + 1) * width]


def dense(sums, cot, weight, feats):
    share, columns, width = sums[0].shape
    features = weight.shape[0]
    return call(
        functools.partial(dense_kernel, feats),
        "dense",
        [
            shape((share, columns, width), BF16),
            shape((columns, 2 * share * width), BF16),
            shape((share, columns, width), BF16),
            shape((columns, features), BF16),
        ],
        [vmem()] * (feats + 2),
        [
            pltpu.VMEM((features, share * width), BF16),
            pltpu.VMEM((features, share * width), F32),
            pltpu.VMEM((features, share * width), BF16),
        ],
        flops=2 ** 28,
        moved=2 ** 20,
    )(*sums, cot, weight)


def send_kernel(peers, *refs):
    ids_refs, refs = refs[: peers - 1], refs[peers - 1 :]
    mine_ref, came_ref, m_ref, refs = refs[0], refs[1], refs[2], refs[3:]
    x3, refs = refs[0], refs[1:]
    send_refs, refs = refs[: peers - 1], refs[peers - 1 :]
    self_ref, mir = refs
    share, _, width = mine_ref.shape
    both = CAP * width
    half = lax.axis_index("rep")
    x3[pl.ds(half * share, share)] = mine_ref[...]
    for b in range(share):
        x3[(1 - half) * share + b] = came_ref[:, b * width : (b + 1) * width]
    mirrored(lanes(x3), m_ref, mir, peers * CAP, width)
    self_ref[...] = mir[:, :both]
    for k in range(1, peers):
        out = send_refs[k - 1]
        out[:, :both] = mir[:, k * both : (k + 1) * both].astype(BF16)
        for s in range(CAP):
            at = (CAP + s) * width
            out[:, at : at + width] = x3[pick(ids_refs[k - 1], s)]


def sends_of(mine, came, operator, ids, peers, reps):
    share, columns, width = mine.shape
    chunk = 2 * CAP * width
    outs = call(
        functools.partial(send_kernel, peers),
        "sends",
        [shape((share * reps, columns, width), BF16)]
        + [shape((columns, chunk), BF16)] * (peers - 1)
        + [shape((columns, CAP * width), F32)],
        [vmem()] * (peers + 2),
        [pltpu.VMEM((columns, peers * CAP * width), F32)],
        flops=2 ** 28,
        moved=2 ** 21,
    )(*ids[1:], mine, came, operator)
    return outs[0], [None] + list(outs[1:peers]), outs[peers]


def pair_kernel(mine_ref, came_ref, out_ref):
    out_ref[...] = (mine_ref[...].astype(F32) + came_ref[...].astype(F32)).astype(out_ref.dtype)


def pair_sum(mine, came, dtype):
    return call(pair_kernel, "pair_sum", shape(mine.shape, dtype), [vmem(), vmem()])(mine, came)


def split_kernel(mine_ref, came_ref, act_ref, shared_ref, give_ref, keep_ref, out_ref, total):
    half = lax.axis_index("rep")
    blocks, _, width = act_ref.shape
    out_ref[pl.ds(half * blocks, blocks)] = act_ref[...]
    for b in range(blocks):
        at = (blocks + b) * width
        out_ref[(1 - half) * blocks + b] = shared_ref[:, at : at + width]
    part = keep_ref.shape[1]
    total[...] = mine_ref[...].astype(F32) + came_ref[...].astype(F32)
    give_ref[...] = total[:, pl.ds(pl.multiple_of((1 - half) * part, part), part)].astype(BF16)
    keep_ref[...] = total[:, pl.ds(pl.multiple_of(half * part, part), part)]


def split_sum(mine, came, act, shared, reps):
    columns, features = mine.shape
    part = (columns, features // reps)
    return call(
        split_kernel,
        "split_sum",
        [shape(part, BF16), shape(part, F32), shape((reps * act.shape[0],) + act.shape[1:], BF16)],
        [vmem()] * 4,
        [pltpu.VMEM(mine.shape, F32)],
    )(mine, came, act, shared)


def total_term(term, act, shared, peers, reps):
    give, total, activated = split_sum(term, across(term, peers, 1), act, shared, reps)
    total = pair_sum(total, ahead(give, "rep", reps, 1), F32 if peers == 2 else BF16)
    bit = 2
    while bit < peers:
        total = pair_sum(total, across(total, peers, bit), F32 if 2 * bit == peers else BF16)
        bit *= 2
    return total, activated


def finish_kernel(mine_ref, other_ref, share_ref, other_share_ref, grad_ref, weight_ref):
    half = lax.axis_index("rep")
    share = share_ref.shape[1]
    grad_ref[...] = (mine_ref[...].astype(F32) + other_ref[...].astype(F32)).astype(BF16)
    weight_ref[pl.ds(pl.multiple_of(half * share, share), share), :] = share_ref[...].T
    weight_ref[pl.ds(pl.multiple_of((1 - half) * share, share), share), :] = other_share_ref[...].T


def finish(mine, other, share, other_share):
    columns, width = share.shape
    return call(
        finish_kernel,
        "finish",
        [shape(mine.shape, BF16), shape((2 * width, columns), F32)],
        [vmem()] * 4,
    )(mine, other, share, other_share)


def ahead(value, axis, size, k):
    return lax.ppermute(value, axis, [(i, (i + k) % size) for i in range(size)])


def across(value, peers, k):
    return lax.ppermute(value, "graph", [(i, i ^ k) for i in range(peers)])


def after(value, first):
    return lax.optimization_barrier((value, first))[0]


def local(features, weight, cotangent, tiles, tile_row, tile_col, tile_count):
    blocks_dev, _, width = features.shape
    peers = lax.axis_size("graph")
    feats = lax.axis_size("feat")
    reps = lax.axis_size("rep")
    far_first = sorted(range(1, peers), key=lambda k: (-(k & (peers // 2)), k))

    half, table = prepare(features, tile_row, tile_col, peers, reps)
    operator, asks = list_operator(tiles, table, tile_count, peers, blocks_dev)
    sends, own_mirror, own_cot = first_sends(features, cotangent, operator, asks[1:], peers, reps)
    cots = lax.all_gather(own_cot, "feat", axis=0, tiled=True)
    pieces, held = {0: [half]}, [0]
    bit = peers // 2
    while bit:
        for k in held:
            parts = pieces[k]
            if k:
                parts = after(halves(after(parts, sends[1])), pieces.get(1, half))
            pieces[k ^ bit] = [across(part, peers, bit) for part in parts]
        held = held + [k ^ bit for k in held]
        bit //= 2
    came = [None] * peers
    for k in far_first:
        came[k] = across(sends[k], peers, k)
    arrived = [part for k in range(1, peers) for part in pieces[k]]
    middle = peers // 2
    came[middle:], arrived, cots = lax.optimization_barrier((came[middle:], arrived, cots))
    came[1:middle], arrived = lax.optimization_barrier((came[1:middle], arrived))
    stacked = stack(arrived)
    swapped = ahead(stacked, "rep", reps, 1)
    acc, ids = first_rows(features, operator, asks[0], came, own_mirror, peers)
    give, asked = give_rows(acc, asks, stacked, swapped, operator, peers, reps)
    keep = keep_rows(acc, asked, operator, reps)

    mine = add_up(keep, ahead(give, "rep", reps, 1))
    cot = widen(cots, feats)
    sums = [mine] + [ahead(mine, "feat", feats, feats - q) for q in range(1, feats)]
    act, give, spread, term = dense(sums, cot, weight, feats)
    shared = ahead(give, "rep", reps, 1)
    total, activated = total_term(term, act, shared, peers, reps)
    values, sends, own_mirror = sends_of(spread, shared, operator, ids, peers, reps)

    came = [None] * peers
    for k in far_first:
        came[k] = across(sends[k], peers, k)
    ordered, total = lax.optimization_barrier(([came[k] for k in far_first], total))
    came = [None] + [ordered[far_first.index(k)] for k in range(1, peers)]
    acc = late_rows([asks[0], values, own_mirror], ids, came, [], operator, True, False)
    part = late_rows([acc], ids, came, far_first, operator, False, True)
    input_grad, weight_grad = finish(
        part, ahead(part, "rep", reps, 1), total, ahead(total, "rep", reps, 1)
    )
    return (activated, input_grad, weight_grad)


def solution(mesh):
    placed = (
        P(("parts", "graph"), "feat", None),
        P(),
        P(("parts", "graph"), "feat", None),
        P(("parts", "graph", "rep"), None, None),
        P(("parts", "graph", "rep")),
        P(("parts", "graph", "rep")),
        P(("parts", "graph", "rep")),
    )
    return jax.shard_map(
        local,
        mesh=mesh,
        in_specs=placed,
        out_specs=(
            P(("parts", "graph"), "feat", None),
            P(("parts", "graph"), "feat", None),
            P("parts", "feat"),
        ),
        check_vma=False,
    )
```

```python
import functools

import jax
import jax.numpy as jnp
from jax import lax
from jax.experimental import pallas as pl
from jax.experimental.pallas import tpu as pltpu
from jax.sharding import PartitionSpec as P

CAP = 2
GROUP = 8
CHUNK = 16
SIDES = 1
PLACE_ROWS = 8
PLACE_BUFFER = 2 ** 22
TAIL = 16
VMEM_LIMIT = 40 * 2 ** 20
VMEM_MOST = 50 * 2 ** 20
VMEM_ALL = 58 * 2 ** 20

NT = (((1,), (1,)), ((), ()))
TN = (((0,), (0,)), ((), ()))
F32 = jnp.float32
BF16 = jnp.bfloat16


def vmem():
    return pl.BlockSpec(memory_space=pltpu.VMEM)


def smem():
    return pl.BlockSpec(memory_space=pltpu.SMEM)


def hbm():
    return pl.BlockSpec(memory_space=pltpu.HBM)


def shape(dims, dtype):
    return jax.ShapeDtypeStruct(tuple(dims), dtype)


def dot(a, b, dims=None):
    if dims is None:
        return jnp.dot(a, b, preferred_element_type=F32)
    return lax.dot_general(a, b, dims, preferred_element_type=F32)


def call(kernel, name, outs, in_specs, scratch=(), flops=0, moved=2 ** 18, limit=VMEM_LIMIT, **kwargs):
    return pl.pallas_call(
        kernel,
        out_shape=outs,
        in_specs=in_specs,
        scratch_shapes=list(scratch),
        compiler_params=pltpu.CompilerParams(vmem_limit_bytes=limit),
        cost_estimate=pl.CostEstimate(flops=flops, bytes_accessed=moved, transcendentals=0),
        name=name,
        **kwargs,
    )


def lanes(x3):
    return jnp.concatenate([x3[b] for b in range(x3.shape[0])], axis=1)


def places(peers, blocks_dev, row, col, table):
    me = lax.axis_index("graph")
    lane = lax.broadcasted_iota(jnp.int32, col.shape, 1)
    place = jnp.zeros(col.shape, jnp.int32)
    for k in range(peers):
        local = col - jnp.bitwise_xor(me, k) * blocks_dev
        inside = (local >= 0) & (local < blocks_dev)
        low = jnp.min(jnp.where(inside, local, blocks_dev - 1), axis=1, keepdims=True)
        high = jnp.max(jnp.where(inside, local, 0), axis=1, keepdims=True)
        table[PLACE_ROWS + k : PLACE_ROWS + k + 1, :] = jnp.where(lane == 0, low, high)
        slot = k * CAP + (local != low).astype(jnp.int32)
        place = jnp.where(inside, slot * blocks_dev + row, place)
    table[:PLACE_ROWS, :] = jnp.broadcast_to(place, (PLACE_ROWS, place.shape[1]))


def table_rows(peers):
    return PLACE_ROWS + -(-peers // 8) * 8


def prepare_kernel(peers, row_ref, col_ref, x3, half_out, table_out, table, half_sem, sem):
    share = half_out.shape[0]
    mine = pl.ds(lax.axis_index("rep") * share, share)
    half_copy = pltpu.make_async_copy(x3.at[mine], half_out, half_sem)
    half_copy.start()
    if table.shape[0] > PLACE_ROWS + peers:
        table[...] = jnp.zeros(table.shape, jnp.int32)
    places(peers, x3.shape[0], row_ref[...], col_ref[...], table)
    copy = pltpu.make_async_copy(table, table_out.at[pl.ds(0, table.shape[0])], sem)
    copy.start()
    half_copy.wait()
    copy.wait()


def prepare(features, tile_row, tile_col, peers, reps):
    per = tile_col.shape[0]
    blocks_dev, columns, width = features.shape
    return call(
        functools.partial(prepare_kernel, peers),
        "prepare",
        [shape((blocks_dev // reps, columns, width), BF16), shape((PLACE_BUFFER // (4 * per), per), jnp.int32)],
        [vmem()] * 3,
        [
            pltpu.VMEM((table_rows(peers), per), jnp.int32),
            pltpu.SemaphoreType.DMA,
            pltpu.SemaphoreType.DMA,
        ],
        limit=VMEM_ALL,
        out_specs=[hbm(), hbm()],
    )(tile_row.reshape(1, per), tile_col.reshape(1, per), features)


def pick(ids_ref, lane):
    ids = ids_ref[...].astype(F32)
    at = lax.broadcasted_iota(jnp.int32, ids.shape, 1)
    return jnp.max(jnp.where(at == lane, ids, 0.0)).astype(jnp.int32)


def operator_kernel(blocks_dev, slots_here, groups, count_ref, table_in, tiles_ref, m_ref, *refs):
    asks, (tiles, acc, place_ref, table, sems, sem, table_sem) = refs[:-7], refs[-7:]
    step = pl.program_id(0)
    per, width = tiles.shape[0], tiles.shape[1]
    chunks = per // CHUNK
    spare = slots_here * blocks_dev

    def chunk_copy(c):
        part = pl.ds(c * CHUNK, CHUNK)
        return pltpu.make_async_copy(tiles_ref.at[part], tiles.at[part], sems.at[c])

    def place_copy():
        return pltpu.make_async_copy(table_in.at[pl.ds(0, PLACE_ROWS)], place_ref, sem)

    def table_copy():
        return pltpu.make_async_copy(table_in.at[pl.ds(0, table.shape[0])], table, table_sem)

    @pl.when(step == 0)
    def _():
        place_copy().start()
        table_copy().start()
        for c in range(chunks):
            chunk_copy(c).start()

    acc[...] = jnp.zeros_like(acc)

    @pl.when(step == 0)
    def _():
        place_copy().wait()

    count = count_ref[0]

    def add_chunk(c, carry):
        @pl.when(step == 0)
        def _():
            chunk_copy(c).wait()

        for u in range(CHUNK):
            t = c * CHUNK + u
            place = place_ref[0, t]
            here = t < count
            if groups > 1:
                place = place - step * spare
                here = here & (place >= 0) & (place < spare)
            place = jnp.where(here, place, spare)
            side = u % SIDES
            acc[side, place] = acc[side, place] + tiles[t].astype(F32)
        return carry

    lax.fori_loop(0, chunks, add_chunk, 0)
    for s in range(slots_here):
        for r in range(blocks_dev):
            total = acc[0, s * blocks_dev + r]
            for side in range(1, SIDES):
                total = total + acc[side, s * blocks_dev + r]
            m_ref[r * width : (r + 1) * width, s * width : (s + 1) * width] = total.astype(BF16)

    @pl.when(step == 0)
    def _():
        table_copy().wait()
        for k, ask_ref in enumerate(asks):
            ask_ref[...] = table[PLACE_ROWS + k : PLACE_ROWS + k + 1, :]


def list_operator(tiles, table, tile_count, peers, blocks_dev):
    per, width = tiles.shape[0], tiles.shape[1]
    slots = peers * CAP
    slots_here = min(slots, GROUP)
    groups = slots // slots_here
    outs = call(
        functools.partial(operator_kernel, blocks_dev, slots_here, groups),
        "operator",
        [shape((blocks_dev * width, slots * width), BF16)] + [shape((1, per), jnp.int32)] * peers,
        [smem(), hbm(), hbm()],
        [
            pltpu.VMEM((per, width, width), BF16),
            pltpu.VMEM((SIDES, slots_here * blocks_dev + 1, width, width), F32),
            pltpu.SMEM((PLACE_ROWS, per), jnp.int32),
            pltpu.VMEM((table_rows(peers), per), jnp.int32),
            pltpu.SemaphoreType.DMA((per // CHUNK,)),
            pltpu.SemaphoreType.DMA,
            pltpu.SemaphoreType.DMA,
        ],
        moved=2 ** 24,
        limit=VMEM_MOST,
        grid=(groups,),
        out_specs=[pl.BlockSpec((blocks_dev * width, slots_here * width), lambda i: (0, i))] + [vmem()] * peers,
    )(tile_count, table, tiles)
    return outs[0], list(outs[1:])


def mirrored(near, m_ref, mir, slots, width):
    if slots <= GROUP:
        mir[...] = dot(near, m_ref[...])
    else:
        part = GROUP * width

        @pl.loop(0, slots // GROUP)
        def _(i):
            where = pl.ds(pl.multiple_of(i * part, part), part)
            mir[:, where] = dot(near, m_ref[:, where])


def first_sends_kernel(peers, *refs):
    ask_refs, refs = refs[: peers - 1], refs[peers - 1 :]
    x3, cot, m_ref, refs = refs[0], refs[1], refs[2], refs[3:]
    send_refs, self_ref, cot_ref, mir = refs[: peers - 1], refs[peers - 1], refs[peers], refs[peers + 1]
    _, columns, width = x3.shape
    share = cot_ref.shape[0]
    cot_ref[...] = cot[pl.ds(lax.axis_index("rep") * share, share)]
    both = CAP * width
    mirrored(lanes(x3), m_ref, mir, peers * CAP, width)
    self_ref[...] = mir[:, :both]
    lane = lax.broadcasted_iota(jnp.int32, (TAIL, both), 1)
    for k in range(1, peers):
        out = send_refs[k - 1]
        out[:columns, :] = mir[:, k * both : (k + 1) * both].astype(BF16)
        low, high = ask_refs[k - 1][:, :1], ask_refs[k - 1][:, 1:2]
        out[columns:, :] = jnp.where(lane < width, low, high).astype(F32).astype(BF16)


def first_sends(values, cotangent, operator, asks, peers, reps):
    blocks_dev, columns, width = values.shape
    outs = call(
        functools.partial(first_sends_kernel, peers),
        "first_sends",
        [shape((columns + TAIL, CAP * width), BF16)] * (peers - 1)
        + [shape((columns, CAP * width), F32), shape((blocks_dev // reps, columns, width), BF16)],
        [vmem()] * (peers + 2),
        [pltpu.VMEM((columns, peers * CAP * width), F32)],
        flops=2 ** 28,
        moved=2 ** 21,
    )(*asks, values, cotangent, operator)
    return [None] + list(outs[: peers - 1]), outs[peers - 1], outs[peers]


def add_sums(acc, block, sums):
    acc[block] = acc[block] + sums.astype(F32)


def own_rows(far, m_ref, k):
    both = far.shape[1]
    return dot(far, m_ref[:, k * both : (k + 1) * both], NT)


def put_rows(acc, own, before=None):
    blocks_dev, _, width = acc.shape
    for b in range(blocks_dev):
        add = own[:, b * width : (b + 1) * width]
        acc[b] = add if before is None else before[b] + add


def self_rows(x3, m_ref, ask_ref):
    far = jnp.concatenate([x3[pick(ask_ref, s)] for s in range(CAP)], axis=1)
    return own_rows(far, m_ref, 0)


def far_of(share, mine_ref, other_ref, ask_ref, at):
    first = lax.axis_index("rep") * share
    blocks = []
    for s in range(CAP):
        local = pick(ask_ref, s) - first
        own = (local >= 0) & (local < share)
        here = at * share + jnp.where(own, local, 0)
        there = at * share + jnp.where(own, 0, jnp.where(local < 0, local + share, local - share))
        blocks.append(jnp.where(own, mine_ref[here], other_ref[there]))
    return jnp.concatenate(blocks, axis=1)


def first_rows_kernel(peers, *refs):
    ask_ref, refs = refs[0], refs[1:]
    came_refs, refs = refs[: peers - 1], refs[peers - 1 :]
    x3, m_ref, self_ref, acc, ids_refs = refs[0], refs[1], refs[2], refs[3], refs[4:]
    _, columns, width = x3.shape
    put_rows(acc, self_rows(x3, m_ref, ask_ref))
    for s in range(CAP):
        add_sums(acc, pick(ask_ref, s), self_ref[:, s * width : (s + 1) * width])
    lane = lax.broadcasted_iota(jnp.int32, ids_refs[0].shape, 1)
    for k in range(1, peers):
        came = came_refs[k - 1]
        ids = jnp.zeros(lane.shape, jnp.int32)
        for s in range(CAP):
            here = slice(s * width, (s + 1) * width)
            asked = jnp.max(came[columns : columns + TAIL, here].astype(F32)).astype(jnp.int32)
            ids = jnp.where(lane == s, asked, ids)
            add_sums(acc, asked, came[:columns, here])
        ids_refs[k - 1][...] = ids


def first_rows(values, operator, ask, came, own_mirror, peers):
    _, columns, width = values.shape
    outs = call(
        functools.partial(first_rows_kernel, peers),
        "first_rows",
        [shape(values.shape, F32)] + [shape((1, width), jnp.int32)] * (peers - 1),
        [vmem()] * (peers + 3),
        flops=2 ** 27,
        moved=2 ** 20,
    )(ask, *came[1:], values, operator, own_mirror)
    return outs[0], [None] + list(outs[1:])


def stack_kernel(*refs):
    at = 0
    for ref in refs[:-1]:
        share = ref.shape[0]
        refs[-1][at : at + share] = ref[...]
        at += share


def halves_kernel(in_ref, low_ref, high_ref):
    share = low_ref.shape[0]
    low_ref[...] = in_ref[:share]
    high_ref[...] = in_ref[share:]


def halves(parts):
    if len(parts) > 1:
        return parts
    share, columns, width = parts[0].shape
    part = shape((share // 2, columns, width), BF16)
    return list(call(halves_kernel, "halves", [part, part], [vmem()])(*parts))


def stack(pieces):
    _, columns, width = pieces[0].shape
    out = shape((sum(piece.shape[0] for piece in pieces), columns, width), BF16)
    return call(stack_kernel, "stack", out, [vmem()] * len(pieces))(*pieces)


def half_rows(before, far_ref, m_ref, first, share):
    columns, width = before.shape[1:]
    both = CAP * width
    rows = pl.ds(pl.multiple_of(first * width, share * width), share * width)
    if m_ref.shape[1] <= GROUP * width:
        own = dot(far_ref[:, both:], m_ref[rows, both:], NT)
    else:

        def add_peer(k, total):
            here = pl.ds(pl.multiple_of(k * both, both), both)
            return total + dot(far_ref[:, here], m_ref[rows, here], NT)

        zeros = jnp.zeros((columns, share * width), F32)
        own = lax.fori_loop(1, m_ref.shape[1] // both, add_peer, zeros)
    return [before[first + b] + own[:, b * width : (b + 1) * width] for b in range(share)]


def give_rows_kernel(peers, *refs):
    ask_refs, refs = refs[: peers - 1], refs[peers - 1 :]
    before, mine_ref, other_ref, m_ref, give_ref, far_ref = refs
    share = give_ref.shape[0]
    both = CAP * before.shape[2]
    for k in range(1, peers):
        far_ref[:, k * both : (k + 1) * both] = far_of(share, mine_ref, other_ref, ask_refs[k - 1], k - 1)
    far_ref[:, :both] = jnp.zeros((far_ref.shape[0], both), BF16)
    rows = half_rows(before, far_ref, m_ref, (1 - lax.axis_index("rep")) * share, share)
    for b in range(share):
        give_ref[b] = rows[b].astype(BF16)


def give_rows(before, asks, mine, other, operator, peers, reps):
    blocks_dev, columns, width = before.shape
    return call(
        functools.partial(give_rows_kernel, peers),
        "give_rows",
        [shape((blocks_dev // reps, columns, width), BF16), shape((columns, peers * CAP * width), BF16)],
        [vmem()] * (peers + 3),
        flops=2 ** 27,
        moved=2 ** 20,
    )(*asks[1:], before, mine, other, operator)


def keep_rows_kernel(before, far_ref, m_ref, keep_ref):
    share = keep_ref.shape[0]
    rows = half_rows(before, far_ref, m_ref, lax.axis_index("rep") * share, share)
    for b in range(share):
        keep_ref[b] = rows[b]


def keep_rows(before, far, operator, reps):
    blocks_dev, columns, width = before.shape
    return call(
        keep_rows_kernel,
        "keep_rows",
        shape((blocks_dev // reps, columns, width), F32),
        [vmem()] * 3,
        flops=2 ** 27,
        moved=2 ** 20,
    )(before, far, operator)


def late_self_kernel(ask_ref, x3, self_ref, m_ref, act_ref, shared_ref, acc, out_ref):
    width = x3.shape[2]
    put_rows(acc, self_rows(x3, m_ref, ask_ref))
    for s in range(CAP):
        add_sums(acc, pick(ask_ref, s), self_ref[:, s * width : (s + 1) * width])
    half = lax.axis_index("rep")
    blocks = act_ref.shape[0]
    out_ref[pl.ds(half * blocks, blocks)] = act_ref[...]
    for b in range(blocks):
        at = (blocks + b) * width
        out_ref[(1 - half) * blocks + b] = shared_ref[:, at : at + width]


def late_self(ask, values, own_mirror, operator, act, shared):
    return call(
        late_self_kernel,
        "late_self",
        [shape(values.shape, F32), shape(values.shape, BF16)],
        [vmem()] * 6,
        flops=2 ** 26,
    )(ask, values, own_mirror, operator, act, shared)


def late_rows_kernel(k, before, ids_ref, came_ref, m_ref, out_ref, acc):
    width = acc.shape[2]
    both = CAP * width
    put_rows(acc, own_rows(came_ref[:, both : 2 * both], m_ref, k), before)
    for s in range(CAP):
        add_sums(acc, pick(ids_ref, s), came_ref[:, s * width : (s + 1) * width])
    out_ref[...] = acc[...].astype(out_ref.dtype)


def late_rows(before, ids, came, operator, k, dtype):
    return call(
        functools.partial(late_rows_kernel, k),
        "late_rows",
        shape(before.shape, dtype),
        [vmem()] * 4,
        [pltpu.VMEM(before.shape, F32)],
        flops=2 ** 26,
    )(before, ids, came, operator)


def add_kernel(keep_ref, came_ref, out_ref):
    out_ref[...] = (keep_ref[...] + came_ref[...].astype(F32)).astype(BF16)


def add_up(keep, came):
    return call(add_kernel, "add_up", shape(came.shape, BF16), [vmem(), vmem()])(keep, came)


def widen_kernel(feats, in_ref, out_ref):
    _, columns, width = in_ref.shape
    share = out_ref.shape[1] // width
    for f in range(feats):
        for b in range(share):
            out_ref[f * columns : (f + 1) * columns, b * width : (b + 1) * width] = in_ref[f * share + b]


def widen(parts, feats):
    blocks, columns, width = parts.shape
    out = shape((feats * columns, blocks // feats * width), BF16)
    return call(functools.partial(widen_kernel, feats), "widen", out, [vmem()])(parts)


def dense_kernel(feats, *refs):
    sums, wide_cot, refs = refs[:feats], refs[feats], refs[feats + 1 :]
    w_ref, act_ref, give_ref, spread_ref, term_ref, wide, pre_scr, grad = refs
    share, columns, width = act_ref.shape
    me = lax.axis_index("feat")
    rows = [pl.ds(pl.multiple_of(lax.rem(me + q, feats) * columns, columns), columns) for q in range(feats)]
    for q in range(feats):
        for b in range(share):
            wide[rows[q], b * width : (b + 1) * width] = sums[q][b]
    pre = dot(w_ref[...], wide[...], TN)
    pre_scr[...] = pre
    sig = jax.nn.sigmoid(pre)
    factor = wide_cot[...].astype(F32) * sig * (1.0 + pre * (1.0 - sig))
    grad[...] = factor.astype(BF16)
    spread = dot(w_ref[rows[0], :], grad[...]).astype(BF16)
    term_ref[...] = dot(grad[rows[0], :], wide[...], NT)
    wide_share = share * width
    give_ref[:, :wide_share] = spread
    for b in range(share):
        spread_ref[b] = spread[:, b * width : (b + 1) * width]
    own = pre_scr[rows[0], :]
    act = (own * jax.nn.sigmoid(own)).astype(BF16)
    give_ref[:, wide_share:] = act
    for b in range(share):
        act_ref[b] = act[:, b * width : (b + 1) * width]


def dense(sums, cot, weight, feats):
    share, columns, width = sums[0].shape
    features = weight.shape[0]
    return call(
        functools.partial(dense_kernel, feats),
        "dense",
        [
            shape((share, columns, width), BF16),
            shape((columns, 2 * share * width), BF16),
            shape((share, columns, width), BF16),
            shape((columns, features), F32),
        ],
        [vmem()] * (feats + 2),
        [
            pltpu.VMEM((features, share * width), BF16),
            pltpu.VMEM((features, share * width), F32),
            pltpu.VMEM((features, share * width), BF16),
        ],
        flops=2 ** 28,
        moved=2 ** 20,
    )(*sums, cot, weight)


def send_kernel(peers, *refs):
    ids_refs, refs = refs[: peers - 1], refs[peers - 1 :]
    mine_ref, came_ref, m_ref, refs = refs[0], refs[1], refs[2], refs[3:]
    x3, refs = refs[0], refs[1:]
    send_refs, refs = refs[: peers - 1], refs[peers - 1 :]
    self_ref, mir = refs
    share, _, width = mine_ref.shape
    both = CAP * width
    half = lax.axis_index("rep")
    x3[pl.ds(half * share, share)] = mine_ref[...]
    for b in range(share):
        x3[(1 - half) * share + b] = came_ref[:, b * width : (b + 1) * width]
    mirrored(lanes(x3), m_ref, mir, peers * CAP, width)
    self_ref[...] = mir[:, :both]
    for k in range(1, peers):
        out = send_refs[k - 1]
        out[:, :both] = mir[:, k * both : (k + 1) * both].astype(BF16)
        for s in range(CAP):
            at = (CAP + s) * width
            out[:, at : at + width] = x3[pick(ids_refs[k - 1], s)]


def sends_of(mine, came, operator, ids, peers, reps):
    share, columns, width = mine.shape
    chunk = 2 * CAP * width
    outs = call(
        functools.partial(send_kernel, peers),
        "sends",
        [shape((share * reps, columns, width), BF16)]
        + [shape((columns, chunk), BF16)] * (peers - 1)
        + [shape((columns, CAP * width), F32)],
        [vmem()] * (peers + 2),
        [pltpu.VMEM((columns, peers * CAP * width), F32)],
        flops=2 ** 28,
        moved=2 ** 21,
    )(*ids[1:], mine, came, operator)
    return outs[0], [None] + list(outs[1:peers]), outs[peers]


def pair_kernel(mine_ref, came_ref, out_ref):
    out_ref[...] = (mine_ref[...].astype(F32) + came_ref[...].astype(F32)).astype(out_ref.dtype)


def pair_sum(mine, came, dtype):
    return call(pair_kernel, "pair_sum", shape(mine.shape, dtype), [vmem(), vmem()])(mine, came)


def split_kernel(mine_ref, came_ref, give_ref, keep_ref, total):
    half = lax.axis_index("rep")
    part = keep_ref.shape[1]
    total[...] = mine_ref[...].astype(F32) + came_ref[...].astype(F32)
    give_ref[...] = total[:, pl.ds(pl.multiple_of((1 - half) * part, part), part)].astype(BF16)
    keep_ref[...] = total[:, pl.ds(pl.multiple_of(half * part, part), part)]


def split_sum(mine, came, reps):
    columns, features = mine.shape
    part = (columns, features // reps)
    return call(
        split_kernel,
        "split_sum",
        [shape(part, BF16), shape(part, F32)],
        [vmem()] * 2,
        [pltpu.VMEM(mine.shape, F32)],
    )(mine, came)


def pair_term(term, peers, reps):
    give, total = split_sum(term, across(term, peers, 1), reps)
    total = pair_sum(total, ahead(give, "rep", reps, 1), F32 if peers == 2 else BF16)
    return total


def finish_kernel(mine_ref, other_ref, share_ref, other_share_ref, grad_ref, weight_ref):
    half = lax.axis_index("rep")
    share = share_ref.shape[1]
    grad_ref[...] = (mine_ref[...].astype(F32) + other_ref[...].astype(F32)).astype(BF16)
    weight_ref[pl.ds(pl.multiple_of(half * share, share), share), :] = share_ref[...].T
    weight_ref[pl.ds(pl.multiple_of((1 - half) * share, share), share), :] = other_share_ref[...].T


def finish(mine, other, share, other_share):
    columns, width = share.shape
    return call(
        finish_kernel,
        "finish",
        [shape(mine.shape, BF16), shape((2 * width, columns), F32)],
        [vmem()] * 4,
    )(mine, other, share, other_share)


def ahead(value, axis, size, k):
    return lax.ppermute(value, axis, [(i, (i + k) % size) for i in range(size)])


def across(value, peers, k):
    return lax.ppermute(value, "graph", [(i, i ^ k) for i in range(peers)])


def after(value, first):
    return lax.optimization_barrier((value, first))[0]


def local(features, weight, cotangent, tiles, tile_row, tile_col, tile_count):
    blocks_dev, _, width = features.shape
    peers = lax.axis_size("graph")
    feats = lax.axis_size("feat")
    reps = lax.axis_size("rep")
    far_first = sorted(range(1, peers), key=lambda k: (-(k & (peers // 2)), k))

    half, table = prepare(features, tile_row, tile_col, peers, reps)
    operator, asks = list_operator(tiles, table, tile_count, peers, blocks_dev)
    sends, own_mirror, own_cot = first_sends(features, cotangent, operator, asks[1:], peers, reps)
    cots = lax.all_gather(own_cot, "feat", axis=0, tiled=True)
    pieces, held = {0: [half]}, [0]
    bit = peers // 2
    while bit:
        for k in held:
            parts = pieces[k]
            if k:
                parts = after(halves(after(parts, sends[1])), pieces.get(1, half))
            pieces[k ^ bit] = [across(part, peers, bit) for part in parts]
        held = held + [k ^ bit for k in held]
        bit //= 2
    came = [None] * peers
    for k in far_first:
        came[k] = across(sends[k], peers, k)
    arrived = [part for k in range(1, peers) for part in pieces[k]]
    middle = peers // 2
    came[middle:], arrived, cots = lax.optimization_barrier((came[middle:], arrived, cots))
    came[1:middle], arrived = lax.optimization_barrier((came[1:middle], arrived))
    stacked = stack(arrived)
    swapped = ahead(stacked, "rep", reps, 1)
    acc, ids = first_rows(features, operator, asks[0], came, own_mirror, peers)
    give, asked = give_rows(acc, asks, stacked, swapped, operator, peers, reps)
    keep = keep_rows(acc, asked, operator, reps)

    mine = add_up(keep, ahead(give, "rep", reps, 1))
    cot = widen(cots, feats)
    sums = [mine] + [ahead(mine, "feat", feats, feats - q) for q in range(1, feats)]
    act, give, spread, term = dense(sums, cot, weight, feats)
    shared = ahead(give, "rep", reps, 1)
    total = pair_term(term, peers, reps)
    values, sends, own_mirror = sends_of(spread, shared, operator, ids, peers, reps)

    came = [None] * peers
    for k in far_first:
        came[k] = across(sends[k], peers, k)
    acc, activated = late_self(asks[0], values, own_mirror, operator, act, shared)
    *firsts, last = sorted(range(1, peers), key=lambda k: (k == peers - 1, -(k & middle), k))
    for k in firsts:
        acc = late_rows(acc, ids[k], came[k], operator, k, F32)
    bit = 2
    while bit < peers:
        other = across(total, peers, bit)
        if 2 * bit == peers:
            total, acc = lax.optimization_barrier((total, acc))
        total = pair_sum(total, other, F32 if 2 * bit == peers else BF16)
        bit *= 2
    acc, total = lax.optimization_barrier((acc, total))
    part = late_rows(acc, ids[last], came[last], operator, last, BF16)
    input_grad, weight_grad = finish(
        part, ahead(part, "rep", reps, 1), total, ahead(total, "rep", reps, 1)
    )
    return (activated, input_grad, weight_grad)


def solution(mesh):
    placed = (
        P(("parts", "graph"), "feat", None),
        P(),
        P(("parts", "graph"), "feat", None),
        P(("parts", "graph", "rep"), None, None),
        P(("parts", "graph", "rep")),
        P(("parts", "graph", "rep")),
        P(("parts", "graph", "rep")),
    )
    return jax.shard_map(
        local,
        mesh=mesh,
        in_specs=placed,
        out_specs=(
            P(("parts", "graph"), "feat", None),
            P(("parts", "graph"), "feat", None),
            P("parts", "feat"),
        ),
        check_vma=False,
    )
```

```python
import functools

import jax
import jax.numpy as jnp
from jax import lax
from jax.experimental import pallas as pl
from jax.experimental.pallas import tpu as pltpu
from jax.sharding import PartitionSpec as P

CAP = 2
GROUP = 8
CHUNK = 8
SIDES = 1
PLACE_ROWS = 8
PLACE_BUFFER = 2 ** 22
TAIL = 16
VMEM_LIMIT = 40 * 2 ** 20
VMEM_MOST = 50 * 2 ** 20
VMEM_ALL = 58 * 2 ** 20

NT = (((1,), (1,)), ((), ()))
TN = (((0,), (0,)), ((), ()))
F32 = jnp.float32
BF16 = jnp.bfloat16


def vmem():
    return pl.BlockSpec(memory_space=pltpu.VMEM)


def smem():
    return pl.BlockSpec(memory_space=pltpu.SMEM)


def hbm():
    return pl.BlockSpec(memory_space=pltpu.HBM)


def shape(dims, dtype):
    return jax.ShapeDtypeStruct(tuple(dims), dtype)


def dot(a, b, dims=None):
    if dims is None:
        return jnp.dot(a, b, preferred_element_type=F32)
    return lax.dot_general(a, b, dims, preferred_element_type=F32)


def call(kernel, name, outs, in_specs, scratch=(), flops=0, moved=2 ** 18, limit=VMEM_LIMIT, **kwargs):
    return pl.pallas_call(
        kernel,
        out_shape=outs,
        in_specs=in_specs,
        scratch_shapes=list(scratch),
        compiler_params=pltpu.CompilerParams(vmem_limit_bytes=limit),
        cost_estimate=pl.CostEstimate(flops=flops, bytes_accessed=moved, transcendentals=0),
        name=name,
        **kwargs,
    )


def lanes(x3):
    return jnp.concatenate([x3[b] for b in range(x3.shape[0])], axis=1)


def places(peers, blocks_dev, row, col, table):
    me = lax.axis_index("graph")
    both = (2 * peers, col.shape[1])
    side = lax.broadcasted_iota(jnp.int32, both, 0)
    k_of = jnp.where(side < peers, side, side - peers)
    local = jnp.broadcast_to(col, both) - jnp.bitwise_xor(me, k_of) * blocks_dev
    inside = (local >= 0) & (local < blocks_dev)
    ends = jnp.where(side < peers, jnp.where(inside, local, blocks_dev - 1), jnp.where(inside, -local, 0))
    ends = jnp.min(ends, axis=1, keepdims=True)
    lane = lax.broadcasted_iota(jnp.int32, col.shape, 1)
    place = jnp.zeros(col.shape, jnp.int32)
    for k in range(peers):
        low, high = ends[k : k + 1], -ends[peers + k : peers + k + 1]
        table[PLACE_ROWS + k : PLACE_ROWS + k + 1, :] = jnp.where(lane == 0, low, high)
        slot = k * CAP + (local[k : k + 1] != low).astype(jnp.int32)
        place = jnp.where(inside[k : k + 1], slot * blocks_dev + row, place)
    table[:PLACE_ROWS, :] = jnp.broadcast_to(place, (PLACE_ROWS, place.shape[1]))


def table_rows(peers):
    return PLACE_ROWS + -(-peers // 8) * 8


def prepare_kernel(peers, row_in, col_in, x3, half_out, table_out, half, row, col, table, in_sem, row_sem, col_sem, sems):
    share = half_out.shape[0]
    mine = pl.ds(lax.axis_index("rep") * share, share)
    half_in = pltpu.make_async_copy(x3.at[mine], half, in_sem)
    row_copy = pltpu.make_async_copy(row_in, row, row_sem)
    col_copy = pltpu.make_async_copy(col_in, col, col_sem)
    col_copy.start()
    row_copy.start()
    half_in.start()
    if table.shape[0] > PLACE_ROWS + peers:
        table[...] = jnp.zeros(table.shape, jnp.int32)
    half_in.wait()
    half_copy = pltpu.make_async_copy(half, half_out, sems.at[0])
    half_copy.start()
    col_copy.wait()
    row_copy.wait()
    places(peers, x3.shape[0], row[...], col[...], table)
    copy = pltpu.make_async_copy(table, table_out.at[pl.ds(0, table.shape[0])], sems.at[1])
    copy.start()
    half_copy.wait()
    copy.wait()


def prepare(features, tile_row, tile_col, peers, reps):
    per = tile_col.shape[0]
    blocks_dev, columns, width = features.shape
    share = (blocks_dev // reps, columns, width)
    return call(
        functools.partial(prepare_kernel, peers),
        "prepare",
        [shape(share, BF16), shape((PLACE_BUFFER // (4 * per), per), jnp.int32)],
        [hbm()] * 3,
        [
            pltpu.VMEM(share, BF16),
            pltpu.VMEM((1, per), jnp.int32),
            pltpu.VMEM((1, per), jnp.int32),
            pltpu.VMEM((table_rows(peers), per), jnp.int32),
            pltpu.SemaphoreType.DMA,
            pltpu.SemaphoreType.DMA,
            pltpu.SemaphoreType.DMA,
            pltpu.SemaphoreType.DMA((2,)),
        ],
        limit=VMEM_ALL,
        out_specs=[hbm(), hbm()],
    )(tile_row.reshape(1, per), tile_col.reshape(1, per), features)


def pick(ids_ref, lane):
    ids = ids_ref[...].astype(F32)
    at = lax.broadcasted_iota(jnp.int32, ids.shape, 1)
    return jnp.max(jnp.where(at == lane, ids, 0.0)).astype(jnp.int32)


def operator_kernel(blocks_dev, slots_here, groups, count_ref, table_in, tiles_ref, m_ref, *refs):
    asks, (tiles, acc, place_ref, table, sems, sem, table_sem) = refs[:-7], refs[-7:]
    step = pl.program_id(0)
    per, width = tiles.shape[0], tiles.shape[1]
    chunks = per // CHUNK
    spare = slots_here * blocks_dev

    def chunk_copy(c):
        part = pl.ds(c * CHUNK, CHUNK)
        return pltpu.make_async_copy(tiles_ref.at[part], tiles.at[part], sems.at[c])

    def place_copy():
        return pltpu.make_async_copy(table_in.at[pl.ds(0, PLACE_ROWS)], place_ref, sem)

    def table_copy():
        return pltpu.make_async_copy(table_in.at[pl.ds(0, table.shape[0])], table, table_sem)

    @pl.when(step == 0)
    def _():
        place_copy().start()
        table_copy().start()
        for c in range(chunks):
            chunk_copy(c).start()

    acc[...] = jnp.zeros_like(acc)

    @pl.when(step == 0)
    def _():
        place_copy().wait()

    count = count_ref[0]

    def add_chunk(c, carry):
        @pl.when(step == 0)
        def _():
            chunk_copy(c).wait()

        for u in range(CHUNK):
            t = c * CHUNK + u
            place = place_ref[0, t]
            here = t < count
            if groups > 1:
                place = place - step * spare
                here = here & (place >= 0) & (place < spare)
            place = jnp.where(here, place, spare)
            side = u % SIDES
            acc[side, place] = acc[side, place] + tiles[t].astype(F32)
        return carry

    lax.fori_loop(0, chunks, add_chunk, 0)
    for s in range(slots_here):
        for r in range(blocks_dev):
            total = acc[0, s * blocks_dev + r]
            for side in range(1, SIDES):
                total = total + acc[side, s * blocks_dev + r]
            m_ref[r * width : (r + 1) * width, s * width : (s + 1) * width] = total.astype(BF16)

    @pl.when(step == 0)
    def _():
        table_copy().wait()
        for k, ask_ref in enumerate(asks):
            ask_ref[...] = table[PLACE_ROWS + k : PLACE_ROWS + k + 1, :]


def list_operator(tiles, table, tile_count, peers, blocks_dev):
    per, width = tiles.shape[0], tiles.shape[1]
    slots = peers * CAP
    slots_here = min(slots, GROUP)
    groups = slots // slots_here
    outs = call(
        functools.partial(operator_kernel, blocks_dev, slots_here, groups),
        "operator",
        [shape((blocks_dev * width, slots * width), BF16)] + [shape((1, per), jnp.int32)] * peers,
        [smem(), hbm(), hbm()],
        [
            pltpu.VMEM((per, width, width), BF16),
            pltpu.VMEM((SIDES, slots_here * blocks_dev + 1, width, width), F32),
            pltpu.SMEM((PLACE_ROWS, per), jnp.int32),
            pltpu.VMEM((table_rows(peers), per), jnp.int32),
            pltpu.SemaphoreType.DMA((per // CHUNK,)),
            pltpu.SemaphoreType.DMA,
            pltpu.SemaphoreType.DMA,
        ],
        moved=2 ** 24,
        limit=VMEM_MOST,
        grid=(groups,),
        out_specs=[pl.BlockSpec((blocks_dev * width, slots_here * width), lambda i: (0, i))] + [vmem()] * peers,
    )(tile_count, table, tiles)
    return outs[0], list(outs[1:])


def mirrored(near, m_ref, mir, slots, width):
    if slots <= GROUP:
        mir[...] = dot(near, m_ref[...])
    else:
        part = GROUP * width

        @pl.loop(0, slots // GROUP)
        def _(i):
            where = pl.ds(pl.multiple_of(i * part, part), part)
            mir[:, where] = dot(near, m_ref[:, where])


def first_sends_kernel(peers, *refs):
    ask_refs, refs = refs[: peers - 1], refs[peers - 1 :]
    x3, cot, m_ref, refs = refs[0], refs[1], refs[2], refs[3:]
    send_refs, self_ref, cot_ref, mir = refs[: peers - 1], refs[peers - 1], refs[peers], refs[peers + 1]
    _, columns, width = x3.shape
    share = cot_ref.shape[0]
    cot_ref[...] = cot[pl.ds(lax.axis_index("rep") * share, share)]
    both = CAP * width
    mirrored(lanes(x3), m_ref, mir, peers * CAP, width)
    self_ref[...] = mir[:, :both]
    lane = lax.broadcasted_iota(jnp.int32, (TAIL, both), 1)
    for k in range(1, peers):
        out = send_refs[k - 1]
        out[:columns, :] = mir[:, k * both : (k + 1) * both].astype(BF16)
        low, high = ask_refs[k - 1][:, :1], ask_refs[k - 1][:, 1:2]
        out[columns:, :] = jnp.where(lane < width, low, high).astype(F32).astype(BF16)


def first_sends(values, cotangent, operator, asks, peers, reps):
    blocks_dev, columns, width = values.shape
    outs = call(
        functools.partial(first_sends_kernel, peers),
        "first_sends",
        [shape((columns + TAIL, CAP * width), BF16)] * (peers - 1)
        + [shape((columns, CAP * width), F32), shape((blocks_dev // reps, columns, width), BF16)],
        [vmem()] * (peers + 2),
        [pltpu.VMEM((columns, peers * CAP * width), F32)],
        flops=2 ** 28,
        moved=2 ** 21,
    )(*asks, values, cotangent, operator)
    return [None] + list(outs[: peers - 1]), outs[peers - 1], outs[peers]


def add_sums(acc, block, sums):
    acc[block] = acc[block] + sums.astype(F32)


def own_rows(far, m_ref, k):
    both = far.shape[1]
    return dot(far, m_ref[:, k * both : (k + 1) * both], NT)


def put_rows(acc, own, before=None):
    blocks_dev, _, width = acc.shape
    for b in range(blocks_dev):
        add = own[:, b * width : (b + 1) * width]
        acc[b] = add if before is None else before[b] + add


def self_rows(x3, m_ref, ask_ref):
    far = jnp.concatenate([x3[pick(ask_ref, s)] for s in range(CAP)], axis=1)
    return own_rows(far, m_ref, 0)


def far_of(share, mine_ref, other_ref, ask_ref, at):
    first = lax.axis_index("rep") * share
    blocks = []
    for s in range(CAP):
        local = pick(ask_ref, s) - first
        own = (local >= 0) & (local < share)
        here = at * share + jnp.where(own, local, 0)
        there = at * share + jnp.where(own, 0, jnp.where(local < 0, local + share, local - share))
        blocks.append(jnp.where(own, mine_ref[here], other_ref[there]))
    return jnp.concatenate(blocks, axis=1)


def first_rows_kernel(peers, *refs):
    ask_ref, refs = refs[0], refs[1:]
    came_refs, refs = refs[: peers - 1], refs[peers - 1 :]
    x3, m_ref, self_ref, acc, ids_refs = refs[0], refs[1], refs[2], refs[3], refs[4:]
    _, columns, width = x3.shape
    put_rows(acc, self_rows(x3, m_ref, ask_ref))
    for s in range(CAP):
        add_sums(acc, pick(ask_ref, s), self_ref[:, s * width : (s + 1) * width])
    lane = lax.broadcasted_iota(jnp.int32, ids_refs[0].shape, 1)
    for k in range(1, peers):
        came = came_refs[k - 1]
        ids = jnp.zeros(lane.shape, jnp.int32)
        for s in range(CAP):
            here = slice(s * width, (s + 1) * width)
            asked = jnp.max(came[columns : columns + TAIL, here].astype(F32)).astype(jnp.int32)
            ids = jnp.where(lane == s, asked, ids)
            add_sums(acc, asked, came[:columns, here])
        ids_refs[k - 1][...] = ids


def first_rows(values, operator, ask, came, own_mirror, peers):
    _, columns, width = values.shape
    outs = call(
        functools.partial(first_rows_kernel, peers),
        "first_rows",
        [shape(values.shape, F32)] + [shape((1, width), jnp.int32)] * (peers - 1),
        [vmem()] * (peers + 3),
        flops=2 ** 27,
        moved=2 ** 20,
    )(ask, *came[1:], values, operator, own_mirror)
    return outs[0], [None] + list(outs[1:])


def stack_kernel(*refs):
    at = 0
    for ref in refs[:-1]:
        share = ref.shape[0]
        refs[-1][at : at + share] = ref[...]
        at += share


def halves_kernel(in_ref, low_ref, high_ref):
    share = low_ref.shape[0]
    low_ref[...] = in_ref[:share]
    high_ref[...] = in_ref[share:]


def halves(parts):
    if len(parts) > 1:
        return parts
    share, columns, width = parts[0].shape
    part = shape((share // 2, columns, width), BF16)
    return list(call(halves_kernel, "halves", [part, part], [vmem()])(*parts))


def stack(pieces):
    _, columns, width = pieces[0].shape
    out = shape((sum(piece.shape[0] for piece in pieces), columns, width), BF16)
    return call(stack_kernel, "stack", out, [vmem()] * len(pieces))(*pieces)


def half_rows(before, far_ref, m_ref, first, share):
    columns, width = before.shape[1:]
    both = CAP * width
    rows = pl.ds(pl.multiple_of(first * width, share * width), share * width)
    if m_ref.shape[1] <= GROUP * width:
        own = dot(far_ref[:, both:], m_ref[rows, both:], NT)
    else:

        def add_peer(k, total):
            here = pl.ds(pl.multiple_of(k * both, both), both)
            return total + dot(far_ref[:, here], m_ref[rows, here], NT)

        zeros = jnp.zeros((columns, share * width), F32)
        own = lax.fori_loop(1, m_ref.shape[1] // both, add_peer, zeros)
    return [before[first + b] + own[:, b * width : (b + 1) * width] for b in range(share)]


def give_rows_kernel(peers, *refs):
    ask_refs, refs = refs[: peers - 1], refs[peers - 1 :]
    before, mine_ref, other_ref, m_ref, give_ref, far_ref = refs
    share = give_ref.shape[0]
    both = CAP * before.shape[2]
    for k in range(1, peers):
        far_ref[:, k * both : (k + 1) * both] = far_of(share, mine_ref, other_ref, ask_refs[k - 1], k - 1)
    far_ref[:, :both] = jnp.zeros((far_ref.shape[0], both), BF16)
    rows = half_rows(before, far_ref, m_ref, (1 - lax.axis_index("rep")) * share, share)
    for b in range(share):
        give_ref[b] = rows[b].astype(BF16)


def give_rows(before, asks, mine, other, operator, peers, reps):
    blocks_dev, columns, width = before.shape
    return call(
        functools.partial(give_rows_kernel, peers),
        "give_rows",
        [shape((blocks_dev // reps, columns, width), BF16), shape((columns, peers * CAP * width), BF16)],
        [vmem()] * (peers + 3),
        flops=2 ** 27,
        moved=2 ** 20,
    )(*asks[1:], before, mine, other, operator)


def keep_rows_kernel(before, far_ref, m_ref, keep_ref):
    share = keep_ref.shape[0]
    rows = half_rows(before, far_ref, m_ref, lax.axis_index("rep") * share, share)
    for b in range(share):
        keep_ref[b] = rows[b]


def keep_rows(before, far, operator, reps):
    blocks_dev, columns, width = before.shape
    return call(
        keep_rows_kernel,
        "keep_rows",
        shape((blocks_dev // reps, columns, width), F32),
        [vmem()] * 3,
        flops=2 ** 27,
        moved=2 ** 20,
    )(before, far, operator)


def late_self_kernel(ask_ref, x3, self_ref, m_ref, act_ref, shared_ref, acc, out_ref):
    width = x3.shape[2]
    put_rows(acc, self_rows(x3, m_ref, ask_ref))
    for s in range(CAP):
        add_sums(acc, pick(ask_ref, s), self_ref[:, s * width : (s + 1) * width])
    half = lax.axis_index("rep")
    blocks = act_ref.shape[0]
    out_ref[pl.ds(half * blocks, blocks)] = act_ref[...]
    for b in range(blocks):
        at = (blocks + b) * width
        out_ref[(1 - half) * blocks + b] = shared_ref[:, at : at + width]


def late_self(ask, values, own_mirror, operator, act, shared):
    return call(
        late_self_kernel,
        "late_self",
        [shape(values.shape, F32), shape(values.shape, BF16)],
        [vmem()] * 6,
        flops=2 ** 26,
    )(ask, values, own_mirror, operator, act, shared)


def late_rows_kernel(k, before, ids_ref, came_ref, m_ref, out_ref, acc):
    width = acc.shape[2]
    both = CAP * width
    put_rows(acc, own_rows(came_ref[:, both : 2 * both], m_ref, k), before)
    for s in range(CAP):
        add_sums(acc, pick(ids_ref, s), came_ref[:, s * width : (s + 1) * width])
    out_ref[...] = acc[...].astype(out_ref.dtype)


def late_rows(before, ids, came, operator, k, dtype):
    return call(
        functools.partial(late_rows_kernel, k),
        "late_rows",
        shape(before.shape, dtype),
        [vmem()] * 4,
        [pltpu.VMEM(before.shape, F32)],
        flops=2 ** 26,
    )(before, ids, came, operator)


def add_kernel(keep_ref, came_ref, out_ref):
    out_ref[...] = (keep_ref[...] + came_ref[...].astype(F32)).astype(BF16)


def add_up(keep, came):
    return call(add_kernel, "add_up", shape(came.shape, BF16), [vmem(), vmem()])(keep, came)


def widen_kernel(feats, in_ref, out_ref):
    _, columns, width = in_ref.shape
    share = out_ref.shape[1] // width
    for f in range(feats):
        for b in range(share):
            out_ref[f * columns : (f + 1) * columns, b * width : (b + 1) * width] = in_ref[f * share + b]


def widen(parts, feats):
    blocks, columns, width = parts.shape
    out = shape((feats * columns, blocks // feats * width), BF16)
    return call(functools.partial(widen_kernel, feats), "widen", out, [vmem()])(parts)


def dense_kernel(feats, *refs):
    sums, wide_cot, refs = refs[:feats], refs[feats], refs[feats + 1 :]
    w_ref, act_ref, give_ref, spread_ref, term_ref, wide, pre_scr, grad = refs
    share, columns, width = act_ref.shape
    me = lax.axis_index("feat")
    rows = [pl.ds(pl.multiple_of(lax.rem(me + q, feats) * columns, columns), columns) for q in range(feats)]
    for q in range(feats):
        for b in range(share):
            wide[rows[q], b * width : (b + 1) * width] = sums[q][b]
    pre = dot(w_ref[...], wide[...], TN)
    pre_scr[...] = pre
    sig = jax.nn.sigmoid(pre)
    factor = wide_cot[...].astype(F32) * sig * (1.0 + pre * (1.0 - sig))
    grad[...] = factor.astype(BF16)
    spread = dot(w_ref[rows[0], :], grad[...]).astype(BF16)
    term_ref[...] = dot(grad[rows[0], :], wide[...], NT)
    wide_share = share * width
    give_ref[:, :wide_share] = spread
    for b in range(share):
        spread_ref[b] = spread[:, b * width : (b + 1) * width]
    own = pre_scr[rows[0], :]
    act = (own * jax.nn.sigmoid(own)).astype(BF16)
    give_ref[:, wide_share:] = act
    for b in range(share):
        act_ref[b] = act[:, b * width : (b + 1) * width]


def dense(sums, cot, weight, feats):
    share, columns, width = sums[0].shape
    features = weight.shape[0]
    return call(
        functools.partial(dense_kernel, feats),
        "dense",
        [
            shape((share, columns, width), BF16),
            shape((columns, 2 * share * width), BF16),
            shape((share, columns, width), BF16),
            shape((columns, features), F32),
        ],
        [vmem()] * (feats + 2),
        [
            pltpu.VMEM((features, share * width), BF16),
            pltpu.VMEM((features, share * width), F32),
            pltpu.VMEM((features, share * width), BF16),
        ],
        flops=2 ** 28,
        moved=2 ** 20,
    )(*sums, cot, weight)


def send_kernel(peers, *refs):
    ids_refs, refs = refs[: peers - 1], refs[peers - 1 :]
    mine_ref, came_ref, m_ref, refs = refs[0], refs[1], refs[2], refs[3:]
    x3, refs = refs[0], refs[1:]
    send_refs, refs = refs[: peers - 1], refs[peers - 1 :]
    self_ref, mir = refs
    share, _, width = mine_ref.shape
    both = CAP * width
    half = lax.axis_index("rep")
    x3[pl.ds(half * share, share)] = mine_ref[...]
    for b in range(share):
        x3[(1 - half) * share + b] = came_ref[:, b * width : (b + 1) * width]
    mirrored(lanes(x3), m_ref, mir, peers * CAP, width)
    self_ref[...] = mir[:, :both]
    for k in range(1, peers):
        out = send_refs[k - 1]
        out[:, :both] = mir[:, k * both : (k + 1) * both].astype(BF16)
        for s in range(CAP):
            at = (CAP + s) * width
            out[:, at : at + width] = x3[pick(ids_refs[k - 1], s)]


def sends_of(mine, came, operator, ids, peers, reps):
    share, columns, width = mine.shape
    chunk = 2 * CAP * width
    outs = call(
        functools.partial(send_kernel, peers),
        "sends",
        [shape((share * reps, columns, width), BF16)]
        + [shape((columns, chunk), BF16)] * (peers - 1)
        + [shape((columns, CAP * width), F32)],
        [vmem()] * (peers + 2),
        [pltpu.VMEM((columns, peers * CAP * width), F32)],
        flops=2 ** 28,
        moved=2 ** 21,
    )(*ids[1:], mine, came, operator)
    return outs[0], [None] + list(outs[1:peers]), outs[peers]


def pair_kernel(mine_ref, came_ref, out_ref):
    out_ref[...] = (mine_ref[...].astype(F32) + came_ref[...].astype(F32)).astype(out_ref.dtype)


def pair_sum(mine, came, dtype):
    return call(pair_kernel, "pair_sum", shape(mine.shape, dtype), [vmem(), vmem()])(mine, came)


def split_kernel(mine_ref, came_ref, give_ref, keep_ref, total):
    half = lax.axis_index("rep")
    part = keep_ref.shape[1]
    total[...] = mine_ref[...].astype(F32) + came_ref[...].astype(F32)
    give_ref[...] = total[:, pl.ds(pl.multiple_of((1 - half) * part, part), part)].astype(BF16)
    keep_ref[...] = total[:, pl.ds(pl.multiple_of(half * part, part), part)]


def split_sum(mine, came, reps):
    columns, features = mine.shape
    part = (columns, features // reps)
    return call(
        split_kernel,
        "split_sum",
        [shape(part, BF16), shape(part, F32)],
        [vmem()] * 2,
        [pltpu.VMEM(mine.shape, F32)],
    )(mine, came)


def pair_term(term, peers, reps):
    give, total = split_sum(term, across(term, peers, 1), reps)
    total = pair_sum(total, ahead(give, "rep", reps, 1), F32 if peers == 2 else BF16)
    return total


def finish_kernel(mine_ref, other_ref, share_ref, other_share_ref, grad_ref, weight_ref):
    half = lax.axis_index("rep")
    share = share_ref.shape[1]
    grad_ref[...] = (mine_ref[...].astype(F32) + other_ref[...].astype(F32)).astype(BF16)
    weight_ref[pl.ds(pl.multiple_of(half * share, share), share), :] = share_ref[...].T
    weight_ref[pl.ds(pl.multiple_of((1 - half) * share, share), share), :] = other_share_ref[...].T


def finish(mine, other, share, other_share):
    columns, width = share.shape
    return call(
        finish_kernel,
        "finish",
        [shape(mine.shape, BF16), shape((2 * width, columns), F32)],
        [vmem()] * 4,
    )(mine, other, share, other_share)


def ahead(value, axis, size, k):
    return lax.ppermute(value, axis, [(i, (i + k) % size) for i in range(size)])


def across(value, peers, k):
    return lax.ppermute(value, "graph", [(i, i ^ k) for i in range(peers)])


def after(value, first):
    return lax.optimization_barrier((value, first))[0]


def local(features, weight, cotangent, tiles, tile_row, tile_col, tile_count):
    blocks_dev, _, width = features.shape
    peers = lax.axis_size("graph")
    feats = lax.axis_size("feat")
    reps = lax.axis_size("rep")
    far_first = sorted(range(1, peers), key=lambda k: (-(k & (peers // 2)), k))

    half, table = prepare(features, tile_row, tile_col, peers, reps)
    operator, asks = list_operator(tiles, table, tile_count, peers, blocks_dev)
    sends, own_mirror, own_cot = first_sends(features, cotangent, operator, asks[1:], peers, reps)
    cots = lax.all_gather(own_cot, "feat", axis=0, tiled=True)
    pieces, held = {0: [half]}, [0]
    bit = peers // 2
    while bit:
        for k in held:
            parts = pieces[k]
            if k:
                parts = after(halves(after(parts, sends[1])), pieces.get(1, half))
            pieces[k ^ bit] = [across(part, peers, bit) for part in parts]
        held = held + [k ^ bit for k in held]
        bit //= 2
    came = [None] * peers
    for k in far_first:
        came[k] = across(sends[k], peers, k)
    arrived = [part for k in range(1, peers) for part in pieces[k]]
    middle = peers // 2
    came[middle:], arrived, cots = lax.optimization_barrier((came[middle:], arrived, cots))
    came[1:middle], arrived = lax.optimization_barrier((came[1:middle], arrived))
    stacked = stack(arrived)
    swapped = ahead(stacked, "rep", reps, 1)
    acc, ids = first_rows(features, operator, asks[0], came, own_mirror, peers)
    give, asked = give_rows(acc, asks, stacked, swapped, operator, peers, reps)
    keep = keep_rows(acc, asked, operator, reps)

    mine = add_up(keep, ahead(give, "rep", reps, 1))
    cot = widen(cots, feats)
    sums = [mine] + [ahead(mine, "feat", feats, feats - q) for q in range(1, feats)]
    act, give, spread, term = dense(sums, cot, weight, feats)
    shared = ahead(give, "rep", reps, 1)
    total = pair_term(term, peers, reps)
    values, sends, own_mirror = sends_of(spread, shared, operator, ids, peers, reps)

    came = [None] * peers
    for k in far_first:
        came[k] = across(sends[k], peers, k)
    acc, activated = late_self(asks[0], values, own_mirror, operator, act, shared)
    *firsts, last = sorted(range(1, peers), key=lambda k: (k == peers - 1, -(k & middle), k))
    for k in firsts:
        acc = late_rows(acc, ids[k], came[k], operator, k, F32)
    bit = 2
    while bit < peers:
        other = across(total, peers, bit)
        if 2 * bit == peers:
            total, acc = lax.optimization_barrier((total, acc))
        total = pair_sum(total, other, F32 if 2 * bit == peers else BF16)
        bit *= 2
    acc, total = lax.optimization_barrier((acc, total))
    part = late_rows(acc, ids[last], came[last], operator, last, BF16)
    input_grad, weight_grad = finish(
        part, ahead(part, "rep", reps, 1), total, ahead(total, "rep", reps, 1)
    )
    return (activated, input_grad, weight_grad)


def solution(mesh):
    placed = (
        P(("parts", "graph"), "feat", None),
        P(),
        P(("parts", "graph"), "feat", None),
        P(("parts", "graph", "rep"), None, None),
        P(("parts", "graph", "rep")),
        P(("parts", "graph", "rep")),
        P(("parts", "graph", "rep")),
    )
    return jax.shard_map(
        local,
        mesh=mesh,
        in_specs=placed,
        out_specs=(
            P(("parts", "graph"), "feat", None),
            P(("parts", "graph"), "feat", None),
            P("parts", "feat"),
        ),
        check_vma=False,
    )
```

```python
import functools

import jax
import jax.numpy as jnp
from jax import lax
from jax.experimental import pallas as pl
from jax.experimental.pallas import tpu as pltpu
from jax.sharding import PartitionSpec as P

CAP = 2
GROUP = 8
CHUNK = 16
SIDES = 1
PLACE_ROWS = 8
PLACE_BUFFER = 2 ** 22
TAIL = 16
VMEM_LIMIT = 40 * 2 ** 20
VMEM_MOST = 50 * 2 ** 20
VMEM_ALL = 58 * 2 ** 20

NT = (((1,), (1,)), ((), ()))
TN = (((0,), (0,)), ((), ()))
F32 = jnp.float32
BF16 = jnp.bfloat16


def vmem():
    return pl.BlockSpec(memory_space=pltpu.VMEM)


def smem():
    return pl.BlockSpec(memory_space=pltpu.SMEM)


def hbm():
    return pl.BlockSpec(memory_space=pltpu.HBM)


def shape(dims, dtype):
    return jax.ShapeDtypeStruct(tuple(dims), dtype)


def dot(a, b, dims=None):
    if dims is None:
        return jnp.dot(a, b, preferred_element_type=F32)
    return lax.dot_general(a, b, dims, preferred_element_type=F32)


def call(kernel, name, outs, in_specs, scratch=(), flops=0, moved=2 ** 18, limit=VMEM_LIMIT, **kwargs):
    return pl.pallas_call(
        kernel,
        out_shape=outs,
        in_specs=in_specs,
        scratch_shapes=list(scratch),
        compiler_params=pltpu.CompilerParams(vmem_limit_bytes=limit),
        cost_estimate=pl.CostEstimate(flops=flops, bytes_accessed=moved, transcendentals=0),
        name=name,
        **kwargs,
    )


def lanes(x3):
    return jnp.concatenate([x3[b] for b in range(x3.shape[0])], axis=1)


def places(peers, blocks_dev, row, col, table):
    me = lax.axis_index("graph")
    lane = lax.broadcasted_iota(jnp.int32, col.shape, 1)
    place = jnp.zeros(col.shape, jnp.int32)
    for k in range(peers):
        local = col - jnp.bitwise_xor(me, k) * blocks_dev
        inside = (local >= 0) & (local < blocks_dev)
        low = jnp.min(jnp.where(inside, local, blocks_dev - 1), axis=1, keepdims=True)
        high = jnp.max(jnp.where(inside, local, 0), axis=1, keepdims=True)
        table[PLACE_ROWS + k : PLACE_ROWS + k + 1, :] = jnp.where(lane == 0, low, high)
        slot = k * CAP + (local != low).astype(jnp.int32)
        place = jnp.where(inside, slot * blocks_dev + row, place)
    table[:PLACE_ROWS, :] = jnp.broadcast_to(place, (PLACE_ROWS, place.shape[1]))


def table_rows(peers):
    return PLACE_ROWS + -(-peers // 8) * 8


def prepare_kernel(peers, row_ref, col_ref, x3, half_out, table_out, table, half_sem, sem):
    share = half_out.shape[0]
    mine = pl.ds(lax.axis_index("rep") * share, share)
    half_copy = pltpu.make_async_copy(x3.at[mine], half_out, half_sem)
    half_copy.start()
    if table.shape[0] > PLACE_ROWS + peers:
        table[...] = jnp.zeros(table.shape, jnp.int32)
    places(peers, x3.shape[0], row_ref[...], col_ref[...], table)
    copy = pltpu.make_async_copy(table, table_out.at[pl.ds(0, table.shape[0])], sem)
    copy.start()
    half_copy.wait()
    copy.wait()


def prepare(features, tile_row, tile_col, peers, reps):
    per = tile_col.shape[0]
    blocks_dev, columns, width = features.shape
    return call(
        functools.partial(prepare_kernel, peers),
        "prepare",
        [shape((blocks_dev // reps, columns, width), BF16), shape((PLACE_BUFFER // (4 * per), per), jnp.int32)],
        [vmem()] * 3,
        [
            pltpu.VMEM((table_rows(peers), per), jnp.int32),
            pltpu.SemaphoreType.DMA,
            pltpu.SemaphoreType.DMA,
        ],
        limit=VMEM_ALL,
        out_specs=[hbm(), hbm()],
    )(tile_row.reshape(1, per), tile_col.reshape(1, per), features)


def pick(ids_ref, lane):
    ids = ids_ref[...].astype(F32)
    at = lax.broadcasted_iota(jnp.int32, ids.shape, 1)
    return jnp.max(jnp.where(at == lane, ids, 0.0)).astype(jnp.int32)


def operator_kernel(blocks_dev, slots_here, groups, count_ref, table_in, tiles_ref, m_ref, *refs):
    asks, (tiles, acc, place_ref, table, sems, sem, table_sem) = refs[:-7], refs[-7:]
    step = pl.program_id(0)
    per, width = tiles.shape[0], tiles.shape[1]
    chunks = per // CHUNK
    spare = slots_here * blocks_dev

    def chunk_copy(c):
        part = pl.ds(c * CHUNK, CHUNK)
        return pltpu.make_async_copy(tiles_ref.at[part], tiles.at[part], sems.at[c])

    def place_copy():
        return pltpu.make_async_copy(table_in.at[pl.ds(0, PLACE_ROWS)], place_ref, sem)

    def table_copy():
        return pltpu.make_async_copy(table_in.at[pl.ds(0, table.shape[0])], table, table_sem)

    @pl.when(step == 0)
    def _():
        place_copy().start()
        table_copy().start()
        for c in range(chunks):
            chunk_copy(c).start()

    acc[...] = jnp.zeros_like(acc)

    @pl.when(step == 0)
    def _():
        place_copy().wait()

    count = count_ref[0]

    def add_chunk(c, carry):
        @pl.when(step == 0)
        def _():
            chunk_copy(c).wait()

        for u in range(CHUNK):
            t = c * CHUNK + u
            place = place_ref[0, t]
            here = t < count
            if groups > 1:
                place = place - step * spare
                here = here & (place >= 0) & (place < spare)
            place = jnp.where(here, place, spare)
            side = u % SIDES
            acc[side, place] = acc[side, place] + tiles[t].astype(F32)
        return carry

    lax.fori_loop(0, chunks, add_chunk, 0)
    for s in range(slots_here):
        for r in range(blocks_dev):
            total = acc[0, s * blocks_dev + r]
            for side in range(1, SIDES):
                total = total + acc[side, s * blocks_dev + r]
            m_ref[r * width : (r + 1) * width, s * width : (s + 1) * width] = total.astype(BF16)

    @pl.when(step == 0)
    def _():
        table_copy().wait()
        for k, ask_ref in enumerate(asks):
            ask_ref[...] = table[PLACE_ROWS + k : PLACE_ROWS + k + 1, :]


def list_operator(tiles, table, tile_count, peers, blocks_dev):
    per, width = tiles.shape[0], tiles.shape[1]
    slots = peers * CAP
    slots_here = min(slots, GROUP)
    groups = slots // slots_here
    outs = call(
        functools.partial(operator_kernel, blocks_dev, slots_here, groups),
        "operator",
        [shape((blocks_dev * width, slots * width), BF16)] + [shape((1, per), jnp.int32)] * peers,
        [smem(), hbm(), hbm()],
        [
            pltpu.VMEM((per, width, width), BF16),
            pltpu.VMEM((SIDES, slots_here * blocks_dev + 1, width, width), F32),
            pltpu.SMEM((PLACE_ROWS, per), jnp.int32),
            pltpu.VMEM((table_rows(peers), per), jnp.int32),
            pltpu.SemaphoreType.DMA((per // CHUNK,)),
            pltpu.SemaphoreType.DMA,
            pltpu.SemaphoreType.DMA,
        ],
        moved=2 ** 24,
        limit=VMEM_MOST,
        grid=(groups,),
        out_specs=[pl.BlockSpec((blocks_dev * width, slots_here * width), lambda i: (0, i))] + [vmem()] * peers,
    )(tile_count, table, tiles)
    return outs[0], list(outs[1:])


def mirrored(near, m_ref, mir, slots, width):
    if slots <= GROUP:
        mir[...] = dot(near, m_ref[...])
    else:
        part = GROUP * width

        @pl.loop(0, slots // GROUP)
        def _(i):
            where = pl.ds(pl.multiple_of(i * part, part), part)
            mir[:, where] = dot(near, m_ref[:, where])


def first_sends_kernel(peers, *refs):
    ask_refs, refs = refs[: peers - 1], refs[peers - 1 :]
    x3, cot, m_ref, refs = refs[0], refs[1], refs[2], refs[3:]
    send_refs, self_ref, cot_ref, mir = refs[: peers - 1], refs[peers - 1], refs[peers], refs[peers + 1]
    _, columns, width = x3.shape
    share = cot_ref.shape[0]
    cot_ref[...] = cot[pl.ds(lax.axis_index("rep") * share, share)]
    both = CAP * width
    mirrored(lanes(x3), m_ref, mir, peers * CAP, width)
    self_ref[...] = mir[:, :both]
    lane = lax.broadcasted_iota(jnp.int32, (TAIL, both), 1)
    for k in range(1, peers):
        out = send_refs[k - 1]
        out[:columns, :] = mir[:, k * both : (k + 1) * both].astype(BF16)
        low, high = ask_refs[k - 1][:, :1], ask_refs[k - 1][:, 1:2]
        out[columns:, :] = jnp.where(lane < width, low, high).astype(F32).astype(BF16)


def first_sends(values, cotangent, operator, asks, peers, reps):
    blocks_dev, columns, width = values.shape
    outs = call(
        functools.partial(first_sends_kernel, peers),
        "first_sends",
        [shape((columns + TAIL, CAP * width), BF16)] * (peers - 1)
        + [shape((columns, CAP * width), F32), shape((blocks_dev // reps, columns, width), BF16)],
        [vmem()] * (peers + 2),
        [pltpu.VMEM((columns, peers * CAP * width), F32)],
        flops=2 ** 28,
        moved=2 ** 21,
    )(*asks, values, cotangent, operator)
    return [None] + list(outs[: peers - 1]), outs[peers - 1], outs[peers]


def add_sums(acc, block, sums):
    acc[block] = acc[block] + sums.astype(F32)


def own_rows(far, m_ref, k):
    both = far.shape[1]
    return dot(far, m_ref[:, k * both : (k + 1) * both], NT)


def put_rows(acc, own, before=None):
    blocks_dev, _, width = acc.shape
    for b in range(blocks_dev):
        add = own[:, b * width : (b + 1) * width]
        acc[b] = add if before is None else before[b] + add


def self_rows(x3, m_ref, ask_ref):
    far = jnp.concatenate([x3[pick(ask_ref, s)] for s in range(CAP)], axis=1)
    return own_rows(far, m_ref, 0)


def far_of(share, mine_ref, other_ref, ask_ref, at):
    first = lax.axis_index("rep") * share
    blocks = []
    for s in range(CAP):
        local = pick(ask_ref, s) - first
        own = (local >= 0) & (local < share)
        here = at * share + jnp.where(own, local, 0)
        there = at * share + jnp.where(own, 0, jnp.where(local < 0, local + share, local - share))
        blocks.append(jnp.where(own, mine_ref[here], other_ref[there]))
    return jnp.concatenate(blocks, axis=1)


def first_rows_kernel(peers, *refs):
    ask_ref, refs = refs[0], refs[1:]
    came_refs, refs = refs[: peers - 1], refs[peers - 1 :]
    x3, m_ref, self_ref, acc, ids_refs = refs[0], refs[1], refs[2], refs[3], refs[4:]
    _, columns, width = x3.shape
    put_rows(acc, self_rows(x3, m_ref, ask_ref))
    for s in range(CAP):
        add_sums(acc, pick(ask_ref, s), self_ref[:, s * width : (s + 1) * width])
    lane = lax.broadcasted_iota(jnp.int32, ids_refs[0].shape, 1)
    for k in range(1, peers):
        came = came_refs[k - 1]
        ids = jnp.zeros(lane.shape, jnp.int32)
        for s in range(CAP):
            here = slice(s * width, (s + 1) * width)
            asked = jnp.max(came[columns : columns + TAIL, here].astype(F32)).astype(jnp.int32)
            ids = jnp.where(lane == s, asked, ids)
            add_sums(acc, asked, came[:columns, here])
        ids_refs[k - 1][...] = ids


def first_rows(values, operator, ask, came, own_mirror, peers):
    _, columns, width = values.shape
    outs = call(
        functools.partial(first_rows_kernel, peers),
        "first_rows",
        [shape(values.shape, F32)] + [shape((1, width), jnp.int32)] * (peers - 1),
        [vmem()] * (peers + 3),
        flops=2 ** 27,
        moved=2 ** 20,
    )(ask, *came[1:], values, operator, own_mirror)
    return outs[0], [None] + list(outs[1:])


def below_kernel(sums_ref, half_ref, out_ref):
    top = sums_ref.shape[0]
    share, columns, width = half_ref.shape
    out_ref[:top, :] = sums_ref[...]
    for b in range(share):
        row, left = top + b // CAP * columns, b % CAP * width
        out_ref[row : row + columns, left : left + width] = half_ref[b]


def below(sums, half):
    share, columns, width = half.shape
    out = shape((sums.shape[0] + share // CAP * columns, sums.shape[1]), BF16)
    return call(below_kernel, "below", out, [vmem(), vmem()])(sums, half)


def stack_kernel(count, *refs):
    share = refs[0].shape[0]
    for k, ref in enumerate(refs[:count]):
        refs[-1][k * share : (k + 1) * share] = ref[...]


def stack(pieces, sums):
    share, columns, width = pieces[0].shape
    out = shape((len(pieces) * share, columns, width), BF16)
    kernel = functools.partial(stack_kernel, len(pieces))
    return call(kernel, "stack", out, [vmem()] * (len(pieces) + len(sums)), flops=2 ** 31)(*pieces, *sums)


def stack_more_kernel(first_ref, *refs):
    out_ref = refs[-1]
    at, columns, width = first_ref.shape
    out_ref[:at] = first_ref[...]
    for ref in refs[:-1]:
        share = (ref.shape[0] - TAIL) // columns * CAP - CAP
        for b in range(share):
            row, left = columns + TAIL + b // CAP * columns, b % CAP * width
            out_ref[at + b] = ref[row : row + columns, left : left + width]
        at += share


def stack_more(first, chunks):
    at, columns, width = first.shape
    share = (chunks[0].shape[0] - TAIL) // columns * CAP - CAP
    out = shape((at + len(chunks) * share, columns, width), BF16)
    return call(stack_more_kernel, "stack_more", out, [vmem()] * (1 + len(chunks)))(first, *chunks)


def half_rows(before, far_ref, m_ref, first, share):
    columns, width = before.shape[1:]
    both = CAP * width
    rows = pl.ds(pl.multiple_of(first * width, share * width), share * width)
    if m_ref.shape[1] <= GROUP * width:
        own = dot(far_ref[:, both:], m_ref[rows, both:], NT)
    else:

        def add_peer(k, total):
            here = pl.ds(pl.multiple_of(k * both, both), both)
            return total + dot(far_ref[:, here], m_ref[rows, here], NT)

        zeros = jnp.zeros((columns, share * width), F32)
        own = lax.fori_loop(1, m_ref.shape[1] // both, add_peer, zeros)
    return [before[first + b] + own[:, b * width : (b + 1) * width] for b in range(share)]


def give_rows_kernel(peers, *refs):
    ask_refs, refs = refs[: peers - 1], refs[peers - 1 :]
    before, mine_ref, other_ref, m_ref, give_ref, far_ref = refs
    share = give_ref.shape[0]
    both = CAP * before.shape[2]
    for k in range(1, peers):
        far_ref[:, k * both : (k + 1) * both] = far_of(share, mine_ref, other_ref, ask_refs[k - 1], k - 1)
    far_ref[:, :both] = jnp.zeros((far_ref.shape[0], both), BF16)
    rows = half_rows(before, far_ref, m_ref, (1 - lax.axis_index("rep")) * share, share)
    for b in range(share):
        give_ref[b] = rows[b].astype(BF16)


def give_rows(before, asks, mine, other, operator, peers, reps):
    blocks_dev, columns, width = before.shape
    return call(
        functools.partial(give_rows_kernel, peers),
        "give_rows",
        [shape((blocks_dev // reps, columns, width), BF16), shape((columns, peers * CAP * width), BF16)],
        [vmem()] * (peers + 3),
        flops=2 ** 27,
        moved=2 ** 20,
    )(*asks[1:], before, mine, other, operator)


def keep_rows_kernel(before, far_ref, m_ref, keep_ref):
    share = keep_ref.shape[0]
    rows = half_rows(before, far_ref, m_ref, lax.axis_index("rep") * share, share)
    for b in range(share):
        keep_ref[b] = rows[b]


def keep_rows(before, far, operator, reps):
    blocks_dev, columns, width = before.shape
    return call(
        keep_rows_kernel,
        "keep_rows",
        shape((blocks_dev // reps, columns, width), F32),
        [vmem()] * 3,
        flops=2 ** 27,
        moved=2 ** 20,
    )(before, far, operator)


def late_self_kernel(ask_ref, x3, self_ref, m_ref, act_ref, shared_ref, acc, out_ref):
    width = x3.shape[2]
    put_rows(acc, self_rows(x3, m_ref, ask_ref))
    for s in range(CAP):
        add_sums(acc, pick(ask_ref, s), self_ref[:, s * width : (s + 1) * width])
    half = lax.axis_index("rep")
    blocks = act_ref.shape[0]
    out_ref[pl.ds(half * blocks, blocks)] = act_ref[...]
    for b in range(blocks):
        at = (blocks + b) * width
        out_ref[(1 - half) * blocks + b] = shared_ref[:, at : at + width]


def late_self(ask, values, own_mirror, operator, act, shared):
    return call(
        late_self_kernel,
        "late_self",
        [shape(values.shape, F32), shape(values.shape, BF16)],
        [vmem()] * 6,
        flops=2 ** 26,
    )(ask, values, own_mirror, operator, act, shared)


def late_rows_kernel(k, before, ids_ref, came_ref, m_ref, out_ref, acc):
    width = acc.shape[2]
    both = CAP * width
    put_rows(acc, own_rows(came_ref[:, both : 2 * both], m_ref, k), before)
    for s in range(CAP):
        add_sums(acc, pick(ids_ref, s), came_ref[:, s * width : (s + 1) * width])
    out_ref[...] = acc[...].astype(out_ref.dtype)


def late_rows(before, ids, came, operator, k, dtype):
    return call(
        functools.partial(late_rows_kernel, k),
        "late_rows",
        shape(before.shape, dtype),
        [vmem()] * 4,
        [pltpu.VMEM(before.shape, F32)],
        flops=2 ** 26,
    )(before, ids, came, operator)


def add_kernel(keep_ref, came_ref, out_ref):
    out_ref[...] = (keep_ref[...] + came_ref[...].astype(F32)).astype(BF16)


def add_up(keep, came):
    return call(add_kernel, "add_up", shape(came.shape, BF16), [vmem(), vmem()])(keep, came)


def widen_kernel(feats, *refs):
    out_ref = refs[feats]
    share, columns, width = refs[0].shape
    me = lax.axis_index("feat")
    for q in range(feats):
        rows = pl.ds(pl.multiple_of(lax.rem(me + q, feats) * columns, columns), columns)
        for b in range(share):
            out_ref[rows, b * width : (b + 1) * width] = refs[q][b]


def widen(parts):
    share, columns, width = parts[0].shape
    out = shape((len(parts) * columns, share * width), BF16)
    return call(functools.partial(widen_kernel, len(parts)), "widen", out, [vmem()] * len(parts))(*parts)


def dense_kernel(feats, *refs):
    sums, wide_cot, refs = refs[:feats], refs[feats], refs[feats + 1 :]
    w_ref, act_ref, give_ref, spread_ref, term_ref, wide, pre_scr, grad = refs
    share, columns, width = act_ref.shape
    me = lax.axis_index("feat")
    rows = [pl.ds(pl.multiple_of(lax.rem(me + q, feats) * columns, columns), columns) for q in range(feats)]
    for q in range(feats):
        for b in range(share):
            wide[rows[q], b * width : (b + 1) * width] = sums[q][b]
    pre = dot(w_ref[...], wide[...], TN)
    pre_scr[...] = pre
    sig = jax.nn.sigmoid(pre)
    factor = wide_cot[...].astype(F32) * sig * (1.0 + pre * (1.0 - sig))
    grad[...] = factor.astype(BF16)
    spread = dot(w_ref[rows[0], :], grad[...]).astype(BF16)
    term_ref[...] = dot(grad[rows[0], :], wide[...], NT)
    wide_share = share * width
    give_ref[:, :wide_share] = spread
    for b in range(share):
        spread_ref[b] = spread[:, b * width : (b + 1) * width]
    own = pre_scr[rows[0], :]
    act = (own * jax.nn.sigmoid(own)).astype(BF16)
    give_ref[:, wide_share:] = act
    for b in range(share):
        act_ref[b] = act[:, b * width : (b + 1) * width]


def dense(sums, cot, weight, feats):
    share, columns, width = sums[0].shape
    features = weight.shape[0]
    return call(
        functools.partial(dense_kernel, feats),
        "dense",
        [
            shape((share, columns, width), BF16),
            shape((columns, 2 * share * width), BF16),
            shape((share, columns, width), BF16),
            shape((columns, features), F32),
        ],
        [vmem()] * (feats + 2),
        [
            pltpu.VMEM((features, share * width), BF16),
            pltpu.VMEM((features, share * width), F32),
            pltpu.VMEM((features, share * width), BF16),
        ],
        flops=2 ** 28,
        moved=2 ** 20,
    )(*sums, cot, weight)


def send_kernel(peers, *refs):
    ids_refs, refs = refs[: peers - 1], refs[peers - 1 :]
    mine_ref, came_ref, m_ref, refs = refs[0], refs[1], refs[2], refs[3:]
    x3, refs = refs[0], refs[1:]
    send_refs, refs = refs[: peers - 1], refs[peers - 1 :]
    self_ref, mir = refs
    share, _, width = mine_ref.shape
    both = CAP * width
    half = lax.axis_index("rep")
    x3[pl.ds(half * share, share)] = mine_ref[...]
    for b in range(share):
        x3[(1 - half) * share + b] = came_ref[:, b * width : (b + 1) * width]
    mirrored(lanes(x3), m_ref, mir, peers * CAP, width)
    self_ref[...] = mir[:, :both]
    for k in range(1, peers):
        out = send_refs[k - 1]
        out[:, :both] = mir[:, k * both : (k + 1) * both].astype(BF16)
        for s in range(CAP):
            at = (CAP + s) * width
            out[:, at : at + width] = x3[pick(ids_refs[k - 1], s)]


def sends_of(mine, came, operator, ids, peers, reps):
    share, columns, width = mine.shape
    chunk = 2 * CAP * width
    outs = call(
        functools.partial(send_kernel, peers),
        "sends",
        [shape((share * reps, columns, width), BF16)]
        + [shape((columns, chunk), BF16)] * (peers - 1)
        + [shape((columns, CAP * width), F32)],
        [vmem()] * (peers + 2),
        [pltpu.VMEM((columns, peers * CAP * width), F32)],
        flops=2 ** 28,
        moved=2 ** 21,
    )(*ids[1:], mine, came, operator)
    return outs[0], [None] + list(outs[1:peers]), outs[peers]


def pair_kernel(mine_ref, came_ref, out_ref):
    out_ref[...] = (mine_ref[...].astype(F32) + came_ref[...].astype(F32)).astype(out_ref.dtype)


def pair_sum(mine, came, dtype):
    return call(pair_kernel, "pair_sum", shape(mine.shape, dtype), [vmem(), vmem()])(mine, came)


def split_kernel(mine_ref, came_ref, give_ref, keep_ref, total):
    half = lax.axis_index("rep")
    part = keep_ref.shape[1]
    total[...] = mine_ref[...].astype(F32) + came_ref[...].astype(F32)
    give_ref[...] = total[:, pl.ds(pl.multiple_of((1 - half) * part, part), part)].astype(BF16)
    keep_ref[...] = total[:, pl.ds(pl.multiple_of(half * part, part), part)]


def split_sum(mine, came, reps):
    columns, features = mine.shape
    part = (columns, features // reps)
    return call(
        split_kernel,
        "split_sum",
        [shape(part, BF16), shape(part, F32)],
        [vmem()] * 2,
        [pltpu.VMEM(mine.shape, F32)],
    )(mine, came)


def pair_term(term, peers, reps):
    give, total = split_sum(term, across(term, peers, 1), reps)
    total = pair_sum(total, ahead(give, "rep", reps, 1), F32 if peers == 2 else BF16)
    return total


def finish_kernel(mine_ref, other_ref, share_ref, other_share_ref, grad_ref, weight_ref):
    half = lax.axis_index("rep")
    share = share_ref.shape[1]
    grad_ref[...] = (mine_ref[...].astype(F32) + other_ref[...].astype(F32)).astype(BF16)
    weight_ref[pl.ds(pl.multiple_of(half * share, share), share), :] = share_ref[...].T
    weight_ref[pl.ds(pl.multiple_of((1 - half) * share, share), share), :] = other_share_ref[...].T


def finish(mine, other, share, other_share):
    columns, width = share.shape
    return call(
        finish_kernel,
        "finish",
        [shape(mine.shape, BF16), shape((2 * width, columns), F32)],
        [vmem()] * 4,
    )(mine, other, share, other_share)


def ahead(value, axis, size, k):
    return lax.ppermute(value, axis, [(i, (i + k) % size) for i in range(size)])


def across(value, peers, k):
    return lax.ppermute(value, "graph", [(i, i ^ k) for i in range(peers)])


def after(value, first):
    return lax.optimization_barrier((value, first))[0]


def local(features, weight, cotangent, tiles, tile_row, tile_col, tile_count):
    blocks_dev, _, width = features.shape
    peers = lax.axis_size("graph")
    feats = lax.axis_size("feat")
    reps = lax.axis_size("rep")
    far_first = sorted(range(1, peers), key=lambda k: (-(k & (peers // 2)), k))

    half, table = prepare(features, tile_row, tile_col, peers, reps)
    operator, asks = list_operator(tiles, table, tile_count, peers, blocks_dev)
    sends, own_mirror, own_cot = first_sends(features, cotangent, operator, asks[1:], peers, reps)
    middle = peers // 2
    pieces = [across(half, peers, j) for j in range(1, middle)]
    crossed = across(half, peers, middle)
    came = [None] * peers
    for k in far_first:
        if k >= middle:
            came[k] = across(sends[k], peers, k)
    for j in range(1, middle):
        chunk, pieces[j - 1] = lax.optimization_barrier((below(sends[j], crossed), pieces[j - 1]))
        came[j] = across(chunk, peers, j)
    held = after(own_cot, crossed)
    cots = [own_cot] + [ahead(held, "feat", feats, feats - q) for q in range(1, feats)]
    stacked = stack(pieces + [crossed], came[middle:])
    came[1:middle], stacked = lax.optimization_barrier((came[1:middle], stacked))
    stacked, cots = lax.optimization_barrier((stacked, cots))
    stacked = stack_more(stacked, came[1:middle])
    swapped = ahead(stacked, "rep", reps, 1)
    acc, ids = first_rows(features, operator, asks[0], came, own_mirror, peers)
    give, asked = give_rows(acc, asks, stacked, swapped, operator, peers, reps)
    keep = keep_rows(acc, asked, operator, reps)

    mine = add_up(keep, ahead(give, "rep", reps, 1))
    cot = widen(cots)
    sums = [mine] + [ahead(mine, "feat", feats, feats - q) for q in range(1, feats)]
    act, give, spread, term = dense(sums, cot, weight, feats)
    shared = ahead(give, "rep", reps, 1)
    total = pair_term(term, peers, reps)
    values, sends, own_mirror = sends_of(spread, shared, operator, ids, peers, reps)

    came = [None] * peers
    for k in far_first:
        came[k] = across(sends[k], peers, k)
    acc, activated = late_self(asks[0], values, own_mirror, operator, act, shared)
    *firsts, last = sorted(range(1, peers), key=lambda k: (k == peers - 1, -(k & middle), k))
    for k in firsts:
        acc = late_rows(acc, ids[k], came[k], operator, k, F32)
    bit = 2
    while bit < peers:
        other = across(total, peers, bit)
        if 2 * bit == peers:
            total, acc = lax.optimization_barrier((total, acc))
        total = pair_sum(total, other, F32 if 2 * bit == peers else BF16)
        bit *= 2
    acc, total = lax.optimization_barrier((acc, total))
    part = late_rows(acc, ids[last], came[last], operator, last, BF16)
    input_grad, weight_grad = finish(
        part, ahead(part, "rep", reps, 1), total, ahead(total, "rep", reps, 1)
    )
    return (activated, input_grad, weight_grad)


def solution(mesh):
    placed = (
        P(("parts", "graph"), "feat", None),
        P(),
        P(("parts", "graph"), "feat", None),
        P(("parts", "graph", "rep"), None, None),
        P(("parts", "graph", "rep")),
        P(("parts", "graph", "rep")),
        P(("parts", "graph", "rep")),
    )
    return jax.shard_map(
        local,
        mesh=mesh,
        in_specs=placed,
        out_specs=(
            P(("parts", "graph"), "feat", None),
            P(("parts", "graph"), "feat", None),
            P("parts", "feat"),
        ),
        check_vma=False,
    )
```

```python
import functools

import jax
import jax.numpy as jnp
from jax import lax
from jax.experimental import pallas as pl
from jax.experimental.pallas import tpu as pltpu
from jax.sharding import PartitionSpec as P

CAP = 2
GROUP = 8
CHUNK = 16
SIDES = 1
PLACE_ROWS = 8
PLACE_BUFFER = 2 ** 22
TAIL = 16
VMEM_LIMIT = 40 * 2 ** 20
VMEM_MOST = 50 * 2 ** 20
VMEM_ALL = 58 * 2 ** 20

NT = (((1,), (1,)), ((), ()))
TN = (((0,), (0,)), ((), ()))
F32 = jnp.float32
BF16 = jnp.bfloat16


def vmem():
    return pl.BlockSpec(memory_space=pltpu.VMEM)


def smem():
    return pl.BlockSpec(memory_space=pltpu.SMEM)


def hbm():
    return pl.BlockSpec(memory_space=pltpu.HBM)


def shape(dims, dtype):
    return jax.ShapeDtypeStruct(tuple(dims), dtype)


def dot(a, b, dims=None):
    if dims is None:
        return jnp.dot(a, b, preferred_element_type=F32)
    return lax.dot_general(a, b, dims, preferred_element_type=F32)


def call(kernel, name, outs, in_specs, scratch=(), flops=0, moved=2 ** 18, limit=VMEM_LIMIT, **kwargs):
    return pl.pallas_call(
        kernel,
        out_shape=outs,
        in_specs=in_specs,
        scratch_shapes=list(scratch),
        compiler_params=pltpu.CompilerParams(vmem_limit_bytes=limit),
        cost_estimate=pl.CostEstimate(flops=flops, bytes_accessed=moved, transcendentals=0),
        name=name,
        **kwargs,
    )


def lanes(x3):
    return jnp.concatenate([x3[b] for b in range(x3.shape[0])], axis=1)


def places(peers, blocks_dev, row, col, table):
    me = lax.axis_index("graph")
    lane = lax.broadcasted_iota(jnp.int32, col.shape, 1)
    place = jnp.zeros(col.shape, jnp.int32)
    for k in range(peers):
        local = col - jnp.bitwise_xor(me, k) * blocks_dev
        inside = (local >= 0) & (local < blocks_dev)
        low = jnp.min(jnp.where(inside, local, blocks_dev - 1), axis=1, keepdims=True)
        high = jnp.max(jnp.where(inside, local, 0), axis=1, keepdims=True)
        table[PLACE_ROWS + k : PLACE_ROWS + k + 1, :] = jnp.where(lane == 0, low, high)
        slot = k * CAP + (local != low).astype(jnp.int32)
        place = jnp.where(inside, slot * blocks_dev + row, place)
    table[:PLACE_ROWS, :] = jnp.broadcast_to(place, (PLACE_ROWS, place.shape[1]))


def table_rows(peers):
    return PLACE_ROWS + -(-peers // 8) * 8


def prepare_kernel(peers, row_ref, col_ref, x3, half_out, table_out, table, half_sem, sem):
    share = half_out.shape[0]
    mine = pl.ds(lax.axis_index("rep") * share, share)
    half_copy = pltpu.make_async_copy(x3.at[mine], half_out, half_sem)
    half_copy.start()
    if table.shape[0] > PLACE_ROWS + peers:
        table[...] = jnp.zeros(table.shape, jnp.int32)
    places(peers, x3.shape[0], row_ref[...], col_ref[...], table)
    copy = pltpu.make_async_copy(table, table_out.at[pl.ds(0, table.shape[0])], sem)
    copy.start()
    half_copy.wait()
    copy.wait()


def prepare(features, tile_row, tile_col, peers, reps):
    per = tile_col.shape[0]
    blocks_dev, columns, width = features.shape
    return call(
        functools.partial(prepare_kernel, peers),
        "prepare",
        [shape((blocks_dev // reps, columns, width), BF16), shape((PLACE_BUFFER // (4 * per), per), jnp.int32)],
        [vmem()] * 3,
        [
            pltpu.VMEM((table_rows(peers), per), jnp.int32),
            pltpu.SemaphoreType.DMA,
            pltpu.SemaphoreType.DMA,
        ],
        limit=VMEM_ALL,
        out_specs=[hbm(), hbm()],
    )(tile_row.reshape(1, per), tile_col.reshape(1, per), features)


def pick(ids_ref, lane):
    ids = ids_ref[...].astype(F32)
    at = lax.broadcasted_iota(jnp.int32, ids.shape, 1)
    return jnp.max(jnp.where(at == lane, ids, 0.0)).astype(jnp.int32)


def operator_kernel(blocks_dev, slots_here, groups, count_ref, table_in, tiles_ref, m_ref, *refs):
    asks, (tiles, acc, place_ref, table, sems, sem, table_sem) = refs[:-7], refs[-7:]
    step = pl.program_id(0)
    per, width = tiles.shape[0], tiles.shape[1]
    chunks = per // CHUNK
    spare = slots_here * blocks_dev

    def chunk_copy(c):
        part = pl.ds(c * CHUNK, CHUNK)
        return pltpu.make_async_copy(tiles_ref.at[part], tiles.at[part], sems.at[c])

    def place_copy():
        return pltpu.make_async_copy(table_in.at[pl.ds(0, PLACE_ROWS)], place_ref, sem)

    def table_copy():
        return pltpu.make_async_copy(table_in.at[pl.ds(0, table.shape[0])], table, table_sem)

    @pl.when(step == 0)
    def _():
        place_copy().start()
        table_copy().start()
        for c in range(chunks):
            chunk_copy(c).start()

    acc[...] = jnp.zeros_like(acc)

    @pl.when(step == 0)
    def _():
        place_copy().wait()

    count = count_ref[0]

    def add_chunk(c, carry):
        @pl.when(step == 0)
        def _():
            chunk_copy(c).wait()

        for u in range(CHUNK):
            t = c * CHUNK + u
            place = place_ref[0, t]
            here = t < count
            if groups > 1:
                place = place - step * spare
                here = here & (place >= 0) & (place < spare)
            place = jnp.where(here, place, spare)
            side = u % SIDES
            acc[side, place] = acc[side, place] + tiles[t].astype(F32)
        return carry

    lax.fori_loop(0, chunks, add_chunk, 0)
    for s in range(slots_here):
        for r in range(blocks_dev):
            total = acc[0, s * blocks_dev + r]
            for side in range(1, SIDES):
                total = total + acc[side, s * blocks_dev + r]
            m_ref[r * width : (r + 1) * width, s * width : (s + 1) * width] = total.astype(BF16)

    @pl.when(step == 0)
    def _():
        table_copy().wait()
        for k, ask_ref in enumerate(asks):
            ask_ref[...] = table[PLACE_ROWS + k : PLACE_ROWS + k + 1, :]

    rows = blocks_dev * width
    for s in range(slots_here):
        row = PLACE_ROWS + (step * slots_here + s) // CAP
        block = table[pl.ds(row, 1), s % CAP : s % CAP + 1].astype(F32).astype(BF16)
        m_ref[rows:, s * width : (s + 1) * width] = jnp.broadcast_to(block, (TAIL, width))


def list_operator(tiles, table, tile_count, peers, blocks_dev):
    per, width = tiles.shape[0], tiles.shape[1]
    slots = peers * CAP
    slots_here = min(slots, GROUP)
    groups = slots // slots_here
    outs = call(
        functools.partial(operator_kernel, blocks_dev, slots_here, groups),
        "operator",
        [shape((blocks_dev * width + TAIL, slots * width), BF16)] + [shape((1, per), jnp.int32)] * peers,
        [smem(), hbm(), hbm()],
        [
            pltpu.VMEM((per, width, width), BF16),
            pltpu.VMEM((SIDES, slots_here * blocks_dev + 1, width, width), F32),
            pltpu.SMEM((PLACE_ROWS, per), jnp.int32),
            pltpu.VMEM((table_rows(peers), per), jnp.int32),
            pltpu.SemaphoreType.DMA((per // CHUNK,)),
            pltpu.SemaphoreType.DMA,
            pltpu.SemaphoreType.DMA,
        ],
        moved=2 ** 24,
        limit=VMEM_MOST,
        grid=(groups,),
        out_specs=[pl.BlockSpec((blocks_dev * width + TAIL, slots_here * width), lambda i: (0, i))] + [vmem()] * peers,
    )(tile_count, table, tiles)
    return outs[0], list(outs[1:])


def mirrored(near, m_ref, mir, slots, width):
    if slots <= GROUP:
        mir[...] = dot(near, m_ref[: near.shape[1], :])
    else:
        part = GROUP * width

        @pl.loop(0, slots // GROUP)
        def _(i):
            where = pl.ds(pl.multiple_of(i * part, part), part)
            mir[:, where] = dot(near, m_ref[: near.shape[1], where])


def first_sends_kernel(peers, *refs):
    ask_refs, refs = refs[: peers - 1], refs[peers - 1 :]
    x3, cot, m_ref, refs = refs[0], refs[1], refs[2], refs[3:]
    send_refs, self_ref, cot_ref, mir = refs[: peers - 1], refs[peers - 1], refs[peers], refs[peers + 1]
    _, columns, width = x3.shape
    share = cot_ref.shape[0]
    cot_ref[...] = cot[pl.ds(lax.axis_index("rep") * share, share)]
    both = CAP * width
    mirrored(lanes(x3), m_ref, mir, peers * CAP, width)
    self_ref[...] = mir[:, :both]
    lane = lax.broadcasted_iota(jnp.int32, (TAIL, both), 1)
    for k in range(1, peers):
        out = send_refs[k - 1]
        out[:columns, :] = mir[:, k * both : (k + 1) * both].astype(BF16)
        low, high = ask_refs[k - 1][:, :1], ask_refs[k - 1][:, 1:2]
        out[columns:, :] = jnp.where(lane < width, low, high).astype(F32).astype(BF16)


def first_sends(values, cotangent, operator, asks, peers, reps):
    blocks_dev, columns, width = values.shape
    outs = call(
        functools.partial(first_sends_kernel, peers),
        "first_sends",
        [shape((columns + TAIL, CAP * width), BF16)] * (peers - 1)
        + [shape((columns, CAP * width), F32), shape((blocks_dev // reps, columns, width), BF16)],
        [vmem()] * (peers + 2),
        [pltpu.VMEM((columns, peers * CAP * width), F32)],
        flops=2 ** 28,
        moved=2 ** 21,
    )(*asks, values, cotangent, operator)
    return [None] + list(outs[: peers - 1]), outs[peers - 1], outs[peers]


def add_sums(acc, block, sums):
    acc[block] = acc[block] + sums.astype(F32)


def own_rows(far, m_ref, k):
    both = far.shape[1]
    return dot(far, m_ref[: m_ref.shape[0] - TAIL, k * both : (k + 1) * both], NT)


def put_rows(acc, own, before=None):
    blocks_dev, _, width = acc.shape
    for b in range(blocks_dev):
        add = own[:, b * width : (b + 1) * width]
        acc[b] = add if before is None else before[b] + add


def self_rows(x3, m_ref, ask_ref):
    far = jnp.concatenate([x3[pick(ask_ref, s)] for s in range(CAP)], axis=1)
    return own_rows(far, m_ref, 0)


def far_of(share, mine_ref, asked, at):
    first = lax.axis_index("rep") * share
    blocks = []
    for block in asked:
        local = block - first
        own = (local >= 0) & (local < share)
        blocks.append(jnp.where(own, mine_ref[at * share + jnp.where(own, local, 0)], jnp.bfloat16(0)))
    return jnp.concatenate(blocks, axis=1)


def first_rows_kernel(peers, *refs):
    ask_ref, refs = refs[0], refs[1:]
    came_refs, refs = refs[: peers - 1], refs[peers - 1 :]
    x3, m_ref, self_ref, acc, ids_refs = refs[0], refs[1], refs[2], refs[3], refs[4:]
    _, columns, width = x3.shape
    put_rows(acc, self_rows(x3, m_ref, ask_ref))
    for s in range(CAP):
        add_sums(acc, pick(ask_ref, s), self_ref[:, s * width : (s + 1) * width])
    lane = lax.broadcasted_iota(jnp.int32, ids_refs[0].shape, 1)
    for k in range(1, peers):
        came = came_refs[k - 1]
        ids = jnp.zeros(lane.shape, jnp.int32)
        for s in range(CAP):
            here = slice(s * width, (s + 1) * width)
            asked = jnp.max(came[columns : columns + TAIL, here].astype(F32)).astype(jnp.int32)
            ids = jnp.where(lane == s, asked, ids)
            add_sums(acc, asked, came[:columns, here])
        ids_refs[k - 1][...] = ids


def first_rows(values, operator, ask, came, own_mirror, peers):
    _, columns, width = values.shape
    outs = call(
        functools.partial(first_rows_kernel, peers),
        "first_rows",
        [shape(values.shape, F32)] + [shape((1, width), jnp.int32)] * (peers - 1),
        [vmem()] * (peers + 3),
        flops=2 ** 27,
        moved=2 ** 20,
    )(ask, *came[1:], values, operator, own_mirror)
    return outs[0], [None] + list(outs[1:])


def below_kernel(sums_ref, half_ref, out_ref):
    top = sums_ref.shape[0]
    share, columns, width = half_ref.shape
    out_ref[:top, :] = sums_ref[...]
    for b in range(share):
        row, left = top + b // CAP * columns, b % CAP * width
        out_ref[row : row + columns, left : left + width] = half_ref[b]


def below(sums, half):
    share, columns, width = half.shape
    out = shape((sums.shape[0] + share // CAP * columns, sums.shape[1]), BF16)
    return call(below_kernel, "below", out, [vmem(), vmem()])(sums, half)


def stack_kernel(count, *refs):
    share = refs[0].shape[0]
    for k, ref in enumerate(refs[:count]):
        refs[-1][k * share : (k + 1) * share] = ref[...]


def stack(pieces, sums):
    share, columns, width = pieces[0].shape
    out = shape((len(pieces) * share, columns, width), BF16)
    kernel = functools.partial(stack_kernel, len(pieces))
    return call(kernel, "stack", out, [vmem()] * (len(pieces) + len(sums)), flops=2 ** 36)(*pieces, *sums)


def stack_more_kernel(first_ref, *refs):
    out_ref = refs[-1]
    at, columns, width = first_ref.shape
    out_ref[:at] = first_ref[...]
    for ref in refs[:-1]:
        share = (ref.shape[0] - TAIL) // columns * CAP - CAP
        for b in range(share):
            row, left = columns + TAIL + b // CAP * columns, b % CAP * width
            out_ref[at + b] = ref[row : row + columns, left : left + width]
        at += share


def stack_more(first, chunks):
    at, columns, width = first.shape
    share = (chunks[0].shape[0] - TAIL) // columns * CAP - CAP
    out = shape((at + len(chunks) * share, columns, width), BF16)
    return call(stack_more_kernel, "stack_more", out, [vmem()] * (1 + len(chunks)))(first, *chunks)


def half_rows(before, far_refs, m_refs, first, share):
    columns, width = before.shape[1:]
    both = CAP * width
    rows = pl.ds(pl.multiple_of(first * width, share * width), share * width)
    slots_wide = m_refs[0].shape[1]
    own = jnp.zeros((columns, share * width), F32)
    for far_ref, m_ref in zip(far_refs, m_refs):
        if slots_wide <= GROUP * width:
            own = own + dot(far_ref[:, both:], m_ref[rows, both:], NT)
        else:

            def add_peer(k, total):
                here = pl.ds(pl.multiple_of(k * both, both), both)
                return total + dot(far_ref[:, here], m_ref[rows, here], NT)

            own = lax.fori_loop(1, slots_wide // both, add_peer, own)
    return [before[first + b] + own[:, b * width : (b + 1) * width] for b in range(share)]


def give_rows_kernel(peers, *refs):
    ask_refs, refs = refs[: peers - 1], refs[peers - 1 :]
    before, mine_ref, m_ref, other_m_ref, give_ref, far_ref, other_far_ref = refs
    share, columns, width = give_ref.shape
    both = CAP * width
    tail = m_ref.shape[0] - TAIL
    for k in range(1, peers):
        here = slice(k * both, (k + 1) * both)
        asked = [pick(ask_refs[k - 1], s) for s in range(CAP)]
        far_ref[:, here] = far_of(share, mine_ref, asked, k - 1)
        marks = [other_m_ref[tail:, k * both + s * width : k * both + (s + 1) * width] for s in range(CAP)]
        asked = [jnp.max(mark.astype(F32)).astype(jnp.int32) for mark in marks]
        other_far_ref[:, here] = far_of(share, mine_ref, asked, k - 1)
    far_ref[:, :both] = jnp.zeros((columns, both), BF16)
    other_far_ref[:, :both] = jnp.zeros((columns, both), BF16)
    first = (1 - lax.axis_index("rep")) * share
    rows = half_rows(before, [far_ref, other_far_ref], [m_ref, other_m_ref], first, share)
    for b in range(share):
        give_ref[b] = rows[b].astype(BF16)


def give_rows(before, asks, mine, operator, other_operator, peers, reps):
    blocks_dev, columns, width = before.shape
    far = shape((columns, peers * CAP * width), BF16)
    return call(
        functools.partial(give_rows_kernel, peers),
        "give_rows",
        [shape((blocks_dev // reps, columns, width), BF16), far, far],
        [vmem()] * (peers + 3),
        flops=2 ** 27,
        moved=2 ** 20,
    )(*asks[1:], before, mine, operator, other_operator)


def keep_rows_kernel(before, far_ref, other_far_ref, m_ref, other_m_ref, keep_ref):
    share = keep_ref.shape[0]
    first = lax.axis_index("rep") * share
    rows = half_rows(before, [far_ref, other_far_ref], [m_ref, other_m_ref], first, share)
    for b in range(share):
        keep_ref[b] = rows[b]


def keep_rows(before, far, other_far, operator, other_operator, reps):
    blocks_dev, columns, width = before.shape
    return call(
        keep_rows_kernel,
        "keep_rows",
        shape((blocks_dev // reps, columns, width), F32),
        [vmem()] * 5,
        flops=2 ** 27,
        moved=2 ** 20,
    )(before, far, other_far, operator, other_operator)


def late_self_kernel(ask_ref, x3, self_ref, m_ref, act_ref, shared_ref, acc, out_ref):
    width = x3.shape[2]
    put_rows(acc, self_rows(x3, m_ref, ask_ref))
    for s in range(CAP):
        add_sums(acc, pick(ask_ref, s), self_ref[:, s * width : (s + 1) * width])
    half = lax.axis_index("rep")
    blocks = act_ref.shape[0]
    out_ref[pl.ds(half * blocks, blocks)] = act_ref[...]
    for b in range(blocks):
        at = (blocks + b) * width
        out_ref[(1 - half) * blocks + b] = shared_ref[:, at : at + width]


def late_self(ask, values, own_mirror, operator, act, shared):
    return call(
        late_self_kernel,
        "late_self",
        [shape(values.shape, F32), shape(values.shape, BF16)],
        [vmem()] * 6,
        flops=2 ** 26,
    )(ask, values, own_mirror, operator, act, shared)


def late_rows_kernel(k, before, ids_ref, came_ref, m_ref, out_ref, acc):
    width = acc.shape[2]
    both = CAP * width
    put_rows(acc, own_rows(came_ref[:, both : 2 * both], m_ref, k), before)
    for s in range(CAP):
        add_sums(acc, pick(ids_ref, s), came_ref[:, s * width : (s + 1) * width])
    out_ref[...] = acc[...].astype(out_ref.dtype)


def late_rows(before, ids, came, operator, k, dtype):
    return call(
        functools.partial(late_rows_kernel, k),
        "late_rows",
        shape(before.shape, dtype),
        [vmem()] * 4,
        [pltpu.VMEM(before.shape, F32)],
        flops=2 ** 26,
    )(before, ids, came, operator)


def add_kernel(keep_ref, came_ref, out_ref):
    out_ref[...] = (keep_ref[...] + came_ref[...].astype(F32)).astype(BF16)


def add_up(keep, came):
    return call(add_kernel, "add_up", shape(came.shape, BF16), [vmem(), vmem()])(keep, came)


def widen_kernel(feats, in_ref, out_ref):
    _, columns, width = in_ref.shape
    share = out_ref.shape[1] // width
    for f in range(feats):
        for b in range(share):
            out_ref[f * columns : (f + 1) * columns, b * width : (b + 1) * width] = in_ref[f * share + b]


def widen(parts, feats):
    blocks, columns, width = parts.shape
    out = shape((feats * columns, blocks // feats * width), BF16)
    return call(functools.partial(widen_kernel, feats), "widen", out, [vmem()])(parts)


def dense_kernel(feats, *refs):
    sums, wide_cot, refs = refs[:feats], refs[feats], refs[feats + 1 :]
    w_ref, act_ref, give_ref, spread_ref, term_ref, wide, pre_scr, grad = refs
    share, columns, width = act_ref.shape
    me = lax.axis_index("feat")
    rows = [pl.ds(pl.multiple_of(lax.rem(me + q, feats) * columns, columns), columns) for q in range(feats)]
    for q in range(feats):
        for b in range(share):
            wide[rows[q], b * width : (b + 1) * width] = sums[q][b]
    pre = dot(w_ref[...], wide[...], TN)
    pre_scr[...] = pre
    sig = jax.nn.sigmoid(pre)
    factor = wide_cot[...].astype(F32) * sig * (1.0 + pre * (1.0 - sig))
    grad[...] = factor.astype(BF16)
    spread = dot(w_ref[rows[0], :], grad[...]).astype(BF16)
    term_ref[...] = dot(grad[rows[0], :], wide[...], NT)
    wide_share = share * width
    give_ref[:, :wide_share] = spread
    for b in range(share):
        spread_ref[b] = spread[:, b * width : (b + 1) * width]
    own = pre_scr[rows[0], :]
    act = (own * jax.nn.sigmoid(own)).astype(BF16)
    give_ref[:, wide_share:] = act
    for b in range(share):
        act_ref[b] = act[:, b * width : (b + 1) * width]


def dense(sums, cot, weight, feats):
    share, columns, width = sums[0].shape
    features = weight.shape[0]
    return call(
        functools.partial(dense_kernel, feats),
        "dense",
        [
            shape((share, columns, width), BF16),
            shape((columns, 2 * share * width), BF16),
            shape((share, columns, width), BF16),
            shape((columns, features), F32),
        ],
        [vmem()] * (feats + 2),
        [
            pltpu.VMEM((features, share * width), BF16),
            pltpu.VMEM((features, share * width), F32),
            pltpu.VMEM((features, share * width), BF16),
        ],
        flops=2 ** 28,
        moved=2 ** 20,
    )(*sums, cot, weight)


def send_kernel(peers, *refs):
    ids_refs, refs = refs[: peers - 1], refs[peers - 1 :]
    mine_ref, came_ref, m_ref, refs = refs[0], refs[1], refs[2], refs[3:]
    x3, refs = refs[0], refs[1:]
    send_refs, refs = refs[: peers - 1], refs[peers - 1 :]
    self_ref, mir = refs
    share, _, width = mine_ref.shape
    both = CAP * width
    half = lax.axis_index("rep")
    x3[pl.ds(half * share, share)] = mine_ref[...]
    for b in range(share):
        x3[(1 - half) * share + b] = came_ref[:, b * width : (b + 1) * width]
    mirrored(lanes(x3), m_ref, mir, peers * CAP, width)
    self_ref[...] = mir[:, :both]
    for k in range(1, peers):
        out = send_refs[k - 1]
        out[:, :both] = mir[:, k * both : (k + 1) * both].astype(BF16)
        for s in range(CAP):
            at = (CAP + s) * width
            out[:, at : at + width] = x3[pick(ids_refs[k - 1], s)]


def sends_of(mine, came, operator, ids, peers, reps):
    share, columns, width = mine.shape
    chunk = 2 * CAP * width
    outs = call(
        functools.partial(send_kernel, peers),
        "sends",
        [shape((share * reps, columns, width), BF16)]
        + [shape((columns, chunk), BF16)] * (peers - 1)
        + [shape((columns, CAP * width), F32)],
        [vmem()] * (peers + 2),
        [pltpu.VMEM((columns, peers * CAP * width), F32)],
        flops=2 ** 28,
        moved=2 ** 21,
    )(*ids[1:], mine, came, operator)
    return outs[0], [None] + list(outs[1:peers]), outs[peers]


def pair_kernel(mine_ref, came_ref, out_ref):
    out_ref[...] = (mine_ref[...].astype(F32) + came_ref[...].astype(F32)).astype(out_ref.dtype)


def pair_sum(mine, came, dtype):
    return call(pair_kernel, "pair_sum", shape(mine.shape, dtype), [vmem(), vmem()])(mine, came)


def split_kernel(mine_ref, came_ref, give_ref, keep_ref, total):
    half = lax.axis_index("rep")
    part = keep_ref.shape[1]
    total[...] = mine_ref[...].astype(F32) + came_ref[...].astype(F32)
    give_ref[...] = total[:, pl.ds(pl.multiple_of((1 - half) * part, part), part)].astype(BF16)
    keep_ref[...] = total[:, pl.ds(pl.multiple_of(half * part, part), part)]


def split_sum(mine, came, reps):
    columns, features = mine.shape
    part = (columns, features // reps)
    return call(
        split_kernel,
        "split_sum",
        [shape(part, BF16), shape(part, F32)],
        [vmem()] * 2,
        [pltpu.VMEM(mine.shape, F32)],
    )(mine, came)


def pair_term(term, peers, reps):
    give, total = split_sum(term, across(term, peers, 1), reps)
    total = pair_sum(total, ahead(give, "rep", reps, 1), F32 if peers == 2 else BF16)
    return total


def finish_kernel(mine_ref, other_ref, share_ref, other_share_ref, grad_ref, weight_ref):
    half = lax.axis_index("rep")
    share = share_ref.shape[1]
    grad_ref[...] = (mine_ref[...].astype(F32) + other_ref[...].astype(F32)).astype(BF16)
    weight_ref[pl.ds(pl.multiple_of(half * share, share), share), :] = share_ref[...].T
    weight_ref[pl.ds(pl.multiple_of((1 - half) * share, share), share), :] = other_share_ref[...].T


def finish(mine, other, share, other_share):
    columns, width = share.shape
    return call(
        finish_kernel,
        "finish",
        [shape(mine.shape, BF16), shape((2 * width, columns), F32)],
        [vmem()] * 4,
    )(mine, other, share, other_share)


def ahead(value, axis, size, k):
    return lax.ppermute(value, axis, [(i, (i + k) % size) for i in range(size)])


def across(value, peers, k):
    return lax.ppermute(value, "graph", [(i, i ^ k) for i in range(peers)])


def after(value, first):
    return lax.optimization_barrier((value, first))[0]


def local(features, weight, cotangent, tiles, tile_row, tile_col, tile_count):
    blocks_dev, _, width = features.shape
    peers = lax.axis_size("graph")
    feats = lax.axis_size("feat")
    reps = lax.axis_size("rep")
    far_first = sorted(range(1, peers), key=lambda k: (-(k & (peers // 2)), k))

    half, table = prepare(features, tile_row, tile_col, peers, reps)
    operator, asks = list_operator(tiles, table, tile_count, peers, blocks_dev)
    sends, own_mirror, own_cot = first_sends(features, cotangent, operator, asks[1:], peers, reps)
    middle = peers // 2
    pieces = [across(half, peers, j) for j in range(1, middle)]
    crossed = across(half, peers, middle)
    came = [None] * peers
    for k in far_first:
        if k >= middle:
            came[k] = across(sends[k], peers, k)
    for j in range(1, middle):
        chunk, pieces[j - 1] = lax.optimization_barrier((below(sends[j], crossed), pieces[j - 1]))
        came[j] = across(chunk, peers, j)
    cots = lax.all_gather(own_cot, "feat", axis=0, tiled=True)
    pieces, crossed, cots = lax.optimization_barrier((pieces, crossed, cots))
    stacked = stack(pieces + [crossed], came[middle:])
    stacked = stack_more(stacked, came[1:middle])
    other_operator = ahead(operator, "rep", reps, 1)
    acc, ids = first_rows(features, operator, asks[0], came, own_mirror, peers)
    give, asked, other_asked = give_rows(acc, asks, stacked, operator, other_operator, peers, reps)
    keep = keep_rows(acc, asked, other_asked, operator, other_operator, reps)

    mine = add_up(keep, ahead(give, "rep", reps, 1))
    cot = widen(cots, feats)
    sums = [mine] + [ahead(mine, "feat", feats, feats - q) for q in range(1, feats)]
    act, give, spread, term = dense(sums, cot, weight, feats)
    shared = ahead(give, "rep", reps, 1)
    total = pair_term(term, peers, reps)
    values, sends, own_mirror = sends_of(spread, shared, operator, ids, peers, reps)

    came = [None] * peers
    for k in far_first:
        came[k] = across(sends[k], peers, k)
    acc, activated = late_self(asks[0], values, own_mirror, operator, act, shared)
    *firsts, last = sorted(range(1, peers), key=lambda k: (k == peers - 1, -(k & middle), k))
    for k in firsts:
        acc = late_rows(acc, ids[k], came[k], operator, k, F32)
    bit = 2
    while bit < peers:
        other = across(total, peers, bit)
        if 2 * bit == peers:
            total, acc = lax.optimization_barrier((total, acc))
        total = pair_sum(total, other, F32 if 2 * bit == peers else BF16)
        bit *= 2
    acc, total = lax.optimization_barrier((acc, total))
    part = late_rows(acc, ids[last], came[last], operator, last, BF16)
    input_grad, weight_grad = finish(
        part, ahead(part, "rep", reps, 1), total, ahead(total, "rep", reps, 1)
    )
    return (activated, input_grad, weight_grad)


def solution(mesh):
    placed = (
        P(("parts", "graph"), "feat", None),
        P(),
        P(("parts", "graph"), "feat", None),
        P(("parts", "graph", "rep"), None, None),
        P(("parts", "graph", "rep")),
        P(("parts", "graph", "rep")),
        P(("parts", "graph", "rep")),
    )
    return jax.shard_map(
        local,
        mesh=mesh,
        in_specs=placed,
        out_specs=(
            P(("parts", "graph"), "feat", None),
            P(("parts", "graph"), "feat", None),
            P("parts", "feat"),
        ),
        check_vma=False,
    )
```

```python
import functools

import jax
import jax.numpy as jnp
from jax import lax
from jax.experimental import pallas as pl
from jax.experimental.pallas import tpu as pltpu
from jax.sharding import PartitionSpec as P

CAP = 2
GROUP = 8
CHUNK = 16
SIDES = 1
PLACE_ROWS = 8
PLACE_BUFFER = 2 ** 22
TAIL = 16
VMEM_LIMIT = 40 * 2 ** 20
VMEM_MOST = 50 * 2 ** 20
VMEM_ALL = 58 * 2 ** 20

NT = (((1,), (1,)), ((), ()))
TN = (((0,), (0,)), ((), ()))
F32 = jnp.float32
BF16 = jnp.bfloat16


def vmem():
    return pl.BlockSpec(memory_space=pltpu.VMEM)


def smem():
    return pl.BlockSpec(memory_space=pltpu.SMEM)


def hbm():
    return pl.BlockSpec(memory_space=pltpu.HBM)


def shape(dims, dtype):
    return jax.ShapeDtypeStruct(tuple(dims), dtype)


def dot(a, b, dims=None):
    if dims is None:
        return jnp.dot(a, b, preferred_element_type=F32)
    return lax.dot_general(a, b, dims, preferred_element_type=F32)


def call(kernel, name, outs, in_specs, scratch=(), flops=0, moved=2 ** 18, limit=VMEM_LIMIT, **kwargs):
    return pl.pallas_call(
        kernel,
        out_shape=outs,
        in_specs=in_specs,
        scratch_shapes=list(scratch),
        compiler_params=pltpu.CompilerParams(vmem_limit_bytes=limit),
        cost_estimate=pl.CostEstimate(flops=flops, bytes_accessed=moved, transcendentals=0),
        name=name,
        **kwargs,
    )


def lanes(x3):
    return jnp.concatenate([x3[b] for b in range(x3.shape[0])], axis=1)


def places(peers, blocks_dev, row, col, table):
    me = lax.axis_index("graph")
    lane = lax.broadcasted_iota(jnp.int32, col.shape, 1)
    place = jnp.zeros(col.shape, jnp.int32)
    for k in range(peers):
        local = col - jnp.bitwise_xor(me, k) * blocks_dev
        inside = (local >= 0) & (local < blocks_dev)
        low = jnp.min(jnp.where(inside, local, blocks_dev - 1), axis=1, keepdims=True)
        high = jnp.max(jnp.where(inside, local, 0), axis=1, keepdims=True)
        table[PLACE_ROWS + k : PLACE_ROWS + k + 1, :] = jnp.where(lane == 0, low, high)
        slot = k * CAP + (local != low).astype(jnp.int32)
        place = jnp.where(inside, slot * blocks_dev + row, place)
    table[:PLACE_ROWS, :] = jnp.broadcast_to(place, (PLACE_ROWS, place.shape[1]))


def table_rows(peers):
    return PLACE_ROWS + -(-peers // 8) * 8


def prepare_kernel(peers, row_ref, col_ref, x3, half_out, table_out, table, half_sem, sem):
    share = half_out.shape[0]
    mine = pl.ds(lax.axis_index("rep") * share, share)
    half_copy = pltpu.make_async_copy(x3.at[mine], half_out, half_sem)
    half_copy.start()
    if table.shape[0] > PLACE_ROWS + peers:
        table[...] = jnp.zeros(table.shape, jnp.int32)
    places(peers, x3.shape[0], row_ref[...], col_ref[...], table)
    copy = pltpu.make_async_copy(table, table_out.at[pl.ds(0, table.shape[0])], sem)
    copy.start()
    half_copy.wait()
    copy.wait()


def prepare(features, tile_row, tile_col, peers, reps):
    per = tile_col.shape[0]
    blocks_dev, columns, width = features.shape
    return call(
        functools.partial(prepare_kernel, peers),
        "prepare",
        [shape((blocks_dev // reps, columns, width), BF16), shape((PLACE_BUFFER // (4 * per), per), jnp.int32)],
        [vmem()] * 3,
        [
            pltpu.VMEM((table_rows(peers), per), jnp.int32),
            pltpu.SemaphoreType.DMA,
            pltpu.SemaphoreType.DMA,
        ],
        limit=VMEM_ALL,
        out_specs=[hbm(), hbm()],
    )(tile_row.reshape(1, per), tile_col.reshape(1, per), features)


def pick(ids_ref, lane):
    ids = ids_ref[...].astype(F32)
    at = lax.broadcasted_iota(jnp.int32, ids.shape, 1)
    return jnp.max(jnp.where(at == lane, ids, 0.0)).astype(jnp.int32)


def operator_kernel(blocks_dev, slots_here, groups, count_ref, table_in, tiles_ref, m_ref, *refs):
    asks, (tiles, acc, place_ref, table, sems, sem, table_sem) = refs[:-7], refs[-7:]
    step = pl.program_id(0)
    per, width = tiles.shape[0], tiles.shape[1]
    chunks = per // CHUNK
    spare = slots_here * blocks_dev

    def chunk_copy(c):
        part = pl.ds(c * CHUNK, CHUNK)
        return pltpu.make_async_copy(tiles_ref.at[part], tiles.at[part], sems.at[c])

    def place_copy():
        return pltpu.make_async_copy(table_in.at[pl.ds(0, PLACE_ROWS)], place_ref, sem)

    def table_copy():
        return pltpu.make_async_copy(table_in.at[pl.ds(0, table.shape[0])], table, table_sem)

    @pl.when(step == 0)
    def _():
        place_copy().start()
        table_copy().start()
        for c in range(chunks):
            chunk_copy(c).start()

    acc[...] = jnp.zeros_like(acc)

    @pl.when(step == 0)
    def _():
        place_copy().wait()

    count = count_ref[0]

    def add_chunk(c, carry):
        @pl.when(step == 0)
        def _():
            chunk_copy(c).wait()

        for u in range(CHUNK):
            t = c * CHUNK + u
            place = place_ref[0, t]
            here = t < count
            if groups > 1:
                place = place - step * spare
                here = here & (place >= 0) & (place < spare)
            place = jnp.where(here, place, spare)
            side = u % SIDES
            acc[side, place] = acc[side, place] + tiles[t].astype(F32)
        return carry

    lax.fori_loop(0, chunks, add_chunk, 0)
    for s in range(slots_here):
        for r in range(blocks_dev):
            total = acc[0, s * blocks_dev + r]
            for side in range(1, SIDES):
                total = total + acc[side, s * blocks_dev + r]
            m_ref[r * width : (r + 1) * width, s * width : (s + 1) * width] = total.astype(BF16)

    @pl.when(step == 0)
    def _():
        table_copy().wait()
        for k, ask_ref in enumerate(asks):
            ask_ref[...] = table[PLACE_ROWS + k : PLACE_ROWS + k + 1, :]


def list_operator(tiles, table, tile_count, peers, blocks_dev):
    per, width = tiles.shape[0], tiles.shape[1]
    slots = peers * CAP
    slots_here = min(slots, GROUP)
    groups = slots // slots_here
    outs = call(
        functools.partial(operator_kernel, blocks_dev, slots_here, groups),
        "operator",
        [shape((blocks_dev * width, slots * width), BF16)] + [shape((1, per), jnp.int32)] * peers,
        [smem(), hbm(), hbm()],
        [
            pltpu.VMEM((per, width, width), BF16),
            pltpu.VMEM((SIDES, slots_here * blocks_dev + 1, width, width), F32),
            pltpu.SMEM((PLACE_ROWS, per), jnp.int32),
            pltpu.VMEM((table_rows(peers), per), jnp.int32),
            pltpu.SemaphoreType.DMA((per // CHUNK,)),
            pltpu.SemaphoreType.DMA,
            pltpu.SemaphoreType.DMA,
        ],
        moved=2 ** 24,
        limit=VMEM_MOST,
        grid=(groups,),
        out_specs=[pl.BlockSpec((blocks_dev * width, slots_here * width), lambda i: (0, i))] + [vmem()] * peers,
    )(tile_count, table, tiles)
    return outs[0], list(outs[1:])


def mirrored(near, m_ref, mir, slots, width):
    if slots <= GROUP:
        mir[...] = dot(near, m_ref[...])
    else:
        part = GROUP * width

        @pl.loop(0, slots // GROUP)
        def _(i):
            where = pl.ds(pl.multiple_of(i * part, part), part)
            mir[:, where] = dot(near, m_ref[:, where])


def first_sends_kernel(peers, *refs):
    ask_refs, refs = refs[: peers - 1], refs[peers - 1 :]
    x3, cot, m_ref, refs = refs[0], refs[1], refs[2], refs[3:]
    send_refs, self_ref, cot_ref, mir = refs[: peers - 1], refs[peers - 1], refs[peers], refs[peers + 1]
    _, columns, width = x3.shape
    share = cot_ref.shape[0]
    cot_ref[...] = cot[pl.ds(lax.axis_index("rep") * share, share)]
    both = CAP * width
    mirrored(lanes(x3), m_ref, mir, peers * CAP, width)
    self_ref[...] = mir[:, :both]
    lane = lax.broadcasted_iota(jnp.int32, (TAIL, both), 1)
    for k in range(1, peers):
        out = send_refs[k - 1]
        out[:columns, :] = mir[:, k * both : (k + 1) * both].astype(BF16)
        low, high = ask_refs[k - 1][:, :1], ask_refs[k - 1][:, 1:2]
        out[columns:, :] = jnp.where(lane < width, low, high).astype(F32).astype(BF16)


def first_sends(values, cotangent, operator, asks, peers, reps):
    blocks_dev, columns, width = values.shape
    outs = call(
        functools.partial(first_sends_kernel, peers),
        "first_sends",
        [shape((columns + TAIL, CAP * width), BF16)] * (peers - 1)
        + [shape((columns, CAP * width), F32), shape((blocks_dev // reps, columns, width), BF16)],
        [vmem()] * (peers + 2),
        [pltpu.VMEM((columns, peers * CAP * width), F32)],
        flops=2 ** 28,
        moved=2 ** 21,
    )(*asks, values, cotangent, operator)
    return [None] + list(outs[: peers - 1]), outs[peers - 1], outs[peers]


def add_sums(acc, block, sums):
    acc[block] = acc[block] + sums.astype(F32)


def own_rows(far, m_ref, k):
    both = far.shape[1]
    return dot(far, m_ref[:, k * both : (k + 1) * both], NT)


def put_rows(acc, own, before=None):
    blocks_dev, _, width = acc.shape
    for b in range(blocks_dev):
        add = own[:, b * width : (b + 1) * width]
        acc[b] = add if before is None else before[b] + add


def self_rows(x3, m_ref, ask_ref):
    far = jnp.concatenate([x3[pick(ask_ref, s)] for s in range(CAP)], axis=1)
    return own_rows(far, m_ref, 0)


def far_of(share, mine_ref, other_ref, ask_ref, at):
    first = lax.axis_index("rep") * share
    blocks = []
    for s in range(CAP):
        local = pick(ask_ref, s) - first
        own = (local >= 0) & (local < share)
        here = at * share + jnp.where(own, local, 0)
        there = at * share + jnp.where(own, 0, jnp.where(local < 0, local + share, local - share))
        blocks.append(jnp.where(own, mine_ref[here], other_ref[there]))
    return jnp.concatenate(blocks, axis=1)


def first_rows_kernel(peers, *refs):
    ask_ref, refs = refs[0], refs[1:]
    came_refs, refs = refs[: peers - 1], refs[peers - 1 :]
    x3, m_ref, self_ref, acc, ids_refs = refs[0], refs[1], refs[2], refs[3], refs[4:]
    _, columns, width = x3.shape
    put_rows(acc, self_rows(x3, m_ref, ask_ref))
    for s in range(CAP):
        add_sums(acc, pick(ask_ref, s), self_ref[:, s * width : (s + 1) * width])
    lane = lax.broadcasted_iota(jnp.int32, ids_refs[0].shape, 1)
    for k in range(1, peers):
        came = came_refs[k - 1]
        ids = jnp.zeros(lane.shape, jnp.int32)
        for s in range(CAP):
            here = slice(s * width, (s + 1) * width)
            asked = jnp.max(came[columns : columns + TAIL, here].astype(F32)).astype(jnp.int32)
            ids = jnp.where(lane == s, asked, ids)
            add_sums(acc, asked, came[:columns, here])
        ids_refs[k - 1][...] = ids


def first_rows(values, operator, ask, came, own_mirror, peers):
    _, columns, width = values.shape
    outs = call(
        functools.partial(first_rows_kernel, peers),
        "first_rows",
        [shape(values.shape, F32)] + [shape((1, width), jnp.int32)] * (peers - 1),
        [vmem()] * (peers + 3),
        flops=2 ** 27,
        moved=2 ** 20,
    )(ask, *came[1:], values, operator, own_mirror)
    return outs[0], [None] + list(outs[1:])


def below_kernel(sums_ref, half_ref, out_ref):
    top = sums_ref.shape[0]
    share, columns, width = half_ref.shape
    out_ref[:top, :] = sums_ref[...]
    for b in range(share):
        row, left = top + b // CAP * columns, b % CAP * width
        out_ref[row : row + columns, left : left + width] = half_ref[b]


def below(sums, half):
    share, columns, width = half.shape
    out = shape((sums.shape[0] + share // CAP * columns, sums.shape[1]), BF16)
    return call(below_kernel, "below", out, [vmem(), vmem()])(sums, half)


def stack_kernel(count, *refs):
    share = refs[0].shape[0]
    for k, ref in enumerate(refs[:count]):
        refs[-1][k * share : (k + 1) * share] = ref[...]


def stack(pieces, sums):
    share, columns, width = pieces[0].shape
    out = shape((len(pieces) * share, columns, width), BF16)
    kernel = functools.partial(stack_kernel, len(pieces))
    return call(kernel, "stack", out, [vmem()] * (len(pieces) + len(sums)), flops=2 ** 31)(*pieces, *sums)


def stack_more_kernel(first_ref, *refs):
    out_ref = refs[-1]
    at, columns, width = first_ref.shape
    out_ref[:at] = first_ref[...]
    for ref in refs[:-1]:
        share = (ref.shape[0] - TAIL) // columns * CAP - CAP
        for b in range(share):
            row, left = columns + TAIL + b // CAP * columns, b % CAP * width
            out_ref[at + b] = ref[row : row + columns, left : left + width]
        at += share


def stack_more(first, chunks):
    at, columns, width = first.shape
    share = (chunks[0].shape[0] - TAIL) // columns * CAP - CAP
    out = shape((at + len(chunks) * share, columns, width), BF16)
    return call(stack_more_kernel, "stack_more", out, [vmem()] * (1 + len(chunks)))(first, *chunks)


def half_rows(before, far_ref, m_ref, first, share):
    columns, width = before.shape[1:]
    both = CAP * width
    rows = pl.ds(pl.multiple_of(first * width, share * width), share * width)
    if m_ref.shape[1] <= GROUP * width:
        own = dot(far_ref[:, both:], m_ref[rows, both:], NT)
    else:

        def add_peer(k, total):
            here = pl.ds(pl.multiple_of(k * both, both), both)
            return total + dot(far_ref[:, here], m_ref[rows, here], NT)

        zeros = jnp.zeros((columns, share * width), F32)
        own = lax.fori_loop(1, m_ref.shape[1] // both, add_peer, zeros)
    return [before[first + b] + own[:, b * width : (b + 1) * width] for b in range(share)]


def give_rows_kernel(peers, *refs):
    ask_refs, refs = refs[: peers - 1], refs[peers - 1 :]
    before, mine_ref, other_ref, m_ref, give_ref, far_ref = refs
    share = give_ref.shape[0]
    both = CAP * before.shape[2]
    for k in range(1, peers):
        far_ref[:, k * both : (k + 1) * both] = far_of(share, mine_ref, other_ref, ask_refs[k - 1], k - 1)
    far_ref[:, :both] = jnp.zeros((far_ref.shape[0], both), BF16)
    rows = half_rows(before, far_ref, m_ref, (1 - lax.axis_index("rep")) * share, share)
    for b in range(share):
        give_ref[b] = rows[b].astype(BF16)


def give_rows(before, asks, mine, other, operator, peers, reps):
    blocks_dev, columns, width = before.shape
    return call(
        functools.partial(give_rows_kernel, peers),
        "give_rows",
        [shape((blocks_dev // reps, columns, width), BF16), shape((columns, peers * CAP * width), BF16)],
        [vmem()] * (peers + 3),
        flops=2 ** 27,
        moved=2 ** 20,
    )(*asks[1:], before, mine, other, operator)


def keep_rows_kernel(before, far_ref, m_ref, keep_ref):
    share = keep_ref.shape[0]
    rows = half_rows(before, far_ref, m_ref, lax.axis_index("rep") * share, share)
    for b in range(share):
        keep_ref[b] = rows[b]


def keep_rows(before, far, operator, reps):
    blocks_dev, columns, width = before.shape
    return call(
        keep_rows_kernel,
        "keep_rows",
        shape((blocks_dev // reps, columns, width), F32),
        [vmem()] * 3,
        flops=2 ** 27,
        moved=2 ** 20,
    )(before, far, operator)


def late_self_kernel(ask_ref, x3, self_ref, m_ref, act_ref, shared_ref, acc, out_ref):
    width = x3.shape[2]
    put_rows(acc, self_rows(x3, m_ref, ask_ref))
    for s in range(CAP):
        add_sums(acc, pick(ask_ref, s), self_ref[:, s * width : (s + 1) * width])
    half = lax.axis_index("rep")
    blocks = act_ref.shape[0]
    out_ref[pl.ds(half * blocks, blocks)] = act_ref[...]
    for b in range(blocks):
        at = (blocks + b) * width
        out_ref[(1 - half) * blocks + b] = shared_ref[:, at : at + width]


def late_self(ask, values, own_mirror, operator, act, shared):
    return call(
        late_self_kernel,
        "late_self",
        [shape(values.shape, F32), shape(values.shape, BF16)],
        [vmem()] * 6,
        flops=2 ** 26,
    )(ask, values, own_mirror, operator, act, shared)


def late_rows_kernel(k, before, ids_ref, came_ref, m_ref, out_ref, acc):
    width = acc.shape[2]
    both = CAP * width
    put_rows(acc, own_rows(came_ref[:, both : 2 * both], m_ref, k), before)
    for s in range(CAP):
        add_sums(acc, pick(ids_ref, s), came_ref[:, s * width : (s + 1) * width])
    out_ref[...] = acc[...].astype(out_ref.dtype)


def late_rows(before, ids, came, operator, k, dtype):
    return call(
        functools.partial(late_rows_kernel, k),
        "late_rows",
        shape(before.shape, dtype),
        [vmem()] * 4,
        [pltpu.VMEM(before.shape, F32)],
        flops=2 ** 26,
    )(before, ids, came, operator)


def add_kernel(keep_ref, came_ref, out_ref):
    out_ref[...] = (keep_ref[...] + came_ref[...].astype(F32)).astype(BF16)


def add_up(keep, came):
    return call(add_kernel, "add_up", shape(came.shape, BF16), [vmem(), vmem()])(keep, came)


def widen_kernel(feats, *refs):
    out_ref = refs[feats]
    share, columns, width = refs[0].shape
    me = lax.axis_index("feat")
    for q in range(feats):
        rows = pl.ds(pl.multiple_of(lax.rem(me + q, feats) * columns, columns), columns)
        for b in range(share):
            out_ref[rows, b * width : (b + 1) * width] = refs[q][b]


def widen(parts):
    share, columns, width = parts[0].shape
    out = shape((len(parts) * columns, share * width), BF16)
    return call(functools.partial(widen_kernel, len(parts)), "widen", out, [vmem()] * len(parts))(*parts)


def dense_kernel(feats, *refs):
    sums, wide_cot, refs = refs[:feats], refs[feats], refs[feats + 1 :]
    w_ref, act_ref, give_ref, spread_ref, term_ref, wide, pre_scr, grad = refs
    share, columns, width = act_ref.shape
    me = lax.axis_index("feat")
    rows = [pl.ds(pl.multiple_of(lax.rem(me + q, feats) * columns, columns), columns) for q in range(feats)]
    for q in range(feats):
        for b in range(share):
            wide[rows[q], b * width : (b + 1) * width] = sums[q][b]
    pre = dot(w_ref[...], wide[...], TN)
    pre_scr[...] = pre
    sig = jax.nn.sigmoid(pre)
    factor = wide_cot[...].astype(F32) * sig * (1.0 + pre * (1.0 - sig))
    grad[...] = factor.astype(BF16)
    spread = dot(w_ref[rows[0], :], grad[...]).astype(BF16)
    term_ref[...] = dot(grad[rows[0], :], wide[...], NT)
    wide_share = share * width
    give_ref[:, :wide_share] = spread
    for b in range(share):
        spread_ref[b] = spread[:, b * width : (b + 1) * width]
    own = pre_scr[rows[0], :]
    act = (own * jax.nn.sigmoid(own)).astype(BF16)
    give_ref[:, wide_share:] = act
    for b in range(share):
        act_ref[b] = act[:, b * width : (b + 1) * width]


def dense(sums, cot, weight, feats):
    share, columns, width = sums[0].shape
    features = weight.shape[0]
    return call(
        functools.partial(dense_kernel, feats),
        "dense",
        [
            shape((share, columns, width), BF16),
            shape((columns, 2 * share * width), BF16),
            shape((share, columns, width), BF16),
            shape((columns, features), F32),
        ],
        [vmem()] * (feats + 2),
        [
            pltpu.VMEM((features, share * width), BF16),
            pltpu.VMEM((features, share * width), F32),
            pltpu.VMEM((features, share * width), BF16),
        ],
        flops=2 ** 28,
        moved=2 ** 20,
    )(*sums, cot, weight)


def send_kernel(peers, *refs):
    ids_refs, refs = refs[: peers - 1], refs[peers - 1 :]
    mine_ref, came_ref, m_ref, refs = refs[0], refs[1], refs[2], refs[3:]
    x3, refs = refs[0], refs[1:]
    send_refs, refs = refs[: peers - 1], refs[peers - 1 :]
    self_ref, mir = refs
    share, _, width = mine_ref.shape
    both = CAP * width
    half = lax.axis_index("rep")
    x3[pl.ds(half * share, share)] = mine_ref[...]
    for b in range(share):
        x3[(1 - half) * share + b] = came_ref[:, b * width : (b + 1) * width]
    mirrored(lanes(x3), m_ref, mir, peers * CAP, width)
    self_ref[...] = mir[:, :both]
    for k in range(1, peers):
        out = send_refs[k - 1]
        out[:, :both] = mir[:, k * both : (k + 1) * both].astype(BF16)
        for s in range(CAP):
            at = (CAP + s) * width
            out[:, at : at + width] = x3[pick(ids_refs[k - 1], s)]


def sends_of(mine, came, operator, ids, peers, reps):
    share, columns, width = mine.shape
    chunk = 2 * CAP * width
    outs = call(
        functools.partial(send_kernel, peers),
        "sends",
        [shape((share * reps, columns, width), BF16)]
        + [shape((columns, chunk), BF16)] * (peers - 1)
        + [shape((columns, CAP * width), F32)],
        [vmem()] * (peers + 2),
        [pltpu.VMEM((columns, peers * CAP * width), F32)],
        flops=2 ** 28,
        moved=2 ** 21,
    )(*ids[1:], mine, came, operator)
    return outs[0], [None] + list(outs[1:peers]), outs[peers]


def pair_kernel(mine_ref, came_ref, out_ref):
    out_ref[...] = (mine_ref[...].astype(F32) + came_ref[...].astype(F32)).astype(out_ref.dtype)


def pair_sum(mine, came, dtype):
    return call(pair_kernel, "pair_sum", shape(mine.shape, dtype), [vmem(), vmem()])(mine, came)


def split_kernel(mine_ref, came_ref, give_ref, keep_ref, total):
    half = lax.axis_index("rep")
    part = keep_ref.shape[1]
    total[...] = mine_ref[...].astype(F32) + came_ref[...].astype(F32)
    give_ref[...] = total[:, pl.ds(pl.multiple_of((1 - half) * part, part), part)].astype(BF16)
    keep_ref[...] = total[:, pl.ds(pl.multiple_of(half * part, part), part)]


def split_sum(mine, came, reps):
    columns, features = mine.shape
    part = (columns, features // reps)
    return call(
        split_kernel,
        "split_sum",
        [shape(part, BF16), shape(part, F32)],
        [vmem()] * 2,
        [pltpu.VMEM(mine.shape, F32)],
    )(mine, came)


def pair_term(term, peers, reps):
    give, total = split_sum(term, across(term, peers, 1), reps)
    total = pair_sum(total, ahead(give, "rep", reps, 1), F32 if peers == 2 else BF16)
    return total


def finish_kernel(mine_ref, other_ref, share_ref, other_share_ref, grad_ref, weight_ref):
    half = lax.axis_index("rep")
    share = share_ref.shape[1]
    grad_ref[...] = (mine_ref[...].astype(F32) + other_ref[...].astype(F32)).astype(BF16)
    weight_ref[pl.ds(pl.multiple_of(half * share, share), share), :] = share_ref[...].T
    weight_ref[pl.ds(pl.multiple_of((1 - half) * share, share), share), :] = other_share_ref[...].T


def finish(mine, other, share, other_share):
    columns, width = share.shape
    return call(
        finish_kernel,
        "finish",
        [shape(mine.shape, BF16), shape((2 * width, columns), F32)],
        [vmem()] * 4,
    )(mine, other, share, other_share)


def ahead(value, axis, size, k):
    return lax.ppermute(value, axis, [(i, (i + k) % size) for i in range(size)])


def across(value, peers, k):
    return lax.ppermute(value, "graph", [(i, i ^ k) for i in range(peers)])


def after(value, first):
    return lax.optimization_barrier((value, first))[0]


def local(features, weight, cotangent, tiles, tile_row, tile_col, tile_count):
    blocks_dev, _, width = features.shape
    peers = lax.axis_size("graph")
    feats = lax.axis_size("feat")
    reps = lax.axis_size("rep")
    far_first = sorted(range(1, peers), key=lambda k: (-(k & (peers // 2)), k))

    half, table = prepare(features, tile_row, tile_col, peers, reps)
    operator, asks = list_operator(tiles, table, tile_count, peers, blocks_dev)
    sends, own_mirror, own_cot = first_sends(features, cotangent, operator, asks[1:], peers, reps)
    middle = peers // 2
    pieces = [across(half, peers, j) for j in range(1, middle)]
    crossed = across(half, peers, middle)
    came = [None] * peers
    for k in far_first:
        if k >= middle:
            came[k] = across(sends[k], peers, k)
    for j in range(1, middle):
        chunk, pieces[j - 1] = lax.optimization_barrier((below(sends[j], crossed), pieces[j - 1]))
        came[j] = across(chunk, peers, j)
    held = after(own_cot, crossed)
    cots = [own_cot] + [ahead(held, "feat", feats, feats - q) for q in range(1, feats)]
    stacked = stack(pieces + [crossed], came[middle:-1])
    came[1:middle], came[-1], stacked = lax.optimization_barrier((came[1:middle], came[-1], stacked))
    stacked, cots = lax.optimization_barrier((stacked, cots))
    stacked = stack_more(stacked, came[1:middle])
    swapped = ahead(stacked, "rep", reps, 1)
    acc, ids = first_rows(features, operator, asks[0], came, own_mirror, peers)
    give, asked = give_rows(acc, asks, stacked, swapped, operator, peers, reps)
    keep = keep_rows(acc, asked, operator, reps)

    mine = add_up(keep, ahead(give, "rep", reps, 1))
    cot = widen(cots)
    sums = [mine] + [ahead(mine, "feat", feats, feats - q) for q in range(1, feats)]
    act, give, spread, term = dense(sums, cot, weight, feats)
    shared = ahead(give, "rep", reps, 1)
    total = pair_term(term, peers, reps)
    values, sends, own_mirror = sends_of(spread, shared, operator, ids, peers, reps)

    came = [None] * peers
    for k in far_first:
        came[k] = across(sends[k], peers, k)
    acc, activated = late_self(asks[0], values, own_mirror, operator, act, shared)
    *firsts, last = sorted(range(1, peers), key=lambda k: (k == peers - 1, -(k & middle), k))
    for k in firsts:
        acc = late_rows(acc, ids[k], came[k], operator, k, F32)
    bit = 2
    while bit < peers:
        other = across(total, peers, bit)
        if 2 * bit == peers:
            total, acc = lax.optimization_barrier((total, acc))
        total = pair_sum(total, other, F32 if 2 * bit == peers else BF16)
        bit *= 2
    acc, total = lax.optimization_barrier((acc, total))
    part = late_rows(acc, ids[last], came[last], operator, last, BF16)
    input_grad, weight_grad = finish(
        part, ahead(part, "rep", reps, 1), total, ahead(total, "rep", reps, 1)
    )
    return (activated, input_grad, weight_grad)


def solution(mesh):
    placed = (
        P(("parts", "graph"), "feat", None),
        P(),
        P(("parts", "graph"), "feat", None),
        P(("parts", "graph", "rep"), None, None),
        P(("parts", "graph", "rep")),
        P(("parts", "graph", "rep")),
        P(("parts", "graph", "rep")),
    )
    return jax.shard_map(
        local,
        mesh=mesh,
        in_specs=placed,
        out_specs=(
            P(("parts", "graph"), "feat", None),
            P(("parts", "graph"), "feat", None),
            P("parts", "feat"),
        ),
        check_vma=False,
    )
```

```python
import functools

import jax
import jax.numpy as jnp
from jax import lax
from jax.experimental import pallas as pl
from jax.experimental.pallas import tpu as pltpu
from jax.sharding import PartitionSpec as P

CAP = 2
GROUP = 8
CHUNK = 16
SIDES = 1
PLACE_ROWS = 8
PLACE_BUFFER = 2 ** 22
TAIL = 16
VMEM_LIMIT = 40 * 2 ** 20
VMEM_MOST = 50 * 2 ** 20
VMEM_ALL = 58 * 2 ** 20

NT = (((1,), (1,)), ((), ()))
TN = (((0,), (0,)), ((), ()))
F32 = jnp.float32
BF16 = jnp.bfloat16


def vmem():
    return pl.BlockSpec(memory_space=pltpu.VMEM)


def smem():
    return pl.BlockSpec(memory_space=pltpu.SMEM)


def hbm():
    return pl.BlockSpec(memory_space=pltpu.HBM)


def shape(dims, dtype):
    return jax.ShapeDtypeStruct(tuple(dims), dtype)


def dot(a, b, dims=None):
    if dims is None:
        return jnp.dot(a, b, preferred_element_type=F32)
    return lax.dot_general(a, b, dims, preferred_element_type=F32)


def call(kernel, name, outs, in_specs, scratch=(), flops=0, moved=2 ** 18, limit=VMEM_LIMIT, **kwargs):
    return pl.pallas_call(
        kernel,
        out_shape=outs,
        in_specs=in_specs,
        scratch_shapes=list(scratch),
        compiler_params=pltpu.CompilerParams(vmem_limit_bytes=limit),
        cost_estimate=pl.CostEstimate(flops=flops, bytes_accessed=moved, transcendentals=0),
        name=name,
        **kwargs,
    )


def lanes(x3):
    return jnp.concatenate([x3[b] for b in range(x3.shape[0])], axis=1)


def places(peers, blocks_dev, row, col, table):
    me = lax.axis_index("graph")
    lane = lax.broadcasted_iota(jnp.int32, col.shape, 1)
    place = jnp.zeros(col.shape, jnp.int32)
    for k in range(peers):
        local = col - jnp.bitwise_xor(me, k) * blocks_dev
        inside = (local >= 0) & (local < blocks_dev)
        low = jnp.min(jnp.where(inside, local, blocks_dev - 1), axis=1, keepdims=True)
        high = jnp.max(jnp.where(inside, local, 0), axis=1, keepdims=True)
        table[PLACE_ROWS + k : PLACE_ROWS + k + 1, :] = jnp.where(lane == 0, low, high)
        slot = k * CAP + (local != low).astype(jnp.int32)
        place = jnp.where(inside, slot * blocks_dev + row, place)
    table[:PLACE_ROWS, :] = jnp.broadcast_to(place, (PLACE_ROWS, place.shape[1]))


def table_rows(peers):
    return PLACE_ROWS + -(-peers // 8) * 8


def prepare_kernel(peers, row_ref, col_ref, x3, half_out, table_out, table, half_sem, sem):
    share = half_out.shape[0]
    mine = pl.ds(lax.axis_index("rep") * share, share)
    half_copy = pltpu.make_async_copy(x3.at[mine], half_out, half_sem)
    half_copy.start()
    if table.shape[0] > PLACE_ROWS + peers:
        table[...] = jnp.zeros(table.shape, jnp.int32)
    places(peers, x3.shape[0], row_ref[...], col_ref[...], table)
    copy = pltpu.make_async_copy(table, table_out.at[pl.ds(0, table.shape[0])], sem)
    copy.start()
    half_copy.wait()
    copy.wait()


def prepare(features, tile_row, tile_col, peers, reps):
    per = tile_col.shape[0]
    blocks_dev, columns, width = features.shape
    return call(
        functools.partial(prepare_kernel, peers),
        "prepare",
        [shape((blocks_dev // reps, columns, width), BF16), shape((PLACE_BUFFER // (4 * per), per), jnp.int32)],
        [vmem()] * 3,
        [
            pltpu.VMEM((table_rows(peers), per), jnp.int32),
            pltpu.SemaphoreType.DMA,
            pltpu.SemaphoreType.DMA,
        ],
        limit=VMEM_ALL,
        out_specs=[hbm(), hbm()],
    )(tile_row.reshape(1, per), tile_col.reshape(1, per), features)


def pick(ids_ref, lane):
    ids = ids_ref[...].astype(F32)
    at = lax.broadcasted_iota(jnp.int32, ids.shape, 1)
    return jnp.max(jnp.where(at == lane, ids, 0.0)).astype(jnp.int32)


def operator_kernel(blocks_dev, slots_here, groups, count_ref, table_in, tiles_ref, m_ref, *refs):
    asks, (tiles, acc, place_ref, table, sems, sem, table_sem) = refs[:-7], refs[-7:]
    step = pl.program_id(0)
    per, width = tiles.shape[0], tiles.shape[1]
    chunks = per // CHUNK
    spare = slots_here * blocks_dev

    def chunk_copy(c):
        part = pl.ds(c * CHUNK, CHUNK)
        return pltpu.make_async_copy(tiles_ref.at[part], tiles.at[part], sems.at[c])

    def place_copy():
        return pltpu.make_async_copy(table_in.at[pl.ds(0, PLACE_ROWS)], place_ref, sem)

    def table_copy():
        return pltpu.make_async_copy(table_in.at[pl.ds(0, table.shape[0])], table, table_sem)

    @pl.when(step == 0)
    def _():
        place_copy().start()
        table_copy().start()
        for c in range(chunks):
            chunk_copy(c).start()

    acc[...] = jnp.zeros_like(acc)

    @pl.when(step == 0)
    def _():
        place_copy().wait()

    count = count_ref[0]

    def add_chunk(c, carry):
        @pl.when(step == 0)
        def _():
            chunk_copy(c).wait()

        for u in range(CHUNK):
            t = c * CHUNK + u
            place = place_ref[0, t]
            here = t < count
            if groups > 1:
                place = place - step * spare
                here = here & (place >= 0) & (place < spare)
            place = jnp.where(here, place, spare)
            side = u % SIDES
            acc[side, place] = acc[side, place] + tiles[t].astype(F32)
        return carry

    lax.fori_loop(0, chunks, add_chunk, 0)
    for s in range(slots_here):
        for r in range(blocks_dev):
            total = acc[0, s * blocks_dev + r]
            for side in range(1, SIDES):
                total = total + acc[side, s * blocks_dev + r]
            m_ref[r * width : (r + 1) * width, s * width : (s + 1) * width] = total.astype(BF16)

    @pl.when(step == 0)
    def _():
        table_copy().wait()
        for k, ask_ref in enumerate(asks):
            ask_ref[...] = table[PLACE_ROWS + k : PLACE_ROWS + k + 1, :]


def list_operator(tiles, table, tile_count, peers, blocks_dev):
    per, width = tiles.shape[0], tiles.shape[1]
    slots = peers * CAP
    slots_here = min(slots, GROUP)
    groups = slots // slots_here
    outs = call(
        functools.partial(operator_kernel, blocks_dev, slots_here, groups),
        "operator",
        [shape((blocks_dev * width, slots * width), BF16)] + [shape((1, per), jnp.int32)] * peers,
        [smem(), hbm(), hbm()],
        [
            pltpu.VMEM((per, width, width), BF16),
            pltpu.VMEM((SIDES, slots_here * blocks_dev + 1, width, width), F32),
            pltpu.SMEM((PLACE_ROWS, per), jnp.int32),
            pltpu.VMEM((table_rows(peers), per), jnp.int32),
            pltpu.SemaphoreType.DMA((per // CHUNK,)),
            pltpu.SemaphoreType.DMA,
            pltpu.SemaphoreType.DMA,
        ],
        moved=2 ** 24,
        limit=VMEM_MOST,
        grid=(groups,),
        out_specs=[pl.BlockSpec((blocks_dev * width, slots_here * width), lambda i: (0, i))] + [vmem()] * peers,
    )(tile_count, table, tiles)
    return outs[0], list(outs[1:])


def mirrored(near, m_ref, mir, slots, width):
    if slots <= GROUP:
        mir[...] = dot(near, m_ref[...])
    else:
        part = GROUP * width

        @pl.loop(0, slots // GROUP)
        def _(i):
            where = pl.ds(pl.multiple_of(i * part, part), part)
            mir[:, where] = dot(near, m_ref[:, where])


def first_sends_kernel(peers, *refs):
    ask_refs, refs = refs[: peers - 1], refs[peers - 1 :]
    x3, cot, m_ref, refs = refs[0], refs[1], refs[2], refs[3:]
    send_refs, self_ref, cot_ref, mir = refs[: peers - 1], refs[peers - 1], refs[peers], refs[peers + 1]
    _, columns, width = x3.shape
    share = cot_ref.shape[0]
    cot_ref[...] = cot[pl.ds(lax.axis_index("rep") * share, share)]
    both = CAP * width
    mirrored(lanes(x3), m_ref, mir, peers * CAP, width)
    self_ref[...] = mir[:, :both]
    lane = lax.broadcasted_iota(jnp.int32, (TAIL, both), 1)
    for k in range(1, peers):
        out = send_refs[k - 1]
        out[:columns, :] = mir[:, k * both : (k + 1) * both].astype(BF16)
        low, high = ask_refs[k - 1][:, :1], ask_refs[k - 1][:, 1:2]
        out[columns:, :] = jnp.where(lane < width, low, high).astype(F32).astype(BF16)


def first_sends(values, cotangent, operator, asks, peers, reps):
    blocks_dev, columns, width = values.shape
    outs = call(
        functools.partial(first_sends_kernel, peers),
        "first_sends",
        [shape((columns + TAIL, CAP * width), BF16)] * (peers - 1)
        + [shape((columns, CAP * width), F32), shape((blocks_dev // reps, columns, width), BF16)],
        [vmem()] * (peers + 2),
        [pltpu.VMEM((columns, peers * CAP * width), F32)],
        flops=2 ** 28,
        moved=2 ** 21,
    )(*asks, values, cotangent, operator)
    return [None] + list(outs[: peers - 1]), outs[peers - 1], outs[peers]


def add_sums(acc, block, sums):
    acc[block] = acc[block] + sums.astype(F32)


def own_rows(far, m_ref, k):
    both = far.shape[1]
    return dot(far, m_ref[:, k * both : (k + 1) * both], NT)


def put_rows(acc, own, before=None):
    blocks_dev, _, width = acc.shape
    for b in range(blocks_dev):
        add = own[:, b * width : (b + 1) * width]
        acc[b] = add if before is None else before[b] + add


def self_rows(x3, m_ref, ask_ref):
    far = jnp.concatenate([x3[pick(ask_ref, s)] for s in range(CAP)], axis=1)
    return own_rows(far, m_ref, 0)


def far_of(share, mine_ref, other_ref, ask_ref, at):
    first = lax.axis_index("rep") * share
    blocks = []
    for s in range(CAP):
        local = pick(ask_ref, s) - first
        own = (local >= 0) & (local < share)
        here = at * share + jnp.where(own, local, 0)
        there = at * share + jnp.where(own, 0, jnp.where(local < 0, local + share, local - share))
        blocks.append(jnp.where(own, mine_ref[here], other_ref[there]))
    return jnp.concatenate(blocks, axis=1)


def first_rows_kernel(peers, *refs):
    ask_ref, refs = refs[0], refs[1:]
    came_refs, refs = refs[: peers - 1], refs[peers - 1 :]
    x3, m_ref, self_ref, acc, ids_refs = refs[0], refs[1], refs[2], refs[3], refs[4:]
    _, columns, width = x3.shape
    put_rows(acc, self_rows(x3, m_ref, ask_ref))
    for s in range(CAP):
        add_sums(acc, pick(ask_ref, s), self_ref[:, s * width : (s + 1) * width])
    lane = lax.broadcasted_iota(jnp.int32, ids_refs[0].shape, 1)
    for k in range(1, peers):
        came = came_refs[k - 1]
        ids = jnp.zeros(lane.shape, jnp.int32)
        for s in range(CAP):
            here = slice(s * width, (s + 1) * width)
            asked = jnp.max(came[columns : columns + TAIL, here].astype(F32)).astype(jnp.int32)
            ids = jnp.where(lane == s, asked, ids)
            add_sums(acc, asked, came[:columns, here])
        ids_refs[k - 1][...] = ids


def first_rows(values, operator, ask, came, own_mirror, peers):
    _, columns, width = values.shape
    outs = call(
        functools.partial(first_rows_kernel, peers),
        "first_rows",
        [shape(values.shape, F32)] + [shape((1, width), jnp.int32)] * (peers - 1),
        [vmem()] * (peers + 3),
        flops=2 ** 27,
        moved=2 ** 20,
    )(ask, *came[1:], values, operator, own_mirror)
    return outs[0], [None] + list(outs[1:])


def below_kernel(sums_ref, half_ref, out_ref):
    top = sums_ref.shape[0]
    share, columns, width = half_ref.shape
    out_ref[:top, :] = sums_ref[...]
    for b in range(share):
        row, left = top + b // CAP * columns, b % CAP * width
        out_ref[row : row + columns, left : left + width] = half_ref[b]


def below(sums, half):
    share, columns, width = half.shape
    out = shape((sums.shape[0] + share // CAP * columns, sums.shape[1]), BF16)
    return call(below_kernel, "below", out, [vmem(), vmem()])(sums, half)


def stack_kernel(count, *refs):
    share = refs[0].shape[0]
    for k, ref in enumerate(refs[:count]):
        refs[-1][k * share : (k + 1) * share] = ref[...]


def stack(pieces, sums):
    share, columns, width = pieces[0].shape
    out = shape((len(pieces) * share, columns, width), BF16)
    kernel = functools.partial(stack_kernel, len(pieces))
    return call(kernel, "stack", out, [vmem()] * (len(pieces) + len(sums)), flops=2 ** 31)(*pieces, *sums)


def stack_more_kernel(first_ref, *refs):
    out_ref = refs[-1]
    at, columns, width = first_ref.shape
    out_ref[:at] = first_ref[...]
    for ref in refs[:-1]:
        share = (ref.shape[0] - TAIL) // columns * CAP - CAP
        for b in range(share):
            row, left = columns + TAIL + b // CAP * columns, b % CAP * width
            out_ref[at + b] = ref[row : row + columns, left : left + width]
        at += share


def stack_more(first, chunks):
    at, columns, width = first.shape
    share = (chunks[0].shape[0] - TAIL) // columns * CAP - CAP
    out = shape((at + len(chunks) * share, columns, width), BF16)
    return call(stack_more_kernel, "stack_more", out, [vmem()] * (1 + len(chunks)))(first, *chunks)


def half_rows(before, far_ref, m_ref, first, share):
    columns, width = before.shape[1:]
    both = CAP * width
    rows = pl.ds(pl.multiple_of(first * width, share * width), share * width)
    if m_ref.shape[1] <= GROUP * width:
        own = dot(far_ref[:, both:], m_ref[rows, both:], NT)
    else:

        def add_peer(k, total):
            here = pl.ds(pl.multiple_of(k * both, both), both)
            return total + dot(far_ref[:, here], m_ref[rows, here], NT)

        zeros = jnp.zeros((columns, share * width), F32)
        own = lax.fori_loop(1, m_ref.shape[1] // both, add_peer, zeros)
    return [before[first + b] + own[:, b * width : (b + 1) * width] for b in range(share)]


def give_rows_kernel(peers, *refs):
    ask_refs, refs = refs[: peers - 1], refs[peers - 1 :]
    before, mine_ref, other_ref, m_ref, give_ref, far_ref = refs
    share = give_ref.shape[0]
    both = CAP * before.shape[2]
    for k in range(1, peers):
        far_ref[:, k * both : (k + 1) * both] = far_of(share, mine_ref, other_ref, ask_refs[k - 1], k - 1)
    far_ref[:, :both] = jnp.zeros((far_ref.shape[0], both), BF16)
    rows = half_rows(before, far_ref, m_ref, (1 - lax.axis_index("rep")) * share, share)
    for b in range(share):
        give_ref[b] = rows[b].astype(BF16)


def give_rows(before, asks, mine, other, operator, peers, reps):
    blocks_dev, columns, width = before.shape
    return call(
        functools.partial(give_rows_kernel, peers),
        "give_rows",
        [shape((blocks_dev // reps, columns, width), BF16), shape((columns, peers * CAP * width), BF16)],
        [vmem()] * (peers + 3),
        flops=2 ** 27,
        moved=2 ** 20,
    )(*asks[1:], before, mine, other, operator)


def keep_rows_kernel(before, far_ref, m_ref, keep_ref):
    share = keep_ref.shape[0]
    rows = half_rows(before, far_ref, m_ref, lax.axis_index("rep") * share, share)
    for b in range(share):
        keep_ref[b] = rows[b]


def keep_rows(before, far, operator, reps):
    blocks_dev, columns, width = before.shape
    return call(
        keep_rows_kernel,
        "keep_rows",
        shape((blocks_dev // reps, columns, width), F32),
        [vmem()] * 3,
        flops=2 ** 27,
        moved=2 ** 20,
    )(before, far, operator)


def late_self_kernel(ask_ref, x3, self_ref, m_ref, act_ref, shared_ref, acc, out_ref):
    width = x3.shape[2]
    put_rows(acc, self_rows(x3, m_ref, ask_ref))
    for s in range(CAP):
        add_sums(acc, pick(ask_ref, s), self_ref[:, s * width : (s + 1) * width])
    half = lax.axis_index("rep")
    blocks = act_ref.shape[0]
    out_ref[pl.ds(half * blocks, blocks)] = act_ref[...]
    for b in range(blocks):
        at = (blocks + b) * width
        out_ref[(1 - half) * blocks + b] = shared_ref[:, at : at + width]


def late_self(ask, values, own_mirror, operator, act, shared):
    return call(
        late_self_kernel,
        "late_self",
        [shape(values.shape, F32), shape(values.shape, BF16)],
        [vmem()] * 6,
        flops=2 ** 26,
    )(ask, values, own_mirror, operator, act, shared)


def late_rows_kernel(k, before, ids_ref, came_ref, m_ref, out_ref, acc):
    width = acc.shape[2]
    both = CAP * width
    put_rows(acc, own_rows(came_ref[:, both : 2 * both], m_ref, k), before)
    for s in range(CAP):
        add_sums(acc, pick(ids_ref, s), came_ref[:, s * width : (s + 1) * width])
    out_ref[...] = acc[...].astype(out_ref.dtype)


def late_rows(before, ids, came, operator, k, dtype):
    return call(
        functools.partial(late_rows_kernel, k),
        "late_rows",
        shape(before.shape, dtype),
        [vmem()] * 4,
        [pltpu.VMEM(before.shape, F32)],
        flops=2 ** 29,
    )(before, ids, came, operator)


def add_kernel(keep_ref, came_ref, out_ref):
    out_ref[...] = (keep_ref[...] + came_ref[...].astype(F32)).astype(BF16)


def add_up(keep, came):
    return call(add_kernel, "add_up", shape(came.shape, BF16), [vmem(), vmem()])(keep, came)


def widen_kernel(feats, *refs):
    out_ref = refs[feats]
    share, columns, width = refs[0].shape
    me = lax.axis_index("feat")
    for q in range(feats):
        rows = pl.ds(pl.multiple_of(lax.rem(me + q, feats) * columns, columns), columns)
        for b in range(share):
            out_ref[rows, b * width : (b + 1) * width] = refs[q][b]


def widen(parts):
    share, columns, width = parts[0].shape
    out = shape((len(parts) * columns, share * width), BF16)
    return call(functools.partial(widen_kernel, len(parts)), "widen", out, [vmem()] * len(parts))(*parts)


def dense_kernel(feats, *refs):
    sums, wide_cot, refs = refs[:feats], refs[feats], refs[feats + 1 :]
    w_ref, act_ref, give_ref, spread_ref, term_ref, wide, pre_scr, grad = refs
    share, columns, width = act_ref.shape
    me = lax.axis_index("feat")
    rows = [pl.ds(pl.multiple_of(lax.rem(me + q, feats) * columns, columns), columns) for q in range(feats)]
    for q in range(feats):
        for b in range(share):
            wide[rows[q], b * width : (b + 1) * width] = sums[q][b]
    pre = dot(w_ref[...], wide[...], TN)
    pre_scr[...] = pre
    sig = jax.nn.sigmoid(pre)
    factor = wide_cot[...].astype(F32) * sig * (1.0 + pre * (1.0 - sig))
    grad[...] = factor.astype(BF16)
    spread = dot(w_ref[rows[0], :], grad[...]).astype(BF16)
    term_ref[...] = dot(grad[rows[0], :], wide[...], NT).astype(BF16)
    wide_share = share * width
    give_ref[:, :wide_share] = spread
    for b in range(share):
        spread_ref[b] = spread[:, b * width : (b + 1) * width]
    own = pre_scr[rows[0], :]
    act = (own * jax.nn.sigmoid(own)).astype(BF16)
    give_ref[:, wide_share:] = act
    for b in range(share):
        act_ref[b] = act[:, b * width : (b + 1) * width]


def dense(sums, cot, weight, feats):
    share, columns, width = sums[0].shape
    features = weight.shape[0]
    return call(
        functools.partial(dense_kernel, feats),
        "dense",
        [
            shape((share, columns, width), BF16),
            shape((columns, 2 * share * width), BF16),
            shape((share, columns, width), BF16),
            shape((columns, features), BF16),
        ],
        [vmem()] * (feats + 2),
        [
            pltpu.VMEM((features, share * width), BF16),
            pltpu.VMEM((features, share * width), F32),
            pltpu.VMEM((features, share * width), BF16),
        ],
        flops=2 ** 28,
        moved=2 ** 20,
    )(*sums, cot, weight)


def send_kernel(peers, *refs):
    ids_refs, refs = refs[: peers - 1], refs[peers - 1 :]
    mine_ref, came_ref, m_ref, refs = refs[0], refs[1], refs[2], refs[3:]
    x3, refs = refs[0], refs[1:]
    send_refs, refs = refs[: peers - 1], refs[peers - 1 :]
    self_ref, mir = refs
    share, _, width = mine_ref.shape
    both = CAP * width
    half = lax.axis_index("rep")
    x3[pl.ds(half * share, share)] = mine_ref[...]
    for b in range(share):
        x3[(1 - half) * share + b] = came_ref[:, b * width : (b + 1) * width]
    mirrored(lanes(x3), m_ref, mir, peers * CAP, width)
    self_ref[...] = mir[:, :both]
    for k in range(1, peers):
        out = send_refs[k - 1]
        out[:, :both] = mir[:, k * both : (k + 1) * both].astype(BF16)
        for s in range(CAP):
            at = (CAP + s) * width
            out[:, at : at + width] = x3[pick(ids_refs[k - 1], s)]


def sends_of(mine, came, operator, ids, peers, reps):
    share, columns, width = mine.shape
    chunk = 2 * CAP * width
    outs = call(
        functools.partial(send_kernel, peers),
        "sends",
        [shape((share * reps, columns, width), BF16)]
        + [shape((columns, chunk), BF16)] * (peers - 1)
        + [shape((columns, CAP * width), F32)],
        [vmem()] * (peers + 2),
        [pltpu.VMEM((columns, peers * CAP * width), F32)],
        flops=2 ** 28,
        moved=2 ** 21,
    )(*ids[1:], mine, came, operator)
    return outs[0], [None] + list(outs[1:peers]), outs[peers]


def pair_kernel(at, mine_ref, came_ref, out_ref):
    out_ref[...] = (mine_ref[...].astype(F32) + came_ref[:, at:].astype(F32)).astype(out_ref.dtype)


def pair_sum(mine, came, dtype, at=0):
    kernel = functools.partial(pair_kernel, at)
    return call(kernel, "pair_sum", shape(mine.shape, dtype), [vmem(), vmem()])(mine, came)


def beside_kernel(chunk_ref, term_ref, out_ref):
    width = chunk_ref.shape[1]
    out_ref[:, :width] = chunk_ref[...]
    out_ref[:, width:] = term_ref[...]


def beside(chunk, term):
    out = shape((chunk.shape[0], chunk.shape[1] + term.shape[1]), BF16)
    return call(beside_kernel, "beside", out, [vmem(), vmem()])(chunk, term)


def split_kernel(mine_ref, came_ref, give_ref, keep_ref, total):
    half = lax.axis_index("rep")
    part = keep_ref.shape[1]
    total[...] = mine_ref[...].astype(F32) + came_ref[...].astype(F32)
    give_ref[...] = total[:, pl.ds(pl.multiple_of((1 - half) * part, part), part)].astype(BF16)
    keep_ref[...] = total[:, pl.ds(pl.multiple_of(half * part, part), part)]


def split_sum(mine, came, reps):
    columns, features = mine.shape
    part = (columns, features // reps)
    return call(
        split_kernel,
        "split_sum",
        [shape(part, BF16), shape(part, F32)],
        [vmem()] * 2,
        [pltpu.VMEM(mine.shape, F32)],
    )(mine, came)


def half_term(term, peers, reps):
    give, total = split_sum(term, across(term, peers, 1), reps)
    total = pair_sum(total, ahead(give, "rep", reps, 1), BF16)
    bit = 2
    while 2 * bit < peers:
        total = pair_sum(total, across(total, peers, bit), BF16)
        bit *= 2
    return total


def finish_kernel(mine_ref, other_ref, share_ref, other_share_ref, grad_ref, weight_ref):
    half = lax.axis_index("rep")
    share = share_ref.shape[1]
    grad_ref[...] = (mine_ref[...].astype(F32) + other_ref[...].astype(F32)).astype(BF16)
    weight_ref[pl.ds(pl.multiple_of(half * share, share), share), :] = share_ref[...].T
    weight_ref[pl.ds(pl.multiple_of((1 - half) * share, share), share), :] = other_share_ref[...].T


def finish(mine, other, share, other_share):
    columns, width = share.shape
    return call(
        finish_kernel,
        "finish",
        [shape(mine.shape, BF16), shape((2 * width, columns), F32)],
        [vmem()] * 4,
    )(mine, other, share, other_share)


def ahead(value, axis, size, k):
    return lax.ppermute(value, axis, [(i, (i + k) % size) for i in range(size)])


def across(value, peers, k):
    return lax.ppermute(value, "graph", [(i, i ^ k) for i in range(peers)])


def after(value, first):
    return lax.optimization_barrier((value, first))[0]


def local(features, weight, cotangent, tiles, tile_row, tile_col, tile_count):
    blocks_dev, _, width = features.shape
    peers = lax.axis_size("graph")
    feats = lax.axis_size("feat")
    reps = lax.axis_size("rep")
    far_first = sorted(range(1, peers), key=lambda k: (-(k & (peers // 2)), k))

    half, table = prepare(features, tile_row, tile_col, peers, reps)
    operator, asks = list_operator(tiles, table, tile_count, peers, blocks_dev)
    sends, own_mirror, own_cot = first_sends(features, cotangent, operator, asks[1:], peers, reps)
    middle = peers // 2
    pieces = [across(half, peers, j) for j in range(1, middle)]
    crossed = across(half, peers, middle)
    came = [None] * peers
    for k in far_first:
        if k >= middle:
            came[k] = across(sends[k], peers, k)
    for j in range(1, middle):
        chunk, pieces[j - 1] = lax.optimization_barrier((below(sends[j], crossed), pieces[j - 1]))
        came[j] = across(chunk, peers, j)
    held = after(own_cot, crossed)
    cots = [own_cot] + [ahead(held, "feat", feats, feats - q) for q in range(1, feats)]
    stacked = stack(pieces + [crossed], came[middle:-1])
    came[1:middle], came[-1], stacked = lax.optimization_barrier((came[1:middle], came[-1], stacked))
    stacked, cots = lax.optimization_barrier((stacked, cots))
    stacked = stack_more(stacked, came[1:middle])
    swapped = ahead(stacked, "rep", reps, 1)
    acc, ids = first_rows(features, operator, asks[0], came, own_mirror, peers)
    give, asked = give_rows(acc, asks, stacked, swapped, operator, peers, reps)
    keep = keep_rows(acc, asked, operator, reps)

    mine = add_up(keep, ahead(give, "rep", reps, 1))
    cot = widen(cots)
    sums = [mine] + [ahead(mine, "feat", feats, feats - q) for q in range(1, feats)]
    act, give, spread, term = dense(sums, cot, weight, feats)
    shared = ahead(give, "rep", reps, 1)
    term = half_term(term, peers, reps)
    values, sends, own_mirror = sends_of(spread, shared, operator, ids, peers, reps)

    *firsts, last = sorted(range(1, peers), key=lambda k: (k == peers - 1, -(k & middle), k))
    sends[last] = beside(sends[last], term)
    came = [None] + [across(sends[k], peers, k) for k in range(1, peers)]
    acc, activated = late_self(asks[0], values, own_mirror, operator, act, shared)
    for k in firsts:
        acc = late_rows(acc, ids[k], came[k], operator, k, F32)
    part = late_rows(acc, ids[last], came[last], operator, last, BF16)
    total = pair_sum(term, came[last], F32, 2 * CAP * width)
    input_grad, weight_grad = finish(
        part, ahead(part, "rep", reps, 1), total, ahead(total, "rep", reps, 1)
    )
    return (activated, input_grad, weight_grad)


def solution(mesh):
    placed = (
        P(("parts", "graph"), "feat", None),
        P(),
        P(("parts", "graph"), "feat", None),
        P(("parts", "graph", "rep"), None, None),
        P(("parts", "graph", "rep")),
        P(("parts", "graph", "rep")),
        P(("parts", "graph", "rep")),
    )
    return jax.shard_map(
        local,
        mesh=mesh,
        in_specs=placed,
        out_specs=(
            P(("parts", "graph"), "feat", None),
            P(("parts", "graph"), "feat", None),
            P("parts", "feat"),
        ),
        check_vma=False,
    )
```

```python
import functools

import jax
import jax.numpy as jnp
from jax import lax
from jax.experimental import pallas as pl
from jax.experimental.pallas import tpu as pltpu
from jax.sharding import PartitionSpec as P

CAP = 2
GROUP = 8
CHUNK = 16
SIDES = 1
PLACE_ROWS = 8
PLACE_BUFFER = 2 ** 22
TAIL = 16
VMEM_LIMIT = 40 * 2 ** 20
VMEM_MOST = 50 * 2 ** 20
VMEM_ALL = 58 * 2 ** 20

NT = (((1,), (1,)), ((), ()))
TN = (((0,), (0,)), ((), ()))
F32 = jnp.float32
BF16 = jnp.bfloat16


def vmem():
    return pl.BlockSpec(memory_space=pltpu.VMEM)


def smem():
    return pl.BlockSpec(memory_space=pltpu.SMEM)


def hbm():
    return pl.BlockSpec(memory_space=pltpu.HBM)


def shape(dims, dtype):
    return jax.ShapeDtypeStruct(tuple(dims), dtype)


def dot(a, b, dims=None):
    if dims is None:
        return jnp.dot(a, b, preferred_element_type=F32)
    return lax.dot_general(a, b, dims, preferred_element_type=F32)


def call(kernel, name, outs, in_specs, scratch=(), flops=0, moved=2 ** 18, limit=VMEM_LIMIT, **kwargs):
    return pl.pallas_call(
        kernel,
        out_shape=outs,
        in_specs=in_specs,
        scratch_shapes=list(scratch),
        compiler_params=pltpu.CompilerParams(vmem_limit_bytes=limit),
        cost_estimate=pl.CostEstimate(flops=flops, bytes_accessed=moved, transcendentals=0),
        name=name,
        **kwargs,
    )


def lanes(x3):
    return jnp.concatenate([x3[b] for b in range(x3.shape[0])], axis=1)


def places(peers, blocks_dev, row, col, table):
    me = lax.axis_index("graph")
    lane = lax.broadcasted_iota(jnp.int32, col.shape, 1)
    place = jnp.zeros(col.shape, jnp.int32)
    for k in range(peers):
        local = col - jnp.bitwise_xor(me, k) * blocks_dev
        inside = (local >= 0) & (local < blocks_dev)
        low = jnp.min(jnp.where(inside, local, blocks_dev - 1), axis=1, keepdims=True)
        high = jnp.max(jnp.where(inside, local, 0), axis=1, keepdims=True)
        table[PLACE_ROWS + k : PLACE_ROWS + k + 1, :] = jnp.where(lane == 0, low, high)
        slot = k * CAP + (local != low).astype(jnp.int32)
        place = jnp.where(inside, slot * blocks_dev + row, place)
    table[:PLACE_ROWS, :] = jnp.broadcast_to(place, (PLACE_ROWS, place.shape[1]))


def table_rows(peers):
    return PLACE_ROWS + -(-peers // 8) * 8


def prepare_kernel(peers, row_ref, col_ref, x3, half_out, table_out, table, half_sem, sem):
    share = half_out.shape[0]
    mine = pl.ds(lax.axis_index("rep") * share, share)
    half_copy = pltpu.make_async_copy(x3.at[mine], half_out, half_sem)
    half_copy.start()
    if table.shape[0] > PLACE_ROWS + peers:
        table[...] = jnp.zeros(table.shape, jnp.int32)
    places(peers, x3.shape[0], row_ref[...], col_ref[...], table)
    copy = pltpu.make_async_copy(table, table_out.at[pl.ds(0, table.shape[0])], sem)
    copy.start()
    half_copy.wait()
    copy.wait()


def prepare(features, tile_row, tile_col, peers, reps):
    per = tile_col.shape[0]
    blocks_dev, columns, width = features.shape
    return call(
        functools.partial(prepare_kernel, peers),
        "prepare",
        [shape((blocks_dev // reps, columns, width), BF16), shape((PLACE_BUFFER // (4 * per), per), jnp.int32)],
        [vmem()] * 3,
        [
            pltpu.VMEM((table_rows(peers), per), jnp.int32),
            pltpu.SemaphoreType.DMA,
            pltpu.SemaphoreType.DMA,
        ],
        limit=VMEM_ALL,
        out_specs=[hbm(), hbm()],
    )(tile_row.reshape(1, per), tile_col.reshape(1, per), features)


def pick(ids_ref, lane):
    ids = ids_ref[...].astype(F32)
    at = lax.broadcasted_iota(jnp.int32, ids.shape, 1)
    return jnp.max(jnp.where(at == lane, ids, 0.0)).astype(jnp.int32)


def operator_kernel(blocks_dev, slots_here, groups, count_ref, table_in, tiles_ref, m_ref, *refs):
    asks, (tiles, acc, place_ref, table, sems, sem, table_sem) = refs[:-7], refs[-7:]
    step = pl.program_id(0)
    per, width = tiles.shape[0], tiles.shape[1]
    chunks = per // CHUNK
    spare = slots_here * blocks_dev

    def chunk_copy(c):
        part = pl.ds(c * CHUNK, CHUNK)
        return pltpu.make_async_copy(tiles_ref.at[part], tiles.at[part], sems.at[c])

    def place_copy():
        return pltpu.make_async_copy(table_in.at[pl.ds(0, PLACE_ROWS)], place_ref, sem)

    def table_copy():
        return pltpu.make_async_copy(table_in.at[pl.ds(0, table.shape[0])], table, table_sem)

    @pl.when(step == 0)
    def _():
        place_copy().start()
        table_copy().start()
        for c in range(chunks):
            chunk_copy(c).start()

    acc[...] = jnp.zeros_like(acc)

    @pl.when(step == 0)
    def _():
        place_copy().wait()

    count = count_ref[0]

    def add_chunk(c, carry):
        @pl.when(step == 0)
        def _():
            chunk_copy(c).wait()

        for u in range(CHUNK):
            t = c * CHUNK + u
            place = place_ref[0, t]
            here = t < count
            if groups > 1:
                place = place - step * spare
                here = here & (place >= 0) & (place < spare)
            place = jnp.where(here, place, spare)
            side = u % SIDES
            acc[side, place] = acc[side, place] + tiles[t].astype(F32)
        return carry

    lax.fori_loop(0, chunks, add_chunk, 0)
    for s in range(slots_here):
        for r in range(blocks_dev):
            total = acc[0, s * blocks_dev + r]
            for side in range(1, SIDES):
                total = total + acc[side, s * blocks_dev + r]
            m_ref[r * width : (r + 1) * width, s * width : (s + 1) * width] = total.astype(BF16)

    @pl.when(step == 0)
    def _():
        table_copy().wait()
        for k, ask_ref in enumerate(asks):
            ask_ref[...] = table[PLACE_ROWS + k : PLACE_ROWS + k + 1, :]


def list_operator(tiles, table, tile_count, peers, blocks_dev):
    per, width = tiles.shape[0], tiles.shape[1]
    slots = peers * CAP
    slots_here = min(slots, GROUP)
    groups = slots // slots_here
    outs = call(
        functools.partial(operator_kernel, blocks_dev, slots_here, groups),
        "operator",
        [shape((blocks_dev * width, slots * width), BF16)] + [shape((1, per), jnp.int32)] * peers,
        [smem(), hbm(), hbm()],
        [
            pltpu.VMEM((per, width, width), BF16),
            pltpu.VMEM((SIDES, slots_here * blocks_dev + 1, width, width), F32),
            pltpu.SMEM((PLACE_ROWS, per), jnp.int32),
            pltpu.VMEM((table_rows(peers), per), jnp.int32),
            pltpu.SemaphoreType.DMA((per // CHUNK,)),
            pltpu.SemaphoreType.DMA,
            pltpu.SemaphoreType.DMA,
        ],
        moved=2 ** 24,
        limit=VMEM_MOST,
        grid=(groups,),
        out_specs=[pl.BlockSpec((blocks_dev * width, slots_here * width), lambda i: (0, i))] + [vmem()] * peers,
    )(tile_count, table, tiles)
    return outs[0], list(outs[1:])


def mirrored(near, m_ref, mir, slots, width):
    if slots <= GROUP:
        mir[...] = dot(near, m_ref[...])
    else:
        part = GROUP * width

        @pl.loop(0, slots // GROUP)
        def _(i):
            where = pl.ds(pl.multiple_of(i * part, part), part)
            mir[:, where] = dot(near, m_ref[:, where])


def first_sends_kernel(peers, *refs):
    ask_refs, refs = refs[: peers - 1], refs[peers - 1 :]
    x3, cot, m_ref, refs = refs[0], refs[1], refs[2], refs[3:]
    send_refs, self_ref, cot_ref, mir = refs[: peers - 1], refs[peers - 1], refs[peers], refs[peers + 1]
    _, columns, width = x3.shape
    share = cot_ref.shape[0]
    cot_ref[...] = cot[pl.ds(lax.axis_index("rep") * share, share)]
    both = CAP * width
    mirrored(lanes(x3), m_ref, mir, peers * CAP, width)
    self_ref[...] = mir[:, :both]
    lane = lax.broadcasted_iota(jnp.int32, (TAIL, both), 1)
    for k in range(1, peers):
        out = send_refs[k - 1]
        out[:columns, :] = mir[:, k * both : (k + 1) * both].astype(BF16)
        low, high = ask_refs[k - 1][:, :1], ask_refs[k - 1][:, 1:2]
        out[columns:, :] = jnp.where(lane < width, low, high).astype(F32).astype(BF16)


def first_sends(values, cotangent, operator, asks, peers, reps):
    blocks_dev, columns, width = values.shape
    outs = call(
        functools.partial(first_sends_kernel, peers),
        "first_sends",
        [shape((columns + TAIL, CAP * width), BF16)] * (peers - 1)
        + [shape((columns, CAP * width), F32), shape((blocks_dev // reps, columns, width), BF16)],
        [vmem()] * (peers + 2),
        [pltpu.VMEM((columns, peers * CAP * width), F32)],
        flops=2 ** 28,
        moved=2 ** 21,
    )(*asks, values, cotangent, operator)
    return [None] + list(outs[: peers - 1]), outs[peers - 1], outs[peers]


def add_sums(acc, block, sums):
    acc[block] = acc[block] + sums.astype(F32)


def own_rows(far, m_ref, k):
    both = far.shape[1]
    return dot(far, m_ref[:, k * both : (k + 1) * both], NT)


def put_rows(acc, own, before=None):
    blocks_dev, _, width = acc.shape
    for b in range(blocks_dev):
        add = own[:, b * width : (b + 1) * width]
        acc[b] = add if before is None else before[b] + add


def self_rows(x3, m_ref, ask_ref):
    far = jnp.concatenate([x3[pick(ask_ref, s)] for s in range(CAP)], axis=1)
    return own_rows(far, m_ref, 0)


def far_of(share, mine_ref, other_ref, ask_ref, at):
    first = lax.axis_index("rep") * share
    blocks = []
    for s in range(CAP):
        local = pick(ask_ref, s) - first
        own = (local >= 0) & (local < share)
        here = at * share + jnp.where(own, local, 0)
        there = at * share + jnp.where(own, 0, jnp.where(local < 0, local + share, local - share))
        blocks.append(jnp.where(own, mine_ref[here], other_ref[there]))
    return jnp.concatenate(blocks, axis=1)


def first_rows_kernel(peers, *refs):
    ask_ref, refs = refs[0], refs[1:]
    came_refs, refs = refs[: peers - 1], refs[peers - 1 :]
    x3, m_ref, self_ref, acc, ids_refs = refs[0], refs[1], refs[2], refs[3], refs[4:]
    _, columns, width = x3.shape
    put_rows(acc, self_rows(x3, m_ref, ask_ref))
    for s in range(CAP):
        add_sums(acc, pick(ask_ref, s), self_ref[:, s * width : (s + 1) * width])
    lane = lax.broadcasted_iota(jnp.int32, ids_refs[0].shape, 1)
    for k in range(1, peers):
        came = came_refs[k - 1]
        ids = jnp.zeros(lane.shape, jnp.int32)
        for s in range(CAP):
            here = slice(s * width, (s + 1) * width)
            asked = jnp.max(came[columns : columns + TAIL, here].astype(F32)).astype(jnp.int32)
            ids = jnp.where(lane == s, asked, ids)
            add_sums(acc, asked, came[:columns, here])
        ids_refs[k - 1][...] = ids


def first_rows(values, operator, ask, came, own_mirror, peers):
    _, columns, width = values.shape
    outs = call(
        functools.partial(first_rows_kernel, peers),
        "first_rows",
        [shape(values.shape, F32)] + [shape((1, width), jnp.int32)] * (peers - 1),
        [vmem()] * (peers + 3),
        flops=2 ** 27,
        moved=2 ** 20,
    )(ask, *came[1:], values, operator, own_mirror)
    return outs[0], [None] + list(outs[1:])


def below_kernel(sums_ref, half_ref, out_ref):
    top = sums_ref.shape[0]
    share, columns, width = half_ref.shape
    out_ref[:top, :] = sums_ref[...]
    for b in range(share):
        row, left = top + b // CAP * columns, b % CAP * width
        out_ref[row : row + columns, left : left + width] = half_ref[b]


def below(sums, half):
    share, columns, width = half.shape
    out = shape((sums.shape[0] + share // CAP * columns, sums.shape[1]), BF16)
    return call(below_kernel, "below", out, [vmem(), vmem()])(sums, half)


def stack_kernel(count, *refs):
    share = refs[0].shape[0]
    for k, ref in enumerate(refs[:count]):
        refs[-1][k * share : (k + 1) * share] = ref[...]


def stack(pieces, sums):
    share, columns, width = pieces[0].shape
    out = shape((len(pieces) * share, columns, width), BF16)
    kernel = functools.partial(stack_kernel, len(pieces))
    return call(kernel, "stack", out, [vmem()] * (len(pieces) + len(sums)), flops=2 ** 31)(*pieces, *sums)


def stack_more_kernel(first_ref, *refs):
    out_ref = refs[-1]
    at, columns, width = first_ref.shape
    out_ref[:at] = first_ref[...]
    for ref in refs[:-1]:
        share = (ref.shape[0] - TAIL) // columns * CAP - CAP
        for b in range(share):
            row, left = columns + TAIL + b // CAP * columns, b % CAP * width
            out_ref[at + b] = ref[row : row + columns, left : left + width]
        at += share


def stack_more(first, chunks):
    at, columns, width = first.shape
    share = (chunks[0].shape[0] - TAIL) // columns * CAP - CAP
    out = shape((at + len(chunks) * share, columns, width), BF16)
    return call(stack_more_kernel, "stack_more", out, [vmem()] * (1 + len(chunks)))(first, *chunks)


def half_rows(before, far_ref, m_ref, first, share):
    columns, width = before.shape[1:]
    both = CAP * width
    rows = pl.ds(pl.multiple_of(first * width, share * width), share * width)
    if m_ref.shape[1] <= GROUP * width:
        own = dot(far_ref[:, both:], m_ref[rows, both:], NT)
    else:

        def add_peer(k, total):
            here = pl.ds(pl.multiple_of(k * both, both), both)
            return total + dot(far_ref[:, here], m_ref[rows, here], NT)

        zeros = jnp.zeros((columns, share * width), F32)
        own = lax.fori_loop(1, m_ref.shape[1] // both, add_peer, zeros)
    return [before[first + b] + own[:, b * width : (b + 1) * width] for b in range(share)]


def give_rows_kernel(peers, *refs):
    ask_refs, refs = refs[: peers - 1], refs[peers - 1 :]
    before, mine_ref, other_ref, m_ref, give_ref, far_ref = refs
    share = give_ref.shape[0]
    both = CAP * before.shape[2]
    for k in range(1, peers):
        far_ref[:, k * both : (k + 1) * both] = far_of(share, mine_ref, other_ref, ask_refs[k - 1], k - 1)
    far_ref[:, :both] = jnp.zeros((far_ref.shape[0], both), BF16)
    rows = half_rows(before, far_ref, m_ref, (1 - lax.axis_index("rep")) * share, share)
    for b in range(share):
        give_ref[b] = rows[b].astype(BF16)


def give_rows(before, asks, mine, other, operator, peers, reps):
    blocks_dev, columns, width = before.shape
    return call(
        functools.partial(give_rows_kernel, peers),
        "give_rows",
        [shape((blocks_dev // reps, columns, width), BF16), shape((columns, peers * CAP * width), BF16)],
        [vmem()] * (peers + 3),
        flops=2 ** 27,
        moved=2 ** 20,
    )(*asks[1:], before, mine, other, operator)


def keep_rows_kernel(before, far_ref, m_ref, keep_ref):
    share = keep_ref.shape[0]
    rows = half_rows(before, far_ref, m_ref, lax.axis_index("rep") * share, share)
    for b in range(share):
        keep_ref[b] = rows[b]


def keep_rows(before, far, operator, reps):
    blocks_dev, columns, width = before.shape
    return call(
        keep_rows_kernel,
        "keep_rows",
        shape((blocks_dev // reps, columns, width), F32),
        [vmem()] * 3,
        flops=2 ** 27,
        moved=2 ** 20,
    )(before, far, operator)


def late_self_kernel(ask_ref, x3, self_ref, m_ref, act_ref, shared_ref, acc, out_ref):
    width = x3.shape[2]
    put_rows(acc, self_rows(x3, m_ref, ask_ref))
    for s in range(CAP):
        add_sums(acc, pick(ask_ref, s), self_ref[:, s * width : (s + 1) * width])
    half = lax.axis_index("rep")
    blocks = act_ref.shape[0]
    out_ref[pl.ds(half * blocks, blocks)] = act_ref[...]
    for b in range(blocks):
        at = (blocks + b) * width
        out_ref[(1 - half) * blocks + b] = shared_ref[:, at : at + width]


def late_self(ask, values, own_mirror, operator, act, shared):
    return call(
        late_self_kernel,
        "late_self",
        [shape(values.shape, F32), shape(values.shape, BF16)],
        [vmem()] * 6,
        flops=2 ** 26,
    )(ask, values, own_mirror, operator, act, shared)


def late_rows_kernel(k, before, ids_ref, came_ref, m_ref, out_ref, acc):
    width = acc.shape[2]
    both = CAP * width
    put_rows(acc, own_rows(came_ref[:, both : 2 * both], m_ref, k), before)
    for s in range(CAP):
        add_sums(acc, pick(ids_ref, s), came_ref[:, s * width : (s + 1) * width])
    out_ref[...] = acc[...].astype(out_ref.dtype)


def late_rows(before, ids, came, operator, k, dtype):
    return call(
        functools.partial(late_rows_kernel, k),
        "late_rows",
        shape(before.shape, dtype),
        [vmem()] * 4,
        [pltpu.VMEM(before.shape, F32)],
        flops=2 ** 29,
    )(before, ids, came, operator)


def add_kernel(keep_ref, came_ref, out_ref):
    out_ref[...] = (keep_ref[...] + came_ref[...].astype(F32)).astype(BF16)


def add_up(keep, came):
    return call(add_kernel, "add_up", shape(came.shape, BF16), [vmem(), vmem()])(keep, came)


def widen_kernel(feats, *refs):
    out_ref = refs[feats]
    share, columns, width = refs[0].shape
    me = lax.axis_index("feat")
    for q in range(feats):
        rows = pl.ds(pl.multiple_of(lax.rem(me + q, feats) * columns, columns), columns)
        for b in range(share):
            out_ref[rows, b * width : (b + 1) * width] = refs[q][b]


def widen(parts):
    share, columns, width = parts[0].shape
    out = shape((len(parts) * columns, share * width), BF16)
    return call(functools.partial(widen_kernel, len(parts)), "widen", out, [vmem()] * len(parts))(*parts)


def dense_kernel(feats, *refs):
    sums, wide_cot, refs = refs[:feats], refs[feats], refs[feats + 1 :]
    w_ref, act_ref, give_ref, spread_ref, own_grad_ref, wide, pre_scr, grad = refs
    share, columns, width = act_ref.shape
    me = lax.axis_index("feat")
    rows = [pl.ds(pl.multiple_of(lax.rem(me + q, feats) * columns, columns), columns) for q in range(feats)]
    for q in range(feats):
        for b in range(share):
            wide[rows[q], b * width : (b + 1) * width] = sums[q][b]
    pre = dot(w_ref[...], wide[...], TN)
    pre_scr[...] = pre
    sig = jax.nn.sigmoid(pre)
    factor = wide_cot[...].astype(F32) * sig * (1.0 + pre * (1.0 - sig))
    grad[...] = factor.astype(BF16)
    spread = dot(w_ref[rows[0], :], grad[...]).astype(BF16)
    own_grad_ref[...] = grad[rows[0], :]
    wide_share = share * width
    give_ref[:, :wide_share] = spread
    for b in range(share):
        spread_ref[b] = spread[:, b * width : (b + 1) * width]
    own = pre_scr[rows[0], :]
    act = (own * jax.nn.sigmoid(own)).astype(BF16)
    give_ref[:, wide_share:] = act
    for b in range(share):
        act_ref[b] = act[:, b * width : (b + 1) * width]


def dense(sums, cot, weight, feats):
    share, columns, width = sums[0].shape
    features = weight.shape[0]
    return call(
        functools.partial(dense_kernel, feats),
        "dense",
        [
            shape((share, columns, width), BF16),
            shape((columns, 2 * share * width), BF16),
            shape((share, columns, width), BF16),
            shape((columns, share * width), BF16),
            shape((features, share * width), BF16),
        ],
        [vmem()] * (feats + 2),
        [
            pltpu.VMEM((features, share * width), F32),
            pltpu.VMEM((features, share * width), BF16),
        ],
        flops=2 ** 28,
        moved=2 ** 20,
    )(*sums, cot, weight)


def term_kernel(own_grad_ref, wide, term_ref):
    term_ref[...] = dot(own_grad_ref[...], wide[...], NT).astype(BF16)


def term_of(own_grad, wide):
    out = shape((own_grad.shape[0], wide.shape[0]), BF16)
    return call(term_kernel, "term", out, [vmem(), vmem()], flops=2 ** 26)(own_grad, wide)


def send_kernel(peers, *refs):
    ids_refs, refs = refs[: peers - 1], refs[peers - 1 :]
    mine_ref, came_ref, m_ref, refs = refs[0], refs[1], refs[2], refs[3:]
    x3, refs = refs[0], refs[1:]
    send_refs, refs = refs[: peers - 1], refs[peers - 1 :]
    self_ref, mir = refs
    share, _, width = mine_ref.shape
    both = CAP * width
    half = lax.axis_index("rep")
    x3[pl.ds(half * share, share)] = mine_ref[...]
    for b in range(share):
        x3[(1 - half) * share + b] = came_ref[:, b * width : (b + 1) * width]
    mirrored(lanes(x3), m_ref, mir, peers * CAP, width)
    self_ref[...] = mir[:, :both]
    for k in range(1, peers):
        out = send_refs[k - 1]
        out[:, :both] = mir[:, k * both : (k + 1) * both].astype(BF16)
        for s in range(CAP):
            at = (CAP + s) * width
            out[:, at : at + width] = x3[pick(ids_refs[k - 1], s)]


def sends_of(mine, came, operator, ids, peers, reps):
    share, columns, width = mine.shape
    chunk = 2 * CAP * width
    outs = call(
        functools.partial(send_kernel, peers),
        "sends",
        [shape((share * reps, columns, width), BF16)]
        + [shape((columns, chunk), BF16)] * (peers - 1)
        + [shape((columns, CAP * width), F32)],
        [vmem()] * (peers + 2),
        [pltpu.VMEM((columns, peers * CAP * width), F32)],
        flops=2 ** 28,
        moved=2 ** 21,
    )(*ids[1:], mine, came, operator)
    return outs[0], [None] + list(outs[1:peers]), outs[peers]


def pair_kernel(at, mine_ref, came_ref, out_ref):
    out_ref[...] = (mine_ref[...].astype(F32) + came_ref[:, at:].astype(F32)).astype(out_ref.dtype)


def pair_sum(mine, came, dtype, at=0):
    kernel = functools.partial(pair_kernel, at)
    return call(kernel, "pair_sum", shape(mine.shape, dtype), [vmem(), vmem()])(mine, came)


def beside_kernel(chunk_ref, term_ref, out_ref):
    width = chunk_ref.shape[1]
    out_ref[:, :width] = chunk_ref[...]
    out_ref[:, width:] = term_ref[...]


def beside(chunk, term):
    out = shape((chunk.shape[0], chunk.shape[1] + term.shape[1]), BF16)
    return call(beside_kernel, "beside", out, [vmem(), vmem()])(chunk, term)


def split_kernel(mine_ref, came_ref, give_ref, keep_ref, total):
    half = lax.axis_index("rep")
    part = keep_ref.shape[1]
    total[...] = mine_ref[...].astype(F32) + came_ref[...].astype(F32)
    give_ref[...] = total[:, pl.ds(pl.multiple_of((1 - half) * part, part), part)].astype(BF16)
    keep_ref[...] = total[:, pl.ds(pl.multiple_of(half * part, part), part)]


def split_sum(mine, came, reps):
    columns, features = mine.shape
    part = (columns, features // reps)
    return call(
        split_kernel,
        "split_sum",
        [shape(part, BF16), shape(part, F32)],
        [vmem()] * 2,
        [pltpu.VMEM(mine.shape, F32)],
    )(mine, came)


def half_term(term, peers, reps):
    give, total = split_sum(term, across(term, peers, 1), reps)
    total = pair_sum(total, ahead(give, "rep", reps, 1), BF16)
    bit = 2
    while 2 * bit < peers:
        total = pair_sum(total, across(total, peers, bit), BF16)
        bit *= 2
    return total


def finish_kernel(mine_ref, other_ref, share_ref, other_share_ref, grad_ref, weight_ref):
    half = lax.axis_index("rep")
    share = share_ref.shape[1]
    grad_ref[...] = (mine_ref[...].astype(F32) + other_ref[...].astype(F32)).astype(BF16)
    weight_ref[pl.ds(pl.multiple_of(half * share, share), share), :] = share_ref[...].T
    weight_ref[pl.ds(pl.multiple_of((1 - half) * share, share), share), :] = other_share_ref[...].T


def finish(mine, other, share, other_share):
    columns, width = share.shape
    return call(
        finish_kernel,
        "finish",
        [shape(mine.shape, BF16), shape((2 * width, columns), F32)],
        [vmem()] * 4,
    )(mine, other, share, other_share)


def ahead(value, axis, size, k):
    return lax.ppermute(value, axis, [(i, (i + k) % size) for i in range(size)])


def across(value, peers, k):
    return lax.ppermute(value, "graph", [(i, i ^ k) for i in range(peers)])


def after(value, first):
    return lax.optimization_barrier((value, first))[0]


def local(features, weight, cotangent, tiles, tile_row, tile_col, tile_count):
    blocks_dev, _, width = features.shape
    peers = lax.axis_size("graph")
    feats = lax.axis_size("feat")
    reps = lax.axis_size("rep")
    far_first = sorted(range(1, peers), key=lambda k: (-(k & (peers // 2)), k))

    half, table = prepare(features, tile_row, tile_col, peers, reps)
    operator, asks = list_operator(tiles, table, tile_count, peers, blocks_dev)
    sends, own_mirror, own_cot = first_sends(features, cotangent, operator, asks[1:], peers, reps)
    middle = peers // 2
    pieces = [across(half, peers, j) for j in range(1, middle)]
    crossed = across(half, peers, middle)
    came = [None] * peers
    for k in far_first:
        if k >= middle:
            came[k] = across(sends[k], peers, k)
    for j in range(1, middle):
        chunk, pieces[j - 1] = lax.optimization_barrier((below(sends[j], crossed), pieces[j - 1]))
        came[j] = across(chunk, peers, j)
    held = after(own_cot, crossed)
    cots = [own_cot] + [ahead(held, "feat", feats, feats - q) for q in range(1, feats)]
    stacked = stack(pieces + [crossed], came[middle:-1])
    came[1:middle], came[-1], stacked = lax.optimization_barrier((came[1:middle], came[-1], stacked))
    stacked, cots = lax.optimization_barrier((stacked, cots))
    stacked = stack_more(stacked, came[1:middle])
    swapped = ahead(stacked, "rep", reps, 1)
    acc, ids = first_rows(features, operator, asks[0], came, own_mirror, peers)
    give, asked = give_rows(acc, asks, stacked, swapped, operator, peers, reps)
    keep = keep_rows(acc, asked, operator, reps)

    mine = add_up(keep, ahead(give, "rep", reps, 1))
    cot = widen(cots)
    sums = [mine] + [ahead(mine, "feat", feats, feats - q) for q in range(1, feats)]
    act, give, spread, own_grad, wide = dense(sums, cot, weight, feats)
    term = term_of(own_grad, wide)
    shared = ahead(give, "rep", reps, 1)
    term = half_term(term, peers, reps)
    values, sends, own_mirror = sends_of(spread, shared, operator, ids, peers, reps)

    *firsts, last = sorted(range(1, peers), key=lambda k: (k == peers - 1, -(k & middle), k))
    sends[last] = beside(sends[last], term)
    came = [None] + [across(sends[k], peers, k) for k in range(1, peers)]
    acc, activated = late_self(asks[0], values, own_mirror, operator, act, shared)
    for k in firsts:
        acc = late_rows(acc, ids[k], came[k], operator, k, F32)
    part = late_rows(acc, ids[last], came[last], operator, last, BF16)
    total = pair_sum(term, came[last], F32, 2 * CAP * width)
    input_grad, weight_grad = finish(
        part, ahead(part, "rep", reps, 1), total, ahead(total, "rep", reps, 1)
    )
    return (activated, input_grad, weight_grad)


def solution(mesh):
    placed = (
        P(("parts", "graph"), "feat", None),
        P(),
        P(("parts", "graph"), "feat", None),
        P(("parts", "graph", "rep"), None, None),
        P(("parts", "graph", "rep")),
        P(("parts", "graph", "rep")),
        P(("parts", "graph", "rep")),
    )
    return jax.shard_map(
        local,
        mesh=mesh,
        in_specs=placed,
        out_specs=(
            P(("parts", "graph"), "feat", None),
            P(("parts", "graph"), "feat", None),
            P("parts", "feat"),
        ),
        check_vma=False,
    )
```

```python
import functools

import jax
import jax.numpy as jnp
from jax import lax
from jax.experimental import pallas as pl
from jax.experimental.pallas import tpu as pltpu
from jax.sharding import PartitionSpec as P

CAP = 2
GROUP = 8
CHUNK = 16
SIDES = 1
PLACE_ROWS = 8
PLACE_BUFFER = 2 ** 22
TAIL = 16
VMEM_LIMIT = 40 * 2 ** 20
VMEM_MOST = 50 * 2 ** 20
VMEM_ALL = 58 * 2 ** 20

NT = (((1,), (1,)), ((), ()))
TN = (((0,), (0,)), ((), ()))
F32 = jnp.float32
BF16 = jnp.bfloat16


def vmem():
    return pl.BlockSpec(memory_space=pltpu.VMEM)


def smem():
    return pl.BlockSpec(memory_space=pltpu.SMEM)


def hbm():
    return pl.BlockSpec(memory_space=pltpu.HBM)


def shape(dims, dtype):
    return jax.ShapeDtypeStruct(tuple(dims), dtype)


def dot(a, b, dims=None):
    if dims is None:
        return jnp.dot(a, b, preferred_element_type=F32)
    return lax.dot_general(a, b, dims, preferred_element_type=F32)


def call(kernel, name, outs, in_specs, scratch=(), flops=0, moved=2 ** 18, limit=VMEM_LIMIT, **kwargs):
    return pl.pallas_call(
        kernel,
        out_shape=outs,
        in_specs=in_specs,
        scratch_shapes=list(scratch),
        compiler_params=pltpu.CompilerParams(vmem_limit_bytes=limit),
        cost_estimate=pl.CostEstimate(flops=flops, bytes_accessed=moved, transcendentals=0),
        name=name,
        **kwargs,
    )


def lanes(x3):
    return jnp.concatenate([x3[b] for b in range(x3.shape[0])], axis=1)


def places(peers, blocks_dev, row, col, table):
    me = lax.axis_index("graph")
    lane = lax.broadcasted_iota(jnp.int32, col.shape, 1)
    place = jnp.zeros(col.shape, jnp.int32)
    for k in range(peers):
        local = col - jnp.bitwise_xor(me, k) * blocks_dev
        inside = (local >= 0) & (local < blocks_dev)
        low = jnp.min(jnp.where(inside, local, blocks_dev - 1), axis=1, keepdims=True)
        high = jnp.max(jnp.where(inside, local, 0), axis=1, keepdims=True)
        table[PLACE_ROWS + k : PLACE_ROWS + k + 1, :] = jnp.where(lane == 0, low, high)
        slot = k * CAP + (local != low).astype(jnp.int32)
        place = jnp.where(inside, slot * blocks_dev + row, place)
    table[:PLACE_ROWS, :] = jnp.broadcast_to(place, (PLACE_ROWS, place.shape[1]))


def table_rows(peers):
    return PLACE_ROWS + -(-peers // 8) * 8


def prepare_kernel(peers, row_ref, col_ref, x3, half_out, table_out, table, half_sem, sem):
    share = half_out.shape[0]
    mine = pl.ds(lax.axis_index("rep") * share, share)
    half_copy = pltpu.make_async_copy(x3.at[mine], half_out, half_sem)
    half_copy.start()
    if table.shape[0] > PLACE_ROWS + peers:
        table[...] = jnp.zeros(table.shape, jnp.int32)
    places(peers, x3.shape[0], row_ref[...], col_ref[...], table)
    copy = pltpu.make_async_copy(table, table_out.at[pl.ds(0, table.shape[0])], sem)
    copy.start()
    half_copy.wait()
    copy.wait()


def prepare(features, tile_row, tile_col, peers, reps):
    per = tile_col.shape[0]
    blocks_dev, columns, width = features.shape
    return call(
        functools.partial(prepare_kernel, peers),
        "prepare",
        [shape((blocks_dev // reps, columns, width), BF16), shape((PLACE_BUFFER // (4 * per), per), jnp.int32)],
        [vmem()] * 3,
        [
            pltpu.VMEM((table_rows(peers), per), jnp.int32),
            pltpu.SemaphoreType.DMA,
            pltpu.SemaphoreType.DMA,
        ],
        limit=VMEM_ALL,
        out_specs=[hbm(), hbm()],
    )(tile_row.reshape(1, per), tile_col.reshape(1, per), features)


def pick(ids_ref, lane):
    ids = ids_ref[...].astype(F32)
    at = lax.broadcasted_iota(jnp.int32, ids.shape, 1)
    return jnp.max(jnp.where(at == lane, ids, 0.0)).astype(jnp.int32)


def operator_kernel(blocks_dev, slots_here, groups, count_ref, table_in, tiles_ref, m_ref, *refs):
    asks, (tiles, acc, place_ref, table, sems, sem, table_sem) = refs[:-7], refs[-7:]
    step = pl.program_id(0)
    per, width = tiles.shape[0], tiles.shape[1]
    chunks = per // CHUNK
    spare = slots_here * blocks_dev

    def chunk_copy(c):
        part = pl.ds(c * CHUNK, CHUNK)
        return pltpu.make_async_copy(tiles_ref.at[part], tiles.at[part], sems.at[c])

    def place_copy():
        return pltpu.make_async_copy(table_in.at[pl.ds(0, PLACE_ROWS)], place_ref, sem)

    def table_copy():
        return pltpu.make_async_copy(table_in.at[pl.ds(0, table.shape[0])], table, table_sem)

    @pl.when(step == 0)
    def _():
        place_copy().start()
        table_copy().start()
        for c in range(chunks):
            chunk_copy(c).start()

    acc[...] = jnp.zeros_like(acc)

    @pl.when(step == 0)
    def _():
        place_copy().wait()

    count = count_ref[0]

    def add_chunk(c, carry):
        @pl.when(step == 0)
        def _():
            chunk_copy(c).wait()

        for u in range(CHUNK):
            t = c * CHUNK + u
            place = place_ref[0, t]
            here = t < count
            if groups > 1:
                place = place - step * spare
                here = here & (place >= 0) & (place < spare)
            place = jnp.where(here, place, spare)
            side = u % SIDES
            acc[side, place] = acc[side, place] + tiles[t].astype(F32)
        return carry

    lax.fori_loop(0, chunks, add_chunk, 0)
    for s in range(slots_here):
        for r in range(blocks_dev):
            total = acc[0, s * blocks_dev + r]
            for side in range(1, SIDES):
                total = total + acc[side, s * blocks_dev + r]
            m_ref[r * width : (r + 1) * width, s * width : (s + 1) * width] = total.astype(BF16)

    @pl.when(step == 0)
    def _():
        table_copy().wait()
        for k, ask_ref in enumerate(asks):
            ask_ref[...] = table[PLACE_ROWS + k : PLACE_ROWS + k + 1, :]


def list_operator(tiles, table, tile_count, peers, blocks_dev):
    per, width = tiles.shape[0], tiles.shape[1]
    slots = peers * CAP
    slots_here = min(slots, GROUP)
    groups = slots // slots_here
    outs = call(
        functools.partial(operator_kernel, blocks_dev, slots_here, groups),
        "operator",
        [shape((blocks_dev * width, slots * width), BF16)] + [shape((1, per), jnp.int32)] * peers,
        [smem(), hbm(), hbm()],
        [
            pltpu.VMEM((per, width, width), BF16),
            pltpu.VMEM((SIDES, slots_here * blocks_dev + 1, width, width), F32),
            pltpu.SMEM((PLACE_ROWS, per), jnp.int32),
            pltpu.VMEM((table_rows(peers), per), jnp.int32),
            pltpu.SemaphoreType.DMA((per // CHUNK,)),
            pltpu.SemaphoreType.DMA,
            pltpu.SemaphoreType.DMA,
        ],
        moved=2 ** 24,
        limit=VMEM_MOST,
        grid=(groups,),
        out_specs=[pl.BlockSpec((blocks_dev * width, slots_here * width), lambda i: (0, i))] + [vmem()] * peers,
    )(tile_count, table, tiles)
    return outs[0], list(outs[1:])


def mirrored(near, m_ref, mir, slots, width):
    if slots <= GROUP:
        mir[...] = dot(near, m_ref[...])
    else:
        part = GROUP * width

        @pl.loop(0, slots // GROUP)
        def _(i):
            where = pl.ds(pl.multiple_of(i * part, part), part)
            mir[:, where] = dot(near, m_ref[:, where])


def first_sends_kernel(peers, *refs):
    ask_refs, refs = refs[: peers - 1], refs[peers - 1 :]
    x3, cot, m_ref, refs = refs[0], refs[1], refs[2], refs[3:]
    send_refs, self_ref, cot_ref, mir = refs[: peers - 1], refs[peers - 1], refs[peers], refs[peers + 1]
    _, columns, width = x3.shape
    share = cot_ref.shape[0]
    cot_ref[...] = cot[pl.ds(lax.axis_index("rep") * share, share)]
    both = CAP * width
    mirrored(lanes(x3), m_ref, mir, peers * CAP, width)
    self_ref[...] = mir[:, :both]
    lane = lax.broadcasted_iota(jnp.int32, (TAIL, both), 1)
    for k in range(1, peers):
        out = send_refs[k - 1]
        out[:columns, :] = mir[:, k * both : (k + 1) * both].astype(BF16)
        low, high = ask_refs[k - 1][:, :1], ask_refs[k - 1][:, 1:2]
        out[columns:, :] = jnp.where(lane < width, low, high).astype(F32).astype(BF16)


def first_sends(values, cotangent, operator, asks, peers, reps):
    blocks_dev, columns, width = values.shape
    outs = call(
        functools.partial(first_sends_kernel, peers),
        "first_sends",
        [shape((columns + TAIL, CAP * width), BF16)] * (peers - 1)
        + [shape((columns, CAP * width), F32), shape((blocks_dev // reps, columns, width), BF16)],
        [vmem()] * (peers + 2),
        [pltpu.VMEM((columns, peers * CAP * width), F32)],
        flops=2 ** 28,
        moved=2 ** 21,
    )(*asks, values, cotangent, operator)
    return [None] + list(outs[: peers - 1]), outs[peers - 1], outs[peers]


def add_sums(acc, block, sums):
    acc[block] = acc[block] + sums.astype(F32)


def own_rows(far, m_ref, k):
    both = far.shape[1]
    return dot(far, m_ref[:, k * both : (k + 1) * both], NT)


def put_rows(acc, own, before=None):
    blocks_dev, _, width = acc.shape
    for b in range(blocks_dev):
        add = own[:, b * width : (b + 1) * width]
        acc[b] = add if before is None else before[b] + add


def self_rows(x3, m_ref, ask_ref):
    far = jnp.concatenate([x3[pick(ask_ref, s)] for s in range(CAP)], axis=1)
    return own_rows(far, m_ref, 0)


def far_of(share, mine_ref, other_ref, ask_ref, at):
    first = lax.axis_index("rep") * share
    blocks = []
    for s in range(CAP):
        local = pick(ask_ref, s) - first
        own = (local >= 0) & (local < share)
        here = at * share + jnp.where(own, local, 0)
        there = at * share + jnp.where(own, 0, jnp.where(local < 0, local + share, local - share))
        blocks.append(jnp.where(own, mine_ref[here], other_ref[there]))
    return jnp.concatenate(blocks, axis=1)


def first_rows_kernel(peers, *refs):
    ask_ref, refs = refs[0], refs[1:]
    came_refs, refs = refs[: peers - 1], refs[peers - 1 :]
    x3, m_ref, self_ref, acc, ids_refs = refs[0], refs[1], refs[2], refs[3], refs[4:]
    _, columns, width = x3.shape
    put_rows(acc, self_rows(x3, m_ref, ask_ref))
    for s in range(CAP):
        add_sums(acc, pick(ask_ref, s), self_ref[:, s * width : (s + 1) * width])
    lane = lax.broadcasted_iota(jnp.int32, ids_refs[0].shape, 1)
    for k in range(1, peers):
        came = came_refs[k - 1]
        ids = jnp.zeros(lane.shape, jnp.int32)
        for s in range(CAP):
            here = slice(s * width, (s + 1) * width)
            asked = jnp.max(came[columns : columns + TAIL, here].astype(F32)).astype(jnp.int32)
            ids = jnp.where(lane == s, asked, ids)
            add_sums(acc, asked, came[:columns, here])
        ids_refs[k - 1][...] = ids


def first_rows(values, operator, ask, came, own_mirror, peers):
    _, columns, width = values.shape
    outs = call(
        functools.partial(first_rows_kernel, peers),
        "first_rows",
        [shape(values.shape, F32)] + [shape((1, width), jnp.int32)] * (peers - 1),
        [vmem()] * (peers + 3),
        flops=2 ** 27,
        moved=2 ** 20,
    )(ask, *came[1:], values, operator, own_mirror)
    return outs[0], [None] + list(outs[1:])


def below_kernel(sums_ref, half_ref, out_ref):
    top = sums_ref.shape[0]
    share, columns, width = half_ref.shape
    out_ref[:top, :] = sums_ref[...]
    for b in range(share):
        row, left = top + b // CAP * columns, b % CAP * width
        out_ref[row : row + columns, left : left + width] = half_ref[b]


def below(sums, half):
    share, columns, width = half.shape
    out = shape((sums.shape[0] + share // CAP * columns, sums.shape[1]), BF16)
    return call(below_kernel, "below", out, [vmem(), vmem()])(sums, half)


def stack_kernel(count, *refs):
    share = refs[0].shape[0]
    for k, ref in enumerate(refs[:count]):
        refs[-1][k * share : (k + 1) * share] = ref[...]


def stack(pieces, sums):
    share, columns, width = pieces[0].shape
    out = shape((len(pieces) * share, columns, width), BF16)
    kernel = functools.partial(stack_kernel, len(pieces))
    return call(kernel, "stack", out, [vmem()] * (len(pieces) + len(sums)), flops=2 ** 31)(*pieces, *sums)


def stack_more_kernel(first_ref, *refs):
    out_ref = refs[-1]
    at, columns, width = first_ref.shape
    out_ref[:at] = first_ref[...]
    for ref in refs[:-1]:
        share = (ref.shape[0] - TAIL) // columns * CAP - CAP
        for b in range(share):
            row, left = columns + TAIL + b // CAP * columns, b % CAP * width
            out_ref[at + b] = ref[row : row + columns, left : left + width]
        at += share


def stack_more(first, chunks):
    at, columns, width = first.shape
    share = (chunks[0].shape[0] - TAIL) // columns * CAP - CAP
    out = shape((at + len(chunks) * share, columns, width), BF16)
    return call(stack_more_kernel, "stack_more", out, [vmem()] * (1 + len(chunks)))(first, *chunks)


def half_rows(before, far_ref, m_ref, first, share):
    columns, width = before.shape[1:]
    both = CAP * width
    rows = pl.ds(pl.multiple_of(first * width, share * width), share * width)
    if m_ref.shape[1] <= GROUP * width:
        own = dot(far_ref[:, both:], m_ref[rows, both:], NT)
    else:

        def add_peer(k, total):
            here = pl.ds(pl.multiple_of(k * both, both), both)
            return total + dot(far_ref[:, here], m_ref[rows, here], NT)

        zeros = jnp.zeros((columns, share * width), F32)
        own = lax.fori_loop(1, m_ref.shape[1] // both, add_peer, zeros)
    return [before[first + b] + own[:, b * width : (b + 1) * width] for b in range(share)]


def give_rows_kernel(peers, *refs):
    ask_refs, refs = refs[: peers - 1], refs[peers - 1 :]
    before, mine_ref, other_ref, m_ref, give_ref, far_ref = refs
    share = give_ref.shape[0]
    both = CAP * before.shape[2]
    for k in range(1, peers):
        far_ref[:, k * both : (k + 1) * both] = far_of(share, mine_ref, other_ref, ask_refs[k - 1], k - 1)
    far_ref[:, :both] = jnp.zeros((far_ref.shape[0], both), BF16)
    rows = half_rows(before, far_ref, m_ref, (1 - lax.axis_index("rep")) * share, share)
    for b in range(share):
        give_ref[b] = rows[b].astype(BF16)


def give_rows(before, asks, mine, other, operator, peers, reps):
    blocks_dev, columns, width = before.shape
    return call(
        functools.partial(give_rows_kernel, peers),
        "give_rows",
        [shape((blocks_dev // reps, columns, width), BF16), shape((columns, peers * CAP * width), BF16)],
        [vmem()] * (peers + 3),
        flops=2 ** 27,
        moved=2 ** 20,
    )(*asks[1:], before, mine, other, operator)


def keep_rows_kernel(before, far_ref, m_ref, keep_ref):
    share = keep_ref.shape[0]
    rows = half_rows(before, far_ref, m_ref, lax.axis_index("rep") * share, share)
    for b in range(share):
        keep_ref[b] = rows[b]


def keep_rows(before, far, operator, reps):
    blocks_dev, columns, width = before.shape
    return call(
        keep_rows_kernel,
        "keep_rows",
        shape((blocks_dev // reps, columns, width), F32),
        [vmem()] * 3,
        flops=2 ** 27,
        moved=2 ** 20,
    )(before, far, operator)


def late_self_kernel(ask_ref, x3, self_ref, m_ref, act_ref, shared_ref, acc, out_ref):
    width = x3.shape[2]
    put_rows(acc, self_rows(x3, m_ref, ask_ref))
    for s in range(CAP):
        add_sums(acc, pick(ask_ref, s), self_ref[:, s * width : (s + 1) * width])
    half = lax.axis_index("rep")
    blocks = act_ref.shape[0]
    out_ref[pl.ds(half * blocks, blocks)] = act_ref[...]
    for b in range(blocks):
        at = (blocks + b) * width
        out_ref[(1 - half) * blocks + b] = shared_ref[:, at : at + width]


def late_self(ask, values, own_mirror, operator, act, shared):
    return call(
        late_self_kernel,
        "late_self",
        [shape(values.shape, F32), shape(values.shape, BF16)],
        [vmem()] * 6,
        flops=2 ** 26,
    )(ask, values, own_mirror, operator, act, shared)


def late_rows_kernel(k, before, ids_ref, came_ref, m_ref, out_ref, acc):
    width = acc.shape[2]
    both = CAP * width
    put_rows(acc, own_rows(came_ref[:, both : 2 * both], m_ref, k), before)
    for s in range(CAP):
        add_sums(acc, pick(ids_ref, s), came_ref[:, s * width : (s + 1) * width])
    out_ref[...] = acc[...].astype(out_ref.dtype)


def late_rows(before, ids, came, operator, k, dtype):
    return call(
        functools.partial(late_rows_kernel, k),
        "late_rows",
        shape(before.shape, dtype),
        [vmem()] * 4,
        [pltpu.VMEM(before.shape, F32)],
        flops=2 ** 29,
    )(before, ids, came, operator)


def add_kernel(keep_ref, came_ref, out_ref):
    out_ref[...] = (keep_ref[...] + came_ref[...].astype(F32)).astype(BF16)


def add_up(keep, came):
    return call(add_kernel, "add_up", shape(came.shape, BF16), [vmem(), vmem()])(keep, came)


def widen_kernel(feats, *refs):
    out_ref = refs[feats]
    share, columns, width = refs[0].shape
    me = lax.axis_index("feat")
    for q in range(feats):
        rows = pl.ds(pl.multiple_of(lax.rem(me + q, feats) * columns, columns), columns)
        for b in range(share):
            out_ref[rows, b * width : (b + 1) * width] = refs[q][b]


def widen(parts):
    share, columns, width = parts[0].shape
    out = shape((len(parts) * columns, share * width), BF16)
    return call(functools.partial(widen_kernel, len(parts)), "widen", out, [vmem()] * len(parts))(*parts)


def dense_kernel(feats, *refs):
    sums, wide_cot, refs = refs[:feats], refs[feats], refs[feats + 1 :]
    w_ref, act_ref, give_ref, spread_ref, term_ref, wide, pre_scr, grad = refs
    share, columns, width = act_ref.shape
    me = lax.axis_index("feat")
    rows = [pl.ds(pl.multiple_of(lax.rem(me + q, feats) * columns, columns), columns) for q in range(feats)]
    for q in range(feats):
        for b in range(share):
            wide[rows[q], b * width : (b + 1) * width] = sums[q][b]
    pre = dot(w_ref[...], wide[...], TN)
    pre_scr[...] = pre
    sig = jax.nn.sigmoid(pre)
    factor = wide_cot[...].astype(F32) * sig * (1.0 + pre * (1.0 - sig))
    grad[...] = factor.astype(BF16)
    spread = dot(w_ref[rows[0], :], grad[...]).astype(BF16)
    term_ref[...] = dot(grad[rows[0], :], wide[...], NT).astype(BF16)
    wide_share = share * width
    give_ref[:, :wide_share] = spread
    for b in range(share):
        spread_ref[b] = spread[:, b * width : (b + 1) * width]
    own = pre_scr[rows[0], :]
    act = (own * jax.nn.sigmoid(own)).astype(BF16)
    give_ref[:, wide_share:] = act
    for b in range(share):
        act_ref[b] = act[:, b * width : (b + 1) * width]


def dense(sums, cot, weight, feats):
    share, columns, width = sums[0].shape
    features = weight.shape[0]
    return call(
        functools.partial(dense_kernel, feats),
        "dense",
        [
            shape((share, columns, width), BF16),
            shape((columns, 2 * share * width), BF16),
            shape((share, columns, width), BF16),
            shape((columns, features), BF16),
        ],
        [vmem()] * (feats + 2),
        [
            pltpu.VMEM((features, share * width), BF16),
            pltpu.VMEM((features, share * width), F32),
            pltpu.VMEM((features, share * width), BF16),
        ],
        flops=2 ** 28,
        moved=2 ** 20,
    )(*sums, cot, weight)


def send_kernel(peers, *refs):
    ids_refs, refs = refs[: peers - 1], refs[peers - 1 :]
    mine_ref, came_ref, m_ref, refs = refs[0], refs[1], refs[2], refs[3:]
    x3, refs = refs[0], refs[1:]
    send_refs, refs = refs[: peers - 1], refs[peers - 1 :]
    self_ref, mir = refs
    share, _, width = mine_ref.shape
    both = CAP * width
    half = lax.axis_index("rep")
    x3[pl.ds(half * share, share)] = mine_ref[...]
    for b in range(share):
        x3[(1 - half) * share + b] = came_ref[:, b * width : (b + 1) * width]
    mirrored(lanes(x3), m_ref, mir, peers * CAP, width)
    self_ref[...] = mir[:, :both]
    for k in range(1, peers):
        out = send_refs[k - 1]
        out[:, :both] = mir[:, k * both : (k + 1) * both].astype(BF16)
        for s in range(CAP):
            at = (CAP + s) * width
            out[:, at : at + width] = x3[pick(ids_refs[k - 1], s)]


def sends_of(mine, came, operator, ids, peers, reps):
    share, columns, width = mine.shape
    chunk = 2 * CAP * width
    outs = call(
        functools.partial(send_kernel, peers),
        "sends",
        [shape((share * reps, columns, width), BF16)]
        + [shape((columns, chunk), BF16)] * (peers - 1)
        + [shape((columns, CAP * width), F32)],
        [vmem()] * (peers + 2),
        [pltpu.VMEM((columns, peers * CAP * width), F32)],
        flops=2 ** 28,
        moved=2 ** 21,
    )(*ids[1:], mine, came, operator)
    return outs[0], [None] + list(outs[1:peers]), outs[peers]


def pair_kernel(at, mine_ref, came_ref, out_ref):
    out_ref[...] = (mine_ref[...].astype(F32) + came_ref[:, at:].astype(F32)).astype(out_ref.dtype)


def pair_sum(mine, came, dtype, at=0):
    kernel = functools.partial(pair_kernel, at)
    return call(kernel, "pair_sum", shape(mine.shape, dtype), [vmem(), vmem()])(mine, came)


def beside_kernel(chunk_ref, term_ref, out_ref):
    width = chunk_ref.shape[1]
    out_ref[:, :width] = chunk_ref[...]
    out_ref[:, width:] = term_ref[...]


def beside(chunk, term):
    out = shape((chunk.shape[0], chunk.shape[1] + term.shape[1]), BF16)
    return call(beside_kernel, "beside", out, [vmem(), vmem()])(chunk, term)


def split_kernel(mine_ref, came_ref, give_ref, keep_ref, total):
    half = lax.axis_index("rep")
    part = keep_ref.shape[1]
    total[...] = mine_ref[...].astype(F32) + came_ref[...].astype(F32)
    give_ref[...] = total[:, pl.ds(pl.multiple_of((1 - half) * part, part), part)].astype(BF16)
    keep_ref[...] = total[:, pl.ds(pl.multiple_of(half * part, part), part)]


def split_sum(mine, came, reps):
    columns, features = mine.shape
    part = (columns, features // reps)
    return call(
        split_kernel,
        "split_sum",
        [shape(part, BF16), shape(part, F32)],
        [vmem()] * 2,
        [pltpu.VMEM(mine.shape, F32)],
    )(mine, came)


def half_term(term, peers, reps):
    give, total = split_sum(term, across(term, peers, 1), reps)
    total = pair_sum(total, ahead(give, "rep", reps, 1), BF16)
    bit = 2
    while 2 * bit < peers:
        total = pair_sum(total, across(total, peers, bit), BF16)
        bit *= 2
    return total


def finish_kernel(mine_ref, other_ref, share_ref, other_share_ref, grad_ref, weight_ref):
    half = lax.axis_index("rep")
    share = share_ref.shape[1]
    grad_ref[...] = (mine_ref[...].astype(F32) + other_ref[...].astype(F32)).astype(BF16)
    weight_ref[pl.ds(pl.multiple_of(half * share, share), share), :] = share_ref[...].T
    weight_ref[pl.ds(pl.multiple_of((1 - half) * share, share), share), :] = other_share_ref[...].T


def finish(mine, other, share, other_share):
    columns, width = share.shape
    return call(
        finish_kernel,
        "finish",
        [shape(mine.shape, BF16), shape((2 * width, columns), F32)],
        [vmem()] * 4,
    )(mine, other, share, other_share)


def ahead(value, axis, size, k):
    return lax.ppermute(value, axis, [(i, (i + k) % size) for i in range(size)])


def across(value, peers, k):
    return lax.ppermute(value, "graph", [(i, i ^ k) for i in range(peers)])


def after(value, first):
    return lax.optimization_barrier((value, first))[0]


def local(features, weight, cotangent, tiles, tile_row, tile_col, tile_count):
    blocks_dev, _, width = features.shape
    peers = lax.axis_size("graph")
    feats = lax.axis_size("feat")
    reps = lax.axis_size("rep")
    far_first = sorted(range(1, peers), key=lambda k: (-(k & (peers // 2)), k))

    half, table = prepare(features, tile_row, tile_col, peers, reps)
    operator, asks = list_operator(tiles, table, tile_count, peers, blocks_dev)
    sends, own_mirror, own_cot = first_sends(features, cotangent, operator, asks[1:], peers, reps)
    middle = peers // 2
    pieces = [across(half, peers, j) for j in range(1, middle)]
    crossed = across(half, peers, middle)
    came = [None] * peers
    for k in far_first:
        if k >= middle:
            came[k] = across(sends[k], peers, k)
    for j in range(1, middle):
        chunk, pieces[j - 1] = lax.optimization_barrier((below(sends[j], crossed), pieces[j - 1]))
        came[j] = across(chunk, peers, j)
    held = after(own_cot, crossed)
    cots = [own_cot] + [ahead(held, "feat", feats, feats - q) for q in range(1, feats)]
    stacked = stack(pieces + [crossed], came[middle:])
    came[1:middle], stacked = lax.optimization_barrier((came[1:middle], stacked))
    stacked, cots = lax.optimization_barrier((stacked, cots))
    stacked = stack_more(stacked, came[1:middle])
    swapped = ahead(stacked, "rep", reps, 1)
    acc, ids = first_rows(features, operator, asks[0], came, own_mirror, peers)
    give, asked = give_rows(acc, asks, stacked, swapped, operator, peers, reps)
    keep = keep_rows(acc, asked, operator, reps)

    mine = add_up(keep, ahead(give, "rep", reps, 1))
    cot = widen(cots)
    sums = [mine] + [ahead(mine, "feat", feats, feats - q) for q in range(1, feats)]
    act, give, spread, term = dense(sums, cot, weight, feats)
    shared = ahead(give, "rep", reps, 1)
    term = half_term(term, peers, reps)
    values, sends, own_mirror = sends_of(spread, shared, operator, ids, peers, reps)

    *firsts, last = sorted(range(1, peers), key=lambda k: (k == peers - 1, -(k & middle), k))
    sends[last] = beside(sends[last], term)
    came = [None] + [across(sends[k], peers, k) for k in range(1, peers)]
    acc, activated = late_self(asks[0], values, own_mirror, operator, act, shared)
    for k in firsts:
        acc = late_rows(acc, ids[k], came[k], operator, k, F32)
    part = late_rows(acc, ids[last], came[last], operator, last, BF16)
    total = pair_sum(term, came[last], F32, 2 * CAP * width)
    input_grad, weight_grad = finish(
        part, ahead(part, "rep", reps, 1), total, ahead(total, "rep", reps, 1)
    )
    return (activated, input_grad, weight_grad)


def solution(mesh):
    placed = (
        P(("parts", "graph"), "feat", None),
        P(),
        P(("parts", "graph"), "feat", None),
        P(("parts", "graph", "rep"), None, None),
        P(("parts", "graph", "rep")),
        P(("parts", "graph", "rep")),
        P(("parts", "graph", "rep")),
    )
    return jax.shard_map(
        local,
        mesh=mesh,
        in_specs=placed,
        out_specs=(
            P(("parts", "graph"), "feat", None),
            P(("parts", "graph"), "feat", None),
            P("parts", "feat"),
        ),
        check_vma=False,
    )
```
